32 devices in a mesh: replica: 2 (over x), tile: 16 (over z, y, core).
Axes of the slice: x: 2, y: 2, z: 4, core: 2. Of those that a mesh axis runs over, the one named last changes fastest.
Arguments:
- fields: bfloat16 [2, 64, 64, 8, 128], P('replica', None, 'tile'), may hold values from -6 to 6
- convolution_weight: bfloat16 [64, 1728], replicated, may hold values from -0.15625 to 0.15625
- convolution_bias: float32 [64], replicated, may hold values from -3 to 3
- query_owner: int32 [2, 2048, 1], P('replica', 'tile'), may hold values from 0 to 15; in each aligned block of 128 rows (0 to 127, 128 to 255, ..., all dimensions but the last counted through in order) at most 16 rows name the same one
- query_cell: int32 [2, 2048], P('replica', 'tile'), may hold values from 0 to 4095
- query_frac: float32 [2, 3, 2048], P('replica', None, 'tile'), may hold values from 0 to 1
- target: float32 [2, 5, 2048], P('replica', None, 'tile'), may hold values from -6 to 6
- w_latent: float32 [64, 512], replicated, may hold values from -3 to 3
- w_pos: float32 [3, 512], replicated, may hold values from -3.5 to 3.5
- bias_one: float32 [512], replicated, may hold values from -2 to 2
- w_mid: float32 [512, 512], replicated, may hold values from -0.5 to 0.5
- bias_two: float32 [512], replicated, may hold values from -2 to 2
- w_out: float32 [5, 512], replicated, may hold values from -0.25 to 0.25
- bias_out: float32 [5], replicated, may hold values from -3 to 3
Outputs:
- prediction: float32 [2, 5, 2048], P('replica', None, 'tile')
- grad_latent: float32 [64, 512], replicated
- grad_pos: float32 [3, 512], replicated
- grad_bias_one: float32 [512], replicated
- grad_mid: float32 [512, 512], replicated
- grad_bias_two: float32 [512], replicated
- grad_out: float32 [5, 512], replicated
- grad_bias_out: float32 [5], replicated
- loss: float32 [], replicated
The draws below stay inside these ranges and needn't reach their ends.
Inputs may be any that keep to these rules, and one draw needn't show every extreme that they name: `query_owner`: among the query points of one device, no tile is named more than 16 times; in every draw some device names some tile exactly 16 times.
All inputs are finite; a program needn't handle non-finite values.
Results may differ from the reference program's by a relative error of at most 0.0009.
The reference program's roundings to bfloat16 on the way count: a program that leaves them out, or rounds other values in their place, can miss the bound.
Values may be sent and summed in bfloat16 or wider, within the bound.
No kernel may reach another device: no remote copies, remote signals or barrier semaphores. Data moves between devices by JAX's collectives and lax.ppermute only.
A program may use at most 64 MiB of HBM per device.

```python
import math
import jax
import jax.numpy as jnp
import numpy as np
from jax import lax

C = 64
H = 512
DILATION_RATE = 2
NY = 8
NZ = 128
CX = 4
Q_DEV = 128
SNAPS = 2
NX = 64
QTOT = 2048
CAP = 16
N_TILE = 16


def place_ends(array, key, least, high):
    longest = array.shape.index(max(array.shape))
    spots = []
    for shift in (0, 1):
        where = [jax.random.randint(jax.random.fold_in(key, axis), (), 0, length) for axis, length in enumerate(array.shape)]
        where[longest] = (where[longest] + shift) % array.shape[longest]
        spots.append(tuple(where))
    return array.at[spots[0]].set(least).at[spots[1]].set(high)


def block_scale(stream_key, dims, cuts, low, top_value):
    gain, own = 1.0, jax.random.fold_in(stream_key, 6)
    for dim, shards_of in cuts:
        draws = jnp.exp(jax.random.uniform(jax.random.fold_in(own, dim), (shards_of,), jnp.float32, low / len(cuts), top_value / len(cuts)))
        gain = gain * jnp.repeat(draws, dims[dim] // shards_of).reshape([-1 if axis == dim else 1 for axis in range(len(dims))])
    return gain


def routed_block(rng, own, number, rows, amount, top, limit, lean):
    ranking = jax.random.permutation(rng, amount)
    heavy_load, common = shares(amount, rows * top, limit, lean, True), shares(amount, rows * top, limit, lean, False)
    places = jnp.arange(amount)

    def named(sizes, rotation):
        used = int((sizes > 0).sum())
        fixed = max(1, used // 4)
        passed = fixed + (places - fixed + rotation * (used - fixed)) % max(1, amount - fixed)
        return jnp.zeros((amount,), jnp.int32).at[ranking[jnp.where(places < fixed, places, passed)]].set(jnp.asarray(sizes, jnp.int32))

    sizes = jnp.where(number % 4 == 0, named(heavy_load, number // 4), named(common, number - number // 4 - 1))
    mixed = jax.random.permutation(jax.random.fold_in(own, 3), amount)
    giver, receiver = mixed[0:amount // 2 * 2:2], mixed[1:amount // 2 * 2:2]
    room = jnp.minimum(sizes[giver] - 1, limit - sizes[receiver]) // 2
    room = jnp.where((giver == ranking[0]) | (receiver == ranking[0]) | (sizes[receiver] == 0), 0, jnp.maximum(room, 0))
    passed = jax.random.randint(jax.random.fold_in(own, 4), (amount // 2,), 0, 1 << 20) % (room + 1)
    sizes = sizes.at[giver].add(-passed).at[receiver].add(passed)
    members = jnp.searchsorted(jnp.cumsum(sizes), jnp.arange(rows * top), side="right").astype(jnp.int32)
    listing = members.reshape(top, rows).T
    listing = listing[jax.random.permutation(jax.random.fold_in(own, 1), rows)]
    rotation = jax.random.randint(jax.random.fold_in(own, 2), (rows, 1), 0, top)
    return jnp.take_along_axis(listing, (jnp.arange(top)[None, :] + rotation) % top, axis=1)


def shares(number_of, total, most, lean, full):
    loads = [(1 << 20) // math.isqrt(grade ** lean) + 1 for grade in range(1, number_of + 1)]
    largest = most if full else min(most, max(-(-total // number_of), total * loads[0] // sum(loads)))
    least = 1 if total - largest >= number_of - 1 else 0
    given, spare = [largest] + [least] * (number_of - 1), total - largest - least * (number_of - 1)
    while spare > 0:
        movable = [i for i in range(1, number_of) if given[i] < largest] or [i for i in range(1, number_of) if given[i] < most]
        pool, budget = sum([loads[i] for i in movable]), spare
        for i in movable:
            more = min(most - given[i], max(1, budget * loads[i] // pool), spare)
            given[i] = given[i] + more
            spare = spare - more
    return np.array(given)


def bell_draw(rng, shape, spread, bound, cuts=(), kind=jnp.bfloat16):
    level = block_scale(rng, shape, cuts, -0.22, 0.18) if cuts else 1.0
    entries = jax.random.normal(rng, shape, jnp.float32) * spread * level
    return jnp.minimum(jnp.maximum(entries, -bound), bound).astype(kind)


def setup_inputs(seed: int = 0) -> dict:
    key_of = jax.random.split(jax.random.key(seed), 15)
    fields = bell_draw(key_of[0], (SNAPS, C, NX, NY, NZ), 1.0, 6.0, ((0, 2), (2, 16)))
    convolution_weight = bell_draw(key_of[1], (C, 27 * C), (27 * C) ** -0.5, 0.15625)
    convolution_bias = bell_draw(key_of[2], (C,), 0.5, 3.0, (), jnp.float32)
    query_owner_keys = jax.random.split(jax.random.fold_in(key_of[3], 1), SNAPS * QTOT // Q_DEV)
    query_owner_turns = jax.random.permutation(jax.random.fold_in(key_of[3], 3), SNAPS * QTOT // Q_DEV)
    query_owner = jax.vmap(lambda own, number: routed_block(jax.random.fold_in(key_of[3], 2), own, number, Q_DEV, N_TILE, 1, CAP, 2))(query_owner_keys, query_owner_turns).reshape((SNAPS, QTOT, 1))
    query_cell = place_ends(jax.random.randint(key_of[4], (SNAPS, QTOT), 0, CX * NY * NZ), jax.random.fold_in(key_of[4], 1), 0, (CX * NY * NZ) - 1).astype(jnp.int32)
    query_frac = jnp.clip(1.0 * jax.random.uniform(key_of[5], (SNAPS, 3, QTOT), jnp.float32) ** block_scale(key_of[5], (SNAPS, 3, QTOT), ((0, 2), (2, 16)), -0.2, 0.2), 0.0, 1.0)
    target = bell_draw(key_of[6], (SNAPS, 5, QTOT), 1.0, 6.0, ((0, 2), (2, 16)), jnp.float32)
    w_latent = bell_draw(key_of[7], (C, H), (C // 16) ** -0.5, 3.0, (), jnp.float32)
    w_pos = bell_draw(key_of[8], (3, H), 3 ** -0.5, 3.5, (), jnp.float32)
    bias_one = jnp.clip(jax.random.uniform(key_of[9], (H,), jnp.float32, -2.0, 2.0), -2.0, 2.0)
    w_mid = bell_draw(key_of[10], (H, H), (H // 4) ** -0.5, 0.5, (), jnp.float32)
    bias_two = jnp.clip(jax.random.uniform(key_of[11], (H,), jnp.float32, -2.0, 2.0), -2.0, 2.0)
    w_out = bell_draw(key_of[12], (5, H), H ** -0.5, 0.25, (), jnp.float32)
    bias_out = bell_draw(key_of[13], (5,), 0.5, 3.0, (), jnp.float32)
    return {"fields": fields, "convolution_weight": convolution_weight, "convolution_bias": convolution_bias, "query_owner": query_owner, "query_cell": query_cell, "query_frac": query_frac, "target": target, "w_latent": w_latent, "w_pos": w_pos, "bias_one": bias_one, "w_mid": w_mid, "bias_two": bias_two, "w_out": w_out, "bias_out": bias_out}


VISCOSITY = 0.05
DIFFUSIVITY = 0.05
RESIDUAL_WEIGHT = 0.5

def corner_index(start_x, start_y, start_z, span_x, span_y, span_z):
    listed = []
    for corner in range(8):
        high_x = corner // 4
        high_y = corner // 2 % 2
        high_z = corner % 2
        listed.append((start_x + high_x) % span_x * (span_y * span_z) + (start_y + high_y) % span_y * span_z + (start_z + high_z) % span_z)
    return jnp.stack(listed, axis=0)

def corner_weight(fraction):
    frac_x, frac_y, frac_z = (fraction[0], fraction[1], fraction[2])
    listed = []
    for corner in range(8):
        part_x = frac_x if corner // 4 == 1 else 1.0 - frac_x
        part_y = frac_y if corner // 2 % 2 == 1 else 1.0 - frac_y
        part_z = frac_z if corner % 2 == 1 else 1.0 - frac_z
        listed.append(part_x * part_y * part_z)
    return jnp.stack(listed, axis=0).astype(jnp.bfloat16)

def make_position(global_x, start_y, start_z, fraction, span_x, span_y, span_z):
    return jnp.stack([(global_x.astype(jnp.float32) + fraction[0]) / span_x, (start_y.astype(jnp.float32) + fraction[1]) / span_y, (start_z.astype(jnp.float32) + fraction[2]) / span_z], axis=1)

def tanh_jet(pre_act, tangent, second):
    activation = jnp.tanh(pre_act)
    slope_one = 1.0 - activation * activation
    curvature = -2.0 * activation * slope_one
    return (activation, slope_one[None] * tangent, slope_one[None] * second + curvature[None] * tangent * tangent)

def decode(params, latent_code, position):
    w_latent, w_pos, bias_one, w_mid, bias_two, w_out, bias_out = params
    highest = lax.Precision.HIGHEST
    row_count = latent_code.shape[0]
    hidden_width = w_mid.shape[0]
    first_sum = jnp.dot(latent_code, w_latent, precision=highest) + jnp.dot(position, w_pos, precision=highest) + bias_one
    tangent = jnp.broadcast_to(w_pos[:, None, :], (3, row_count, hidden_width))
    second = jnp.zeros((3, row_count, hidden_width), jnp.float32)
    activation, tangent, second = tanh_jet(first_sum, tangent, second)
    stacked = jnp.concatenate([activation[None], tangent, second], axis=0).reshape(7 * row_count, hidden_width)
    mixed_jet = jnp.dot(stacked, w_mid, precision=highest).reshape(7, row_count, hidden_width)
    activation, tangent, second = tanh_jet(mixed_jet[0] + bias_two, mixed_jet[1:4], mixed_jet[4:7])
    stacked = jnp.concatenate([activation[None], tangent, second], axis=0).reshape(7 * row_count, hidden_width)
    result_jet = jnp.dot(stacked, w_out.T, precision=highest).reshape(7, row_count, 5)
    return (result_jet[0] + bias_out, result_jet[1:4], result_jet[4:7])

def point_loss(params, latent_code, position, target_rows, query_total):
    value, first_jet, second_jet = decode(params, latent_code, position)
    laplace = lax.optimization_barrier(jnp.sum(second_jet, axis=0))
    velocity = value[:, 2:5]
    advection = lax.optimization_barrier(jnp.sum(velocity.T[:, :, None] * first_jet, axis=0))
    continuity = first_jet[0][:, 2] + first_jet[1][:, 3] + first_jet[2][:, 4]
    pressure = jnp.stack([first_jet[0][:, 1], first_jet[1][:, 1], first_jet[2][:, 1]], axis=1)
    momentum = advection[:, 2:5] + pressure - VISCOSITY * laplace[:, 2:5]
    momentum = momentum - jnp.concatenate([jnp.zeros_like(value[:, :2]), value[:, 0:1]], axis=1)
    energy = advection[:, 0] - DIFFUSIVITY * laplace[:, 0]
    misfit = lax.optimization_barrier(jnp.sum((value - target_rows) * (value - target_rows), axis=1))
    physics = continuity * continuity + lax.optimization_barrier(jnp.sum(momentum * momentum, axis=1)) + energy * energy
    return (jnp.sum(misfit + RESIDUAL_WEIGHT * physics) / query_total, value)

def reference(fields, convolution_weight, convolution_bias, query_owner, query_cell, query_frac, target, w_latent, w_pos, bias_one, w_mid, bias_two, w_out, bias_out):

    def encode(snapshot_frame):
        summed = jnp.zeros((C, NX * NY * NZ), jnp.float32)
        for spacing_along_x in (-1, 0, 1):
            for spacing_along_y in (-1, 0, 1):
                for spacing_along_z in (-1, 0, 1):
                    tap_index = 9 * (spacing_along_x + 1) + 3 * (spacing_along_y + 1) + spacing_along_z + 1
                    shifted_field = jnp.roll(snapshot_frame, (-DILATION_RATE * spacing_along_x, -spacing_along_y, -spacing_along_z), axis=(1, 2, 3))
                    summed = summed + jnp.dot(convolution_weight[:, tap_index * C:(tap_index + 1) * C], shifted_field.reshape(C, NX * NY * NZ), preferred_element_type=jnp.float32)
        return jax.nn.gelu(summed + convolution_bias[:, None]).astype(jnp.bfloat16)
    latent_all = lax.map(encode, fields)
    blocks = SNAPS * N_TILE
    owner_tile = query_owner[:, :, 0].reshape(blocks, Q_DEV)
    base_cell = query_cell.reshape(blocks, Q_DEV)
    fraction = query_frac.reshape(SNAPS, 3, N_TILE, Q_DEV).transpose(0, 2, 1, 3).reshape(blocks, 3, Q_DEV)
    target_rows = target.reshape(SNAPS, 5, N_TILE, Q_DEV).transpose(0, 2, 3, 1).reshape(blocks, Q_DEV, 5)
    snap_ids = (jnp.arange(blocks, dtype=jnp.int32) // N_TILE).astype(jnp.int32)

    def interpolate(inputs):
        owner, base, frac, snap = inputs
        global_x = owner * CX + base // (NY * NZ)
        start_y = base // NZ % NY
        start_z = base % NZ
        corner_cells = corner_index(global_x, start_y, start_z, NX, NY, NZ)
        weights = corner_weight(frac)
        corner_rows = latent_all[snap][:, corner_cells]
        blended = lax.optimization_barrier(jnp.sum(corner_rows.astype(jnp.float32) * weights.astype(jnp.float32)[None], axis=1)).astype(jnp.bfloat16)
        return (blended.T, make_position(global_x, start_y, start_z, frac, NX, NY, NZ))
    interp_all, position_all = lax.map(interpolate, (owner_tile, base_cell, fraction, snap_ids))
    params = (w_latent, w_pos, bias_one, w_mid, bias_two, w_out, bias_out)
    query_total = float(SNAPS * QTOT)

    def accumulate(carry, inputs):
        latent_rows, position, block_target = inputs

        def local_loss(weights_all):
            return point_loss(weights_all, latent_rows.astype(jnp.float32), position, block_target, query_total)
        loss_value, pullback, value = jax.vjp(local_loss, params, has_aux=True)
        gradients = pullback(jnp.ones((), jnp.float32))[0]
        merged = tuple((left + right for left, right in zip(carry[0], gradients)))
        return ((merged, carry[1] + loss_value), value)
    start_carry = (tuple((jnp.zeros_like(weight_array) for weight_array in params)), jnp.zeros((), jnp.float32))
    (gradients, loss_value), values = lax.scan(accumulate, start_carry, (interp_all, position_all, target_rows))
    prediction = values.reshape(SNAPS, N_TILE, Q_DEV, 5).transpose(0, 3, 1, 2).reshape(SNAPS, 5, QTOT)
    return (prediction, gradients[0], gradients[1], gradients[2], gradients[3], gradients[4], gradients[5], gradients[6], loss_value)
```

```python
import functools

import jax
import jax.numpy as jnp
from jax import lax
from jax.experimental import pallas as pl
from jax.experimental.pallas import tpu as pltpu
from jax.sharding import PartitionSpec as P

DILATION_RATE = 2
VISCOSITY = 0.05
DIFFUSIVITY = 0.05
RESIDUAL_WEIGHT = 0.5

F32 = jnp.float32
BF16 = jnp.bfloat16
LANES = 128
BLOCK = 32
WORDS = 128
MISC = 16
NN = (((1,), (0,)), ((), ()))
NT = (((1,), (1,)), ((), ()))
TN = (((0,), (0,)), ((), ()))
VMEM = pl.BlockSpec(memory_space=pltpu.VMEM)
SMEM = pl.BlockSpec(memory_space=pltpu.SMEM)


def mul(left, right, dims=NN):
    return lax.dot_general(left, right, dims, preferred_element_type=F32)


def halves(value):
    high = value.astype(BF16)
    return high, (value - high.astype(F32)).astype(BF16)


def thirds(value):
    high = value.astype(BF16)
    rest = value - high.astype(F32)
    middle = rest.astype(BF16)
    return high, middle, (rest - middle.astype(F32)).astype(BF16)


def mul3(left, right, dims=NN):
    return mul(left[0], right[0], dims) + mul(left[0], right[1], dims) + mul(left[1], right[0], dims)


def route_kernel(tiles, slots, owner_ref, cell_ref, frac_ref, target_ref, out_ref, words):
    queries = owner_ref.shape[1]
    owner = owner_ref[...]
    hits = (lax.broadcasted_iota(jnp.int32, (tiles, queries), 0) == owner).astype(F32)
    before = lax.broadcasted_iota(jnp.int32, (queries, queries), 0) < lax.broadcasted_iota(
        jnp.int32, (queries, queries), 1
    )
    earlier = mul(hits.astype(BF16), before.astype(F32).astype(BF16))
    slot = jnp.sum(hits * earlier, axis=0, keepdims=True)
    place = owner * slots + slot.astype(jnp.int32)
    chosen = (lax.broadcasted_iota(jnp.int32, (tiles * slots, queries), 0) == place).astype(F32).astype(BF16)
    words[...] = jnp.zeros_like(words)
    words[0:1, :] = cell_ref[...].astype(F32)
    words[1:4, :] = frac_ref[...]
    words[4:9, :] = target_ref[...]
    words[9:10, :] = jnp.ones((1, queries), F32)
    words[10:11, :] = lax.broadcasted_iota(jnp.int32, (1, queries), 1).astype(F32)
    high, middle, low = thirds(words[...])
    out_ref[...] = mul(chosen, high, NT) + mul(chosen, middle, NT) + mul(chosen, low, NT)


def route(owner, cell, frac, target, tiles, slots):
    queries = owner.shape[1]
    return pl.pallas_call(
        functools.partial(route_kernel, tiles, slots),
        out_shape=jax.ShapeDtypeStruct((tiles * slots, WORDS), F32),
        in_specs=[VMEM] * 4,
        out_specs=VMEM,
        scratch_shapes=[pltpu.VMEM((WORDS, queries), F32)],
        name="route",
    )(owner, cell, frac, target)


def convolve(left_ref, here_ref, right_ref, weight_ref, bias_ref, lat):
    planes, rows_y = here_ref.shape[0], here_ref.shape[1]
    channels = here_ref.shape[2]
    behind = left_ref.shape[0]

    def plane(index):
        if index < behind:
            return left_ref, index
        if index < behind + planes:
            return here_ref, index - behind
        return right_ref, index - behind - planes

    weight = weight_ref[...]
    bias = bias_ref[...]
    for x in range(planes + 1):
        for pair in range(rows_y // 2):
            blocks = []
            for step_x in range(3):
                ref, index = plane(x + DILATION_RATE * step_x)
                for step_y in (-1, 0, 1):
                    blocks.append(
                        jnp.concatenate(
                            [ref[index, (2 * pair + half + step_y) % rows_y] for half in (0, 1)],
                            axis=1,
                        )
                    )
            partial = mul(weight, jnp.concatenate(blocks, axis=0))
            for half in (0, 1):
                part = partial[:, half * LANES : (half + 1) * LANES]
                summed = (
                    part[channels : 2 * channels]
                    + pltpu.roll(part[:channels], 1, 1)
                    + pltpu.roll(part[2 * channels :], LANES - 1, 1)
                    + bias
                )
                lat[x * (rows_y // 2) + pair, :, half * LANES : (half + 1) * LANES] = jax.nn.gelu(
                    summed
                ).astype(BF16)


def interpolate(words, lat, planes, rows_y, rows_z):
    rows = words.shape[0]
    cell = jnp.broadcast_to(words[:, 0:1], (rows, LANES)).astype(jnp.int32)
    frac = [jnp.broadcast_to(words[:, 1 + d : 2 + d], (rows, LANES)) for d in range(3)]
    shift_z = rows_z.bit_length() - 1
    shift_y = rows_y.bit_length() - 1
    base_x = cell >> (shift_z + shift_y)
    base_y = (cell >> shift_z) & (rows_y - 1)
    base_z = cell & (rows_z - 1)
    spot = lax.broadcasted_iota(jnp.int32, (rows, rows_z), 1)
    part_z = jnp.where(spot == base_z, 1.0 - frac[2], 0.0) + jnp.where(
        spot == ((base_z + 1) & (rows_z - 1)), frac[2], 0.0
    )
    total = None
    for x in range(planes + 1):
        part_x = jnp.where(base_x == x, 1.0 - frac[0], jnp.where(base_x == x - 1, frac[0], 0.0))
        for pair in range(rows_y // 2):
            sides = []
            for y in (2 * pair, 2 * pair + 1):
                part_y = jnp.where(
                    base_y == y, 1.0 - frac[1], jnp.where(base_y == (y - 1) % rows_y, frac[1], 0.0)
                )
                sides.append((part_x * part_y * part_z).astype(BF16))
            term = mul(jnp.concatenate(sides, axis=1), lat[x * (rows_y // 2) + pair], NT)
            total = term if total is None else total + term
    return total.astype(BF16), base_x, base_y, base_z, frac


def folded(value):
    return jnp.sum(value.reshape(value.shape[0] // 8, 8, value.shape[1]), axis=0)


def main_kernel(
    plan,
    place_ref,
    left_ref,
    here_ref,
    right_ref,
    conv_weight_ref,
    conv_bias_ref,
    words_ref,
    w_latent_ref,
    w_pos_ref,
    bias_one_ref,
    w_mid_ref,
    bias_two_ref,
    w_out_ref,
    bias_out_ref,
    send_ref,
    keep_ref,
    lat,
    code,
    pos,
    z_one,
    mid_high,
    mid_low,
    one_high,
    one_low,
    mixed,
    two_high,
    two_low,
    back,
    d_high,
    d_low,
    out_t,
    d_out_t,
    packed,
):
    rows = words_ref.shape[0]
    hidden = w_mid_ref.shape[0]
    latents = w_latent_ref.shape[0]
    planes, rows_y, rows_z = here_ref.shape[0], here_ref.shape[1], here_ref.shape[3]
    my_chunk = place_ref[0]
    my_tile = place_ref[1]
    my_replica = place_ref[2]

    convolve(left_ref, here_ref, right_ref, conv_weight_ref, conv_bias_ref, lat)
    words = words_ref[...]
    interp, base_x, base_y, base_z, frac = interpolate(words, lat, planes, rows_y, rows_z)
    code[...] = interp
    global_x = my_tile * planes + base_x
    lane = lax.broadcasted_iota(jnp.int32, (rows, LANES), 1)
    pos[...] = jnp.where(
        lane == 0,
        (global_x.astype(F32) + frac[0]) / (planes * plan.tiles),
        jnp.where(
            lane == 1,
            (base_y.astype(F32) + frac[1]) / rows_y,
            (base_z.astype(F32) + frac[2]) / rows_z,
        ),
    )

    wl_high, wl_low = halves(w_latent_ref[...])
    z_one[...] = mul(interp, wl_high) + mul(interp, wl_low)
    high, low = halves(w_mid_ref[...])
    mid_high[...] = high
    mid_low[...] = low
    w_pos = [w_pos_ref[d : d + 1, :] for d in range(3)]
    square = w_pos[0] * w_pos[0] + w_pos[1] * w_pos[1] + w_pos[2] * w_pos[2]
    bias_one = bias_one_ref[...]
    bias_two = bias_two_ref[...]

    def store(index, block, refs, value):
        high, low = halves(value)
        refs[0][pl.ds(pl.multiple_of(index * rows + block * BLOCK, BLOCK), BLOCK), :] = high
        refs[1][pl.ds(pl.multiple_of(index * rows + block * BLOCK, BLOCK), BLOCK), :] = low

    def fetch(ref, index, block):
        return ref[pl.ds(pl.multiple_of(index * rows + block * BLOCK, BLOCK), BLOCK), :]

    def layer_one(block, carry):
        where = fetch(pos, 0, block)
        pre = (
            fetch(z_one, 0, block)
            + (where[:, 0:1] * w_pos[0] + where[:, 1:2] * w_pos[1] + where[:, 2:3] * w_pos[2])
            + bias_one
        )
        act = jnp.tanh(pre)
        slope = 1.0 - act * act
        curve = -2.0 * act * slope
        z_one[pl.ds(pl.multiple_of(block * BLOCK, BLOCK), BLOCK), :] = act
        refs = (one_high, one_low)
        store(0, block, refs, act)
        for d in range(3):
            store(1 + d, block, refs, slope * w_pos[d])
        store(4, block, refs, curve * square)
        return carry

    lax.fori_loop(0, rows // BLOCK, layer_one, 0)

    def times_mid(dims, source, result, index, carry):
        span = pl.ds(pl.multiple_of(index * rows, rows), rows)
        result[span, :] = mul3((source[0][span, :], source[1][span, :]), (mid_high[...], mid_low[...]), dims)
        return carry

    lax.fori_loop(0, 5, functools.partial(times_mid, NN, (one_high, one_low), mixed), 0)

    def layer_two(block, carry):
        act = jnp.tanh(fetch(mixed, 0, block) + bias_two)
        slope = 1.0 - act * act
        curve = -2.0 * act * slope
        refs = (two_high, two_low)
        store(0, block, refs, act)
        mixed[pl.ds(pl.multiple_of(block * BLOCK, BLOCK), BLOCK), :] = act
        norm = None
        for d in range(3):
            tangent = fetch(mixed, 1 + d, block)
            store(1 + d, block, refs, slope * tangent)
            norm = tangent * tangent if norm is None else norm + tangent * tangent
        store(4, block, refs, slope * fetch(mixed, 4, block) + curve * norm)
        return carry

    lax.fori_loop(0, rows // BLOCK, layer_two, 0)

    out_fields = jnp.concatenate([w_out_ref[...], jnp.zeros((3, hidden), F32)], axis=0)
    wo_high, wo_low = halves(out_fields)
    wo_both = jnp.concatenate([out_fields, wo_low.astype(F32)], axis=0).astype(BF16)
    for s in range(5):
        span = slice(s * rows, (s + 1) * rows)
        both = mul(wo_both, two_high[span, :], NT)
        out_t[8 * s : 8 * s + 8, :] = both[:8] + both[8:] + mul(wo_high, two_low[span, :], NT)

    words_t = words.T
    target = [words_t[4 + f : 5 + f, :] for f in range(5)]
    valid = words_t[9:10, :]
    value = [out_t[f : f + 1, :] + bias_out_ref[f] for f in range(5)]
    grad = [[out_t[8 * (d + 1) + f : 8 * (d + 1) + f + 1, :] for f in range(5)] for d in range(3)]
    laplace = [out_t[32 + f : 33 + f, :] for f in range(5)]
    velocity = value[2:5]
    advection = [
        velocity[0] * grad[0][f] + velocity[1] * grad[1][f] + velocity[2] * grad[2][f] for f in range(5)
    ]
    continuity = grad[0][2] + grad[1][3] + grad[2][4]
    momentum = [advection[2 + j] + grad[j][1] - VISCOSITY * laplace[2 + j] for j in range(3)]
    momentum[2] = momentum[2] - value[0]
    energy = advection[0] - DIFFUSIVITY * laplace[0]
    misfit = [value[f] - target[f] for f in range(5)]
    physics = (
        continuity * continuity
        + (momentum[0] * momentum[0] + momentum[1] * momentum[1] + momentum[2] * momentum[2])
        + energy * energy
    )
    squares = (
        misfit[0] * misfit[0]
        + misfit[1] * misfit[1]
        + misfit[2] * misfit[2]
        + misfit[3] * misfit[3]
        + misfit[4] * misfit[4]
    )
    point_loss = valid * (squares + RESIDUAL_WEIGHT * physics) * (1.0 / plan.query_total)

    rate = valid * (1.0 / plan.query_total)
    twice = RESIDUAL_WEIGHT * 2.0
    d_cont = rate * twice * continuity
    d_mom = [rate * twice * m for m in momentum]
    d_energy = rate * twice * energy
    d_value = [2.0 * rate * m for m in misfit]
    for d in range(3):
        d_value[2 + d] = d_value[2 + d] + (
            d_mom[0] * grad[d][2] + d_mom[1] * grad[d][3] + d_mom[2] * grad[d][4] + d_energy * grad[d][0]
        )
    d_value[0] = d_value[0] - d_mom[2]
    d_out_t[...] = jnp.zeros_like(d_out_t)
    for f in range(5):
        d_out_t[f : f + 1, :] = d_value[f]
    for d in range(3):
        first = 8 * (d + 1)
        d_out_t[first : first + 1, :] = d_energy * velocity[d]
        d_out_t[first + 1 : first + 2, :] = d_mom[d]
        for j in range(3):
            term = d_mom[j] * velocity[d]
            if j == d:
                term = term + d_cont
            d_out_t[first + 2 + j : first + 3 + j, :] = term
    d_out_t[32:33, :] = -DIFFUSIVITY * d_energy
    for j in range(3):
        d_out_t[34 + j : 35 + j, :] = -VISCOSITY * d_mom[j]

    for s in range(5):
        span = slice(s * rows, (s + 1) * rows)
        wanted = d_out_t[8 * s : 8 * s + 8, :]
        do_high, do_low = halves(wanted)
        back[span, :] = mul3((do_high, do_low), (wo_high, wo_low), TN)

    def second_back(block, total):
        act = fetch(mixed, 0, block)
        slope = 1.0 - act * act
        curve = -2.0 * act * slope
        tangent = [fetch(mixed, 1 + d, block) for d in range(3)]
        cot_t = [fetch(back, 1 + d, block) for d in range(3)]
        cot_l = fetch(back, 4, block)
        refs = (d_high, d_low)
        d_slope = cot_l * fetch(mixed, 4, block)
        norm = None
        bent = 2.0 * curve * cot_l
        for d in range(3):
            store(1 + d, block, refs, slope * cot_t[d] + bent * tangent[d])
            d_slope = d_slope + cot_t[d] * tangent[d]
            norm = tangent[d] * tangent[d] if norm is None else norm + tangent[d] * tangent[d]
        store(4, block, refs, slope * cot_l)
        d_curve = cot_l * norm
        d_slope = d_slope - 2.0 * act * d_curve
        d_act = fetch(back, 0, block) - 2.0 * slope * d_curve - 2.0 * act * d_slope
        d_pre = slope * d_act
        store(0, block, refs, d_pre)
        return total + folded(d_pre)

    grad_two = lax.fori_loop(0, rows // BLOCK, second_back, jnp.zeros((8, hidden), F32))

    packed[...] = jnp.zeros_like(packed)
    main_rows = hidden + latents + MISC
    wide = 2 * LANES
    for left in range(hidden // wide):
        for right in range(hidden // wide):
            lefts = slice(left * wide, (left + 1) * wide)
            rights = slice(right * wide, (right + 1) * wide)
            part = mul3(
                (one_high[:, lefts], one_low[:, lefts]), (d_high[:, rights], d_low[:, rights]), TN
            )
            for side in range(2):
                first = (2 * right + side) * main_rows + left * wide
                packed[first : first + wide, :] = part[:, side * LANES : (side + 1) * LANES]

    lax.fori_loop(0, 5, functools.partial(times_mid, NT, (d_high, d_low), back), 0)

    def first_back(block, totals):
        act = fetch(z_one, 0, block)
        slope = 1.0 - act * act
        curve = -2.0 * act * slope
        where = fetch(pos, 0, block)
        cot_t = [fetch(back, 1 + d, block) for d in range(3)]
        cot_l = fetch(back, 4, block)
        d_curve = cot_l * square
        d_slope = cot_t[0] * w_pos[0] + cot_t[1] * w_pos[1] + cot_t[2] * w_pos[2] - 2.0 * act * d_curve
        d_act = fetch(back, 0, block) - 2.0 * slope * d_curve - 2.0 * act * d_slope
        d_pre = slope * d_act
        store(0, block, (d_high, d_low), d_pre)
        sums = [totals[0] + folded(d_pre)]
        for d in range(3):
            sums.append(totals[1 + d] + folded(where[:, d : d + 1] * d_pre + slope * cot_t[d]))
        sums.append(totals[4] + folded(curve * cot_l))
        return tuple(sums)

    sums = lax.fori_loop(
        0, rows // BLOCK, first_back, tuple(jnp.zeros((8, hidden), F32) for _ in range(5))
    )
    d_square = jnp.sum(sums[4], axis=0, keepdims=True)
    grad_latent = mul(code[...], d_high[0:rows, :], TN) + mul(code[...], d_low[0:rows, :], TN)

    grad_out = None
    for s in range(5):
        span = slice(s * rows, (s + 1) * rows)
        wanted = d_out_t[8 * s : 8 * s + 8, :]
        do_high, do_low = halves(wanted)
        do_both = jnp.concatenate([wanted, do_low.astype(F32)], axis=0).astype(BF16)
        both = mul(do_both, two_high[span, :])
        term = both[:8] + both[8:] + mul(do_high, two_low[span, :])
        grad_out = term if grad_out is None else grad_out + term

    lane_row = lax.broadcasted_iota(jnp.int32, (1, hidden), 1)
    last = jnp.where(lane_row == 5, jnp.sum(point_loss), 0.0)
    for f in range(5):
        last = last + jnp.where(lane_row == f, jnp.sum(d_value[f]), 0.0)
    grad_pos = [jnp.sum(sums[1 + d], axis=0, keepdims=True) + 2.0 * w_pos[d] * d_square for d in range(3)]
    misc = grad_pos + [
        jnp.sum(sums[0], axis=0, keepdims=True),
        jnp.sum(grad_two, axis=0, keepdims=True),
        last,
    ]
    for part in range(hidden // LANES):
        lanes = slice(part * LANES, (part + 1) * LANES)
        first = part * main_rows + hidden
        packed[first : first + latents, :] = grad_latent[:, lanes]
        first = first + latents
        for number, row in enumerate(misc):
            packed[first + number : first + number + 1, :] = row[:, lanes]
        packed[first + 8 : first + 16, :] = grad_out[:, lanes]

    slots = rows // plan.tiles
    chosen = jnp.where(
        lane == jnp.broadcast_to(words[:, 10:11], (rows, LANES)).astype(jnp.int32), words[:, 9:10], 0.0
    ).astype(BF16)
    source = lax.broadcasted_iota(jnp.int32, (plan.tiles, rows), 0)
    inside = lax.broadcasted_iota(jnp.int32, (plan.tiles, rows), 1)
    mine = (inside >= source * slots) & (inside < (source + 1) * slots)
    for f in range(5):
        high, middle, low = thirds(jnp.where(mine, jnp.broadcast_to(value[f], (plan.tiles, rows)), 0.0))
        first = pl.multiple_of((hidden // LANES) * main_rows + f * plan.devices + my_replica * plan.tiles, 16)
        packed[pl.ds(first, plan.tiles), :] = mul(high, chosen) + mul(middle, chosen) + mul(low, chosen)

    half = plan.devices // 2
    chunk = plan.chunk
    my_half = my_chunk // half
    for number in range(plan.devices):
        spot = jnp.bitwise_xor(number, my_chunk) & (half - 1)

        @pl.when(my_half == number // half)
        def _():
            keep_ref[spot] = packed[number * chunk : (number + 1) * chunk, :]

        @pl.when(my_half != number // half)
        def _():
            send_ref[spot] = packed[number * chunk : (number + 1) * chunk, :]


class Plan:
    def __init__(self, tiles, replicas, queries, hidden, latents):
        self.tiles, self.replicas = tiles, replicas
        self.devices = tiles * replicas
        self.query_total = float(queries * self.devices)
        self.main_rows = hidden + latents + MISC
        needed = (hidden // LANES) * self.main_rows + 5 * self.devices
        self.chunk = -(-needed // (8 * self.devices)) * 8
        bits = self.devices.bit_length() - 1
        middle = list(range(2, bits - 1))
        self.stages = [[0], [1, bits - 1]] + [middle[i : i + 2] for i in range(0, len(middle), 2)]

    def mask(self, bits, steps):
        return sum(1 << bit for number, bit in enumerate(bits) if steps >> number & 1)

    def my_chunk(self, device):
        chunk = 0
        for bits in self.stages:
            for bit in reversed(bits):
                chunk = chunk * 2 + (device >> bit & 1)
        return chunk


def swapped(value, plan, bits, steps):
    mask = plan.mask(bits, steps)
    return lax.ppermute(value, ("replica", "tile"), [(i, i ^ mask) for i in range(plan.devices)])


def main(place, left, here, right, conv_weight, conv_bias, words, params, plan):
    w_latent, w_pos, bias_one, w_mid, bias_two, w_out, bias_out = params
    rows = words.shape[0]
    hidden = w_mid.shape[0]
    channels = here.shape[2]
    outs = jax.ShapeDtypeStruct((plan.devices // 2, plan.chunk, LANES), F32)
    pairs = (here.shape[0] + 1) * here.shape[1] // 2
    wide = lambda kind: pltpu.VMEM((5 * rows, hidden), kind)
    return pl.pallas_call(
        functools.partial(main_kernel, plan),
        out_shape=(outs, outs),
        in_specs=[SMEM] + [VMEM] * 12 + [SMEM],
        out_specs=(VMEM, VMEM),
        scratch_shapes=[
            pltpu.VMEM((pairs, channels, 2 * LANES), BF16),
            pltpu.VMEM((rows, channels), BF16),
            pltpu.VMEM((rows, LANES), F32),
            pltpu.VMEM((rows, hidden), F32),
            pltpu.VMEM((hidden, hidden), BF16),
            pltpu.VMEM((hidden, hidden), BF16),
            wide(BF16),
            wide(BF16),
            wide(F32),
            wide(BF16),
            wide(BF16),
            wide(F32),
            wide(BF16),
            wide(BF16),
            pltpu.VMEM((40, rows), F32),
            pltpu.VMEM((40, rows), F32),
            pltpu.VMEM((plan.devices * plan.chunk, LANES), F32),
        ],
        compiler_params=pltpu.CompilerParams(vmem_limit_bytes=48 << 20),
        name="encode_decode",
    )(place, left, here, right, conv_weight, conv_bias, words, w_latent, w_pos, bias_one, w_mid, bias_two, w_out, bias_out)


def unpack_kernel(
    plan,
    place_ref,
    mine_ref,
    other_ref,
    prediction_ref,
    latent_ref,
    pos_ref,
    one_ref,
    mid_ref,
    two_ref,
    out_ref,
    tail_ref,
    packed,
):
    my_chunk = place_ref[0]
    device = place_ref[2] * plan.tiles + place_ref[1]
    half = plan.devices // 2
    chunk = plan.chunk
    my_half = my_chunk // half
    for number in range(plan.devices):
        spot = jnp.bitwise_xor(number, my_chunk) & (half - 1)

        @pl.when(my_half == number // half)
        def _():
            packed[number * chunk : (number + 1) * chunk, :] = mine_ref[spot]

        @pl.when(my_half != number // half)
        def _():
            packed[number * chunk : (number + 1) * chunk, :] = other_ref[spot]

    hidden = mid_ref.shape[0]
    latents = latent_ref.shape[0]
    for part in range(hidden // LANES):
        lanes = slice(part * LANES, (part + 1) * LANES)
        first = part * plan.main_rows
        mid_ref[:, lanes] = packed[first : first + hidden, :]
        first = first + hidden
        latent_ref[:, lanes] = packed[first : first + latents, :]
        first = first + latents
        pos_ref[:, lanes] = packed[first : first + 3, :]
        one_ref[:, lanes] = packed[first + 3 : first + 4, :]
        two_ref[:, lanes] = packed[first + 4 : first + 5, :]
        out_ref[:, lanes] = packed[first + 8 : first + 13, :]
        if part == 0:
            tail_ref[...] = packed[first + 5 : first + 6, :]
    first = (hidden // LANES) * plan.main_rows
    for f in range(5):
        prediction_ref[0, f : f + 1, :] = packed[pl.ds(first + f * plan.devices + device, 1), :]


def unpack(place, mine, other, plan, hidden, latents):
    shapes = [(1, 5, LANES), (latents, hidden), (3, hidden), (1, hidden), (hidden, hidden), (1, hidden), (5, hidden), (1, LANES)]
    return pl.pallas_call(
        functools.partial(unpack_kernel, plan),
        out_shape=tuple(jax.ShapeDtypeStruct(shape, F32) for shape in shapes),
        in_specs=[SMEM, VMEM, VMEM],
        out_specs=tuple([VMEM] * len(shapes)),
        scratch_shapes=[pltpu.VMEM((plan.devices * plan.chunk, LANES), F32)],
        compiler_params=pltpu.CompilerParams(vmem_limit_bytes=16 << 20),
        name="unpack",
    )(place, mine, other)


def body(
    fields,
    convolution_weight,
    convolution_bias,
    query_owner,
    query_cell,
    query_frac,
    target,
    w_latent,
    w_pos,
    bias_one,
    w_mid,
    bias_two,
    w_out,
    bias_out,
):
    tiles = lax.axis_size("tile")
    replicas = lax.axis_size("replica")
    my_tile = lax.axis_index("tile")
    my_replica = lax.axis_index("replica")
    channels = fields.shape[1]
    queries = query_cell.shape[1]
    hidden = w_mid.shape[0]
    slots = 2 * queries // tiles
    plan = Plan(tiles, replicas, queries, hidden, channels)
    device = my_replica * tiles + my_tile
    place = jnp.stack([plan.my_chunk(device), my_tile, my_replica]).astype(jnp.int32)

    words = route(query_owner[:, :, 0], query_cell, query_frac[0], target[0], tiles, slots)
    words = lax.all_to_all(
        words.reshape(tiles, slots, WORDS), "tile", split_axis=0, concat_axis=0, tiled=True
    ).reshape(tiles * slots, WORDS)

    here = fields[0].transpose(1, 2, 0, 3)
    up = [(i, (i + 1) % tiles) for i in range(tiles)]
    down = [((i + 1) % tiles, i) for i in range(tiles)]
    left = lax.ppermute(here[-DILATION_RATE:], "tile", up)
    right = lax.ppermute(here[: DILATION_RATE + 1], "tile", down)
    taps = convolution_weight.reshape(channels, 9, 3, channels)
    taps = taps.transpose(2, 0, 1, 3).reshape(3 * channels, 9 * channels)

    params = (w_latent, w_pos, bias_one[None], w_mid, bias_two[None], w_out, bias_out)
    send, keep = main(place, left, here, right, taps, convolution_bias[:, None], words, params, plan)

    keep = keep + swapped(send, plan, plan.stages[0], 1)
    for bits in plan.stages[1:]:
        group = 1 << len(bits)
        keep = keep.reshape(group, keep.shape[0] // group, plan.chunk, LANES)
        arrived = [swapped(keep[step], plan, bits, step) for step in range(1, group)]
        keep = keep[0]
        for block in arrived:
            keep = keep + block
    for bits in reversed(plan.stages[1:]):
        group = 1 << len(bits)
        keep = jnp.concatenate([keep] + [swapped(keep, plan, bits, step) for step in range(1, group)], axis=0)
    other = swapped(keep, plan, plan.stages[0], 1)
    prediction, g_latent, g_pos, g_one, g_mid, g_two, g_out, tail = unpack(
        place, keep, other, plan, hidden, channels
    )
    return (prediction, g_latent, g_pos, g_one[0], g_mid, g_two[0], g_out, tail[0, :5], tail[0, 5])


def solution(mesh):
    return jax.shard_map(
        body,
        mesh=mesh,
        in_specs=(
            P("replica", None, "tile", None, None),
            P(),
            P(),
            P("replica", "tile", None),
            P("replica", "tile"),
            P("replica", None, "tile"),
            P("replica", None, "tile"),
            P(),
            P(),
            P(),
            P(),
            P(),
            P(),
            P(),
        ),
        out_specs=(P("replica", None, "tile"), P(), P(), P(), P(), P(), P(), P(), P()),
        check_vma=False,
    )
```

```python
import functools

import jax
import jax.numpy as jnp
from jax import lax
from jax.experimental import pallas as pl
from jax.experimental.pallas import tpu as pltpu
from jax.sharding import PartitionSpec as P

DILATION_RATE = 2
VISCOSITY = 0.05
DIFFUSIVITY = 0.05
RESIDUAL_WEIGHT = 0.5

F32 = jnp.float32
BF16 = jnp.bfloat16
LANES = 128
BLOCK = 32
WORDS = 128
MISC = 16
NN = (((1,), (0,)), ((), ()))
NT = (((1,), (1,)), ((), ()))
TN = (((0,), (0,)), ((), ()))
VMEM = pl.BlockSpec(memory_space=pltpu.VMEM)
SMEM = pl.BlockSpec(memory_space=pltpu.SMEM)


def mul(left, right, dims=NN):
    return lax.dot_general(left, right, dims, preferred_element_type=F32)


def halves(value):
    high = value.astype(BF16)
    return high, (value - high.astype(F32)).astype(BF16)


def thirds(value):
    high = value.astype(BF16)
    rest = value - high.astype(F32)
    middle = rest.astype(BF16)
    return high, middle, (rest - middle.astype(F32)).astype(BF16)


def mul3(left, right, dims=NN):
    return mul(left[0], right[0], dims) + mul(left[0], right[1], dims) + mul(left[1], right[0], dims)


def select(gathered_ref, my_tile, slots, words_ref):
    tiles, kinds, queries = gathered_ref.shape
    owner = jnp.concatenate([gathered_ref[r, 0:1, :] for r in range(tiles)], axis=0)
    hits = jnp.where(owner == my_tile.astype(F32), 1.0, 0.0)
    before = lax.broadcasted_iota(jnp.int32, (queries, queries), 0) < lax.broadcasted_iota(
        jnp.int32, (queries, queries), 1
    )
    earlier = mul(hits.astype(BF16), jnp.where(before, 1.0, 0.0).astype(BF16))
    place = jnp.where(hits > 0.0, earlier, -1.0)
    slot = lax.broadcasted_iota(jnp.int32, (slots, queries), 0).astype(F32)
    chosen = jnp.concatenate([jnp.where(slot == place[r : r + 1, :], 1.0, 0.0) for r in range(tiles)], axis=0)
    chosen = chosen.astype(BF16)
    high, middle, low = thirds(gathered_ref[...].reshape(tiles * kinds, queries))
    picked = mul(chosen, high, NT) + mul(chosen, middle, NT) + mul(chosen, low, NT)
    words_ref[...] = jnp.zeros_like(words_ref)
    for r in range(tiles):
        words_ref[r * slots : (r + 1) * slots, 0:kinds] = picked[
            r * slots : (r + 1) * slots, r * kinds : (r + 1) * kinds
        ]


def tap_sum(weight_ref, planes, pair):
    total = None
    for step_x, ref, index in planes:
        rows_y = ref.shape[1]
        blocks = [
            jnp.concatenate([ref[index, (2 * pair + half + step_y) % rows_y] for half in (0, 1)], axis=1)
            for step_y in (-1, 0, 1)
        ]
        term = mul(weight_ref[step_x], jnp.concatenate(blocks, axis=0))
        total = term if total is None else total + term
    channels = total.shape[0] // 3
    sides = []
    for half in (0, 1):
        part = total[:, half * LANES : (half + 1) * LANES]
        sides.append(
            part[channels : 2 * channels]
            + pltpu.roll(part[:channels], 1, 1)
            + pltpu.roll(part[2 * channels :], LANES - 1, 1)
        )
    return jnp.concatenate(sides, axis=1)


def local_kernel(here_ref, weight_ref, w_mid_ref, partial_ref, high_ref, low_ref):
    planes, rows_y = here_ref.shape[0], here_ref.shape[1]
    for x in range(planes + 1):
        taps = [
            (step, here_ref, x + DILATION_RATE * (step - 1))
            for step in range(3)
            if 0 <= x + DILATION_RATE * (step - 1) < planes
        ]
        for pair in range(rows_y // 2):
            partial_ref[x * (rows_y // 2) + pair] = tap_sum(weight_ref, taps, pair)
    high, low = halves(w_mid_ref[...])
    high_ref[...] = high
    low_ref[...] = low


def local_part(here, taps, w_mid):
    planes, rows_y, channels, rows_z = here.shape
    pairs = (planes + 1) * rows_y // 2
    split = jax.ShapeDtypeStruct(w_mid.shape, BF16)
    return pl.pallas_call(
        local_kernel,
        out_shape=(jax.ShapeDtypeStruct((pairs, channels, 2 * rows_z), F32), split, split),
        in_specs=[VMEM] * 3,
        out_specs=(VMEM, VMEM, VMEM),
        compiler_params=pltpu.CompilerParams(vmem_limit_bytes=16 << 20),
        cost_estimate=pl.CostEstimate(flops=3 << 30, bytes_accessed=4 << 20, transcendentals=0),
        name="conv_local",
    )(here, taps, w_mid)


def finish_latent(left_ref, right_ref, partial_ref, weight_ref, bias_ref, planes, lat):
    rows_y = left_ref.shape[1]
    bias = bias_ref[...]
    for x in range(planes + 1):
        taps = []
        for step in range(3):
            plane = x + DILATION_RATE * (step - 1)
            if plane < 0:
                taps.append((step, left_ref, plane + left_ref.shape[0]))
            elif plane >= planes:
                taps.append((step, right_ref, plane - planes))
        for pair in range(rows_y // 2):
            number = x * (rows_y // 2) + pair
            summed = partial_ref[number] + tap_sum(weight_ref, taps, pair) + bias
            lat[number] = jax.nn.gelu(summed).astype(BF16)


def interpolate(words, lat, planes, rows_y, rows_z):
    rows = words.shape[0]
    cell = jnp.broadcast_to(words[:, 1:2], (rows, LANES)).astype(jnp.int32)
    frac = [jnp.broadcast_to(words[:, 2 + d : 3 + d], (rows, LANES)) for d in range(3)]
    shift_z = rows_z.bit_length() - 1
    shift_y = rows_y.bit_length() - 1
    base_x = cell >> (shift_z + shift_y)
    base_y = (cell >> shift_z) & (rows_y - 1)
    base_z = cell & (rows_z - 1)
    spot = lax.broadcasted_iota(jnp.int32, (rows, rows_z), 1)
    part_z = jnp.where(spot == base_z, 1.0 - frac[2], 0.0) + jnp.where(
        spot == ((base_z + 1) & (rows_z - 1)), frac[2], 0.0
    )
    total = None
    for x in range(planes + 1):
        part_x = jnp.where(base_x == x, 1.0 - frac[0], jnp.where(base_x == x - 1, frac[0], 0.0))
        for pair in range(rows_y // 2):
            sides = []
            for y in (2 * pair, 2 * pair + 1):
                part_y = jnp.where(
                    base_y == y, 1.0 - frac[1], jnp.where(base_y == (y - 1) % rows_y, frac[1], 0.0)
                )
                sides.append((part_x * part_y * part_z).astype(BF16))
            term = mul(jnp.concatenate(sides, axis=1), lat[x * (rows_y // 2) + pair], NT)
            total = term if total is None else total + term
    return total.astype(BF16), base_x, base_y, base_z, frac


def folded(value):
    return jnp.sum(value.reshape(value.shape[0] // 8, 8, value.shape[1]), axis=0)


def main_kernel(
    plan,
    place_ref,
    left_ref,
    right_ref,
    partial_ref,
    conv_weight_ref,
    conv_bias_ref,
    gathered_ref,
    w_latent_ref,
    w_pos_ref,
    bias_one_ref,
    mid_high,
    mid_low,
    bias_two_ref,
    w_out_ref,
    bias_out_ref,
    send_ref,
    keep_ref,
    lat,
    code,
    pos,
    z_one,
    words_ref,
    one_high,
    one_low,
    mixed,
    two_high,
    two_low,
    back,
    d_high,
    d_low,
    out_t,
    d_out_t,
    packed,
):
    rows = plan.tiles * plan.slots
    hidden = mid_high.shape[0]
    latents = w_latent_ref.shape[0]
    planes, rows_y, rows_z = plan.planes, left_ref.shape[1], left_ref.shape[3]
    slots = rows // plan.tiles
    my_chunk = place_ref[0]
    my_tile = place_ref[1]
    my_replica = place_ref[2]

    select(gathered_ref, my_tile, slots, words_ref)
    finish_latent(left_ref, right_ref, partial_ref, conv_weight_ref, conv_bias_ref, planes, lat)
    words = words_ref[...]
    interp, base_x, base_y, base_z, frac = interpolate(words, lat, planes, rows_y, rows_z)
    code[...] = interp
    global_x = my_tile * planes + base_x
    lane = lax.broadcasted_iota(jnp.int32, (rows, LANES), 1)
    pos[...] = jnp.where(
        lane == 0,
        (global_x.astype(F32) + frac[0]) / (planes * plan.tiles),
        jnp.where(
            lane == 1,
            (base_y.astype(F32) + frac[1]) / rows_y,
            (base_z.astype(F32) + frac[2]) / rows_z,
        ),
    )

    wl_high, wl_low = halves(w_latent_ref[...])
    z_one[...] = mul(interp, wl_high) + mul(interp, wl_low)
    w_pos = [w_pos_ref[d : d + 1, :] for d in range(3)]
    square = w_pos[0] * w_pos[0] + w_pos[1] * w_pos[1] + w_pos[2] * w_pos[2]
    bias_one = bias_one_ref[...]
    bias_two = bias_two_ref[...]

    def store(index, block, refs, value):
        high, low = halves(value)
        refs[0][pl.ds(pl.multiple_of(index * rows + block * BLOCK, BLOCK), BLOCK), :] = high
        refs[1][pl.ds(pl.multiple_of(index * rows + block * BLOCK, BLOCK), BLOCK), :] = low

    def fetch(ref, index, block):
        return ref[pl.ds(pl.multiple_of(index * rows + block * BLOCK, BLOCK), BLOCK), :]

    def layer_one(block, carry):
        where = fetch(pos, 0, block)
        pre = (
            fetch(z_one, 0, block)
            + (where[:, 0:1] * w_pos[0] + where[:, 1:2] * w_pos[1] + where[:, 2:3] * w_pos[2])
            + bias_one
        )
        act = jnp.tanh(pre)
        slope = 1.0 - act * act
        curve = -2.0 * act * slope
        z_one[pl.ds(pl.multiple_of(block * BLOCK, BLOCK), BLOCK), :] = act
        refs = (one_high, one_low)
        store(0, block, refs, act)
        for d in range(3):
            store(1 + d, block, refs, slope * w_pos[d])
        store(4, block, refs, curve * square)
        return carry

    lax.fori_loop(0, rows // BLOCK, layer_one, 0)

    def times_mid(dims, source, result, index, carry):
        span = pl.ds(pl.multiple_of(index * rows, rows), rows)
        result[span, :] = mul3((source[0][span, :], source[1][span, :]), (mid_high[...], mid_low[...]), dims)
        return carry

    lax.fori_loop(0, 5, functools.partial(times_mid, NN, (one_high, one_low), mixed), 0)

    def layer_two(block, carry):
        act = jnp.tanh(fetch(mixed, 0, block) + bias_two)
        slope = 1.0 - act * act
        curve = -2.0 * act * slope
        refs = (two_high, two_low)
        store(0, block, refs, act)
        mixed[pl.ds(pl.multiple_of(block * BLOCK, BLOCK), BLOCK), :] = act
        norm = None
        for d in range(3):
            tangent = fetch(mixed, 1 + d, block)
            store(1 + d, block, refs, slope * tangent)
            norm = tangent * tangent if norm is None else norm + tangent * tangent
        store(4, block, refs, slope * fetch(mixed, 4, block) + curve * norm)
        return carry

    lax.fori_loop(0, rows // BLOCK, layer_two, 0)

    out_fields = jnp.concatenate([w_out_ref[...], jnp.zeros((3, hidden), F32)], axis=0)
    wo_high, wo_low = halves(out_fields)
    wo_both = jnp.concatenate([out_fields, wo_low.astype(F32)], axis=0).astype(BF16)
    for s in range(5):
        span = slice(s * rows, (s + 1) * rows)
        both = mul(wo_both, two_high[span, :], NT)
        out_t[8 * s : 8 * s + 8, :] = both[:8] + both[8:] + mul(wo_high, two_low[span, :], NT)

    words_t = words.T
    target = [words_t[5 + f : 6 + f, :] for f in range(5)]
    valid = words_t[10:11, :]
    value = [out_t[f : f + 1, :] + bias_out_ref[f] for f in range(5)]
    grad = [[out_t[8 * (d + 1) + f : 8 * (d + 1) + f + 1, :] for f in range(5)] for d in range(3)]
    laplace = [out_t[32 + f : 33 + f, :] for f in range(5)]
    velocity = value[2:5]
    advection = [
        velocity[0] * grad[0][f] + velocity[1] * grad[1][f] + velocity[2] * grad[2][f] for f in range(5)
    ]
    continuity = grad[0][2] + grad[1][3] + grad[2][4]
    momentum = [advection[2 + j] + grad[j][1] - VISCOSITY * laplace[2 + j] for j in range(3)]
    momentum[2] = momentum[2] - value[0]
    energy = advection[0] - DIFFUSIVITY * laplace[0]
    misfit = [value[f] - target[f] for f in range(5)]
    physics = (
        continuity * continuity
        + (momentum[0] * momentum[0] + momentum[1] * momentum[1] + momentum[2] * momentum[2])
        + energy * energy
    )
    squares = (
        misfit[0] * misfit[0]
        + misfit[1] * misfit[1]
        + misfit[2] * misfit[2]
        + misfit[3] * misfit[3]
        + misfit[4] * misfit[4]
    )
    point_loss = valid * (squares + RESIDUAL_WEIGHT * physics) * (1.0 / plan.query_total)

    rate = valid * (1.0 / plan.query_total)
    twice = RESIDUAL_WEIGHT * 2.0
    d_cont = rate * twice * continuity
    d_mom = [rate * twice * m for m in momentum]
    d_energy = rate * twice * energy
    d_value = [2.0 * rate * m for m in misfit]
    for d in range(3):
        d_value[2 + d] = d_value[2 + d] + (
            d_mom[0] * grad[d][2] + d_mom[1] * grad[d][3] + d_mom[2] * grad[d][4] + d_energy * grad[d][0]
        )
    d_value[0] = d_value[0] - d_mom[2]
    d_out_t[...] = jnp.zeros_like(d_out_t)
    for f in range(5):
        d_out_t[f : f + 1, :] = d_value[f]
    for d in range(3):
        first = 8 * (d + 1)
        d_out_t[first : first + 1, :] = d_energy * velocity[d]
        d_out_t[first + 1 : first + 2, :] = d_mom[d]
        for j in range(3):
            term = d_mom[j] * velocity[d]
            if j == d:
                term = term + d_cont
            d_out_t[first + 2 + j : first + 3 + j, :] = term
    d_out_t[32:33, :] = -DIFFUSIVITY * d_energy
    for j in range(3):
        d_out_t[34 + j : 35 + j, :] = -VISCOSITY * d_mom[j]

    for s in range(5):
        span = slice(s * rows, (s + 1) * rows)
        wanted = d_out_t[8 * s : 8 * s + 8, :]
        do_high, do_low = halves(wanted)
        back[span, :] = mul3((do_high, do_low), (wo_high, wo_low), TN)

    def second_back(block, total):
        act = fetch(mixed, 0, block)
        slope = 1.0 - act * act
        curve = -2.0 * act * slope
        tangent = [fetch(mixed, 1 + d, block) for d in range(3)]
        cot_t = [fetch(back, 1 + d, block) for d in range(3)]
        cot_l = fetch(back, 4, block)
        refs = (d_high, d_low)
        d_slope = cot_l * fetch(mixed, 4, block)
        norm = None
        bent = 2.0 * curve * cot_l
        for d in range(3):
            store(1 + d, block, refs, slope * cot_t[d] + bent * tangent[d])
            d_slope = d_slope + cot_t[d] * tangent[d]
            norm = tangent[d] * tangent[d] if norm is None else norm + tangent[d] * tangent[d]
        store(4, block, refs, slope * cot_l)
        d_curve = cot_l * norm
        d_slope = d_slope - 2.0 * act * d_curve
        d_act = fetch(back, 0, block) - 2.0 * slope * d_curve - 2.0 * act * d_slope
        d_pre = slope * d_act
        store(0, block, refs, d_pre)
        return total + folded(d_pre)

    grad_two = lax.fori_loop(0, rows // BLOCK, second_back, jnp.zeros((8, hidden), F32))

    packed[...] = jnp.zeros_like(packed)
    main_rows = hidden + latents + MISC
    wide = 2 * LANES
    for left in range(hidden // wide):
        for right in range(hidden // wide):
            lefts = slice(left * wide, (left + 1) * wide)
            rights = slice(right * wide, (right + 1) * wide)
            part = mul3(
                (one_high[:, lefts], one_low[:, lefts]), (d_high[:, rights], d_low[:, rights]), TN
            )
            for side in range(2):
                first = (2 * right + side) * main_rows + left * wide
                packed[first : first + wide, :] = part[:, side * LANES : (side + 1) * LANES]

    lax.fori_loop(0, 5, functools.partial(times_mid, NT, (d_high, d_low), back), 0)

    def first_back(block, totals):
        act = fetch(z_one, 0, block)
        slope = 1.0 - act * act
        curve = -2.0 * act * slope
        where = fetch(pos, 0, block)
        cot_t = [fetch(back, 1 + d, block) for d in range(3)]
        cot_l = fetch(back, 4, block)
        d_curve = cot_l * square
        d_slope = cot_t[0] * w_pos[0] + cot_t[1] * w_pos[1] + cot_t[2] * w_pos[2] - 2.0 * act * d_curve
        d_act = fetch(back, 0, block) - 2.0 * slope * d_curve - 2.0 * act * d_slope
        d_pre = slope * d_act
        store(0, block, (d_high, d_low), d_pre)
        sums = [totals[0] + folded(d_pre)]
        for d in range(3):
            sums.append(totals[1 + d] + folded(where[:, d : d + 1] * d_pre + slope * cot_t[d]))
        sums.append(totals[4] + folded(curve * cot_l))
        return tuple(sums)

    sums = lax.fori_loop(
        0, rows // BLOCK, first_back, tuple(jnp.zeros((8, hidden), F32) for _ in range(5))
    )
    d_square = jnp.sum(sums[4], axis=0, keepdims=True)
    grad_latent = mul(code[...], d_high[0:rows, :], TN) + mul(code[...], d_low[0:rows, :], TN)

    grad_out = None
    for s in range(5):
        span = slice(s * rows, (s + 1) * rows)
        wanted = d_out_t[8 * s : 8 * s + 8, :]
        do_high, do_low = halves(wanted)
        do_both = jnp.concatenate([wanted, do_low.astype(F32)], axis=0).astype(BF16)
        both = mul(do_both, two_high[span, :])
        term = both[:8] + both[8:] + mul(do_high, two_low[span, :])
        grad_out = term if grad_out is None else grad_out + term

    lane_row = lax.broadcasted_iota(jnp.int32, (1, hidden), 1)
    last = jnp.where(lane_row == 5, jnp.sum(point_loss), 0.0)
    for f in range(5):
        last = last + jnp.where(lane_row == f, jnp.sum(d_value[f]), 0.0)
    grad_pos = [jnp.sum(sums[1 + d], axis=0, keepdims=True) + 2.0 * w_pos[d] * d_square for d in range(3)]
    misc = grad_pos + [
        jnp.sum(sums[0], axis=0, keepdims=True),
        jnp.sum(grad_two, axis=0, keepdims=True),
        last,
    ]
    for part in range(hidden // LANES):
        lanes = slice(part * LANES, (part + 1) * LANES)
        first = part * main_rows + hidden
        packed[first : first + latents, :] = grad_latent[:, lanes]
        first = first + latents
        for number, row in enumerate(misc):
            packed[first + number : first + number + 1, :] = row[:, lanes]
        packed[first + 8 : first + 16, :] = grad_out[:, lanes]

    chosen = jnp.where(
        lane == jnp.broadcast_to(words[:, 11:12], (rows, LANES)).astype(jnp.int32), words[:, 10:11], 0.0
    ).astype(BF16)
    source = lax.broadcasted_iota(jnp.int32, (plan.tiles, rows), 0)
    inside = lax.broadcasted_iota(jnp.int32, (plan.tiles, rows), 1)
    mine = jnp.bitwise_xor(inside >> (slots.bit_length() - 1), my_tile) == source
    for f in range(5):
        high, middle, low = thirds(jnp.where(mine, jnp.broadcast_to(value[f], (plan.tiles, rows)), 0.0))
        first = pl.multiple_of((hidden // LANES) * main_rows + f * plan.devices + my_replica * plan.tiles, 16)
        packed[pl.ds(first, plan.tiles), :] = mul(high, chosen) + mul(middle, chosen) + mul(low, chosen)

    half = plan.devices // 2
    chunk = plan.chunk
    my_half = my_chunk // half
    for number in range(plan.devices):
        spot = jnp.bitwise_xor(number, my_chunk) & (half - 1)

        @pl.when(my_half == number // half)
        def _():
            keep_ref[spot] = packed[number * chunk : (number + 1) * chunk, :]

        @pl.when(my_half != number // half)
        def _():
            send_ref[spot] = packed[number * chunk : (number + 1) * chunk, :]


class Plan:
    def __init__(self, tiles, replicas, queries, planes, hidden, latents):
        self.tiles, self.replicas, self.planes = tiles, replicas, planes
        self.slots = 2 * queries // tiles
        self.devices = tiles * replicas
        self.query_total = float(queries * self.devices)
        self.main_rows = hidden + latents + MISC
        needed = (hidden // LANES) * self.main_rows + 5 * self.devices
        self.chunk = -(-needed // (8 * self.devices)) * 8
        bits = self.devices.bit_length() - 1
        middle = list(range(2, bits - 1))
        along = list(range(1, tiles.bit_length() - 1))
        odd = len(along) % 2
        self.tile_stages = [[0]] + [along[:1]] * odd + [along[i : i + 2] for i in range(odd, len(along), 2)]
        self.stages = [[0], [1, bits - 1]] + [middle[i : i + 2] for i in range(0, len(middle), 2)]

    def mask(self, bits, steps):
        return sum(1 << bit for number, bit in enumerate(bits) if steps >> number & 1)

    def my_chunk(self, device):
        chunk = 0
        for bits in self.stages:
            for bit in reversed(bits):
                chunk = chunk * 2 + (device >> bit & 1)
        return chunk


def swapped(value, plan, bits, steps):
    mask = plan.mask(bits, steps)
    return lax.ppermute(value, ("replica", "tile"), [(i, i ^ mask) for i in range(plan.devices)])


def main(place, left, right, partial, taps, conv_bias, gathered, params, plan):
    w_latent, w_pos, bias_one, mid_high, mid_low, bias_two, w_out, bias_out = params
    rows = plan.tiles * plan.slots
    hidden = mid_high.shape[0]
    channels = left.shape[2]
    outs = jax.ShapeDtypeStruct((plan.devices // 2, plan.chunk, LANES), F32)
    wide = lambda kind: pltpu.VMEM((5 * rows, hidden), kind)
    return pl.pallas_call(
        functools.partial(main_kernel, plan),
        out_shape=(outs, outs),
        in_specs=[SMEM] + [VMEM] * 13 + [SMEM],
        out_specs=(VMEM, VMEM),
        scratch_shapes=[
            pltpu.VMEM((partial.shape[0], channels, 2 * LANES), BF16),
            pltpu.VMEM((rows, channels), BF16),
            pltpu.VMEM((rows, LANES), F32),
            pltpu.VMEM((rows, hidden), F32),
            pltpu.VMEM((rows, WORDS), F32),
            wide(BF16),
            wide(BF16),
            wide(F32),
            wide(BF16),
            wide(BF16),
            wide(F32),
            wide(BF16),
            wide(BF16),
            pltpu.VMEM((40, rows), F32),
            pltpu.VMEM((40, rows), F32),
            pltpu.VMEM((plan.devices * plan.chunk, LANES), F32),
        ],
        compiler_params=pltpu.CompilerParams(vmem_limit_bytes=48 << 20),
        name="encode_decode",
    )(place, left, right, partial, taps, conv_bias, gathered, *params)


def unpack_kernel(
    plan,
    place_ref,
    mine_ref,
    other_ref,
    prediction_ref,
    latent_ref,
    pos_ref,
    one_ref,
    mid_ref,
    two_ref,
    out_ref,
    bias_out_ref,
    loss_ref,
    packed,
):
    my_chunk = place_ref[0]
    device = place_ref[2] * plan.tiles + place_ref[1]
    half = plan.devices // 2
    chunk = plan.chunk
    my_half = my_chunk // half
    for number in range(plan.devices):
        spot = jnp.bitwise_xor(number, my_chunk) & (half - 1)

        @pl.when(my_half == number // half)
        def _():
            packed[number * chunk : (number + 1) * chunk, :] = mine_ref[spot]

        @pl.when(my_half != number // half)
        def _():
            packed[number * chunk : (number + 1) * chunk, :] = other_ref[spot]

    hidden = mid_ref.shape[0]
    latents = latent_ref.shape[0]
    for part in range(hidden // LANES):
        lanes = slice(part * LANES, (part + 1) * LANES)
        first = part * plan.main_rows
        mid_ref[:, lanes] = packed[first : first + hidden, :]
        first = first + hidden
        latent_ref[:, lanes] = packed[first : first + latents, :]
        first = first + latents
        pos_ref[:, lanes] = packed[first : first + 3, :]
        one_ref[:, lanes] = packed[first + 3 : first + 4, :]
        two_ref[:, lanes] = packed[first + 4 : first + 5, :]
        out_ref[:, lanes] = packed[first + 8 : first + 13, :]
        if part == 0:
            bias_out_ref[...] = packed[first + 5 : first + 6, 0:5]
            loss_ref[...] = packed[first + 5 : first + 6, 5:6]
    first = (hidden // LANES) * plan.main_rows
    for f in range(5):
        prediction_ref[f] = packed[pl.ds(first + f * plan.devices + device, 1), :]


def unpack(place, mine, other, plan, hidden, latents):
    shapes = [
        (5, 1, LANES),
        (latents, hidden),
        (3, hidden),
        (1, hidden),
        (hidden, hidden),
        (1, hidden),
        (5, hidden),
        (1, 5),
        (1, 1),
    ]
    return pl.pallas_call(
        functools.partial(unpack_kernel, plan),
        out_shape=tuple(jax.ShapeDtypeStruct(shape, F32) for shape in shapes),
        in_specs=[SMEM, VMEM, VMEM],
        out_specs=tuple([VMEM] * len(shapes)),
        scratch_shapes=[pltpu.VMEM((plan.devices * plan.chunk, LANES), F32)],
        compiler_params=pltpu.CompilerParams(vmem_limit_bytes=16 << 20),
        name="unpack",
    )(place, mine, other)


def body(
    fields,
    convolution_weight,
    convolution_bias,
    query_owner,
    query_cell,
    query_frac,
    target,
    w_latent,
    w_pos,
    bias_one,
    w_mid,
    bias_two,
    w_out,
    bias_out,
):
    tiles = lax.axis_size("tile")
    replicas = lax.axis_size("replica")
    my_tile = lax.axis_index("tile")
    my_replica = lax.axis_index("replica")
    channels = fields.shape[1]
    queries = query_cell.shape[1]
    hidden = w_mid.shape[0]
    plan = Plan(tiles, replicas, queries, fields.shape[2], hidden, channels)
    device = my_replica * tiles + my_tile
    place = jnp.stack([plan.my_chunk(device), my_tile, my_replica]).astype(jnp.int32)

    gathered = jnp.concatenate(
        [
            query_owner[:, :, 0].astype(F32),
            query_cell.astype(F32),
            query_frac[0],
            target[0],
            jnp.ones((1, queries), F32),
            lax.broadcasted_iota(jnp.int32, (1, queries), 1).astype(F32),
            jnp.zeros((4, queries), F32),
        ],
        axis=0,
    )[None]
    for bits in plan.tile_stages:
        moved = [swapped(gathered, plan, bits, step) for step in range(1, 1 << len(bits))]
        gathered = jnp.concatenate([gathered] + moved, axis=0)

    here = fields[0].transpose(1, 2, 0, 3)
    up = [(i, (i + 1) % tiles) for i in range(tiles)]
    down = [((i + 1) % tiles, i) for i in range(tiles)]
    left = lax.ppermute(here[-DILATION_RATE:], "tile", up)
    right = lax.ppermute(here[: DILATION_RATE + 1], "tile", down)
    taps = convolution_weight.reshape(channels, 3, 3, 3, channels)
    taps = taps.transpose(1, 3, 0, 2, 4).reshape(3, 3 * channels, 3 * channels)
    partial, mid_high, mid_low = local_part(here, taps, w_mid)

    params = (w_latent, w_pos, bias_one[None], mid_high, mid_low, bias_two[None], w_out, bias_out)
    send, keep = main(place, left, right, partial, taps, convolution_bias[:, None], gathered, params, plan)

    keep = keep + swapped(send, plan, plan.stages[0], 1)
    for bits in plan.stages[1:]:
        group = 1 << len(bits)
        keep = keep.reshape(group, keep.shape[0] // group, plan.chunk, LANES)
        arrived = [swapped(keep[step], plan, bits, step) for step in range(1, group)]
        keep = keep[0]
        for block in arrived:
            keep = keep + block
    for bits in reversed(plan.stages[1:]):
        group = 1 << len(bits)
        keep = jnp.concatenate([keep] + [swapped(keep, plan, bits, step) for step in range(1, group)], axis=0)
    other = swapped(keep, plan, plan.stages[0], 1)
    prediction, g_latent, g_pos, g_one, g_mid, g_two, g_out, g_bias, loss = unpack(
        place, keep, other, plan, hidden, channels
    )
    return (
        prediction.transpose(1, 0, 2),
        g_latent,
        g_pos,
        g_one.reshape(hidden),
        g_mid,
        g_two.reshape(hidden),
        g_out,
        g_bias.reshape(5),
        loss.reshape(()),
    )


def solution(mesh):
    return jax.shard_map(
        body,
        mesh=mesh,
        in_specs=(
            P("replica", None, "tile", None, None),
            P(),
            P(),
            P("replica", "tile", None),
            P("replica", "tile"),
            P("replica", None, "tile"),
            P("replica", None, "tile"),
            P(),
            P(),
            P(),
            P(),
            P(),
            P(),
            P(),
        ),
        out_specs=(P("replica", None, "tile"), P(), P(), P(), P(), P(), P(), P(), P()),
        check_vma=False,
    )
```

```python
import functools

import jax
import jax.numpy as jnp
from jax import lax
from jax.experimental import pallas as pl
from jax.experimental.pallas import tpu as pltpu
from jax.sharding import PartitionSpec as P

DILATION_RATE = 2
VISCOSITY = 0.05
DIFFUSIVITY = 0.05
RESIDUAL_WEIGHT = 0.5

F32 = jnp.float32
BF16 = jnp.bfloat16
LANES = 128
BLOCK = 32
WORDS = 128
MISC = 16
NN = (((1,), (0,)), ((), ()))
NT = (((1,), (1,)), ((), ()))
TN = (((0,), (0,)), ((), ()))
VMEM = pl.BlockSpec(memory_space=pltpu.VMEM)
SMEM = pl.BlockSpec(memory_space=pltpu.SMEM)


def mul(left, right, dims=NN):
    return lax.dot_general(left, right, dims, preferred_element_type=F32)


def halves(value):
    high = value.astype(BF16)
    return high, (value - high.astype(F32)).astype(BF16)


def thirds(value):
    high = value.astype(BF16)
    rest = value - high.astype(F32)
    middle = rest.astype(BF16)
    return high, middle, (rest - middle.astype(F32)).astype(BF16)


def mul3(left, right, dims=NN):
    return mul(left[0], right[0], dims) + mul(left[0], right[1], dims) + mul(left[1], right[0], dims)


def route_kernel(tiles, slots, owner_ref, cell_ref, frac_ref, target_ref, out_ref, words):
    queries = owner_ref.shape[1]
    owner = owner_ref[...]
    hits = (lax.broadcasted_iota(jnp.int32, (tiles, queries), 0) == owner).astype(F32)
    before = lax.broadcasted_iota(jnp.int32, (queries, queries), 0) < lax.broadcasted_iota(
        jnp.int32, (queries, queries), 1
    )
    earlier = mul(hits.astype(BF16), before.astype(F32).astype(BF16))
    slot = jnp.sum(hits * earlier, axis=0, keepdims=True)
    place = owner * slots + slot.astype(jnp.int32)
    chosen = (lax.broadcasted_iota(jnp.int32, (tiles * slots, queries), 0) == place).astype(F32).astype(BF16)
    words[...] = jnp.zeros_like(words)
    words[0:1, :] = cell_ref[...].astype(F32)
    for d in range(3):
        words[1 + d : 2 + d, :] = frac_ref[d]
    for f in range(5):
        words[4 + f : 5 + f, :] = target_ref[f]
    words[9:10, :] = jnp.ones((1, queries), F32)
    words[10:11, :] = lax.broadcasted_iota(jnp.int32, (1, queries), 1).astype(F32)
    high, middle, low = thirds(words[...])
    out_ref[...] = mul(chosen, high, NT) + mul(chosen, middle, NT) + mul(chosen, low, NT)


def route(owner, cell, frac, target, tiles, slots):
    queries = owner.shape[1]
    return pl.pallas_call(
        functools.partial(route_kernel, tiles, slots),
        out_shape=jax.ShapeDtypeStruct((tiles * slots, WORDS), F32),
        in_specs=[VMEM] * 4,
        out_specs=VMEM,
        scratch_shapes=[pltpu.VMEM((WORDS, queries), F32)],
        name="route",
    )(owner, cell, frac, target)


def tap_sum(weight_ref, planes, pair):
    total = None
    for step_x, ref, index in planes:
        rows_y = ref.shape[1]
        blocks = [
            jnp.concatenate([ref[index, (2 * pair + half + step_y) % rows_y] for half in (0, 1)], axis=1)
            for step_y in (-1, 0, 1)
        ]
        term = mul(weight_ref[step_x], jnp.concatenate(blocks, axis=0))
        total = term if total is None else total + term
    channels = total.shape[0] // 3
    sides = []
    for half in (0, 1):
        part = total[:, half * LANES : (half + 1) * LANES]
        sides.append(
            part[channels : 2 * channels]
            + pltpu.roll(part[:channels], 1, 1)
            + pltpu.roll(part[2 * channels :], LANES - 1, 1)
        )
    return jnp.concatenate(sides, axis=1)


def local_kernel(
    here_ref,
    weight_ref,
    bias_ref,
    w_latent_ref,
    w_pos_ref,
    bias_one_ref,
    w_mid_ref,
    bias_two_ref,
    w_out_ref,
    bias_out_ref,
    partial_ref,
    latent_high_ref,
    latent_low_ref,
    mid_high_ref,
    mid_low_ref,
    small_ref,
):
    planes, rows_y = here_ref.shape[0], here_ref.shape[1]
    bias = bias_ref[...]
    for x in range(planes + 1):
        taps = [
            (step, here_ref, x + DILATION_RATE * (step - 1))
            for step in range(3)
            if 0 <= x + DILATION_RATE * (step - 1) < planes
        ]
        for pair in range(rows_y // 2):
            partial_ref[x * (rows_y // 2) + pair] = tap_sum(weight_ref, taps, pair) + bias
    for source, high_ref, low_ref in (
        (w_latent_ref, latent_high_ref, latent_low_ref),
        (w_mid_ref, mid_high_ref, mid_low_ref),
    ):
        high, low = halves(source[...])
        high_ref[...] = high
        low_ref[...] = low
    small_ref[...] = jnp.zeros_like(small_ref)
    small_ref[0:3, :] = w_pos_ref[...]
    small_ref[3:4, :] = bias_one_ref[...]
    small_ref[4:5, :] = bias_two_ref[...]
    small_ref[5:6, 0:5] = bias_out_ref[...]
    small_ref[8:13, :] = w_out_ref[...]


def local_part(here, taps, conv_bias, params):
    w_latent, w_mid = params[0], params[3]
    planes, rows_y, channels, rows_z = here.shape
    pairs = (planes + 1) * rows_y // 2
    split = lambda array: [jax.ShapeDtypeStruct(array.shape, BF16)] * 2
    return pl.pallas_call(
        local_kernel,
        out_shape=tuple(
            [jax.ShapeDtypeStruct((pairs, channels, 2 * rows_z), F32)]
            + split(w_latent)
            + split(w_mid)
            + [jax.ShapeDtypeStruct((16, w_mid.shape[0]), F32)]
        ),
        in_specs=[VMEM] * 10,
        out_specs=tuple([VMEM] * 6),
        compiler_params=pltpu.CompilerParams(vmem_limit_bytes=16 << 20),
        cost_estimate=pl.CostEstimate(flops=3 << 30, bytes_accessed=4 << 20, transcendentals=0),
        name="conv_local",
    )(here, taps, conv_bias, *params)


def finish_latent(left_ref, right_ref, partial_ref, weight_ref, planes, lat):
    rows_y = left_ref.shape[1]
    for x in range(planes + 1):
        taps = []
        for step in range(3):
            plane = x + DILATION_RATE * (step - 1)
            if plane < 0:
                taps.append((step, left_ref, plane + left_ref.shape[0]))
            elif plane >= planes:
                taps.append((step, right_ref, plane - planes))
        for pair in range(rows_y // 2):
            number = x * (rows_y // 2) + pair
            summed = partial_ref[number] + tap_sum(weight_ref, taps, pair)
            lat[number] = jax.nn.gelu(summed).astype(BF16)


def interpolate(words, lat, planes, rows_y, rows_z):
    rows = words.shape[0]
    cell = jnp.broadcast_to(words[:, 0:1], (rows, LANES)).astype(jnp.int32)
    frac = [jnp.broadcast_to(words[:, 1 + d : 2 + d], (rows, LANES)) for d in range(3)]
    shift_z = rows_z.bit_length() - 1
    shift_y = rows_y.bit_length() - 1
    base_x = cell >> (shift_z + shift_y)
    base_y = (cell >> shift_z) & (rows_y - 1)
    base_z = cell & (rows_z - 1)
    spot = lax.broadcasted_iota(jnp.int32, (rows, rows_z), 1)
    part_z = jnp.where(spot == base_z, 1.0 - frac[2], 0.0) + jnp.where(
        spot == ((base_z + 1) & (rows_z - 1)), frac[2], 0.0
    )
    total = None
    for x in range(planes + 1):
        part_x = jnp.where(base_x == x, 1.0 - frac[0], jnp.where(base_x == x - 1, frac[0], 0.0))
        for pair in range(rows_y // 2):
            sides = []
            for y in (2 * pair, 2 * pair + 1):
                part_y = jnp.where(
                    base_y == y, 1.0 - frac[1], jnp.where(base_y == (y - 1) % rows_y, frac[1], 0.0)
                )
                sides.append((part_x * part_y * part_z).astype(BF16))
            term = mul(jnp.concatenate(sides, axis=1), lat[x * (rows_y // 2) + pair], NT)
            total = term if total is None else total + term
    return total.astype(BF16), base_x, base_y, base_z, frac


def folded(value):
    return jnp.sum(value.reshape(value.shape[0] // 8, 8, value.shape[1]), axis=0)


def main_kernel(
    plan,
    place_ref,
    left_ref,
    right_ref,
    partial_ref,
    conv_weight_ref,
    words_ref,
    latent_high,
    latent_low,
    mid_high,
    mid_low,
    small_ref,
    send_ref,
    keep_ref,
    lat,
    code,
    pos,
    z_one,
    one_high,
    one_low,
    mixed,
    two_high,
    two_low,
    back,
    d_high,
    d_low,
    out_t,
    d_out_t,
    packed,
):
    rows = plan.tiles * plan.slots
    hidden = mid_high.shape[0]
    latents = latent_high.shape[0]
    planes, rows_y, rows_z = plan.planes, left_ref.shape[1], left_ref.shape[3]
    slots = rows // plan.tiles
    my_chunk = place_ref[0]
    my_tile = place_ref[1]
    my_replica = place_ref[2]

    finish_latent(left_ref, right_ref, partial_ref, conv_weight_ref, planes, lat)
    words = words_ref[...]
    interp, base_x, base_y, base_z, frac = interpolate(words, lat, planes, rows_y, rows_z)
    code[...] = interp
    global_x = my_tile * planes + base_x
    lane = lax.broadcasted_iota(jnp.int32, (rows, LANES), 1)
    pos[...] = jnp.where(
        lane == 0,
        (global_x.astype(F32) + frac[0]) / (planes * plan.tiles),
        jnp.where(
            lane == 1,
            (base_y.astype(F32) + frac[1]) / rows_y,
            (base_z.astype(F32) + frac[2]) / rows_z,
        ),
    )

    z_one[...] = mul(interp, latent_high[...]) + mul(interp, latent_low[...])
    w_pos = [small_ref[d : d + 1, :] for d in range(3)]
    square = w_pos[0] * w_pos[0] + w_pos[1] * w_pos[1] + w_pos[2] * w_pos[2]
    bias_one = small_ref[3:4, :]
    bias_two = small_ref[4:5, :]

    def store(index, block, refs, value):
        high, low = halves(value)
        refs[0][pl.ds(pl.multiple_of(index * rows + block * BLOCK, BLOCK), BLOCK), :] = high
        refs[1][pl.ds(pl.multiple_of(index * rows + block * BLOCK, BLOCK), BLOCK), :] = low

    def fetch(ref, index, block):
        return ref[pl.ds(pl.multiple_of(index * rows + block * BLOCK, BLOCK), BLOCK), :]

    def layer_one(block, carry):
        where = fetch(pos, 0, block)
        pre = (
            fetch(z_one, 0, block)
            + (where[:, 0:1] * w_pos[0] + where[:, 1:2] * w_pos[1] + where[:, 2:3] * w_pos[2])
            + bias_one
        )
        act = jnp.tanh(pre)
        slope = 1.0 - act * act
        curve = -2.0 * act * slope
        z_one[pl.ds(pl.multiple_of(block * BLOCK, BLOCK), BLOCK), :] = act
        refs = (one_high, one_low)
        store(0, block, refs, act)
        for d in range(3):
            store(1 + d, block, refs, slope * w_pos[d])
        store(4, block, refs, curve * square)
        return carry

    lax.fori_loop(0, rows // BLOCK, layer_one, 0)

    def times_mid(dims, source, result, index, carry):
        span = pl.ds(pl.multiple_of(index * rows, rows), rows)
        result[span, :] = mul3((source[0][span, :], source[1][span, :]), (mid_high[...], mid_low[...]), dims)
        return carry

    lax.fori_loop(0, 5, functools.partial(times_mid, NN, (one_high, one_low), mixed), 0)

    def layer_two(block, carry):
        act = jnp.tanh(fetch(mixed, 0, block) + bias_two)
        slope = 1.0 - act * act
        curve = -2.0 * act * slope
        refs = (two_high, two_low)
        store(0, block, refs, act)
        mixed[pl.ds(pl.multiple_of(block * BLOCK, BLOCK), BLOCK), :] = act
        norm = None
        for d in range(3):
            tangent = fetch(mixed, 1 + d, block)
            store(1 + d, block, refs, slope * tangent)
            norm = tangent * tangent if norm is None else norm + tangent * tangent
        store(4, block, refs, slope * fetch(mixed, 4, block) + curve * norm)
        return carry

    lax.fori_loop(0, rows // BLOCK, layer_two, 0)

    out_fields = small_ref[8:16, :]
    wo_high, wo_low = halves(out_fields)
    wo_both = jnp.concatenate([out_fields, wo_low.astype(F32)], axis=0).astype(BF16)
    for s in range(5):
        span = slice(s * rows, (s + 1) * rows)
        both = mul(wo_both, two_high[span, :], NT)
        out_t[8 * s : 8 * s + 8, :] = both[:8] + both[8:] + mul(wo_high, two_low[span, :], NT)

    words_t = words.T
    target = [words_t[4 + f : 5 + f, :] for f in range(5)]
    valid = words_t[9:10, :]
    value = [out_t[f : f + 1, :] + small_ref[5:6, f : f + 1] for f in range(5)]
    grad = [[out_t[8 * (d + 1) + f : 8 * (d + 1) + f + 1, :] for f in range(5)] for d in range(3)]
    laplace = [out_t[32 + f : 33 + f, :] for f in range(5)]
    velocity = value[2:5]
    advection = [
        velocity[0] * grad[0][f] + velocity[1] * grad[1][f] + velocity[2] * grad[2][f] for f in range(5)
    ]
    continuity = grad[0][2] + grad[1][3] + grad[2][4]
    momentum = [advection[2 + j] + grad[j][1] - VISCOSITY * laplace[2 + j] for j in range(3)]
    momentum[2] = momentum[2] - value[0]
    energy = advection[0] - DIFFUSIVITY * laplace[0]
    misfit = [value[f] - target[f] for f in range(5)]
    physics = (
        continuity * continuity
        + (momentum[0] * momentum[0] + momentum[1] * momentum[1] + momentum[2] * momentum[2])
        + energy * energy
    )
    squares = (
        misfit[0] * misfit[0]
        + misfit[1] * misfit[1]
        + misfit[2] * misfit[2]
        + misfit[3] * misfit[3]
        + misfit[4] * misfit[4]
    )
    point_loss = valid * (squares + RESIDUAL_WEIGHT * physics) * (1.0 / plan.query_total)

    rate = valid * (1.0 / plan.query_total)
    twice = RESIDUAL_WEIGHT * 2.0
    d_cont = rate * twice * continuity
    d_mom = [rate * twice * m for m in momentum]
    d_energy = rate * twice * energy
    d_value = [2.0 * rate * m for m in misfit]
    for d in range(3):
        d_value[2 + d] = d_value[2 + d] + (
            d_mom[0] * grad[d][2] + d_mom[1] * grad[d][3] + d_mom[2] * grad[d][4] + d_energy * grad[d][0]
        )
    d_value[0] = d_value[0] - d_mom[2]
    d_out_t[...] = jnp.zeros_like(d_out_t)
    for f in range(5):
        d_out_t[f : f + 1, :] = d_value[f]
    for d in range(3):
        first = 8 * (d + 1)
        d_out_t[first : first + 1, :] = d_energy * velocity[d]
        d_out_t[first + 1 : first + 2, :] = d_mom[d]
        for j in range(3):
            term = d_mom[j] * velocity[d]
            if j == d:
                term = term + d_cont
            d_out_t[first + 2 + j : first + 3 + j, :] = term
    d_out_t[32:33, :] = -DIFFUSIVITY * d_energy
    for j in range(3):
        d_out_t[34 + j : 35 + j, :] = -VISCOSITY * d_mom[j]

    for s in range(5):
        span = slice(s * rows, (s + 1) * rows)
        wanted = d_out_t[8 * s : 8 * s + 8, :]
        do_high, do_low = halves(wanted)
        back[span, :] = mul3((do_high, do_low), (wo_high, wo_low), TN)

    def second_back(block, total):
        act = fetch(mixed, 0, block)
        slope = 1.0 - act * act
        curve = -2.0 * act * slope
        tangent = [fetch(mixed, 1 + d, block) for d in range(3)]
        cot_t = [fetch(back, 1 + d, block) for d in range(3)]
        cot_l = fetch(back, 4, block)
        refs = (d_high, d_low)
        d_slope = cot_l * fetch(mixed, 4, block)
        norm = None
        bent = 2.0 * curve * cot_l
        for d in range(3):
            store(1 + d, block, refs, slope * cot_t[d] + bent * tangent[d])
            d_slope = d_slope + cot_t[d] * tangent[d]
            norm = tangent[d] * tangent[d] if norm is None else norm + tangent[d] * tangent[d]
        store(4, block, refs, slope * cot_l)
        d_curve = cot_l * norm
        d_slope = d_slope - 2.0 * act * d_curve
        d_act = fetch(back, 0, block) - 2.0 * slope * d_curve - 2.0 * act * d_slope
        d_pre = slope * d_act
        store(0, block, refs, d_pre)
        return total + folded(d_pre)

    grad_two = lax.fori_loop(0, rows // BLOCK, second_back, jnp.zeros((8, hidden), F32))

    packed[...] = jnp.zeros_like(packed)
    main_rows = hidden + latents + MISC
    wide = 2 * LANES
    for left in range(hidden // wide):
        for right in range(hidden // wide):
            lefts = slice(left * wide, (left + 1) * wide)
            rights = slice(right * wide, (right + 1) * wide)
            part = mul3(
                (one_high[:, lefts], one_low[:, lefts]), (d_high[:, rights], d_low[:, rights]), TN
            )
            for side in range(2):
                first = (2 * right + side) * main_rows + left * wide
                packed[first : first + wide, :] = part[:, side * LANES : (side + 1) * LANES]

    lax.fori_loop(0, 5, functools.partial(times_mid, NT, (d_high, d_low), back), 0)

    def first_back(block, totals):
        act = fetch(z_one, 0, block)
        slope = 1.0 - act * act
        curve = -2.0 * act * slope
        where = fetch(pos, 0, block)
        cot_t = [fetch(back, 1 + d, block) for d in range(3)]
        cot_l = fetch(back, 4, block)
        d_curve = cot_l * square
        d_slope = cot_t[0] * w_pos[0] + cot_t[1] * w_pos[1] + cot_t[2] * w_pos[2] - 2.0 * act * d_curve
        d_act = fetch(back, 0, block) - 2.0 * slope * d_curve - 2.0 * act * d_slope
        d_pre = slope * d_act
        store(0, block, (d_high, d_low), d_pre)
        sums = [totals[0] + folded(d_pre)]
        for d in range(3):
            sums.append(totals[1 + d] + folded(where[:, d : d + 1] * d_pre + slope * cot_t[d]))
        sums.append(totals[4] + folded(curve * cot_l))
        return tuple(sums)

    sums = lax.fori_loop(
        0, rows // BLOCK, first_back, tuple(jnp.zeros((8, hidden), F32) for _ in range(5))
    )
    d_square = jnp.sum(sums[4], axis=0, keepdims=True)
    grad_latent = mul(code[...], d_high[0:rows, :], TN) + mul(code[...], d_low[0:rows, :], TN)

    grad_out = None
    for s in range(5):
        span = slice(s * rows, (s + 1) * rows)
        wanted = d_out_t[8 * s : 8 * s + 8, :]
        do_high, do_low = halves(wanted)
        do_both = jnp.concatenate([wanted, do_low.astype(F32)], axis=0).astype(BF16)
        both = mul(do_both, two_high[span, :])
        term = both[:8] + both[8:] + mul(do_high, two_low[span, :])
        grad_out = term if grad_out is None else grad_out + term

    lane_row = lax.broadcasted_iota(jnp.int32, (1, hidden), 1)
    last = jnp.where(lane_row == 5, jnp.sum(point_loss), 0.0)
    for f in range(5):
        last = last + jnp.where(lane_row == f, jnp.sum(d_value[f]), 0.0)
    grad_pos = [jnp.sum(sums[1 + d], axis=0, keepdims=True) + 2.0 * w_pos[d] * d_square for d in range(3)]
    misc = grad_pos + [
        jnp.sum(sums[0], axis=0, keepdims=True),
        jnp.sum(grad_two, axis=0, keepdims=True),
        last,
    ]
    for part in range(hidden // LANES):
        lanes = slice(part * LANES, (part + 1) * LANES)
        first = part * main_rows + hidden
        packed[first : first + latents, :] = grad_latent[:, lanes]
        first = first + latents
        for number, row in enumerate(misc):
            packed[first + number : first + number + 1, :] = row[:, lanes]
        packed[first + 8 : first + 16, :] = grad_out[:, lanes]

    chosen = jnp.where(
        lane == jnp.broadcast_to(words[:, 10:11], (rows, LANES)).astype(jnp.int32), words[:, 9:10], 0.0
    ).astype(BF16)
    source = lax.broadcasted_iota(jnp.int32, (plan.tiles, rows), 0)
    inside = lax.broadcasted_iota(jnp.int32, (plan.tiles, rows), 1)
    mine = (inside >> (slots.bit_length() - 1)) == source
    for f in range(5):
        high, middle, low = thirds(jnp.where(mine, jnp.broadcast_to(value[f], (plan.tiles, rows)), 0.0))
        first = pl.multiple_of((hidden // LANES) * main_rows + f * plan.devices + my_replica * plan.tiles, 16)
        packed[pl.ds(first, plan.tiles), :] = mul(high, chosen) + mul(middle, chosen) + mul(low, chosen)

    half = plan.devices // 2
    chunk = plan.chunk
    my_half = my_chunk // half
    for number in range(plan.devices):
        spot = jnp.bitwise_xor(number, my_chunk) & (half - 1)

        @pl.when(my_half == number // half)
        def _():
            keep_ref[spot] = packed[number * chunk : (number + 1) * chunk, :]

        @pl.when(my_half != number // half)
        def _():
            send_ref[spot] = packed[number * chunk : (number + 1) * chunk, :]


class Plan:
    def __init__(self, tiles, replicas, queries, planes, hidden, latents):
        self.tiles, self.replicas, self.planes = tiles, replicas, planes
        self.slots = 2 * queries // tiles
        self.devices = tiles * replicas
        self.query_total = float(queries * self.devices)
        self.main_rows = hidden + latents + MISC
        needed = (hidden // LANES) * self.main_rows + 5 * self.devices
        self.chunk = -(-needed // (8 * self.devices)) * 8
        bits = self.devices.bit_length() - 1
        middle = list(range(2, bits - 1))
        self.stages = [[0], [1, bits - 1]] + [middle[i : i + 2] for i in range(0, len(middle), 2)]

    def mask(self, bits, steps):
        return sum(1 << bit for number, bit in enumerate(bits) if steps >> number & 1)

    def my_chunk(self, device):
        chunk = 0
        for bits in self.stages:
            for bit in reversed(bits):
                chunk = chunk * 2 + (device >> bit & 1)
        return chunk


def swapped(value, plan, bits, steps):
    mask = plan.mask(bits, steps)
    return lax.ppermute(value, ("replica", "tile"), [(i, i ^ mask) for i in range(plan.devices)])


def main(place, left, right, partial, taps, words, weights, plan):
    rows = plan.tiles * plan.slots
    hidden = weights[-1].shape[1]
    channels = left.shape[2]
    outs = jax.ShapeDtypeStruct((plan.devices // 2, plan.chunk, LANES), F32)
    wide = lambda kind: pltpu.VMEM((5 * rows, hidden), kind)
    return pl.pallas_call(
        functools.partial(main_kernel, plan),
        out_shape=(outs, outs),
        in_specs=[SMEM] + [VMEM] * 10,
        out_specs=(VMEM, VMEM),
        scratch_shapes=[
            pltpu.VMEM((partial.shape[0], channels, 2 * LANES), BF16),
            pltpu.VMEM((rows, channels), BF16),
            pltpu.VMEM((rows, LANES), F32),
            pltpu.VMEM((rows, hidden), F32),
            wide(BF16),
            wide(BF16),
            wide(F32),
            wide(BF16),
            wide(BF16),
            wide(F32),
            wide(BF16),
            wide(BF16),
            pltpu.VMEM((40, rows), F32),
            pltpu.VMEM((40, rows), F32),
            pltpu.VMEM((plan.devices * plan.chunk, LANES), F32),
        ],
        compiler_params=pltpu.CompilerParams(vmem_limit_bytes=48 << 20),
        name="encode_decode",
    )(place, left, right, partial, taps, words, *weights)


def unpack_kernel(
    plan,
    place_ref,
    mine_ref,
    other_ref,
    prediction_ref,
    latent_ref,
    pos_ref,
    one_ref,
    mid_ref,
    two_ref,
    out_ref,
    bias_out_ref,
    loss_ref,
    packed,
):
    my_chunk = place_ref[0]
    device = place_ref[2] * plan.tiles + place_ref[1]
    half = plan.devices // 2
    chunk = plan.chunk
    my_half = my_chunk // half
    for number in range(plan.devices):
        spot = jnp.bitwise_xor(number, my_chunk) & (half - 1)

        @pl.when(my_half == number // half)
        def _():
            packed[number * chunk : (number + 1) * chunk, :] = mine_ref[spot]

        @pl.when(my_half != number // half)
        def _():
            packed[number * chunk : (number + 1) * chunk, :] = other_ref[spot]

    hidden = mid_ref.shape[0]
    latents = latent_ref.shape[0]
    for part in range(hidden // LANES):
        lanes = slice(part * LANES, (part + 1) * LANES)
        first = part * plan.main_rows
        mid_ref[:, lanes] = packed[first : first + hidden, :]
        first = first + hidden
        latent_ref[:, lanes] = packed[first : first + latents, :]
        first = first + latents
        pos_ref[:, lanes] = packed[first : first + 3, :]
        one_ref[:, lanes] = packed[first + 3 : first + 4, :]
        two_ref[:, lanes] = packed[first + 4 : first + 5, :]
        out_ref[:, lanes] = packed[first + 8 : first + 13, :]
        if part == 0:
            bias_out_ref[...] = packed[first + 5 : first + 6, 0:5]
            loss_ref[...] = packed[first + 5 : first + 6, 5:6]
    first = (hidden // LANES) * plan.main_rows
    for f in range(5):
        prediction_ref[f] = packed[pl.ds(first + f * plan.devices + device, 1), :]


def unpack(place, mine, other, plan, hidden, latents):
    shapes = [
        (5, 1, LANES),
        (latents, hidden),
        (3, hidden),
        (1, hidden),
        (hidden, hidden),
        (1, hidden),
        (5, hidden),
        (1, 5),
        (1, 1),
    ]
    return pl.pallas_call(
        functools.partial(unpack_kernel, plan),
        out_shape=tuple(jax.ShapeDtypeStruct(shape, F32) for shape in shapes),
        in_specs=[SMEM, VMEM, VMEM],
        out_specs=tuple([VMEM] * len(shapes)),
        scratch_shapes=[pltpu.VMEM((plan.devices * plan.chunk, LANES), F32)],
        compiler_params=pltpu.CompilerParams(vmem_limit_bytes=16 << 20),
        name="unpack",
    )(place, mine, other)


def body(
    fields,
    convolution_weight,
    convolution_bias,
    query_owner,
    query_cell,
    query_frac,
    target,
    w_latent,
    w_pos,
    bias_one,
    w_mid,
    bias_two,
    w_out,
    bias_out,
):
    tiles = lax.axis_size("tile")
    replicas = lax.axis_size("replica")
    my_tile = lax.axis_index("tile")
    my_replica = lax.axis_index("replica")
    channels = fields.shape[1]
    queries = query_cell.shape[1]
    hidden = w_mid.shape[0]
    plan = Plan(tiles, replicas, queries, fields.shape[2], hidden, channels)
    device = my_replica * tiles + my_tile
    place = jnp.stack([plan.my_chunk(device), my_tile, my_replica]).astype(jnp.int32)

    words = route(
        query_owner[:, :, 0],
        query_cell,
        query_frac.transpose(1, 0, 2),
        target.transpose(1, 0, 2),
        tiles,
        plan.slots,
    )
    words, fields = lax.optimization_barrier((words, fields))
    words = lax.all_to_all(
        words.reshape(tiles, plan.slots, WORDS), "tile", split_axis=0, concat_axis=0, tiled=True
    ).reshape(tiles * plan.slots, WORDS)

    here = fields[0].transpose(1, 2, 0, 3)
    up = [(i, (i + 1) % tiles) for i in range(tiles)]
    down = [((i + 1) % tiles, i) for i in range(tiles)]
    left = lax.ppermute(here[-DILATION_RATE:], "tile", up)
    right = lax.ppermute(here[: DILATION_RATE + 1], "tile", down)
    taps = convolution_weight.reshape(channels, 3, 3, 3, channels)
    taps = taps.transpose(1, 3, 0, 2, 4).reshape(3, 3 * channels, 3 * channels)
    params = (w_latent, w_pos, bias_one[None], w_mid, bias_two[None], w_out, bias_out[None])
    partial, *weights = local_part(here, taps, convolution_bias[:, None], params)
    send, keep = main(place, left, right, partial, taps, words, weights, plan)

    keep = keep + swapped(send, plan, plan.stages[0], 1)
    for bits in plan.stages[1:]:
        group = 1 << len(bits)
        keep = keep.reshape(group, keep.shape[0] // group, plan.chunk, LANES)
        arrived = [swapped(keep[step], plan, bits, step) for step in range(1, group)]
        keep = keep[0]
        for block in arrived:
            keep = keep + block
    for bits in reversed(plan.stages[1:]):
        group = 1 << len(bits)
        keep = jnp.concatenate([keep] + [swapped(keep, plan, bits, step) for step in range(1, group)], axis=0)
    other = swapped(keep, plan, plan.stages[0], 1)
    prediction, g_latent, g_pos, g_one, g_mid, g_two, g_out, g_bias, loss = unpack(
        place, keep, other, plan, hidden, channels
    )
    return (
        prediction.transpose(1, 0, 2),
        g_latent,
        g_pos,
        g_one.reshape(hidden),
        g_mid,
        g_two.reshape(hidden),
        g_out,
        g_bias.reshape(5),
        loss.reshape(()),
    )


def solution(mesh):
    return jax.shard_map(
        body,
        mesh=mesh,
        in_specs=(
            P("replica", None, "tile", None, None),
            P(),
            P(),
            P("replica", "tile", None),
            P("replica", "tile"),
            P("replica", None, "tile"),
            P("replica", None, "tile"),
            P(),
            P(),
            P(),
            P(),
            P(),
            P(),
            P(),
        ),
        out_specs=(P("replica", None, "tile"), P(), P(), P(), P(), P(), P(), P(), P()),
        check_vma=False,
    )
```

```python
import functools

import jax
import jax.numpy as jnp
from jax import lax
from jax.experimental import pallas as pl
from jax.experimental.pallas import tpu as pltpu
from jax.sharding import PartitionSpec as P

DILATION_RATE = 2
VISCOSITY = 0.05
DIFFUSIVITY = 0.05
RESIDUAL_WEIGHT = 0.5

F32 = jnp.float32
BF16 = jnp.bfloat16
LANES = 128
BLOCK = 32
WORDS = 128
SUB = 32
NN = (((1,), (0,)), ((), ()))
NT = (((1,), (1,)), ((), ()))
TN = (((0,), (0,)), ((), ()))
VMEM = pl.BlockSpec(memory_space=pltpu.VMEM)
SMEM = pl.BlockSpec(memory_space=pltpu.SMEM)


def mul(left, right, dims=NN):
    return lax.dot_general(left, right, dims, preferred_element_type=F32)


def halves(value):
    high = value.astype(BF16)
    return high, (value - high.astype(F32)).astype(BF16)


def thirds(value):
    high = value.astype(BF16)
    rest = value - high.astype(F32)
    middle = rest.astype(BF16)
    return high, middle, (rest - middle.astype(F32)).astype(BF16)


def mul3(left, right, dims=NN):
    return mul(left[0], right[0], dims) + mul(left[0], right[1], dims) + mul(left[1], right[0], dims)


def route_kernel(tiles, slots, owner_ref, cell_ref, frac_ref, target_ref, out_ref, words):
    queries = owner_ref.shape[1]
    owner = owner_ref[...]
    hits = (lax.broadcasted_iota(jnp.int32, (tiles, queries), 0) == owner).astype(F32)
    before = lax.broadcasted_iota(jnp.int32, (queries, queries), 0) < lax.broadcasted_iota(
        jnp.int32, (queries, queries), 1
    )
    earlier = mul(hits.astype(BF16), before.astype(F32).astype(BF16))
    slot = jnp.sum(hits * earlier, axis=0, keepdims=True)
    place = owner * slots + slot.astype(jnp.int32)
    chosen = (lax.broadcasted_iota(jnp.int32, (tiles * slots, queries), 0) == place).astype(F32).astype(BF16)
    words[...] = jnp.zeros_like(words)
    words[0:1, :] = cell_ref[...].astype(F32)
    for d in range(3):
        words[1 + d : 2 + d, :] = frac_ref[d]
    for f in range(5):
        words[4 + f : 5 + f, :] = target_ref[f]
    words[9:10, :] = jnp.ones((1, queries), F32)
    words[10:11, :] = lax.broadcasted_iota(jnp.int32, (1, queries), 1).astype(F32)
    high, middle, low = thirds(words[...])
    out_ref[...] = mul(chosen, high, NT) + mul(chosen, middle, NT) + mul(chosen, low, NT)


def route(owner, cell, frac, target, tiles, slots):
    queries = owner.shape[1]
    return pl.pallas_call(
        functools.partial(route_kernel, tiles, slots),
        out_shape=jax.ShapeDtypeStruct((tiles * slots, WORDS), F32),
        in_specs=[VMEM] * 4,
        out_specs=VMEM,
        scratch_shapes=[pltpu.VMEM((WORDS, queries), F32)],
        name="route",
    )(owner, cell, frac, target)


def tap_sum(weight_ref, planes, pair):
    total = None
    for step_x, ref, index in planes:
        rows_y = ref.shape[1]
        blocks = [
            jnp.concatenate([ref[index, (2 * pair + half + step_y) % rows_y] for half in (0, 1)], axis=1)
            for step_y in (-1, 0, 1)
        ]
        term = mul(weight_ref[step_x], jnp.concatenate(blocks, axis=0))
        total = term if total is None else total + term
    channels = total.shape[0] // 3
    sides = []
    for half in (0, 1):
        part = total[:, half * LANES : (half + 1) * LANES]
        sides.append(
            part[channels : 2 * channels]
            + pltpu.roll(part[:channels], 1, 1)
            + pltpu.roll(part[2 * channels :], LANES - 1, 1)
        )
    return jnp.concatenate(sides, axis=1)


def local_kernel(
    here_ref,
    weight_ref,
    bias_ref,
    w_latent_ref,
    w_pos_ref,
    bias_one_ref,
    w_mid_ref,
    bias_two_ref,
    w_out_ref,
    bias_out_ref,
    partial_ref,
    latent_high_ref,
    latent_low_ref,
    mid_high_ref,
    mid_low_ref,
    small_ref,
):
    planes, rows_y = here_ref.shape[0], here_ref.shape[1]
    bias = bias_ref[...]
    for x in range(planes + 1):
        taps = [
            (step, here_ref, x + DILATION_RATE * (step - 1))
            for step in range(3)
            if 0 <= x + DILATION_RATE * (step - 1) < planes
        ]
        for pair in range(rows_y // 2):
            partial_ref[x * (rows_y // 2) + pair] = tap_sum(weight_ref, taps, pair) + bias
    for source, high_ref, low_ref in (
        (w_latent_ref, latent_high_ref, latent_low_ref),
        (w_mid_ref, mid_high_ref, mid_low_ref),
    ):
        high, low = halves(source[...])
        high_ref[...] = high
        low_ref[...] = low
    small_ref[...] = jnp.zeros_like(small_ref)
    small_ref[0:3, :] = w_pos_ref[...]
    small_ref[3:4, :] = bias_one_ref[...]
    small_ref[4:5, :] = bias_two_ref[...]
    small_ref[5:6, 0:5] = bias_out_ref[...]
    small_ref[8:13, :] = w_out_ref[...]


def local_part(here, taps, conv_bias, params):
    w_latent, w_mid = params[0], params[3]
    planes, rows_y, channels, rows_z = here.shape
    pairs = (planes + 1) * rows_y // 2
    split = lambda array: [jax.ShapeDtypeStruct(array.shape, BF16)] * 2
    return pl.pallas_call(
        local_kernel,
        out_shape=tuple(
            [jax.ShapeDtypeStruct((pairs, channels, 2 * rows_z), F32)]
            + split(w_latent)
            + split(w_mid)
            + [jax.ShapeDtypeStruct((16, w_mid.shape[0]), F32)]
        ),
        in_specs=[VMEM] * 10,
        out_specs=tuple([VMEM] * 6),
        compiler_params=pltpu.CompilerParams(vmem_limit_bytes=16 << 20),
        cost_estimate=pl.CostEstimate(flops=3 << 30, bytes_accessed=4 << 20, transcendentals=0),
        name="conv_local",
    )(here, taps, conv_bias, *params)


def finish_latent(left_ref, right_ref, partial_ref, weight_ref, planes, lat):
    rows_y = left_ref.shape[1]
    for x in range(planes + 1):
        taps = []
        for step in range(3):
            plane = x + DILATION_RATE * (step - 1)
            if plane < 0:
                taps.append((step, left_ref, plane + left_ref.shape[0]))
            elif plane >= planes:
                taps.append((step, right_ref, plane - planes))
        for pair in range(rows_y // 2):
            number = x * (rows_y // 2) + pair
            summed = partial_ref[number] + tap_sum(weight_ref, taps, pair)
            lat[number] = jax.nn.gelu(summed).astype(BF16)


def interpolate(words, lat, planes, rows_y, rows_z):
    rows = words.shape[0]
    cell = jnp.broadcast_to(words[:, 0:1], (rows, LANES)).astype(jnp.int32)
    frac = [jnp.broadcast_to(words[:, 1 + d : 2 + d], (rows, LANES)) for d in range(3)]
    shift_z = rows_z.bit_length() - 1
    shift_y = rows_y.bit_length() - 1
    base_x = cell >> (shift_z + shift_y)
    base_y = (cell >> shift_z) & (rows_y - 1)
    base_z = cell & (rows_z - 1)
    spot = lax.broadcasted_iota(jnp.int32, (rows, rows_z), 1)
    part_z = jnp.where(spot == base_z, 1.0 - frac[2], 0.0) + jnp.where(
        spot == ((base_z + 1) & (rows_z - 1)), frac[2], 0.0
    )
    total = None
    for x in range(planes + 1):
        part_x = jnp.where(base_x == x, 1.0 - frac[0], jnp.where(base_x == x - 1, frac[0], 0.0))
        for pair in range(rows_y // 2):
            sides = []
            for y in (2 * pair, 2 * pair + 1):
                part_y = jnp.where(
                    base_y == y, 1.0 - frac[1], jnp.where(base_y == (y - 1) % rows_y, frac[1], 0.0)
                )
                sides.append((part_x * part_y * part_z).astype(BF16))
            term = mul(jnp.concatenate(sides, axis=1), lat[x * (rows_y // 2) + pair], NT)
            total = term if total is None else total + term
    return total.astype(BF16), base_x, base_y, base_z, frac


def folded(value):
    return jnp.sum(value.reshape(value.shape[0] // 8, 8, value.shape[1]), axis=0)


def main_kernel(
    plan,
    place_ref,
    left_ref,
    right_ref,
    partial_ref,
    conv_weight_ref,
    words_ref,
    latent_high,
    latent_low,
    mid_high,
    mid_low,
    small_ref,
    send_ref,
    keep_ref,
    lat,
    code,
    pos,
    z_one,
    one_high,
    one_low,
    mixed,
    two_high,
    two_low,
    back,
    d_high,
    d_low,
    out_t,
    d_out_t,
    packed,
):
    rows = plan.tiles * plan.slots
    hidden = mid_high.shape[0]
    latents = latent_high.shape[0]
    planes, rows_y, rows_z = plan.planes, left_ref.shape[1], left_ref.shape[3]
    slots = rows // plan.tiles
    my_block = place_ref[0]
    my_tile = place_ref[1]
    my_replica = place_ref[2]

    finish_latent(left_ref, right_ref, partial_ref, conv_weight_ref, planes, lat)
    words = words_ref[...]
    interp, base_x, base_y, base_z, frac = interpolate(words, lat, planes, rows_y, rows_z)
    code[...] = interp
    global_x = my_tile * planes + base_x
    lane = lax.broadcasted_iota(jnp.int32, (rows, LANES), 1)
    pos[...] = jnp.where(
        lane == 0,
        (global_x.astype(F32) + frac[0]) / (planes * plan.tiles),
        jnp.where(
            lane == 1,
            (base_y.astype(F32) + frac[1]) / rows_y,
            (base_z.astype(F32) + frac[2]) / rows_z,
        ),
    )

    z_one[...] = mul(interp, latent_high[...]) + mul(interp, latent_low[...])
    w_pos = [small_ref[d : d + 1, :] for d in range(3)]
    square = w_pos[0] * w_pos[0] + w_pos[1] * w_pos[1] + w_pos[2] * w_pos[2]
    bias_one = small_ref[3:4, :]
    bias_two = small_ref[4:5, :]

    def store(index, block, refs, value):
        high, low = halves(value)
        refs[0][pl.ds(pl.multiple_of(index * rows + block * BLOCK, BLOCK), BLOCK), :] = high
        refs[1][pl.ds(pl.multiple_of(index * rows + block * BLOCK, BLOCK), BLOCK), :] = low

    def fetch(ref, index, block):
        return ref[pl.ds(pl.multiple_of(index * rows + block * BLOCK, BLOCK), BLOCK), :]

    def layer_one(block, carry):
        where = fetch(pos, 0, block)
        pre = (
            fetch(z_one, 0, block)
            + (where[:, 0:1] * w_pos[0] + where[:, 1:2] * w_pos[1] + where[:, 2:3] * w_pos[2])
            + bias_one
        )
        act = jnp.tanh(pre)
        slope = 1.0 - act * act
        curve = -2.0 * act * slope
        z_one[pl.ds(pl.multiple_of(block * BLOCK, BLOCK), BLOCK), :] = act
        refs = (one_high, one_low)
        store(0, block, refs, act)
        for d in range(3):
            store(1 + d, block, refs, slope * w_pos[d])
        store(4, block, refs, curve * square)
        return carry

    lax.fori_loop(0, rows // BLOCK, layer_one, 0)

    def times_mid(dims, source, result, index, carry):
        span = pl.ds(pl.multiple_of(index * rows, rows), rows)
        result[span, :] = mul3((source[0][span, :], source[1][span, :]), (mid_high[...], mid_low[...]), dims)
        return carry

    lax.fori_loop(0, 5, functools.partial(times_mid, NN, (one_high, one_low), mixed), 0)

    def layer_two(block, carry):
        act = jnp.tanh(fetch(mixed, 0, block) + bias_two)
        slope = 1.0 - act * act
        curve = -2.0 * act * slope
        refs = (two_high, two_low)
        store(0, block, refs, act)
        mixed[pl.ds(pl.multiple_of(block * BLOCK, BLOCK), BLOCK), :] = act
        norm = None
        for d in range(3):
            tangent = fetch(mixed, 1 + d, block)
            store(1 + d, block, refs, slope * tangent)
            norm = tangent * tangent if norm is None else norm + tangent * tangent
        store(4, block, refs, slope * fetch(mixed, 4, block) + curve * norm)
        return carry

    lax.fori_loop(0, rows // BLOCK, layer_two, 0)

    out_fields = small_ref[8:16, :]
    wo_high, wo_low = halves(out_fields)
    wo_both = jnp.concatenate([out_fields, wo_low.astype(F32)], axis=0).astype(BF16)
    for s in range(5):
        span = slice(s * rows, (s + 1) * rows)
        both = mul(wo_both, two_high[span, :], NT)
        out_t[8 * s : 8 * s + 8, :] = both[:8] + both[8:] + mul(wo_high, two_low[span, :], NT)

    words_t = words.T
    target = [words_t[4 + f : 5 + f, :] for f in range(5)]
    valid = words_t[9:10, :]
    value = [out_t[f : f + 1, :] + small_ref[5:6, f : f + 1] for f in range(5)]
    grad = [[out_t[8 * (d + 1) + f : 8 * (d + 1) + f + 1, :] for f in range(5)] for d in range(3)]
    laplace = [out_t[32 + f : 33 + f, :] for f in range(5)]
    velocity = value[2:5]
    advection = [
        velocity[0] * grad[0][f] + velocity[1] * grad[1][f] + velocity[2] * grad[2][f] for f in range(5)
    ]
    continuity = grad[0][2] + grad[1][3] + grad[2][4]
    momentum = [advection[2 + j] + grad[j][1] - VISCOSITY * laplace[2 + j] for j in range(3)]
    momentum[2] = momentum[2] - value[0]
    energy = advection[0] - DIFFUSIVITY * laplace[0]
    misfit = [value[f] - target[f] for f in range(5)]
    physics = (
        continuity * continuity
        + (momentum[0] * momentum[0] + momentum[1] * momentum[1] + momentum[2] * momentum[2])
        + energy * energy
    )
    squares = (
        misfit[0] * misfit[0]
        + misfit[1] * misfit[1]
        + misfit[2] * misfit[2]
        + misfit[3] * misfit[3]
        + misfit[4] * misfit[4]
    )
    point_loss = valid * (squares + RESIDUAL_WEIGHT * physics) * (1.0 / plan.query_total)

    rate = valid * (1.0 / plan.query_total)
    twice = RESIDUAL_WEIGHT * 2.0
    d_cont = rate * twice * continuity
    d_mom = [rate * twice * m for m in momentum]
    d_energy = rate * twice * energy
    d_value = [2.0 * rate * m for m in misfit]
    for d in range(3):
        d_value[2 + d] = d_value[2 + d] + (
            d_mom[0] * grad[d][2] + d_mom[1] * grad[d][3] + d_mom[2] * grad[d][4] + d_energy * grad[d][0]
        )
    d_value[0] = d_value[0] - d_mom[2]
    d_out_t[...] = jnp.zeros_like(d_out_t)
    for f in range(5):
        d_out_t[f : f + 1, :] = d_value[f]
    for d in range(3):
        first = 8 * (d + 1)
        d_out_t[first : first + 1, :] = d_energy * velocity[d]
        d_out_t[first + 1 : first + 2, :] = d_mom[d]
        for j in range(3):
            term = d_mom[j] * velocity[d]
            if j == d:
                term = term + d_cont
            d_out_t[first + 2 + j : first + 3 + j, :] = term
    d_out_t[32:33, :] = -DIFFUSIVITY * d_energy
    for j in range(3):
        d_out_t[34 + j : 35 + j, :] = -VISCOSITY * d_mom[j]

    for s in range(5):
        span = slice(s * rows, (s + 1) * rows)
        wanted = d_out_t[8 * s : 8 * s + 8, :]
        do_high, do_low = halves(wanted)
        back[span, :] = mul3((do_high, do_low), (wo_high, wo_low), TN)

    def second_back(block, total):
        act = fetch(mixed, 0, block)
        slope = 1.0 - act * act
        curve = -2.0 * act * slope
        tangent = [fetch(mixed, 1 + d, block) for d in range(3)]
        cot_t = [fetch(back, 1 + d, block) for d in range(3)]
        cot_l = fetch(back, 4, block)
        refs = (d_high, d_low)
        d_slope = cot_l * fetch(mixed, 4, block)
        norm = None
        bent = 2.0 * curve * cot_l
        for d in range(3):
            store(1 + d, block, refs, slope * cot_t[d] + bent * tangent[d])
            d_slope = d_slope + cot_t[d] * tangent[d]
            norm = tangent[d] * tangent[d] if norm is None else norm + tangent[d] * tangent[d]
        store(4, block, refs, slope * cot_l)
        d_curve = cot_l * norm
        d_slope = d_slope - 2.0 * act * d_curve
        d_act = fetch(back, 0, block) - 2.0 * slope * d_curve - 2.0 * act * d_slope
        d_pre = slope * d_act
        store(0, block, refs, d_pre)
        return total + folded(d_pre)

    grad_two = lax.fori_loop(0, rows // BLOCK, second_back, jnp.zeros((8, hidden), F32))

    def put(part, first, value):
        while value.shape[0]:
            block, row = first // plan.main_rows, first % plan.main_rows
            count = min(value.shape[0], plan.main_rows - row)
            packed[2 * part + block, row : row + count, :] = value[:count]
            first, value = first + count, value[count:]

    wide = 2 * LANES
    for left in range(hidden // wide):
        for right in range(hidden // wide):
            lefts = slice(left * wide, (left + 1) * wide)
            rights = slice(right * wide, (right + 1) * wide)
            part = mul3(
                (one_high[:, lefts], one_low[:, lefts]), (d_high[:, rights], d_low[:, rights]), TN
            )
            for side in range(2):
                put(2 * right + side, left * wide, part[:, side * LANES : (side + 1) * LANES])

    lax.fori_loop(0, 5, functools.partial(times_mid, NT, (d_high, d_low), back), 0)

    def first_back(block, totals):
        act = fetch(z_one, 0, block)
        slope = 1.0 - act * act
        curve = -2.0 * act * slope
        where = fetch(pos, 0, block)
        cot_t = [fetch(back, 1 + d, block) for d in range(3)]
        cot_l = fetch(back, 4, block)
        d_curve = cot_l * square
        d_slope = cot_t[0] * w_pos[0] + cot_t[1] * w_pos[1] + cot_t[2] * w_pos[2] - 2.0 * act * d_curve
        d_act = fetch(back, 0, block) - 2.0 * slope * d_curve - 2.0 * act * d_slope
        d_pre = slope * d_act
        store(0, block, (d_high, d_low), d_pre)
        sums = [totals[0] + folded(d_pre)]
        for d in range(3):
            sums.append(totals[1 + d] + folded(where[:, d : d + 1] * d_pre + slope * cot_t[d]))
        sums.append(totals[4] + folded(curve * cot_l))
        return tuple(sums)

    sums = lax.fori_loop(
        0, rows // BLOCK, first_back, tuple(jnp.zeros((8, hidden), F32) for _ in range(5))
    )
    d_square = jnp.sum(sums[4], axis=0, keepdims=True)
    grad_latent = mul(code[...], d_high[0:rows, :], TN) + mul(code[...], d_low[0:rows, :], TN)

    grad_out = None
    for s in range(5):
        span = slice(s * rows, (s + 1) * rows)
        wanted = d_out_t[8 * s : 8 * s + 8, :]
        do_high, do_low = halves(wanted)
        do_both = jnp.concatenate([wanted, do_low.astype(F32)], axis=0).astype(BF16)
        both = mul(do_both, two_high[span, :])
        term = both[:8] + both[8:] + mul(do_high, two_low[span, :])
        grad_out = term if grad_out is None else grad_out + term

    lane_row = lax.broadcasted_iota(jnp.int32, (1, hidden), 1)
    last = jnp.where(lane_row == 5, jnp.sum(point_loss), 0.0)
    for f in range(5):
        last = last + jnp.where(lane_row == f, jnp.sum(d_value[f]), 0.0)
    grad_pos = [jnp.sum(sums[1 + d], axis=0, keepdims=True) + 2.0 * w_pos[d] * d_square for d in range(3)]
    misc = grad_pos + [
        jnp.sum(sums[0], axis=0, keepdims=True),
        jnp.sum(grad_two, axis=0, keepdims=True),
        last,
    ]
    misc = jnp.concatenate(misc + [jnp.zeros((2, hidden), F32)], axis=0)
    for part in range(hidden // LANES):
        lanes = slice(part * LANES, (part + 1) * LANES)
        put(part, hidden, grad_latent[:, lanes])
        packed[2 * part, plan.coded_rows :, :] = misc[:, lanes]
        packed[2 * part + 1, plan.coded_rows :, :] = grad_out[:, lanes]

    chosen = jnp.where(
        lane == jnp.broadcast_to(words[:, 10:11], (rows, LANES)).astype(jnp.int32), words[:, 9:10], 0.0
    ).astype(BF16)
    fields = jnp.concatenate(value + [jnp.zeros((3, rows), F32)], axis=0)
    source = lax.broadcasted_iota(jnp.int32, (8, rows), 1) >> (slots.bit_length() - 1)
    spread = jnp.concatenate([jnp.where(source == t, fields, 0.0) for t in range(plan.tiles)], axis=0)
    high, middle, low = thirds(spread)
    spread = mul(high, chosen) + mul(middle, chosen) + mul(low, chosen)
    packed[:, plan.main_rows : plan.coded_rows, :] = jnp.zeros((8, plan.devices, LANES), F32)
    for t in range(plan.tiles):
        row = plan.main_rows + (my_replica * (plan.tiles // 8) + t // 8) * 8
        packed[t % 8, pl.ds(pl.multiple_of(row, 8), 8), :] = spread[8 * t : 8 * t + 8]

    for block in range(8):
        spot = jnp.bitwise_xor(block, my_block) & 3

        @pl.when((my_block >> 2) == block // 4)
        def _():
            keep_ref[spot] = packed[block]

        @pl.when((my_block >> 2) != block // 4)
        def _():
            send_ref[spot] = packed[block]


class Plan:
    def __init__(self, tiles, replicas, queries, planes, hidden, latents):
        self.tiles, self.replicas, self.planes = tiles, replicas, planes
        self.slots = 2 * queries // tiles
        self.devices = tiles * replicas
        self.query_total = float(queries * self.devices)
        self.main_rows = (hidden + latents) // 2
        self.coded_rows = self.main_rows + self.devices
        self.rows = self.coded_rows + 8
        self.scales = -(-(self.coded_rows // SUB + 1) // 16) * 16
        self.sent_rows = self.coded_rows + 16 + self.scales
        top = self.devices.bit_length() - 1
        self.core, self.plane, self.rest = [0], [1, top - 1], list(range(2, top - 1))

    def mask(self, bits, steps):
        return sum(1 << bit for number, bit in enumerate(bits) if steps >> number & 1)

    def my_block(self, device):
        return (device & 1) * 4 + (device >> 1 & 1) + 2 * (device >> self.plane[1] & 1)


def swapped(value, plan, bits, steps):
    mask = plan.mask(bits, steps)
    return lax.ppermute(value, ("replica", "tile"), [(i, i ^ mask) for i in range(plan.devices)])


def encode(plan, read, out_ref):
    starts = list(range(0, plan.coded_rows, SUB))
    parts = [read(start, SUB) for start in starts] + [read(plan.coded_rows, 8)]
    tops = [jnp.max(jnp.abs(part), axis=0, keepdims=True) for part in parts]
    tops = tops + [jnp.zeros_like(tops[0])] * (plan.scales - len(tops))
    power = jnp.floor(jnp.log2(jnp.maximum(jnp.concatenate(tops, axis=0), 1e-30)))
    scale = jnp.exp2(14.0 - power)

    def whole(value):
        return jnp.clip(jnp.round(value), -32767.0, 32767.0)

    def narrow(value):
        return value.astype(jnp.int32).astype(jnp.int16)

    for number, start in enumerate(starts):
        out_ref[start : start + SUB, :] = narrow(whole(parts[number] * scale[number : number + 1]))
    last = len(starts)
    exact = parts[last] * scale[last : last + 1]
    high = whole(exact)
    low = whole((exact - high) * 32768.0)
    out_ref[plan.coded_rows : plan.coded_rows + 16, :] = narrow(jnp.concatenate([high, low], axis=0))
    out_ref[plan.coded_rows + 16 :, :] = narrow(power)


def decoder(plan, ref):
    def widen(value):
        return value.astype(jnp.int32).astype(F32)

    scale = jnp.exp2(widen(ref[plan.coded_rows + 16 :, :]) - 14.0)

    def read(start, count):
        if start < plan.coded_rows:
            number = start // SUB
            return widen(ref[start : start + count, :]) * scale[number : number + 1]
        both = widen(ref[plan.coded_rows : plan.coded_rows + 16, :])
        number = plan.coded_rows // SUB
        return (both[:8] + both[8:] * (1.0 / 32768.0)) * scale[number : number + 1]

    return read


def added(readers):
    def read(start, count):
        total = readers[0](start, count)
        for reader in readers[1:]:
            total = total + reader(start, count)
        return total

    return read


def first_kernel(plan, keep_ref, got_ref, mine_ref, *out_refs):
    def reader(block):
        return lambda start, count: (
            keep_ref[block, start : start + count, :] + got_ref[block, start : start + count, :]
        )

    for number, out_ref in enumerate(out_refs):
        encode(plan, reader(number + 1), out_ref)
    mine_ref[...] = keep_ref[0] + got_ref[0]


def first_sum(keep, got, plan):
    sent = jax.ShapeDtypeStruct((plan.sent_rows, LANES), jnp.int16)
    return pl.pallas_call(
        functools.partial(first_kernel, plan),
        out_shape=(jax.ShapeDtypeStruct(keep.shape[1:], F32), sent, sent, sent),
        in_specs=[VMEM] * 2,
        out_specs=tuple([VMEM] * 4),
        name="sum_core",
    )(keep, got)


def plane_kernel(plan, mine_ref, *refs):
    readers = [lambda start, count: mine_ref[start : start + count, :]]
    encode(plan, added(readers + [decoder(plan, ref) for ref in refs[:-1]]), refs[-1])


def pair_kernel(plan, mine_ref, other_ref, out_ref):
    encode(plan, added([decoder(plan, mine_ref), decoder(plan, other_ref)]), out_ref)


def coded_sum(kernel, blocks, plan, name):
    return pl.pallas_call(
        functools.partial(kernel, plan),
        out_shape=jax.ShapeDtypeStruct((plan.sent_rows, LANES), jnp.int16),
        in_specs=[VMEM] * len(blocks),
        out_specs=VMEM,
        name=name,
    )(*blocks)


def main(place, left, right, partial, taps, words, weights, plan):
    rows = plan.tiles * plan.slots
    hidden = weights[-1].shape[1]
    channels = left.shape[2]
    outs = jax.ShapeDtypeStruct((4, plan.rows, LANES), F32)
    wide = lambda kind: pltpu.VMEM((5 * rows, hidden), kind)
    return pl.pallas_call(
        functools.partial(main_kernel, plan),
        out_shape=(outs, outs),
        in_specs=[SMEM] + [VMEM] * 10,
        out_specs=(VMEM, VMEM),
        scratch_shapes=[
            pltpu.VMEM((partial.shape[0], channels, 2 * LANES), BF16),
            pltpu.VMEM((rows, channels), BF16),
            pltpu.VMEM((rows, LANES), F32),
            pltpu.VMEM((rows, hidden), F32),
            wide(BF16),
            wide(BF16),
            wide(F32),
            wide(BF16),
            wide(BF16),
            wide(F32),
            wide(BF16),
            wide(BF16),
            pltpu.VMEM((40, rows), F32),
            pltpu.VMEM((40, rows), F32),
            pltpu.VMEM((8, plan.rows, LANES), F32),
        ],
        compiler_params=pltpu.CompilerParams(vmem_limit_bytes=48 << 20),
        name="encode_decode",
    )(place, left, right, partial, taps, words, *weights)


def unpack_kernel(plan, place_ref, *refs):
    sources, outs, packed = refs[:8], refs[8:-1], refs[-1]
    prediction_ref, latent_ref, pos_ref, one_ref, mid_ref, two_ref, out_ref, bias_out_ref, loss_ref = outs
    my_block = place_ref[0]
    device = place_ref[2] * plan.tiles + place_ref[1]
    starts = list(range(0, plan.coded_rows, SUB))
    for number, ref in enumerate(sources):
        read = decoder(plan, ref)
        block = jnp.bitwise_xor(number, my_block)
        for start in starts:
            packed[block, start : start + SUB, :] = read(start, SUB)
        packed[block, plan.coded_rows :, :] = read(plan.coded_rows, 8)

    hidden = mid_ref.shape[0]
    latents = latent_ref.shape[0]
    split = plan.main_rows
    for part in range(hidden // LANES):
        lanes = slice(part * LANES, (part + 1) * LANES)
        mid_ref[0:split, lanes] = packed[2 * part, 0:split, :]
        mid_ref[split:, lanes] = packed[2 * part + 1, 0 : hidden - split, :]
        latent_ref[:, lanes] = packed[2 * part + 1, hidden - split : split, :]
        misc = packed[2 * part, plan.coded_rows :, :]
        pos_ref[:, lanes] = misc[0:3]
        one_ref[:, lanes] = misc[3:4]
        two_ref[:, lanes] = misc[4:5]
        out_ref[:, lanes] = packed[2 * part + 1, plan.coded_rows : plan.coded_rows + 5, :]
        if part == 0:
            bias_out_ref[...] = misc[5:6, 0:5]
            loss_ref[...] = misc[5:6, 5:6]
    row = pl.multiple_of(plan.main_rows + (device >> 3) * 8, 8)
    fields = packed[device & 7, pl.ds(row, 8), :]
    for f in range(5):
        prediction_ref[f] = fields[f : f + 1]


def unpack(place, blocks, plan, hidden, latents):
    shapes = [
        (5, 1, LANES),
        (latents, hidden),
        (3, hidden),
        (1, hidden),
        (hidden, hidden),
        (1, hidden),
        (5, hidden),
        (1, 5),
        (1, 1),
    ]
    return pl.pallas_call(
        functools.partial(unpack_kernel, plan),
        out_shape=tuple(jax.ShapeDtypeStruct(shape, F32) for shape in shapes),
        in_specs=[SMEM] + [VMEM] * 8,
        out_specs=tuple([VMEM] * len(shapes)),
        scratch_shapes=[pltpu.VMEM((8, plan.rows, LANES), F32)],
        compiler_params=pltpu.CompilerParams(vmem_limit_bytes=16 << 20),
        name="unpack",
    )(place, *blocks)


def body(
    fields,
    convolution_weight,
    convolution_bias,
    query_owner,
    query_cell,
    query_frac,
    target,
    w_latent,
    w_pos,
    bias_one,
    w_mid,
    bias_two,
    w_out,
    bias_out,
):
    tiles = lax.axis_size("tile")
    replicas = lax.axis_size("replica")
    my_tile = lax.axis_index("tile")
    my_replica = lax.axis_index("replica")
    channels = fields.shape[1]
    queries = query_cell.shape[1]
    hidden = w_mid.shape[0]
    plan = Plan(tiles, replicas, queries, fields.shape[2], hidden, channels)
    device = my_replica * tiles + my_tile
    place = jnp.stack([plan.my_block(device), my_tile, my_replica]).astype(jnp.int32)

    words = route(
        query_owner[:, :, 0],
        query_cell,
        query_frac.transpose(1, 0, 2),
        target.transpose(1, 0, 2),
        tiles,
        plan.slots,
    )
    words, fields = lax.optimization_barrier((words, fields))
    words = lax.all_to_all(
        words.reshape(tiles, plan.slots, WORDS), "tile", split_axis=0, concat_axis=0, tiled=True
    ).reshape(tiles * plan.slots, WORDS)

    here = fields[0].transpose(1, 2, 0, 3)
    up = [(i, (i + 1) % tiles) for i in range(tiles)]
    down = [((i + 1) % tiles, i) for i in range(tiles)]
    left = lax.ppermute(here[-DILATION_RATE:], "tile", up)
    right = lax.ppermute(here[: DILATION_RATE + 1], "tile", down)
    taps = convolution_weight.reshape(channels, 3, 3, 3, channels)
    taps = taps.transpose(1, 3, 0, 2, 4).reshape(3, 3 * channels, 3 * channels)
    params = (w_latent, w_pos, bias_one[None], w_mid, bias_two[None], w_out, bias_out[None])
    partial, *weights = local_part(here, taps, convolution_bias[:, None], params)
    send, keep = main(place, left, right, partial, taps, words, weights, plan)

    mine, *others = first_sum(keep, swapped(send, plan, plan.core, 1), plan)
    arrived = [swapped(block, plan, plan.plane, step + 1) for step, block in enumerate(others)]
    block = coded_sum(plane_kernel, [mine] + arrived, plan, "sum_plane")
    for bit in plan.rest:
        block = coded_sum(pair_kernel, [block, swapped(block, plan, [bit], 1)], plan, "sum_line")
    blocks = [block] + [swapped(block, plan, plan.plane, step) for step in range(1, 4)]
    blocks = blocks + [swapped(block, plan, plan.core, 1) for block in blocks]
    prediction, g_latent, g_pos, g_one, g_mid, g_two, g_out, g_bias, loss = unpack(
        place, blocks, plan, hidden, channels
    )
    return (
        prediction.transpose(1, 0, 2),
        g_latent,
        g_pos,
        g_one.reshape(hidden),
        g_mid,
        g_two.reshape(hidden),
        g_out,
        g_bias.reshape(5),
        loss.reshape(()),
    )


def solution(mesh):
    return jax.shard_map(
        body,
        mesh=mesh,
        in_specs=(
            P("replica", None, "tile", None, None),
            P(),
            P(),
            P("replica", "tile", None),
            P("replica", "tile"),
            P("replica", None, "tile"),
            P("replica", None, "tile"),
            P(),
            P(),
            P(),
            P(),
            P(),
            P(),
            P(),
        ),
        out_specs=(P("replica", None, "tile"), P(), P(), P(), P(), P(), P(), P(), P()),
        check_vma=False,
    )
```

```python
import functools

import jax
import jax.numpy as jnp
from jax import lax
from jax.experimental import pallas as pl
from jax.experimental.pallas import tpu as pltpu
from jax.sharding import PartitionSpec as P

DILATION_RATE = 2
VISCOSITY = 0.05
DIFFUSIVITY = 0.05
RESIDUAL_WEIGHT = 0.5

F32 = jnp.float32
BF16 = jnp.bfloat16
LANES = 128
BLOCK = 32
WORDS = 128
SUB = 32
NN = (((1,), (0,)), ((), ()))
NT = (((1,), (1,)), ((), ()))
TN = (((0,), (0,)), ((), ()))
VMEM = pl.BlockSpec(memory_space=pltpu.VMEM)
SMEM = pl.BlockSpec(memory_space=pltpu.SMEM)


def mul(left, right, dims=NN):
    return lax.dot_general(left, right, dims, preferred_element_type=F32)


def halves(value):
    high = value.astype(BF16)
    return high, (value - high.astype(F32)).astype(BF16)


def thirds(value):
    high = value.astype(BF16)
    rest = value - high.astype(F32)
    middle = rest.astype(BF16)
    return high, middle, (rest - middle.astype(F32)).astype(BF16)


def mul3(left, right, dims=NN):
    return mul(left[0], right[0], dims) + mul(left[0], right[1], dims) + mul(left[1], right[0], dims)


def route_kernel(tiles, slots, owner_ref, cell_ref, frac_ref, target_ref, out_ref, words):
    queries = owner_ref.shape[1]
    owner = owner_ref[...]
    hits = (lax.broadcasted_iota(jnp.int32, (tiles, queries), 0) == owner).astype(F32)
    before = lax.broadcasted_iota(jnp.int32, (queries, queries), 0) < lax.broadcasted_iota(
        jnp.int32, (queries, queries), 1
    )
    earlier = mul(hits.astype(BF16), before.astype(F32).astype(BF16))
    slot = jnp.sum(hits * earlier, axis=0, keepdims=True)
    place = owner * slots + slot.astype(jnp.int32)
    chosen = (lax.broadcasted_iota(jnp.int32, (tiles * slots, queries), 0) == place).astype(F32).astype(BF16)
    words[...] = jnp.zeros_like(words)
    words[0:1, :] = cell_ref[...].astype(F32)
    for d in range(3):
        words[1 + d : 2 + d, :] = frac_ref[d]
    for f in range(5):
        words[4 + f : 5 + f, :] = target_ref[f]
    words[9:10, :] = jnp.ones((1, queries), F32)
    words[10:11, :] = lax.broadcasted_iota(jnp.int32, (1, queries), 1).astype(F32)
    high, middle, low = thirds(words[...])
    out_ref[...] = mul(chosen, high, NT) + mul(chosen, middle, NT) + mul(chosen, low, NT)


def route(owner, cell, frac, target, tiles, slots):
    queries = owner.shape[1]
    return pl.pallas_call(
        functools.partial(route_kernel, tiles, slots),
        out_shape=jax.ShapeDtypeStruct((tiles * slots, WORDS), F32),
        in_specs=[VMEM] * 4,
        out_specs=VMEM,
        scratch_shapes=[pltpu.VMEM((WORDS, queries), F32)],
        compiler_params=pltpu.CompilerParams(vmem_limit_bytes=4 << 20),
        name="route",
    )(owner, cell, frac, target)


def tap_sum(weight_ref, planes, pair):
    total = None
    for step_x, ref, index in planes:
        rows_y = ref.shape[1]
        blocks = [
            jnp.concatenate([ref[index, (2 * pair + half + step_y) % rows_y] for half in (0, 1)], axis=1)
            for step_y in (-1, 0, 1)
        ]
        term = mul(weight_ref[step_x], jnp.concatenate(blocks, axis=0))
        total = term if total is None else total + term
    channels = total.shape[0] // 3
    sides = []
    for half in (0, 1):
        part = total[:, half * LANES : (half + 1) * LANES]
        sides.append(
            part[channels : 2 * channels]
            + pltpu.roll(part[:channels], 1, 1)
            + pltpu.roll(part[2 * channels :], LANES - 1, 1)
        )
    return jnp.concatenate(sides, axis=1)


def local_kernel(
    here_ref,
    weight_ref,
    bias_ref,
    w_latent_ref,
    w_pos_ref,
    bias_one_ref,
    w_mid_ref,
    bias_two_ref,
    w_out_ref,
    bias_out_ref,
    partial_ref,
    latent_high_ref,
    latent_low_ref,
    mid_high_ref,
    mid_low_ref,
    small_ref,
):
    planes, rows_y = here_ref.shape[0], here_ref.shape[1]
    bias = bias_ref[...]
    for x in range(planes + 1):
        taps = [
            (step, here_ref, x + DILATION_RATE * (step - 1))
            for step in range(3)
            if 0 <= x + DILATION_RATE * (step - 1) < planes
        ]
        for pair in range(rows_y // 2):
            partial_ref[x * (rows_y // 2) + pair] = tap_sum(weight_ref, taps, pair) + bias
    for source, high_ref, low_ref in (
        (w_latent_ref, latent_high_ref, latent_low_ref),
        (w_mid_ref, mid_high_ref, mid_low_ref),
    ):
        high, low = halves(source[...])
        high_ref[...] = high
        low_ref[...] = low
    small_ref[...] = jnp.zeros_like(small_ref)
    small_ref[0:3, :] = w_pos_ref[...]
    small_ref[3:4, :] = bias_one_ref[...]
    small_ref[4:5, :] = bias_two_ref[...]
    small_ref[5:6, 0:5] = bias_out_ref[...]
    small_ref[8:13, :] = w_out_ref[...]


def local_part(here, taps, conv_bias, params):
    w_latent, w_mid = params[0], params[3]
    planes, rows_y, channels, rows_z = here.shape
    pairs = (planes + 1) * rows_y // 2
    split = lambda array: [jax.ShapeDtypeStruct(array.shape, BF16)] * 2
    return pl.pallas_call(
        local_kernel,
        out_shape=tuple(
            [jax.ShapeDtypeStruct((pairs, channels, 2 * rows_z), F32)]
            + split(w_latent)
            + split(w_mid)
            + [jax.ShapeDtypeStruct((16, w_mid.shape[0]), F32)]
        ),
        in_specs=[VMEM] * 10,
        out_specs=tuple([VMEM] * 6),
        compiler_params=pltpu.CompilerParams(vmem_limit_bytes=16 << 20),
        cost_estimate=pl.CostEstimate(flops=3 << 30, bytes_accessed=4 << 20, transcendentals=0),
        name="conv_local",
    )(here, taps, conv_bias, *params)


def finish_latent(left_ref, right_ref, partial_ref, weight_ref, planes, lat):
    rows_y = left_ref.shape[1]
    for x in range(planes + 1):
        taps = []
        for step in range(3):
            plane = x + DILATION_RATE * (step - 1)
            if plane < 0:
                taps.append((step, left_ref, plane + left_ref.shape[0]))
            elif plane >= planes:
                taps.append((step, right_ref, plane - planes))
        for pair in range(rows_y // 2):
            number = x * (rows_y // 2) + pair
            summed = partial_ref[number] + tap_sum(weight_ref, taps, pair)
            lat[number] = jax.nn.gelu(summed).astype(BF16)


def interpolate(words, lat, planes, rows_y, rows_z):
    rows = words.shape[0]
    cell = jnp.broadcast_to(words[:, 0:1], (rows, LANES)).astype(jnp.int32)
    frac = [jnp.broadcast_to(words[:, 1 + d : 2 + d], (rows, LANES)) for d in range(3)]
    shift_z = rows_z.bit_length() - 1
    shift_y = rows_y.bit_length() - 1
    base_x = cell >> (shift_z + shift_y)
    base_y = (cell >> shift_z) & (rows_y - 1)
    base_z = cell & (rows_z - 1)
    spot = lax.broadcasted_iota(jnp.int32, (rows, rows_z), 1)
    part_z = jnp.where(spot == base_z, 1.0 - frac[2], 0.0) + jnp.where(
        spot == ((base_z + 1) & (rows_z - 1)), frac[2], 0.0
    )
    total = None
    for x in range(planes + 1):
        part_x = jnp.where(base_x == x, 1.0 - frac[0], jnp.where(base_x == x - 1, frac[0], 0.0))
        for pair in range(rows_y // 2):
            sides = []
            for y in (2 * pair, 2 * pair + 1):
                part_y = jnp.where(
                    base_y == y, 1.0 - frac[1], jnp.where(base_y == (y - 1) % rows_y, frac[1], 0.0)
                )
                sides.append((part_x * part_y * part_z).astype(BF16))
            term = mul(jnp.concatenate(sides, axis=1), lat[x * (rows_y // 2) + pair], NT)
            total = term if total is None else total + term
    return total.astype(BF16), base_x, base_y, base_z, frac


def folded(value):
    return jnp.sum(value.reshape(value.shape[0] // 8, 8, value.shape[1]), axis=0)


def main_kernel(
    plan,
    place_ref,
    left_ref,
    right_ref,
    partial_ref,
    conv_weight_ref,
    words_ref,
    latent_high,
    latent_low,
    mid_high,
    mid_low,
    small_ref,
    send_ref,
    keep_ref,
    lat,
    code,
    pos,
    z_one,
    one_high,
    one_low,
    mixed,
    two_high,
    two_low,
    back,
    d_high,
    d_low,
    out_t,
    d_out_t,
    packed,
):
    rows = plan.tiles * plan.slots
    hidden = mid_high.shape[0]
    latents = latent_high.shape[0]
    planes, rows_y, rows_z = plan.planes, left_ref.shape[1], left_ref.shape[3]
    slots = rows // plan.tiles
    my_block = place_ref[0]
    my_tile = place_ref[1]
    my_replica = place_ref[2]

    finish_latent(left_ref, right_ref, partial_ref, conv_weight_ref, planes, lat)
    words = words_ref[...]
    interp, base_x, base_y, base_z, frac = interpolate(words, lat, planes, rows_y, rows_z)
    code[...] = interp
    global_x = my_tile * planes + base_x
    lane = lax.broadcasted_iota(jnp.int32, (rows, LANES), 1)
    pos[...] = jnp.where(
        lane == 0,
        (global_x.astype(F32) + frac[0]) / (planes * plan.tiles),
        jnp.where(
            lane == 1,
            (base_y.astype(F32) + frac[1]) / rows_y,
            (base_z.astype(F32) + frac[2]) / rows_z,
        ),
    )

    z_one[...] = mul(interp, latent_high[...]) + mul(interp, latent_low[...])
    w_pos = [small_ref[d : d + 1, :] for d in range(3)]
    square = w_pos[0] * w_pos[0] + w_pos[1] * w_pos[1] + w_pos[2] * w_pos[2]
    bias_one = small_ref[3:4, :]
    bias_two = small_ref[4:5, :]

    def store(index, block, refs, value):
        high, low = halves(value)
        refs[0][pl.ds(pl.multiple_of(index * rows + block * BLOCK, BLOCK), BLOCK), :] = high
        refs[1][pl.ds(pl.multiple_of(index * rows + block * BLOCK, BLOCK), BLOCK), :] = low

    def fetch(ref, index, block):
        return ref[pl.ds(pl.multiple_of(index * rows + block * BLOCK, BLOCK), BLOCK), :]

    def layer_one(block, carry):
        where = fetch(pos, 0, block)
        pre = (
            fetch(z_one, 0, block)
            + (where[:, 0:1] * w_pos[0] + where[:, 1:2] * w_pos[1] + where[:, 2:3] * w_pos[2])
            + bias_one
        )
        act = jnp.tanh(pre)
        slope = 1.0 - act * act
        curve = -2.0 * act * slope
        z_one[pl.ds(pl.multiple_of(block * BLOCK, BLOCK), BLOCK), :] = act
        refs = (one_high, one_low)
        store(0, block, refs, act)
        for d in range(3):
            store(1 + d, block, refs, slope * w_pos[d])
        store(4, block, refs, curve * square)
        return carry

    lax.fori_loop(0, rows // BLOCK, layer_one, 0)

    def times_mid(dims, source, result, index, carry):
        span = pl.ds(pl.multiple_of(index * rows, rows), rows)
        result[span, :] = mul3((source[0][span, :], source[1][span, :]), (mid_high[...], mid_low[...]), dims)
        return carry

    lax.fori_loop(0, 5, functools.partial(times_mid, NN, (one_high, one_low), mixed), 0)

    def layer_two(block, carry):
        act = jnp.tanh(fetch(mixed, 0, block) + bias_two)
        slope = 1.0 - act * act
        curve = -2.0 * act * slope
        refs = (two_high, two_low)
        store(0, block, refs, act)
        mixed[pl.ds(pl.multiple_of(block * BLOCK, BLOCK), BLOCK), :] = act
        norm = None
        for d in range(3):
            tangent = fetch(mixed, 1 + d, block)
            store(1 + d, block, refs, slope * tangent)
            norm = tangent * tangent if norm is None else norm + tangent * tangent
        store(4, block, refs, slope * fetch(mixed, 4, block) + curve * norm)
        return carry

    lax.fori_loop(0, rows // BLOCK, layer_two, 0)

    out_fields = small_ref[8:16, :]
    wo_high, wo_low = halves(out_fields)
    wo_both = jnp.concatenate([out_fields, wo_low.astype(F32)], axis=0).astype(BF16)
    for s in range(5):
        span = slice(s * rows, (s + 1) * rows)
        both = mul(wo_both, two_high[span, :], NT)
        out_t[8 * s : 8 * s + 8, :] = both[:8] + both[8:] + mul(wo_high, two_low[span, :], NT)

    words_t = words.T
    target = [words_t[4 + f : 5 + f, :] for f in range(5)]
    valid = words_t[9:10, :]
    value = [out_t[f : f + 1, :] + small_ref[5:6, f : f + 1] for f in range(5)]
    grad = [[out_t[8 * (d + 1) + f : 8 * (d + 1) + f + 1, :] for f in range(5)] for d in range(3)]
    laplace = [out_t[32 + f : 33 + f, :] for f in range(5)]
    velocity = value[2:5]
    advection = [
        velocity[0] * grad[0][f] + velocity[1] * grad[1][f] + velocity[2] * grad[2][f] for f in range(5)
    ]
    continuity = grad[0][2] + grad[1][3] + grad[2][4]
    momentum = [advection[2 + j] + grad[j][1] - VISCOSITY * laplace[2 + j] for j in range(3)]
    momentum[2] = momentum[2] - value[0]
    energy = advection[0] - DIFFUSIVITY * laplace[0]
    misfit = [value[f] - target[f] for f in range(5)]
    physics = (
        continuity * continuity
        + (momentum[0] * momentum[0] + momentum[1] * momentum[1] + momentum[2] * momentum[2])
        + energy * energy
    )
    squares = (
        misfit[0] * misfit[0]
        + misfit[1] * misfit[1]
        + misfit[2] * misfit[2]
        + misfit[3] * misfit[3]
        + misfit[4] * misfit[4]
    )
    point_loss = valid * (squares + RESIDUAL_WEIGHT * physics) * (1.0 / plan.query_total)

    rate = valid * (1.0 / plan.query_total)
    twice = RESIDUAL_WEIGHT * 2.0
    d_cont = rate * twice * continuity
    d_mom = [rate * twice * m for m in momentum]
    d_energy = rate * twice * energy
    d_value = [2.0 * rate * m for m in misfit]
    for d in range(3):
        d_value[2 + d] = d_value[2 + d] + (
            d_mom[0] * grad[d][2] + d_mom[1] * grad[d][3] + d_mom[2] * grad[d][4] + d_energy * grad[d][0]
        )
    d_value[0] = d_value[0] - d_mom[2]
    d_out_t[...] = jnp.zeros_like(d_out_t)
    for f in range(5):
        d_out_t[f : f + 1, :] = d_value[f]
    for d in range(3):
        first = 8 * (d + 1)
        d_out_t[first : first + 1, :] = d_energy * velocity[d]
        d_out_t[first + 1 : first + 2, :] = d_mom[d]
        for j in range(3):
            term = d_mom[j] * velocity[d]
            if j == d:
                term = term + d_cont
            d_out_t[first + 2 + j : first + 3 + j, :] = term
    d_out_t[32:33, :] = -DIFFUSIVITY * d_energy
    for j in range(3):
        d_out_t[34 + j : 35 + j, :] = -VISCOSITY * d_mom[j]

    for s in range(5):
        span = slice(s * rows, (s + 1) * rows)
        wanted = d_out_t[8 * s : 8 * s + 8, :]
        do_high, do_low = halves(wanted)
        back[span, :] = mul3((do_high, do_low), (wo_high, wo_low), TN)

    def second_back(block, total):
        act = fetch(mixed, 0, block)
        slope = 1.0 - act * act
        curve = -2.0 * act * slope
        tangent = [fetch(mixed, 1 + d, block) for d in range(3)]
        cot_t = [fetch(back, 1 + d, block) for d in range(3)]
        cot_l = fetch(back, 4, block)
        refs = (d_high, d_low)
        d_slope = cot_l * fetch(mixed, 4, block)
        norm = None
        bent = 2.0 * curve * cot_l
        for d in range(3):
            store(1 + d, block, refs, slope * cot_t[d] + bent * tangent[d])
            d_slope = d_slope + cot_t[d] * tangent[d]
            norm = tangent[d] * tangent[d] if norm is None else norm + tangent[d] * tangent[d]
        store(4, block, refs, slope * cot_l)
        d_curve = cot_l * norm
        d_slope = d_slope - 2.0 * act * d_curve
        d_act = fetch(back, 0, block) - 2.0 * slope * d_curve - 2.0 * act * d_slope
        d_pre = slope * d_act
        store(0, block, refs, d_pre)
        return total + folded(d_pre)

    grad_two = lax.fori_loop(0, rows // BLOCK, second_back, jnp.zeros((8, hidden), F32))

    def put(part, first, value):
        while value.shape[0]:
            block, row = first // plan.main_rows, first % plan.main_rows
            count = min(value.shape[0], plan.main_rows - row)
            packed[2 * part + block, row : row + count, :] = value[:count]
            first, value = first + count, value[count:]

    wide = 2 * LANES
    for left in range(hidden // wide):
        for right in range(hidden // wide):
            lefts = slice(left * wide, (left + 1) * wide)
            rights = slice(right * wide, (right + 1) * wide)
            part = mul3(
                (one_high[:, lefts], one_low[:, lefts]), (d_high[:, rights], d_low[:, rights]), TN
            )
            for side in range(2):
                put(2 * right + side, left * wide, part[:, side * LANES : (side + 1) * LANES])

    lax.fori_loop(0, 5, functools.partial(times_mid, NT, (d_high, d_low), back), 0)

    def first_back(block, totals):
        act = fetch(z_one, 0, block)
        slope = 1.0 - act * act
        curve = -2.0 * act * slope
        where = fetch(pos, 0, block)
        cot_t = [fetch(back, 1 + d, block) for d in range(3)]
        cot_l = fetch(back, 4, block)
        d_curve = cot_l * square
        d_slope = cot_t[0] * w_pos[0] + cot_t[1] * w_pos[1] + cot_t[2] * w_pos[2] - 2.0 * act * d_curve
        d_act = fetch(back, 0, block) - 2.0 * slope * d_curve - 2.0 * act * d_slope
        d_pre = slope * d_act
        store(0, block, (d_high, d_low), d_pre)
        sums = [totals[0] + folded(d_pre)]
        for d in range(3):
            sums.append(totals[1 + d] + folded(where[:, d : d + 1] * d_pre + slope * cot_t[d]))
        sums.append(totals[4] + folded(curve * cot_l))
        return tuple(sums)

    sums = lax.fori_loop(
        0, rows // BLOCK, first_back, tuple(jnp.zeros((8, hidden), F32) for _ in range(5))
    )
    d_square = jnp.sum(sums[4], axis=0, keepdims=True)
    grad_latent = mul(code[...], d_high[0:rows, :], TN) + mul(code[...], d_low[0:rows, :], TN)

    grad_out = None
    for s in range(5):
        span = slice(s * rows, (s + 1) * rows)
        wanted = d_out_t[8 * s : 8 * s + 8, :]
        do_high, do_low = halves(wanted)
        do_both = jnp.concatenate([wanted, do_low.astype(F32)], axis=0).astype(BF16)
        both = mul(do_both, two_high[span, :])
        term = both[:8] + both[8:] + mul(do_high, two_low[span, :])
        grad_out = term if grad_out is None else grad_out + term

    lane_row = lax.broadcasted_iota(jnp.int32, (1, hidden), 1)
    last = jnp.where(lane_row == 5, jnp.sum(point_loss), 0.0)
    for f in range(5):
        last = last + jnp.where(lane_row == f, jnp.sum(d_value[f]), 0.0)
    grad_pos = [jnp.sum(sums[1 + d], axis=0, keepdims=True) + 2.0 * w_pos[d] * d_square for d in range(3)]
    misc = grad_pos + [
        jnp.sum(sums[0], axis=0, keepdims=True),
        jnp.sum(grad_two, axis=0, keepdims=True),
        last,
    ]
    misc = jnp.concatenate(misc + [jnp.zeros((2, hidden), F32)], axis=0)
    for part in range(hidden // LANES):
        lanes = slice(part * LANES, (part + 1) * LANES)
        put(part, hidden, grad_latent[:, lanes])
        packed[2 * part, plan.coded_rows :, :] = misc[:, lanes]
        packed[2 * part + 1, plan.coded_rows :, :] = grad_out[:, lanes]

    chosen = jnp.where(
        lane == jnp.broadcast_to(words[:, 10:11], (rows, LANES)).astype(jnp.int32), words[:, 9:10], 0.0
    ).astype(BF16)
    fields = jnp.concatenate(value + [jnp.zeros((3, rows), F32)], axis=0)
    source = lax.broadcasted_iota(jnp.int32, (8, rows), 1) >> (slots.bit_length() - 1)
    spread = jnp.concatenate([jnp.where(source == t, fields, 0.0) for t in range(plan.tiles)], axis=0)
    high, middle, low = thirds(spread)
    spread = mul(high, chosen) + mul(middle, chosen) + mul(low, chosen)
    packed[:, plan.main_rows : plan.coded_rows, :] = jnp.zeros((8, plan.devices, LANES), F32)
    for t in range(plan.tiles):
        row = plan.main_rows + (my_replica * (plan.tiles // 8) + t // 8) * 8
        packed[t % 8, pl.ds(pl.multiple_of(row, 8), 8), :] = spread[8 * t : 8 * t + 8]

    for block in range(8):
        spot = jnp.bitwise_xor(block, my_block) & 3

        @pl.when((my_block >> 2) == block // 4)
        def _():
            keep_ref[spot] = packed[block]

        @pl.when((my_block >> 2) != block // 4)
        def _():
            send_ref[spot] = packed[block]


class Plan:
    def __init__(self, tiles, replicas, queries, planes, hidden, latents):
        self.tiles, self.replicas, self.planes = tiles, replicas, planes
        self.slots = 2 * queries // tiles
        self.devices = tiles * replicas
        self.query_total = float(queries * self.devices)
        self.main_rows = (hidden + latents) // 2
        self.coded_rows = self.main_rows + self.devices
        self.rows = self.coded_rows + 8
        self.scales = -(-(self.coded_rows // SUB + 1) // 16) * 16
        self.sent_rows = self.coded_rows + 16 + self.scales
        top = self.devices.bit_length() - 1
        self.core, self.plane, self.rest = [0], [1, top - 1], list(range(2, top - 1))

    def mask(self, bits, steps):
        return sum(1 << bit for number, bit in enumerate(bits) if steps >> number & 1)

    def my_block(self, device):
        return (device & 1) * 4 + (device >> 1 & 1) + 2 * (device >> self.plane[1] & 1)


def swapped(value, plan, bits, steps):
    mask = plan.mask(bits, steps)
    return lax.ppermute(value, ("replica", "tile"), [(i, i ^ mask) for i in range(plan.devices)])


def encode(plan, read, out_ref):
    starts = list(range(0, plan.coded_rows, SUB))
    parts = [read(start, SUB) for start in starts] + [read(plan.coded_rows, 8)]
    tops = [jnp.max(jnp.abs(part), axis=0, keepdims=True) for part in parts]
    tops = tops + [jnp.zeros_like(tops[0])] * (plan.scales - len(tops))
    power = jnp.floor(jnp.log2(jnp.maximum(jnp.concatenate(tops, axis=0), 1e-30)))
    scale = jnp.exp2(14.0 - power)

    def whole(value):
        return jnp.clip(jnp.round(value), -32767.0, 32767.0)

    def narrow(value):
        return value.astype(jnp.int32).astype(jnp.int16)

    for number, start in enumerate(starts):
        out_ref[start : start + SUB, :] = narrow(whole(parts[number] * scale[number : number + 1]))
    last = len(starts)
    exact = parts[last] * scale[last : last + 1]
    high = whole(exact)
    low = whole((exact - high) * 32768.0)
    out_ref[plan.coded_rows : plan.coded_rows + 16, :] = narrow(jnp.concatenate([high, low], axis=0))
    out_ref[plan.coded_rows + 16 :, :] = narrow(power)


def decoder(plan, ref):
    def widen(value):
        return value.astype(jnp.int32).astype(F32)

    scale = jnp.exp2(widen(ref[plan.coded_rows + 16 :, :]) - 14.0)

    def read(start, count):
        if start < plan.coded_rows:
            number = start // SUB
            return widen(ref[start : start + count, :]) * scale[number : number + 1]
        both = widen(ref[plan.coded_rows : plan.coded_rows + 16, :])
        number = plan.coded_rows // SUB
        return (both[:8] + both[8:] * (1.0 / 32768.0)) * scale[number : number + 1]

    return read


def added(readers):
    def read(start, count):
        total = readers[0](start, count)
        for reader in readers[1:]:
            total = total + reader(start, count)
        return total

    return read


def first_kernel(plan, keep_ref, got_ref, mine_ref, *out_refs):
    def reader(block):
        return lambda start, count: (
            keep_ref[block, start : start + count, :] + got_ref[block, start : start + count, :]
        )

    for number, out_ref in enumerate(out_refs):
        encode(plan, reader(number + 1), out_ref)
    mine_ref[...] = keep_ref[0] + got_ref[0]


def first_sum(keep, got, plan):
    sent = jax.ShapeDtypeStruct((plan.sent_rows, LANES), jnp.int16)
    return pl.pallas_call(
        functools.partial(first_kernel, plan),
        out_shape=(jax.ShapeDtypeStruct(keep.shape[1:], F32), sent, sent, sent),
        in_specs=[VMEM] * 2,
        out_specs=tuple([VMEM] * 4),
        compiler_params=pltpu.CompilerParams(vmem_limit_bytes=6 << 20),
        name="sum_core",
    )(keep, got)


def plane_kernel(plan, mine_ref, *refs):
    readers = [lambda start, count: mine_ref[start : start + count, :]]
    encode(plan, added(readers + [decoder(plan, ref) for ref in refs[:-1]]), refs[-1])


def pair_kernel(plan, mine_ref, other_ref, out_ref):
    encode(plan, added([decoder(plan, mine_ref), decoder(plan, other_ref)]), out_ref)


def coded_sum(kernel, blocks, plan, name):
    return pl.pallas_call(
        functools.partial(kernel, plan),
        out_shape=jax.ShapeDtypeStruct((plan.sent_rows, LANES), jnp.int16),
        in_specs=[VMEM] * len(blocks),
        out_specs=VMEM,
        compiler_params=pltpu.CompilerParams(vmem_limit_bytes=4 << 20),
        name=name,
    )(*blocks)


def main(place, left, right, partial, taps, words, weights, plan):
    rows = plan.tiles * plan.slots
    hidden = weights[-1].shape[1]
    channels = left.shape[2]
    outs = jax.ShapeDtypeStruct((4, plan.rows, LANES), F32)
    wide = lambda kind: pltpu.VMEM((5 * rows, hidden), kind)
    return pl.pallas_call(
        functools.partial(main_kernel, plan),
        out_shape=(outs, outs),
        in_specs=[SMEM] + [VMEM] * 10,
        out_specs=(VMEM, VMEM),
        scratch_shapes=[
            pltpu.VMEM((partial.shape[0], channels, 2 * LANES), BF16),
            pltpu.VMEM((rows, channels), BF16),
            pltpu.VMEM((rows, LANES), F32),
            pltpu.VMEM((rows, hidden), F32),
            wide(BF16),
            wide(BF16),
            wide(F32),
            wide(BF16),
            wide(BF16),
            wide(F32),
            wide(BF16),
            wide(BF16),
            pltpu.VMEM((40, rows), F32),
            pltpu.VMEM((40, rows), F32),
            pltpu.VMEM((8, plan.rows, LANES), F32),
        ],
        compiler_params=pltpu.CompilerParams(vmem_limit_bytes=32 << 20),
        name="encode_decode",
    )(place, left, right, partial, taps, words, *weights)


def unpack_kernel(plan, place_ref, *refs):
    sources, outs, packed = refs[:8], refs[8:-1], refs[-1]
    prediction_ref, latent_ref, pos_ref, one_ref, mid_ref, two_ref, out_ref, bias_out_ref, loss_ref = outs
    my_block = place_ref[0]
    device = place_ref[2] * plan.tiles + place_ref[1]
    starts = list(range(0, plan.coded_rows, SUB))
    for number, ref in enumerate(sources):
        read = decoder(plan, ref)
        block = jnp.bitwise_xor(number, my_block)
        for start in starts:
            packed[block, start : start + SUB, :] = read(start, SUB)
        packed[block, plan.coded_rows :, :] = read(plan.coded_rows, 8)

    hidden = mid_ref.shape[0]
    latents = latent_ref.shape[0]
    split = plan.main_rows
    for part in range(hidden // LANES):
        lanes = slice(part * LANES, (part + 1) * LANES)
        mid_ref[0:split, lanes] = packed[2 * part, 0:split, :]
        mid_ref[split:, lanes] = packed[2 * part + 1, 0 : hidden - split, :]
        latent_ref[:, lanes] = packed[2 * part + 1, hidden - split : split, :]
        misc = packed[2 * part, plan.coded_rows :, :]
        pos_ref[:, lanes] = misc[0:3]
        one_ref[:, lanes] = misc[3:4]
        two_ref[:, lanes] = misc[4:5]
        out_ref[:, lanes] = packed[2 * part + 1, plan.coded_rows : plan.coded_rows + 5, :]
        if part == 0:
            bias_out_ref[...] = misc[5:6, 0:5]
            loss_ref[...] = misc[5:6, 5:6]
    row = pl.multiple_of(plan.main_rows + (device >> 3) * 8, 8)
    fields = packed[device & 7, pl.ds(row, 8), :]
    for f in range(5):
        prediction_ref[f] = fields[f : f + 1]


def unpack(place, blocks, plan, hidden, latents):
    shapes = [
        (5, 1, LANES),
        (latents, hidden),
        (3, hidden),
        (1, hidden),
        (hidden, hidden),
        (1, hidden),
        (5, hidden),
        (1, 5),
        (1, 1),
    ]
    return pl.pallas_call(
        functools.partial(unpack_kernel, plan),
        out_shape=tuple(jax.ShapeDtypeStruct(shape, F32) for shape in shapes),
        in_specs=[SMEM] + [VMEM] * 8,
        out_specs=tuple([VMEM] * len(shapes)),
        scratch_shapes=[pltpu.VMEM((8, plan.rows, LANES), F32)],
        compiler_params=pltpu.CompilerParams(vmem_limit_bytes=16 << 20),
        name="unpack",
    )(place, *blocks)


def body(
    fields,
    convolution_weight,
    convolution_bias,
    query_owner,
    query_cell,
    query_frac,
    target,
    w_latent,
    w_pos,
    bias_one,
    w_mid,
    bias_two,
    w_out,
    bias_out,
):
    tiles = lax.axis_size("tile")
    replicas = lax.axis_size("replica")
    my_tile = lax.axis_index("tile")
    my_replica = lax.axis_index("replica")
    channels = fields.shape[1]
    queries = query_cell.shape[1]
    hidden = w_mid.shape[0]
    plan = Plan(tiles, replicas, queries, fields.shape[2], hidden, channels)
    device = my_replica * tiles + my_tile
    place = jnp.stack([plan.my_block(device), my_tile, my_replica]).astype(jnp.int32)

    here = fields[0].transpose(1, 2, 0, 3)
    here, query_owner = lax.optimization_barrier((here, query_owner))
    up = [(i, (i + 1) % tiles) for i in range(tiles)]
    down = [((i + 1) % tiles, i) for i in range(tiles)]
    left = lax.ppermute(here[-DILATION_RATE:], "tile", up)
    right = lax.ppermute(here[: DILATION_RATE + 1], "tile", down)
    words = route(
        query_owner[:, :, 0],
        query_cell,
        query_frac.transpose(1, 0, 2),
        target.transpose(1, 0, 2),
        tiles,
        plan.slots,
    )
    words = lax.all_to_all(
        words.reshape(tiles, plan.slots, WORDS), "tile", split_axis=0, concat_axis=0, tiled=True
    ).reshape(tiles * plan.slots, WORDS)

    taps = convolution_weight.reshape(channels, 3, 3, 3, channels)
    taps = taps.transpose(1, 3, 0, 2, 4).reshape(3, 3 * channels, 3 * channels)
    params = (w_latent, w_pos, bias_one[None], w_mid, bias_two[None], w_out, bias_out[None])
    partial, *weights = local_part(here, taps, convolution_bias[:, None], params)
    send, keep = main(place, left, right, partial, taps, words, weights, plan)

    mine, *others = first_sum(keep, swapped(send, plan, plan.core, 1), plan)
    arrived = [swapped(block, plan, plan.plane, step + 1) for step, block in enumerate(others)]
    block = coded_sum(plane_kernel, [mine] + arrived, plan, "sum_plane")
    for bit in plan.rest:
        block = coded_sum(pair_kernel, [block, swapped(block, plan, [bit], 1)], plan, "sum_line")
    blocks = [block] + [swapped(block, plan, plan.plane, step) for step in range(1, 4)]
    blocks = blocks + [swapped(block, plan, plan.core, 1) for block in blocks]
    prediction, g_latent, g_pos, g_one, g_mid, g_two, g_out, g_bias, loss = unpack(
        place, blocks, plan, hidden, channels
    )
    return (
        prediction.transpose(1, 0, 2),
        g_latent,
        g_pos,
        g_one.reshape(hidden),
        g_mid,
        g_two.reshape(hidden),
        g_out,
        g_bias.reshape(5),
        loss.reshape(()),
    )


def solution(mesh):
    return jax.shard_map(
        body,
        mesh=mesh,
        in_specs=(
            P("replica", None, "tile", None, None),
            P(),
            P(),
            P("replica", "tile", None),
            P("replica", "tile"),
            P("replica", None, "tile"),
            P("replica", None, "tile"),
            P(),
            P(),
            P(),
            P(),
            P(),
            P(),
            P(),
        ),
        out_specs=(P("replica", None, "tile"), P(), P(), P(), P(), P(), P(), P(), P()),
        check_vma=False,
    )
```

```python
import functools

import jax
import jax.numpy as jnp
from jax import lax
from jax.experimental import pallas as pl
from jax.experimental.pallas import tpu as pltpu
from jax.sharding import PartitionSpec as P

DILATION_RATE = 2
VISCOSITY = 0.05
DIFFUSIVITY = 0.05
RESIDUAL_WEIGHT = 0.5

F32 = jnp.float32
BF16 = jnp.bfloat16
LANES = 128
BLOCK = 32
WORDS = 128
SUB = 32
NN = (((1,), (0,)), ((), ()))
NT = (((1,), (1,)), ((), ()))
TN = (((0,), (0,)), ((), ()))
VMEM = pl.BlockSpec(memory_space=pltpu.VMEM)
SMEM = pl.BlockSpec(memory_space=pltpu.SMEM)
HBM = pl.BlockSpec(memory_space=pltpu.HBM)


def mul(left, right, dims=NN):
    return lax.dot_general(left, right, dims, preferred_element_type=F32)


def halves(value):
    high = value.astype(BF16)
    return high, (value - high.astype(F32)).astype(BF16)


def thirds(value):
    high = value.astype(BF16)
    rest = value - high.astype(F32)
    middle = rest.astype(BF16)
    return high, middle, (rest - middle.astype(F32)).astype(BF16)


def mul3(left, right, dims=NN):
    return mul(left[0], right[0], dims) + mul(left[0], right[1], dims) + mul(left[1], right[0], dims)


def fetches(sources, targets, sems):
    copies = [
        pltpu.make_async_copy(source, target, sems.at[number])
        for number, (source, target) in enumerate(zip(sources, targets))
    ]
    for copy in copies:
        copy.start()
    return copies


def route_kernel(tiles, slots, *refs):
    out_ref, owner_ref, cell_ref, frac_ref, target_ref, words, sems = refs[4:]
    queries = owner_ref.shape[1]
    for copy in fetches(refs[:4], (owner_ref, cell_ref, frac_ref, target_ref), sems):
        copy.wait()
    owner = owner_ref[...]
    hits = (lax.broadcasted_iota(jnp.int32, (tiles, queries), 0) == owner).astype(F32)
    before = lax.broadcasted_iota(jnp.int32, (queries, queries), 0) < lax.broadcasted_iota(
        jnp.int32, (queries, queries), 1
    )
    earlier = mul(hits.astype(BF16), before.astype(F32).astype(BF16))
    slot = jnp.sum(hits * earlier, axis=0, keepdims=True)
    place = owner * slots + slot.astype(jnp.int32)
    chosen = (lax.broadcasted_iota(jnp.int32, (tiles * slots, queries), 0) == place).astype(F32).astype(BF16)
    words[...] = jnp.zeros_like(words)
    words[0:1, :] = cell_ref[...].astype(F32)
    for d in range(3):
        words[1 + d : 2 + d, :] = frac_ref[d]
    for f in range(5):
        words[4 + f : 5 + f, :] = target_ref[f]
    words[9:10, :] = jnp.ones((1, queries), F32)
    words[10:11, :] = lax.broadcasted_iota(jnp.int32, (1, queries), 1).astype(F32)
    high, middle, low = thirds(words[...])
    out_ref[...] = mul(chosen, high, NT) + mul(chosen, middle, NT) + mul(chosen, low, NT)


def route(owner, cell, frac, target, tiles, slots):
    queries = owner.shape[1]
    return pl.pallas_call(
        functools.partial(route_kernel, tiles, slots),
        out_shape=jax.ShapeDtypeStruct((tiles * slots, WORDS), F32),
        in_specs=[HBM] * 4,
        out_specs=VMEM,
        scratch_shapes=[
            pltpu.VMEM(owner.shape, owner.dtype),
            pltpu.VMEM(cell.shape, cell.dtype),
            pltpu.VMEM(frac.shape, F32),
            pltpu.VMEM(target.shape, F32),
            pltpu.VMEM((WORDS, queries), F32),
            pltpu.SemaphoreType.DMA((4,)),
        ],
        compiler_params=pltpu.CompilerParams(vmem_limit_bytes=4 << 20),
        name="route",
    )(owner, cell, frac, target)


def tap_sum(weight_ref, planes, pair):
    total = None
    for step_x, ref, index in planes:
        rows_y = ref.shape[1]
        blocks = [
            jnp.concatenate([ref[index, (2 * pair + half + step_y) % rows_y] for half in (0, 1)], axis=1)
            for step_y in (-1, 0, 1)
        ]
        term = mul(weight_ref[step_x], jnp.concatenate(blocks, axis=0))
        total = term if total is None else total + term
    channels = total.shape[0] // 3
    sides = []
    for half in (0, 1):
        part = total[:, half * LANES : (half + 1) * LANES]
        sides.append(
            part[channels : 2 * channels]
            + pltpu.roll(part[:channels], 1, 1)
            + pltpu.roll(part[2 * channels :], LANES - 1, 1)
        )
    return jnp.concatenate(sides, axis=1)


def local_kernel(here_ref, weight_ref, bias_ref, partial_ref):
    planes, rows_y = here_ref.shape[0], here_ref.shape[1]
    bias = bias_ref[...]
    for x in range(planes + 1):
        taps = [
            (step, here_ref, x + DILATION_RATE * (step - 1))
            for step in range(3)
            if 0 <= x + DILATION_RATE * (step - 1) < planes
        ]
        for pair in range(rows_y // 2):
            partial_ref[x * (rows_y // 2) + pair] = tap_sum(weight_ref, taps, pair) + bias


def local_part(here, taps, conv_bias):
    planes, rows_y, channels, rows_z = here.shape
    pairs = (planes + 1) * rows_y // 2
    return pl.pallas_call(
        local_kernel,
        out_shape=jax.ShapeDtypeStruct((pairs, channels, 2 * rows_z), F32),
        in_specs=[VMEM] * 3,
        out_specs=VMEM,
        compiler_params=pltpu.CompilerParams(vmem_limit_bytes=8 << 20),
        cost_estimate=pl.CostEstimate(flops=3 << 30, bytes_accessed=4 << 20, transcendentals=0),
        name="conv_local",
    )(here, taps, conv_bias)


def finish_latent(left_ref, right_ref, partial_ref, weight_ref, planes, lat):
    rows_y = left_ref.shape[1]
    for x in range(planes + 1):
        taps = []
        for step in range(3):
            plane = x + DILATION_RATE * (step - 1)
            if plane < 0:
                taps.append((step, left_ref, plane + left_ref.shape[0]))
            elif plane >= planes:
                taps.append((step, right_ref, plane - planes))
        for pair in range(rows_y // 2):
            number = x * (rows_y // 2) + pair
            summed = partial_ref[number] + tap_sum(weight_ref, taps, pair)
            lat[number] = jax.nn.gelu(summed).astype(BF16)


def interpolate(words, lat, planes, rows_y, rows_z):
    rows = words.shape[0]
    cell = jnp.broadcast_to(words[:, 0:1], (rows, LANES)).astype(jnp.int32)
    frac = [jnp.broadcast_to(words[:, 1 + d : 2 + d], (rows, LANES)) for d in range(3)]
    shift_z = rows_z.bit_length() - 1
    shift_y = rows_y.bit_length() - 1
    base_x = cell >> (shift_z + shift_y)
    base_y = (cell >> shift_z) & (rows_y - 1)
    base_z = cell & (rows_z - 1)
    spot = lax.broadcasted_iota(jnp.int32, (rows, rows_z), 1)
    part_z = jnp.where(spot == base_z, 1.0 - frac[2], 0.0) + jnp.where(
        spot == ((base_z + 1) & (rows_z - 1)), frac[2], 0.0
    )
    total = None
    for x in range(planes + 1):
        part_x = jnp.where(base_x == x, 1.0 - frac[0], jnp.where(base_x == x - 1, frac[0], 0.0))
        for pair in range(rows_y // 2):
            sides = []
            for y in (2 * pair, 2 * pair + 1):
                part_y = jnp.where(
                    base_y == y, 1.0 - frac[1], jnp.where(base_y == (y - 1) % rows_y, frac[1], 0.0)
                )
                sides.append((part_x * part_y * part_z).astype(BF16))
            term = mul(jnp.concatenate(sides, axis=1), lat[x * (rows_y // 2) + pair], NT)
            total = term if total is None else total + term
    return total.astype(BF16), base_x, base_y, base_z, frac


def folded(value):
    return jnp.sum(value.reshape(value.shape[0] // 8, 8, value.shape[1]), axis=0)


def main_kernel(
    plan,
    place_ref,
    left_ref,
    right_ref,
    partial_ref,
    conv_weight_ref,
    words_ref,
    w_latent_hbm,
    w_pos_hbm,
    bias_one_hbm,
    w_mid_hbm,
    bias_two_hbm,
    w_out_hbm,
    bias_out_hbm,
    send_ref,
    keep_ref,
    lat,
    code,
    pos,
    z_one,
    one_high,
    one_low,
    mixed,
    two_high,
    two_low,
    back,
    d_high,
    d_low,
    out_t,
    d_out_t,
    packed,
    mid_high,
    mid_low,
    w_latent_ref,
    w_pos_ref,
    bias_one_ref,
    w_mid_ref,
    bias_two_ref,
    w_out_ref,
    bias_out_ref,
    sems,
):
    rows = plan.tiles * plan.slots
    hidden = w_mid_ref.shape[0]
    latents = w_latent_ref.shape[0]
    weights = fetches(
        (w_latent_hbm, w_pos_hbm, bias_one_hbm, w_mid_hbm, bias_two_hbm, w_out_hbm, bias_out_hbm),
        (w_latent_ref, w_pos_ref, bias_one_ref, w_mid_ref, bias_two_ref, w_out_ref, bias_out_ref),
        sems,
    )
    planes, rows_y, rows_z = plan.planes, left_ref.shape[1], left_ref.shape[3]
    slots = rows // plan.tiles
    my_block = place_ref[0]
    my_tile = place_ref[1]
    my_replica = place_ref[2]

    finish_latent(left_ref, right_ref, partial_ref, conv_weight_ref, planes, lat)
    words = words_ref[...]
    interp, base_x, base_y, base_z, frac = interpolate(words, lat, planes, rows_y, rows_z)
    code[...] = interp
    global_x = my_tile * planes + base_x
    lane = lax.broadcasted_iota(jnp.int32, (rows, LANES), 1)
    pos[...] = jnp.where(
        lane == 0,
        (global_x.astype(F32) + frac[0]) / (planes * plan.tiles),
        jnp.where(
            lane == 1,
            (base_y.astype(F32) + frac[1]) / rows_y,
            (base_z.astype(F32) + frac[2]) / rows_z,
        ),
    )

    for copy in weights:
        copy.wait()
    high, low = halves(w_latent_ref[...])
    z_one[...] = mul(interp, high) + mul(interp, low)
    high, low = halves(w_mid_ref[...])
    mid_high[...] = high
    mid_low[...] = low
    w_pos = [w_pos_ref[d : d + 1, :] for d in range(3)]
    square = w_pos[0] * w_pos[0] + w_pos[1] * w_pos[1] + w_pos[2] * w_pos[2]
    bias_one = bias_one_ref[...]
    bias_two = bias_two_ref[...]

    def store(index, block, refs, value):
        high, low = halves(value)
        refs[0][pl.ds(pl.multiple_of(index * rows + block * BLOCK, BLOCK), BLOCK), :] = high
        refs[1][pl.ds(pl.multiple_of(index * rows + block * BLOCK, BLOCK), BLOCK), :] = low

    def fetch(ref, index, block):
        return ref[pl.ds(pl.multiple_of(index * rows + block * BLOCK, BLOCK), BLOCK), :]

    def layer_one(block, carry):
        where = fetch(pos, 0, block)
        pre = (
            fetch(z_one, 0, block)
            + (where[:, 0:1] * w_pos[0] + where[:, 1:2] * w_pos[1] + where[:, 2:3] * w_pos[2])
            + bias_one
        )
        act = jnp.tanh(pre)
        slope = 1.0 - act * act
        curve = -2.0 * act * slope
        z_one[pl.ds(pl.multiple_of(block * BLOCK, BLOCK), BLOCK), :] = act
        refs = (one_high, one_low)
        store(0, block, refs, act)
        for d in range(3):
            store(1 + d, block, refs, slope * w_pos[d])
        store(4, block, refs, curve * square)
        return carry

    lax.fori_loop(0, rows // BLOCK, layer_one, 0)

    def times_mid(dims, source, result, index, carry):
        span = pl.ds(pl.multiple_of(index * rows, rows), rows)
        result[span, :] = mul3((source[0][span, :], source[1][span, :]), (mid_high[...], mid_low[...]), dims)
        return carry

    lax.fori_loop(0, 5, functools.partial(times_mid, NN, (one_high, one_low), mixed), 0)

    def layer_two(block, carry):
        act = jnp.tanh(fetch(mixed, 0, block) + bias_two)
        slope = 1.0 - act * act
        curve = -2.0 * act * slope
        refs = (two_high, two_low)
        store(0, block, refs, act)
        mixed[pl.ds(pl.multiple_of(block * BLOCK, BLOCK), BLOCK), :] = act
        norm = None
        for d in range(3):
            tangent = fetch(mixed, 1 + d, block)
            store(1 + d, block, refs, slope * tangent)
            norm = tangent * tangent if norm is None else norm + tangent * tangent
        store(4, block, refs, slope * fetch(mixed, 4, block) + curve * norm)
        return carry

    lax.fori_loop(0, rows // BLOCK, layer_two, 0)

    out_fields = jnp.concatenate([w_out_ref[...], jnp.zeros((3, hidden), F32)], axis=0)
    wo_high, wo_low = halves(out_fields)
    wo_both = jnp.concatenate([out_fields, wo_low.astype(F32)], axis=0).astype(BF16)
    for s in range(5):
        span = slice(s * rows, (s + 1) * rows)
        both = mul(wo_both, two_high[span, :], NT)
        out_t[8 * s : 8 * s + 8, :] = both[:8] + both[8:] + mul(wo_high, two_low[span, :], NT)

    words_t = words.T
    target = [words_t[4 + f : 5 + f, :] for f in range(5)]
    valid = words_t[9:10, :]
    value = [out_t[f : f + 1, :] + bias_out_ref[0:1, f : f + 1] for f in range(5)]
    grad = [[out_t[8 * (d + 1) + f : 8 * (d + 1) + f + 1, :] for f in range(5)] for d in range(3)]
    laplace = [out_t[32 + f : 33 + f, :] for f in range(5)]
    velocity = value[2:5]
    advection = [
        velocity[0] * grad[0][f] + velocity[1] * grad[1][f] + velocity[2] * grad[2][f] for f in range(5)
    ]
    continuity = grad[0][2] + grad[1][3] + grad[2][4]
    momentum = [advection[2 + j] + grad[j][1] - VISCOSITY * laplace[2 + j] for j in range(3)]
    momentum[2] = momentum[2] - value[0]
    energy = advection[0] - DIFFUSIVITY * laplace[0]
    misfit = [value[f] - target[f] for f in range(5)]
    physics = (
        continuity * continuity
        + (momentum[0] * momentum[0] + momentum[1] * momentum[1] + momentum[2] * momentum[2])
        + energy * energy
    )
    squares = (
        misfit[0] * misfit[0]
        + misfit[1] * misfit[1]
        + misfit[2] * misfit[2]
        + misfit[3] * misfit[3]
        + misfit[4] * misfit[4]
    )
    point_loss = valid * (squares + RESIDUAL_WEIGHT * physics) * (1.0 / plan.query_total)

    rate = valid * (1.0 / plan.query_total)
    twice = RESIDUAL_WEIGHT * 2.0
    d_cont = rate * twice * continuity
    d_mom = [rate * twice * m for m in momentum]
    d_energy = rate * twice * energy
    d_value = [2.0 * rate * m for m in misfit]
    for d in range(3):
        d_value[2 + d] = d_value[2 + d] + (
            d_mom[0] * grad[d][2] + d_mom[1] * grad[d][3] + d_mom[2] * grad[d][4] + d_energy * grad[d][0]
        )
    d_value[0] = d_value[0] - d_mom[2]
    d_out_t[...] = jnp.zeros_like(d_out_t)
    for f in range(5):
        d_out_t[f : f + 1, :] = d_value[f]
    for d in range(3):
        first = 8 * (d + 1)
        d_out_t[first : first + 1, :] = d_energy * velocity[d]
        d_out_t[first + 1 : first + 2, :] = d_mom[d]
        for j in range(3):
            term = d_mom[j] * velocity[d]
            if j == d:
                term = term + d_cont
            d_out_t[first + 2 + j : first + 3 + j, :] = term
    d_out_t[32:33, :] = -DIFFUSIVITY * d_energy
    for j in range(3):
        d_out_t[34 + j : 35 + j, :] = -VISCOSITY * d_mom[j]

    for s in range(5):
        span = slice(s * rows, (s + 1) * rows)
        wanted = d_out_t[8 * s : 8 * s + 8, :]
        do_high, do_low = halves(wanted)
        back[span, :] = mul3((do_high, do_low), (wo_high, wo_low), TN)

    def second_back(block, total):
        act = fetch(mixed, 0, block)
        slope = 1.0 - act * act
        curve = -2.0 * act * slope
        tangent = [fetch(mixed, 1 + d, block) for d in range(3)]
        cot_t = [fetch(back, 1 + d, block) for d in range(3)]
        cot_l = fetch(back, 4, block)
        refs = (d_high, d_low)
        d_slope = cot_l * fetch(mixed, 4, block)
        norm = None
        bent = 2.0 * curve * cot_l
        for d in range(3):
            store(1 + d, block, refs, slope * cot_t[d] + bent * tangent[d])
            d_slope = d_slope + cot_t[d] * tangent[d]
            norm = tangent[d] * tangent[d] if norm is None else norm + tangent[d] * tangent[d]
        store(4, block, refs, slope * cot_l)
        d_curve = cot_l * norm
        d_slope = d_slope - 2.0 * act * d_curve
        d_act = fetch(back, 0, block) - 2.0 * slope * d_curve - 2.0 * act * d_slope
        d_pre = slope * d_act
        store(0, block, refs, d_pre)
        return total + folded(d_pre)

    grad_two = lax.fori_loop(0, rows // BLOCK, second_back, jnp.zeros((8, hidden), F32))

    def put(part, first, value):
        while value.shape[0]:
            block, row = first // plan.main_rows, first % plan.main_rows
            count = min(value.shape[0], plan.main_rows - row)
            packed[2 * part + block, row : row + count, :] = value[:count]
            first, value = first + count, value[count:]

    wide = 2 * LANES
    for left in range(hidden // wide):
        for right in range(hidden // wide):
            lefts = slice(left * wide, (left + 1) * wide)
            rights = slice(right * wide, (right + 1) * wide)
            part = mul3(
                (one_high[:, lefts], one_low[:, lefts]), (d_high[:, rights], d_low[:, rights]), TN
            )
            for side in range(2):
                put(2 * right + side, left * wide, part[:, side * LANES : (side + 1) * LANES])

    lax.fori_loop(0, 5, functools.partial(times_mid, NT, (d_high, d_low), back), 0)

    def first_back(block, totals):
        act = fetch(z_one, 0, block)
        slope = 1.0 - act * act
        curve = -2.0 * act * slope
        where = fetch(pos, 0, block)
        cot_t = [fetch(back, 1 + d, block) for d in range(3)]
        cot_l = fetch(back, 4, block)
        d_curve = cot_l * square
        d_slope = cot_t[0] * w_pos[0] + cot_t[1] * w_pos[1] + cot_t[2] * w_pos[2] - 2.0 * act * d_curve
        d_act = fetch(back, 0, block) - 2.0 * slope * d_curve - 2.0 * act * d_slope
        d_pre = slope * d_act
        store(0, block, (d_high, d_low), d_pre)
        sums = [totals[0] + folded(d_pre)]
        for d in range(3):
            sums.append(totals[1 + d] + folded(where[:, d : d + 1] * d_pre + slope * cot_t[d]))
        sums.append(totals[4] + folded(curve * cot_l))
        return tuple(sums)

    sums = lax.fori_loop(
        0, rows // BLOCK, first_back, tuple(jnp.zeros((8, hidden), F32) for _ in range(5))
    )
    d_square = jnp.sum(sums[4], axis=0, keepdims=True)
    grad_latent = mul(code[...], d_high[0:rows, :], TN) + mul(code[...], d_low[0:rows, :], TN)

    grad_out = None
    for s in range(5):
        span = slice(s * rows, (s + 1) * rows)
        wanted = d_out_t[8 * s : 8 * s + 8, :]
        do_high, do_low = halves(wanted)
        do_both = jnp.concatenate([wanted, do_low.astype(F32)], axis=0).astype(BF16)
        both = mul(do_both, two_high[span, :])
        term = both[:8] + both[8:] + mul(do_high, two_low[span, :])
        grad_out = term if grad_out is None else grad_out + term

    lane_row = lax.broadcasted_iota(jnp.int32, (1, hidden), 1)
    last = jnp.where(lane_row == 5, jnp.sum(point_loss), 0.0)
    for f in range(5):
        last = last + jnp.where(lane_row == f, jnp.sum(d_value[f]), 0.0)
    grad_pos = [jnp.sum(sums[1 + d], axis=0, keepdims=True) + 2.0 * w_pos[d] * d_square for d in range(3)]
    misc = grad_pos + [
        jnp.sum(sums[0], axis=0, keepdims=True),
        jnp.sum(grad_two, axis=0, keepdims=True),
        last,
    ]
    misc = jnp.concatenate(misc + [jnp.zeros((2, hidden), F32)], axis=0)
    for part in range(hidden // LANES):
        lanes = slice(part * LANES, (part + 1) * LANES)
        put(part, hidden, grad_latent[:, lanes])
        packed[2 * part, plan.coded_rows :, :] = misc[:, lanes]
        packed[2 * part + 1, plan.coded_rows :, :] = grad_out[:, lanes]

    chosen = jnp.where(
        lane == jnp.broadcast_to(words[:, 10:11], (rows, LANES)).astype(jnp.int32), words[:, 9:10], 0.0
    ).astype(BF16)
    fields = jnp.concatenate(value + [jnp.zeros((3, rows), F32)], axis=0)
    source = lax.broadcasted_iota(jnp.int32, (8, rows), 1) >> (slots.bit_length() - 1)
    spread = jnp.concatenate([jnp.where(source == t, fields, 0.0) for t in range(plan.tiles)], axis=0)
    high, middle, low = thirds(spread)
    spread = mul(high, chosen) + mul(middle, chosen) + mul(low, chosen)
    packed[:, plan.main_rows : plan.coded_rows, :] = jnp.zeros((8, plan.devices, LANES), F32)
    for t in range(plan.tiles):
        row = plan.main_rows + (my_replica * (plan.tiles // 8) + t // 8) * 8
        packed[t % 8, pl.ds(pl.multiple_of(row, 8), 8), :] = spread[8 * t : 8 * t + 8]

    for block in range(8):
        spot = jnp.bitwise_xor(block, my_block) & 3

        @pl.when((my_block >> 2) == block // 4)
        def _():
            keep_ref[spot] = packed[block]

        @pl.when((my_block >> 2) != block // 4)
        def _():
            send_ref[spot] = packed[block]


class Plan:
    def __init__(self, tiles, replicas, queries, planes, hidden, latents):
        self.tiles, self.replicas, self.planes = tiles, replicas, planes
        self.slots = 2 * queries // tiles
        self.devices = tiles * replicas
        self.query_total = float(queries * self.devices)
        self.main_rows = (hidden + latents) // 2
        self.coded_rows = self.main_rows + self.devices
        self.rows = self.coded_rows + 8
        self.scales = -(-(self.coded_rows // SUB + 1) // 16) * 16
        self.sent_rows = self.coded_rows + 16 + self.scales
        top = self.devices.bit_length() - 1
        self.core, self.plane, self.rest = [0], [1, top - 1], list(range(2, top - 1))

    def mask(self, bits, steps):
        return sum(1 << bit for number, bit in enumerate(bits) if steps >> number & 1)

    def my_block(self, device):
        return (device & 1) * 4 + (device >> 1 & 1) + 2 * (device >> self.plane[1] & 1)


def swapped(value, plan, bits, steps):
    mask = plan.mask(bits, steps)
    return lax.ppermute(value, ("replica", "tile"), [(i, i ^ mask) for i in range(plan.devices)])


def encode(plan, read, out_ref):
    starts = list(range(0, plan.coded_rows, SUB))
    parts = [read(start, SUB) for start in starts] + [read(plan.coded_rows, 8)]
    tops = [jnp.max(jnp.abs(part), axis=0, keepdims=True) for part in parts]
    tops = tops + [jnp.zeros_like(tops[0])] * (plan.scales - len(tops))
    power = jnp.floor(jnp.log2(jnp.maximum(jnp.concatenate(tops, axis=0), 1e-30)))
    scale = jnp.exp2(14.0 - power)

    def whole(value):
        return jnp.clip(jnp.round(value), -32767.0, 32767.0)

    def narrow(value):
        return value.astype(jnp.int32).astype(jnp.int16)

    for number, start in enumerate(starts):
        out_ref[start : start + SUB, :] = narrow(whole(parts[number] * scale[number : number + 1]))
    last = len(starts)
    exact = parts[last] * scale[last : last + 1]
    high = whole(exact)
    low = whole((exact - high) * 32768.0)
    out_ref[plan.coded_rows : plan.coded_rows + 16, :] = narrow(jnp.concatenate([high, low], axis=0))
    out_ref[plan.coded_rows + 16 :, :] = narrow(power)


def decoder(plan, ref):
    def widen(value):
        return value.astype(jnp.int32).astype(F32)

    scale = jnp.exp2(widen(ref[plan.coded_rows + 16 :, :]) - 14.0)

    def read(start, count):
        if start < plan.coded_rows:
            number = start // SUB
            return widen(ref[start : start + count, :]) * scale[number : number + 1]
        both = widen(ref[plan.coded_rows : plan.coded_rows + 16, :])
        number = plan.coded_rows // SUB
        return (both[:8] + both[8:] * (1.0 / 32768.0)) * scale[number : number + 1]

    return read


def added(readers):
    def read(start, count):
        total = readers[0](start, count)
        for reader in readers[1:]:
            total = total + reader(start, count)
        return total

    return read


def first_kernel(plan, keep_ref, got_ref, mine_ref, *out_refs):
    def reader(block):
        return lambda start, count: (
            keep_ref[block, start : start + count, :] + got_ref[block, start : start + count, :]
        )

    for number, out_ref in enumerate(out_refs):
        encode(plan, reader(number + 1), out_ref)
    mine_ref[...] = keep_ref[0] + got_ref[0]


def first_sum(keep, got, plan):
    sent = jax.ShapeDtypeStruct((plan.sent_rows, LANES), jnp.int16)
    return pl.pallas_call(
        functools.partial(first_kernel, plan),
        out_shape=(jax.ShapeDtypeStruct(keep.shape[1:], F32), sent, sent, sent),
        in_specs=[VMEM] * 2,
        out_specs=tuple([VMEM] * 4),
        compiler_params=pltpu.CompilerParams(vmem_limit_bytes=6 << 20),
        name="sum_core",
    )(keep, got)


def plane_kernel(plan, mine_ref, *refs):
    readers = [lambda start, count: mine_ref[start : start + count, :]]
    encode(plan, added(readers + [decoder(plan, ref) for ref in refs[:-1]]), refs[-1])


def pair_kernel(plan, mine_ref, other_ref, out_ref):
    encode(plan, added([decoder(plan, mine_ref), decoder(plan, other_ref)]), out_ref)


def coded_sum(kernel, blocks, plan, name):
    return pl.pallas_call(
        functools.partial(kernel, plan),
        out_shape=jax.ShapeDtypeStruct((plan.sent_rows, LANES), jnp.int16),
        in_specs=[VMEM] * len(blocks),
        out_specs=VMEM,
        compiler_params=pltpu.CompilerParams(vmem_limit_bytes=4 << 20),
        name=name,
    )(*blocks)


def main(place, left, right, partial, taps, words, weights, plan):
    rows = plan.tiles * plan.slots
    hidden = weights[3].shape[0]
    channels = left.shape[2]
    outs = jax.ShapeDtypeStruct((4, plan.rows, LANES), F32)
    wide = lambda kind: pltpu.VMEM((5 * rows, hidden), kind)
    return pl.pallas_call(
        functools.partial(main_kernel, plan),
        out_shape=(outs, outs),
        in_specs=[SMEM] + [VMEM] * 5 + [HBM] * 7,
        out_specs=(VMEM, VMEM),
        scratch_shapes=[
            pltpu.VMEM((partial.shape[0], channels, 2 * LANES), BF16),
            pltpu.VMEM((rows, channels), BF16),
            pltpu.VMEM((rows, LANES), F32),
            pltpu.VMEM((rows, hidden), F32),
            wide(BF16),
            wide(BF16),
            wide(F32),
            wide(BF16),
            wide(BF16),
            wide(F32),
            wide(BF16),
            wide(BF16),
            pltpu.VMEM((40, rows), F32),
            pltpu.VMEM((40, rows), F32),
            pltpu.VMEM((8, plan.rows, LANES), F32),
            pltpu.VMEM((hidden, hidden), BF16),
            pltpu.VMEM((hidden, hidden), BF16),
        ]
        + [pltpu.VMEM(weight.shape, F32) for weight in weights]
        + [pltpu.SemaphoreType.DMA((7,))],
        compiler_params=pltpu.CompilerParams(vmem_limit_bytes=32 << 20),
        name="encode_decode",
    )(place, left, right, partial, taps, words, *weights)


def unpack_kernel(plan, place_ref, *refs):
    sources, outs, packed = refs[:8], refs[8:-1], refs[-1]
    prediction_ref, latent_ref, pos_ref, one_ref, mid_ref, two_ref, out_ref, bias_out_ref, loss_ref = outs
    my_block = place_ref[0]
    device = place_ref[2] * plan.tiles + place_ref[1]
    starts = list(range(0, plan.coded_rows, SUB))
    for number, ref in enumerate(sources):
        read = decoder(plan, ref)
        block = jnp.bitwise_xor(number, my_block)
        for start in starts:
            packed[block, start : start + SUB, :] = read(start, SUB)
        packed[block, plan.coded_rows :, :] = read(plan.coded_rows, 8)

    hidden = mid_ref.shape[0]
    latents = latent_ref.shape[0]
    split = plan.main_rows
    for part in range(hidden // LANES):
        lanes = slice(part * LANES, (part + 1) * LANES)
        mid_ref[0:split, lanes] = packed[2 * part, 0:split, :]
        mid_ref[split:, lanes] = packed[2 * part + 1, 0 : hidden - split, :]
        latent_ref[:, lanes] = packed[2 * part + 1, hidden - split : split, :]
        misc = packed[2 * part, plan.coded_rows :, :]
        pos_ref[:, lanes] = misc[0:3]
        one_ref[:, lanes] = misc[3:4]
        two_ref[:, lanes] = misc[4:5]
        out_ref[:, lanes] = packed[2 * part + 1, plan.coded_rows : plan.coded_rows + 5, :]
        if part == 0:
            bias_out_ref[...] = misc[5:6, 0:5]
            loss_ref[...] = misc[5:6, 5:6]
    row = pl.multiple_of(plan.main_rows + (device >> 3) * 8, 8)
    fields = packed[device & 7, pl.ds(row, 8), :]
    for f in range(5):
        prediction_ref[f] = fields[f : f + 1]


def unpack(place, blocks, plan, hidden, latents):
    shapes = [
        (5, 1, LANES),
        (latents, hidden),
        (3, hidden),
        (1, hidden),
        (hidden, hidden),
        (1, hidden),
        (5, hidden),
        (1, 5),
        (1, 1),
    ]
    return pl.pallas_call(
        functools.partial(unpack_kernel, plan),
        out_shape=tuple(jax.ShapeDtypeStruct(shape, F32) for shape in shapes),
        in_specs=[SMEM] + [VMEM] * 8,
        out_specs=tuple([VMEM] * len(shapes)),
        scratch_shapes=[pltpu.VMEM((8, plan.rows, LANES), F32)],
        compiler_params=pltpu.CompilerParams(vmem_limit_bytes=16 << 20),
        name="unpack",
    )(place, *blocks)


def body(
    fields,
    convolution_weight,
    convolution_bias,
    query_owner,
    query_cell,
    query_frac,
    target,
    w_latent,
    w_pos,
    bias_one,
    w_mid,
    bias_two,
    w_out,
    bias_out,
):
    tiles = lax.axis_size("tile")
    replicas = lax.axis_size("replica")
    my_tile = lax.axis_index("tile")
    my_replica = lax.axis_index("replica")
    channels = fields.shape[1]
    queries = query_cell.shape[1]
    hidden = w_mid.shape[0]
    plan = Plan(tiles, replicas, queries, fields.shape[2], hidden, channels)
    device = my_replica * tiles + my_tile
    place = jnp.stack([plan.my_block(device), my_tile, my_replica]).astype(jnp.int32)

    here = fields[0].transpose(1, 2, 0, 3)
    up = [(i, (i + 1) % tiles) for i in range(tiles)]
    down = [((i + 1) % tiles, i) for i in range(tiles)]
    to_left, to_right, convolution_weight = lax.optimization_barrier(
        (here[: DILATION_RATE + 1], here[-DILATION_RATE:], convolution_weight)
    )
    taps = convolution_weight.reshape(channels, 3, 3, 3, channels)
    taps = taps.transpose(1, 3, 0, 2, 4).reshape(3, 3 * channels, 3 * channels)
    taps, query_owner = lax.optimization_barrier((taps, query_owner))
    right = lax.ppermute(to_left, "tile", down)
    left = lax.ppermute(to_right, "tile", up)
    words = route(
        query_owner[:, :, 0],
        query_cell,
        query_frac.transpose(1, 0, 2),
        target.transpose(1, 0, 2),
        tiles,
        plan.slots,
    )
    words = lax.all_to_all(
        words.reshape(tiles, plan.slots, WORDS), "tile", split_axis=0, concat_axis=0, tiled=True
    ).reshape(tiles * plan.slots, WORDS)

    partial = local_part(here, taps, convolution_bias[:, None])
    weights = (w_latent, w_pos, bias_one[None], w_mid, bias_two[None], w_out, bias_out[None])
    send, keep = main(place, left, right, partial, taps, words, weights, plan)

    mine, *others = first_sum(keep, swapped(send, plan, plan.core, 1), plan)
    arrived = [swapped(block, plan, plan.plane, step + 1) for step, block in enumerate(others)]
    block = coded_sum(plane_kernel, [mine] + arrived, plan, "sum_plane")
    for bit in plan.rest:
        block = coded_sum(pair_kernel, [block, swapped(block, plan, [bit], 1)], plan, "sum_line")
    blocks = [block] + [swapped(block, plan, plan.plane, step) for step in range(1, 4)]
    blocks = blocks + [swapped(block, plan, plan.core, 1) for block in blocks]
    prediction, g_latent, g_pos, g_one, g_mid, g_two, g_out, g_bias, loss = unpack(
        place, blocks, plan, hidden, channels
    )
    return (
        prediction.transpose(1, 0, 2),
        g_latent,
        g_pos,
        g_one.reshape(hidden),
        g_mid,
        g_two.reshape(hidden),
        g_out,
        g_bias.reshape(5),
        loss.reshape(()),
    )


def solution(mesh):
    return jax.shard_map(
        body,
        mesh=mesh,
        in_specs=(
            P("replica", None, "tile", None, None),
            P(),
            P(),
            P("replica", "tile", None),
            P("replica", "tile"),
            P("replica", None, "tile"),
            P("replica", None, "tile"),
            P(),
            P(),
            P(),
            P(),
            P(),
            P(),
            P(),
        ),
        out_specs=(P("replica", None, "tile"), P(), P(), P(), P(), P(), P(), P(), P()),
        check_vma=False,
    )
```

```python
import functools

import jax
import jax.numpy as jnp
from jax import lax
from jax.experimental import pallas as pl
from jax.experimental.pallas import tpu as pltpu
from jax.sharding import PartitionSpec as P

DILATION_RATE = 2
VISCOSITY = 0.05
DIFFUSIVITY = 0.05
RESIDUAL_WEIGHT = 0.5

F32 = jnp.float32
BF16 = jnp.bfloat16
LANES = 128
BLOCK = 32
WORDS = 128
SUB = 32
NN = (((1,), (0,)), ((), ()))
NT = (((1,), (1,)), ((), ()))
TN = (((0,), (0,)), ((), ()))
VMEM = pl.BlockSpec(memory_space=pltpu.VMEM)
SMEM = pl.BlockSpec(memory_space=pltpu.SMEM)
HBM = pl.BlockSpec(memory_space=pltpu.HBM)


def mul(left, right, dims=NN):
    return lax.dot_general(left, right, dims, preferred_element_type=F32)


def halves(value):
    high = value.astype(BF16)
    return high, (value - high.astype(F32)).astype(BF16)


def thirds(value):
    high = value.astype(BF16)
    rest = value - high.astype(F32)
    middle = rest.astype(BF16)
    return high, middle, (rest - middle.astype(F32)).astype(BF16)


def mul3(left, right, dims=NN):
    return mul(left[0], right[0], dims) + mul(left[0], right[1], dims) + mul(left[1], right[0], dims)


def fetches(sources, targets, sems):
    copies = [
        pltpu.make_async_copy(source, target, sems.at[number])
        for number, (source, target) in enumerate(zip(sources, targets))
    ]
    for copy in copies:
        copy.start()
    return copies


def route_kernel(tiles, slots, *refs):
    out_ref, owner_ref, cell_ref, frac_ref, target_ref, words, sems = refs[4:]
    queries = owner_ref.shape[1]
    for copy in fetches(refs[:4], (owner_ref, cell_ref, frac_ref, target_ref), sems):
        copy.wait()
    owner = owner_ref[...]
    hits = (lax.broadcasted_iota(jnp.int32, (tiles, queries), 0) == owner).astype(F32)
    before = lax.broadcasted_iota(jnp.int32, (queries, queries), 0) < lax.broadcasted_iota(
        jnp.int32, (queries, queries), 1
    )
    earlier = mul(hits.astype(BF16), before.astype(F32).astype(BF16))
    slot = jnp.sum(hits * earlier, axis=0, keepdims=True)
    place = owner * slots + slot.astype(jnp.int32)
    spot = lax.broadcasted_iota(jnp.int32, (tiles * 8, queries), 0)
    spot = (spot >> 3) * slots + (spot & 7)
    groups = slots // 8
    chosen = [jnp.where(spot + 8 * group == place, 1.0, 0.0) for group in range(groups)]
    chosen = jnp.concatenate(chosen, axis=1).astype(BF16)
    words[...] = jnp.zeros_like(words)
    for group in range(groups):
        row, lanes = 16 * group, slice(group * queries, (group + 1) * queries)
        words[row : row + 1, lanes] = cell_ref[...].astype(F32)
        for d in range(3):
            words[row + 1 + d : row + 2 + d, lanes] = frac_ref[d]
        for f in range(5):
            words[row + 4 + f : row + 5 + f, lanes] = target_ref[f]
        words[row + 9 : row + 10, lanes] = jnp.ones((1, queries), F32)
        words[row + 10 : row + 11, lanes] = lax.broadcasted_iota(jnp.int32, (1, queries), 1).astype(F32)
    high, middle, low = thirds(words[...])
    out_ref[...] = mul(chosen, high, NT) + mul(chosen, middle, NT) + mul(chosen, low, NT)


def route(owner, cell, frac, target, tiles, slots):
    queries = owner.shape[1]
    return pl.pallas_call(
        functools.partial(route_kernel, tiles, slots),
        out_shape=jax.ShapeDtypeStruct((tiles * 8, WORDS), F32),
        in_specs=[HBM] * 4,
        out_specs=VMEM,
        scratch_shapes=[
            pltpu.VMEM(owner.shape, owner.dtype),
            pltpu.VMEM(cell.shape, cell.dtype),
            pltpu.VMEM(frac.shape, F32),
            pltpu.VMEM(target.shape, F32),
            pltpu.VMEM((WORDS, queries * (slots // 8)), F32),
            pltpu.SemaphoreType.DMA((4,)),
        ],
        compiler_params=pltpu.CompilerParams(vmem_limit_bytes=4 << 20),
        name="route",
    )(owner, cell, frac, target)


def tap_sum(weight_ref, planes, pair):
    total = None
    for step_x, ref, index in planes:
        rows_y = ref.shape[1]
        blocks = [
            jnp.concatenate([ref[index, (2 * pair + half + step_y) % rows_y] for half in (0, 1)], axis=1)
            for step_y in (-1, 0, 1)
        ]
        term = mul(weight_ref[step_x], jnp.concatenate(blocks, axis=0))
        total = term if total is None else total + term
    channels = total.shape[0] // 3
    sides = []
    for half in (0, 1):
        part = total[:, half * LANES : (half + 1) * LANES]
        sides.append(
            part[channels : 2 * channels]
            + pltpu.roll(part[:channels], 1, 1)
            + pltpu.roll(part[2 * channels :], LANES - 1, 1)
        )
    return jnp.concatenate(sides, axis=1)


def conv_kernel(left_ref, here_ref, right_ref, weight_ref, bias_ref, lat_ref):
    planes, rows_y = here_ref.shape[0], here_ref.shape[1]
    bias = bias_ref[...]
    for x in range(planes + 1):
        taps = []
        for step in range(3):
            plane = x + DILATION_RATE * (step - 1)
            if plane < 0:
                taps.append((step, left_ref, plane + left_ref.shape[0]))
            elif plane >= planes:
                taps.append((step, right_ref, plane - planes))
            else:
                taps.append((step, here_ref, plane))
        for pair in range(rows_y // 2):
            summed = tap_sum(weight_ref, taps, pair) + bias
            lat_ref[x * (rows_y // 2) + pair] = jax.nn.gelu(summed).astype(BF16)


def convolve(left, here, right, taps, conv_bias):
    planes, rows_y, channels, rows_z = here.shape
    pairs = (planes + 1) * rows_y // 2
    return pl.pallas_call(
        conv_kernel,
        out_shape=jax.ShapeDtypeStruct((pairs, channels, 2 * rows_z), BF16),
        in_specs=[VMEM] * 5,
        out_specs=VMEM,
        compiler_params=pltpu.CompilerParams(vmem_limit_bytes=8 << 20),
        cost_estimate=pl.CostEstimate(flops=3 << 30, bytes_accessed=4 << 20, transcendentals=0),
        name="convolve",
    )(left, here, right, taps, conv_bias)


def interpolate(words, lat, planes, rows_y, rows_z):
    rows = words.shape[0]
    cell = jnp.broadcast_to(words[:, 0:1], (rows, LANES)).astype(jnp.int32)
    frac = [jnp.broadcast_to(words[:, 1 + d : 2 + d], (rows, LANES)) for d in range(3)]
    shift_z = rows_z.bit_length() - 1
    shift_y = rows_y.bit_length() - 1
    base_x = cell >> (shift_z + shift_y)
    base_y = (cell >> shift_z) & (rows_y - 1)
    base_z = cell & (rows_z - 1)
    spot = lax.broadcasted_iota(jnp.int32, (rows, rows_z), 1)
    part_z = jnp.where(spot == base_z, 1.0 - frac[2], 0.0) + jnp.where(
        spot == ((base_z + 1) & (rows_z - 1)), frac[2], 0.0
    )
    part_yz = []
    for y in range(rows_y):
        part_y = jnp.where(
            base_y == y, 1.0 - frac[1], jnp.where(base_y == (y - 1) % rows_y, frac[1], 0.0)
        )
        part_yz.append(part_y * part_z)
    total = None
    for x in range(planes + 1):
        part_x = jnp.where(base_x == x, 1.0 - frac[0], jnp.where(base_x == x - 1, frac[0], 0.0))
        for pair in range(rows_y // 2):
            sides = [(part_x * part_yz[2 * pair + half]).astype(BF16) for half in (0, 1)]
            term = mul(jnp.concatenate(sides, axis=1), lat[x * (rows_y // 2) + pair], NT)
            total = term if total is None else total + term
    return total.astype(BF16), base_x, base_y, base_z, frac


def folded(value):
    return jnp.sum(value.reshape(value.shape[0] // 8, 8, value.shape[1]), axis=0)


def main_kernel(
    plan,
    place_ref,
    lat,
    words_ref,
    w_latent_hbm,
    w_pos_hbm,
    bias_one_hbm,
    w_mid_hbm,
    bias_two_hbm,
    w_out_hbm,
    bias_out_hbm,
    send_ref,
    keep_ref,
    code,
    pos,
    z_one,
    one_high,
    one_low,
    mixed,
    two_high,
    two_low,
    back,
    d_high,
    d_low,
    out_t,
    d_out_t,
    packed,
    mid_high,
    mid_low,
    w_latent_ref,
    w_pos_ref,
    bias_one_ref,
    w_mid_ref,
    bias_two_ref,
    w_out_ref,
    bias_out_ref,
    sems,
):
    rows = plan.tiles * plan.slots
    hidden = w_mid_ref.shape[0]
    latents = w_latent_ref.shape[0]
    weights = fetches(
        (w_latent_hbm, w_pos_hbm, bias_one_hbm, w_mid_hbm, bias_two_hbm, w_out_hbm, bias_out_hbm),
        (w_latent_ref, w_pos_ref, bias_one_ref, w_mid_ref, bias_two_ref, w_out_ref, bias_out_ref),
        sems,
    )
    planes, rows_z = plan.planes, lat.shape[2] // 2
    rows_y = lat.shape[0] // (planes + 1) * 2
    slots = rows // plan.tiles
    my_block = place_ref[0]
    my_tile = place_ref[1]
    my_replica = place_ref[2]

    words = words_ref[...]
    words = jnp.concatenate(
        [words] + [pltpu.roll(words, LANES - 16 * group, 1) for group in range(1, slots // 8)], axis=0
    )
    interp, base_x, base_y, base_z, frac = interpolate(words, lat, planes, rows_y, rows_z)
    code[...] = interp
    global_x = my_tile * planes + base_x
    lane = lax.broadcasted_iota(jnp.int32, (rows, LANES), 1)
    pos[...] = jnp.where(
        lane == 0,
        (global_x.astype(F32) + frac[0]) / (planes * plan.tiles),
        jnp.where(
            lane == 1,
            (base_y.astype(F32) + frac[1]) / rows_y,
            (base_z.astype(F32) + frac[2]) / rows_z,
        ),
    )

    for copy in weights:
        copy.wait()
    high, low = halves(w_latent_ref[...])
    z_one[...] = mul(interp, high) + mul(interp, low)
    high, low = halves(w_mid_ref[...])
    mid_high[...] = high
    mid_low[...] = low
    w_pos = [w_pos_ref[d : d + 1, :] for d in range(3)]
    square = w_pos[0] * w_pos[0] + w_pos[1] * w_pos[1] + w_pos[2] * w_pos[2]
    bias_one = bias_one_ref[...]
    bias_two = bias_two_ref[...]

    def store(index, block, refs, value):
        high, low = halves(value)
        refs[0][pl.ds(pl.multiple_of(index * rows + block * BLOCK, BLOCK), BLOCK), :] = high
        refs[1][pl.ds(pl.multiple_of(index * rows + block * BLOCK, BLOCK), BLOCK), :] = low

    def fetch(ref, index, block):
        return ref[pl.ds(pl.multiple_of(index * rows + block * BLOCK, BLOCK), BLOCK), :]

    def layer_one(block, carry):
        where = fetch(pos, 0, block)
        pre = (
            fetch(z_one, 0, block)
            + (where[:, 0:1] * w_pos[0] + where[:, 1:2] * w_pos[1] + where[:, 2:3] * w_pos[2])
            + bias_one
        )
        act = jnp.tanh(pre)
        slope = 1.0 - act * act
        curve = -2.0 * act * slope
        z_one[pl.ds(pl.multiple_of(block * BLOCK, BLOCK), BLOCK), :] = act
        refs = (one_high, one_low)
        store(0, block, refs, act)
        for d in range(3):
            store(1 + d, block, refs, slope * w_pos[d])
        store(4, block, refs, curve * square)
        return carry

    lax.fori_loop(0, rows // BLOCK, layer_one, 0)

    def times_mid(dims, source, result, index, carry):
        span = pl.ds(pl.multiple_of(index * rows, rows), rows)
        result[span, :] = mul3((source[0][span, :], source[1][span, :]), (mid_high[...], mid_low[...]), dims)
        return carry

    lax.fori_loop(0, 5, functools.partial(times_mid, NN, (one_high, one_low), mixed), 0)

    def layer_two(block, carry):
        act = jnp.tanh(fetch(mixed, 0, block) + bias_two)
        slope = 1.0 - act * act
        curve = -2.0 * act * slope
        refs = (two_high, two_low)
        store(0, block, refs, act)
        mixed[pl.ds(pl.multiple_of(block * BLOCK, BLOCK), BLOCK), :] = act
        norm = None
        for d in range(3):
            tangent = fetch(mixed, 1 + d, block)
            store(1 + d, block, refs, slope * tangent)
            norm = tangent * tangent if norm is None else norm + tangent * tangent
        store(4, block, refs, slope * fetch(mixed, 4, block) + curve * norm)
        return carry

    lax.fori_loop(0, rows // BLOCK, layer_two, 0)

    out_fields = jnp.concatenate([w_out_ref[...], jnp.zeros((3, hidden), F32)], axis=0)
    wo_high, wo_low = halves(out_fields)
    wo_three = jnp.concatenate([out_fields, wo_low.astype(F32), out_fields], axis=0).astype(BF16)
    wo_both = jnp.concatenate([out_fields, wo_low.astype(F32)], axis=0).astype(BF16)
    for s in range(5):
        span = slice(s * rows, (s + 1) * rows)
        both = mul(wo_both, two_high[span, :], NT)
        out_t[8 * s : 8 * s + 8, :] = both[:8] + both[8:] + mul(wo_high, two_low[span, :], NT)

    words_t = words.T
    target = [words_t[4 + f : 5 + f, :] for f in range(5)]
    valid = words_t[9:10, :]
    value = [out_t[f : f + 1, :] + bias_out_ref[0:1, f : f + 1] for f in range(5)]
    grad = [[out_t[8 * (d + 1) + f : 8 * (d + 1) + f + 1, :] for f in range(5)] for d in range(3)]
    laplace = [out_t[32 + f : 33 + f, :] for f in range(5)]
    velocity = value[2:5]
    advection = [
        velocity[0] * grad[0][f] + velocity[1] * grad[1][f] + velocity[2] * grad[2][f] for f in range(5)
    ]
    continuity = grad[0][2] + grad[1][3] + grad[2][4]
    momentum = [advection[2 + j] + grad[j][1] - VISCOSITY * laplace[2 + j] for j in range(3)]
    momentum[2] = momentum[2] - value[0]
    energy = advection[0] - DIFFUSIVITY * laplace[0]
    misfit = [value[f] - target[f] for f in range(5)]
    physics = (
        continuity * continuity
        + (momentum[0] * momentum[0] + momentum[1] * momentum[1] + momentum[2] * momentum[2])
        + energy * energy
    )
    squares = (
        misfit[0] * misfit[0]
        + misfit[1] * misfit[1]
        + misfit[2] * misfit[2]
        + misfit[3] * misfit[3]
        + misfit[4] * misfit[4]
    )
    point_loss = valid * (squares + RESIDUAL_WEIGHT * physics) * (1.0 / plan.query_total)

    rate = valid * (1.0 / plan.query_total)
    twice = RESIDUAL_WEIGHT * 2.0
    d_cont = rate * twice * continuity
    d_mom = [rate * twice * m for m in momentum]
    d_energy = rate * twice * energy
    d_value = [2.0 * rate * m for m in misfit]
    for d in range(3):
        d_value[2 + d] = d_value[2 + d] + (
            d_mom[0] * grad[d][2] + d_mom[1] * grad[d][3] + d_mom[2] * grad[d][4] + d_energy * grad[d][0]
        )
    d_value[0] = d_value[0] - d_mom[2]
    d_out_t[...] = jnp.zeros_like(d_out_t)
    for f in range(5):
        d_out_t[f : f + 1, :] = d_value[f]
    for d in range(3):
        first = 8 * (d + 1)
        d_out_t[first : first + 1, :] = d_energy * velocity[d]
        d_out_t[first + 1 : first + 2, :] = d_mom[d]
        for j in range(3):
            term = d_mom[j] * velocity[d]
            if j == d:
                term = term + d_cont
            d_out_t[first + 2 + j : first + 3 + j, :] = term
    d_out_t[32:33, :] = -DIFFUSIVITY * d_energy
    for j in range(3):
        d_out_t[34 + j : 35 + j, :] = -VISCOSITY * d_mom[j]

    for s in range(5):
        span = slice(s * rows, (s + 1) * rows)
        wanted = d_out_t[8 * s : 8 * s + 8, :]
        do_low = halves(wanted)[1].astype(F32)
        back[span, :] = mul(jnp.concatenate([wanted, wanted, do_low], axis=0).astype(BF16), wo_three, TN)

    def second_back(block, total):
        act = fetch(mixed, 0, block)
        slope = 1.0 - act * act
        curve = -2.0 * act * slope
        tangent = [fetch(mixed, 1 + d, block) for d in range(3)]
        cot_t = [fetch(back, 1 + d, block) for d in range(3)]
        cot_l = fetch(back, 4, block)
        refs = (d_high, d_low)
        d_slope = cot_l * fetch(mixed, 4, block)
        norm = None
        bent = 2.0 * curve * cot_l
        for d in range(3):
            store(1 + d, block, refs, slope * cot_t[d] + bent * tangent[d])
            d_slope = d_slope + cot_t[d] * tangent[d]
            norm = tangent[d] * tangent[d] if norm is None else norm + tangent[d] * tangent[d]
        store(4, block, refs, slope * cot_l)
        d_curve = cot_l * norm
        d_slope = d_slope - 2.0 * act * d_curve
        d_act = fetch(back, 0, block) - 2.0 * slope * d_curve - 2.0 * act * d_slope
        d_pre = slope * d_act
        store(0, block, refs, d_pre)
        return total + folded(d_pre)

    grad_two = lax.fori_loop(0, rows // BLOCK, second_back, jnp.zeros((8, hidden), F32))

    def put(part, first, value):
        while value.shape[0]:
            block, row = first // plan.main_rows, first % plan.main_rows
            count = min(value.shape[0], plan.main_rows - row)
            packed[2 * part + block, row : row + count, :] = value[:count]
            first, value = first + count, value[count:]

    wide = 2 * LANES
    for left in range(hidden // wide):
        for right in range(hidden // wide):
            lefts = slice(left * wide, (left + 1) * wide)
            rights = slice(right * wide, (right + 1) * wide)
            part = mul3(
                (one_high[:, lefts], one_low[:, lefts]), (d_high[:, rights], d_low[:, rights]), TN
            )
            for side in range(2):
                put(2 * right + side, left * wide, part[:, side * LANES : (side + 1) * LANES])

    lax.fori_loop(0, 5, functools.partial(times_mid, NT, (d_high, d_low), back), 0)

    def first_back(block, totals):
        act = fetch(z_one, 0, block)
        slope = 1.0 - act * act
        curve = -2.0 * act * slope
        where = fetch(pos, 0, block)
        cot_t = [fetch(back, 1 + d, block) for d in range(3)]
        cot_l = fetch(back, 4, block)
        d_curve = cot_l * square
        d_slope = cot_t[0] * w_pos[0] + cot_t[1] * w_pos[1] + cot_t[2] * w_pos[2] - 2.0 * act * d_curve
        d_act = fetch(back, 0, block) - 2.0 * slope * d_curve - 2.0 * act * d_slope
        d_pre = slope * d_act
        store(0, block, (d_high, d_low), d_pre)
        sums = [totals[0] + folded(d_pre)]
        for d in range(3):
            sums.append(totals[1 + d] + folded(where[:, d : d + 1] * d_pre + slope * cot_t[d]))
        sums.append(totals[4] + folded(curve * cot_l))
        return tuple(sums)

    sums = lax.fori_loop(
        0, rows // BLOCK, first_back, tuple(jnp.zeros((8, hidden), F32) for _ in range(5))
    )
    d_square = jnp.sum(sums[4], axis=0, keepdims=True)
    grad_latent = mul(code[...], d_high[0:rows, :], TN) + mul(code[...], d_low[0:rows, :], TN)

    grad_out = None
    for s in range(5):
        span = slice(s * rows, (s + 1) * rows)
        wanted = d_out_t[8 * s : 8 * s + 8, :]
        do_high, do_low = halves(wanted)
        do_both = jnp.concatenate([wanted, do_low.astype(F32)], axis=0).astype(BF16)
        both = mul(do_both, two_high[span, :])
        term = both[:8] + both[8:] + mul(do_high, two_low[span, :])
        grad_out = term if grad_out is None else grad_out + term

    lane_row = lax.broadcasted_iota(jnp.int32, (1, hidden), 1)
    last = jnp.where(lane_row == 5, jnp.sum(point_loss), 0.0)
    for f in range(5):
        last = last + jnp.where(lane_row == f, jnp.sum(d_value[f]), 0.0)
    grad_pos = [jnp.sum(sums[1 + d], axis=0, keepdims=True) + 2.0 * w_pos[d] * d_square for d in range(3)]
    misc = grad_pos + [
        jnp.sum(sums[0], axis=0, keepdims=True),
        jnp.sum(grad_two, axis=0, keepdims=True),
        last,
    ]
    misc = jnp.concatenate(misc + [jnp.zeros((2, hidden), F32)], axis=0)
    for part in range(hidden // LANES):
        lanes = slice(part * LANES, (part + 1) * LANES)
        put(part, hidden, grad_latent[:, lanes])
        packed[2 * part, plan.coded_rows :, :] = misc[:, lanes]
        packed[2 * part + 1, plan.coded_rows :, :] = grad_out[:, lanes]

    chosen = jnp.where(
        lane == jnp.broadcast_to(words[:, 10:11], (rows, LANES)).astype(jnp.int32), words[:, 9:10], 0.0
    ).astype(BF16)
    fields = jnp.concatenate(value + [jnp.zeros((3, rows), F32)], axis=0)
    source = (lax.broadcasted_iota(jnp.int32, (8, rows), 1) & (plan.tiles * 8 - 1)) >> 3
    spread = jnp.concatenate([jnp.where(source == t, fields, 0.0) for t in range(plan.tiles)], axis=0)
    high, middle, low = thirds(spread)
    spread = mul(high, chosen) + mul(middle, chosen) + mul(low, chosen)
    packed[:, plan.main_rows : plan.coded_rows, :] = jnp.zeros((8, plan.devices, LANES), F32)
    for t in range(plan.tiles):
        row = plan.main_rows + (my_replica * (plan.tiles // 8) + t // 8) * 8
        packed[t % 8, pl.ds(pl.multiple_of(row, 8), 8), :] = spread[8 * t : 8 * t + 8]

    for block in range(8):
        spot = jnp.bitwise_xor(block, my_block) & 3

        @pl.when((my_block >> 2) == block // 4)
        def _():
            keep_ref[spot] = packed[block]

        @pl.when((my_block >> 2) != block // 4)
        def _():
            send_ref[spot] = packed[block]


class Plan:
    def __init__(self, tiles, replicas, queries, planes, hidden, latents):
        self.tiles, self.replicas, self.planes = tiles, replicas, planes
        self.slots = 2 * queries // tiles
        self.devices = tiles * replicas
        self.query_total = float(queries * self.devices)
        self.main_rows = (hidden + latents) // 2
        self.coded_rows = self.main_rows + self.devices
        self.rows = self.coded_rows + 8
        self.scales = -(-(self.coded_rows // SUB + 1) // 16) * 16
        self.sent_rows = self.coded_rows + 16 + self.scales
        top = self.devices.bit_length() - 1
        self.core, self.plane, self.rest = [0], [1, top - 1], list(range(2, top - 1))

    def mask(self, bits, steps):
        return sum(1 << bit for number, bit in enumerate(bits) if steps >> number & 1)

    def my_block(self, device):
        return (device & 1) * 4 + (device >> 1 & 1) + 2 * (device >> self.plane[1] & 1)


def swapped(value, plan, bits, steps):
    mask = plan.mask(bits, steps)
    return lax.ppermute(value, ("replica", "tile"), [(i, i ^ mask) for i in range(plan.devices)])


def encode(plan, read, out_ref):
    starts = list(range(0, plan.coded_rows, SUB))
    parts = [read(start, SUB) for start in starts] + [read(plan.coded_rows, 8)]
    tops = [jnp.max(jnp.abs(part), axis=0, keepdims=True) for part in parts]
    tops = tops + [jnp.zeros_like(tops[0])] * (plan.scales - len(tops))
    power = jnp.floor(jnp.log2(jnp.maximum(jnp.concatenate(tops, axis=0), 1e-30)))
    scale = jnp.exp2(14.0 - power)

    def whole(value):
        return jnp.clip(jnp.round(value), -32767.0, 32767.0)

    def narrow(value):
        return value.astype(jnp.int32).astype(jnp.int16)

    for number, start in enumerate(starts):
        out_ref[start : start + SUB, :] = narrow(whole(parts[number] * scale[number : number + 1]))
    last = len(starts)
    exact = parts[last] * scale[last : last + 1]
    high = whole(exact)
    low = whole((exact - high) * 32768.0)
    out_ref[plan.coded_rows : plan.coded_rows + 16, :] = narrow(jnp.concatenate([high, low], axis=0))
    out_ref[plan.coded_rows + 16 :, :] = narrow(power)


def decoder(plan, ref):
    def widen(value):
        return value.astype(jnp.int32).astype(F32)

    scale = jnp.exp2(widen(ref[plan.coded_rows + 16 :, :]) - 14.0)

    def read(start, count):
        if start < plan.coded_rows:
            number = start // SUB
            return widen(ref[start : start + count, :]) * scale[number : number + 1]
        both = widen(ref[plan.coded_rows : plan.coded_rows + 16, :])
        number = plan.coded_rows // SUB
        return (both[:8] + both[8:] * (1.0 / 32768.0)) * scale[number : number + 1]

    return read


def added(readers):
    def read(start, count):
        total = readers[0](start, count)
        for reader in readers[1:]:
            total = total + reader(start, count)
        return total

    return read


def first_kernel(plan, keep_ref, got_ref, mine_ref, *out_refs):
    def reader(block):
        return lambda start, count: (
            keep_ref[block, start : start + count, :] + got_ref[block, start : start + count, :]
        )

    for number, out_ref in enumerate(out_refs):
        encode(plan, reader(number + 1), out_ref)
    mine_ref[...] = keep_ref[0] + got_ref[0]


def first_sum(keep, got, plan):
    sent = jax.ShapeDtypeStruct((plan.sent_rows, LANES), jnp.int16)
    return pl.pallas_call(
        functools.partial(first_kernel, plan),
        out_shape=(jax.ShapeDtypeStruct(keep.shape[1:], F32), sent, sent, sent),
        in_specs=[VMEM] * 2,
        out_specs=tuple([VMEM] * 4),
        compiler_params=pltpu.CompilerParams(vmem_limit_bytes=6 << 20),
        name="sum_core",
    )(keep, got)


def plane_kernel(plan, mine_ref, *refs):
    readers = [lambda start, count: mine_ref[start : start + count, :]]
    encode(plan, added(readers + [decoder(plan, ref) for ref in refs[:-1]]), refs[-1])


def pair_kernel(plan, mine_ref, other_ref, out_ref):
    encode(plan, added([decoder(plan, mine_ref), decoder(plan, other_ref)]), out_ref)


def coded_sum(kernel, blocks, plan, name):
    return pl.pallas_call(
        functools.partial(kernel, plan),
        out_shape=jax.ShapeDtypeStruct((plan.sent_rows, LANES), jnp.int16),
        in_specs=[VMEM] * len(blocks),
        out_specs=VMEM,
        compiler_params=pltpu.CompilerParams(vmem_limit_bytes=4 << 20),
        name=name,
    )(*blocks)


def main(place, lat, words, weights, plan):
    rows = plan.tiles * plan.slots
    hidden = weights[3].shape[0]
    channels = lat.shape[1]
    outs = jax.ShapeDtypeStruct((4, plan.rows, LANES), F32)
    wide = lambda kind: pltpu.VMEM((5 * rows, hidden), kind)
    return pl.pallas_call(
        functools.partial(main_kernel, plan),
        out_shape=(outs, outs),
        in_specs=[SMEM] + [VMEM] * 2 + [HBM] * 7,
        out_specs=(VMEM, VMEM),
        scratch_shapes=[
            pltpu.VMEM((rows, channels), BF16),
            pltpu.VMEM((rows, LANES), F32),
            pltpu.VMEM((rows, hidden), F32),
            wide(BF16),
            wide(BF16),
            wide(F32),
            wide(BF16),
            wide(BF16),
            wide(F32),
            wide(BF16),
            wide(BF16),
            pltpu.VMEM((40, rows), F32),
            pltpu.VMEM((40, rows), F32),
            pltpu.VMEM((8, plan.rows, LANES), F32),
            pltpu.VMEM((hidden, hidden), BF16),
            pltpu.VMEM((hidden, hidden), BF16),
        ]
        + [pltpu.VMEM(weight.shape, F32) for weight in weights]
        + [pltpu.SemaphoreType.DMA((7,))],
        compiler_params=pltpu.CompilerParams(vmem_limit_bytes=32 << 20),
        name="encode_decode",
    )(place, lat, words, *weights)


def unpack_kernel(plan, place_ref, *refs):
    sources, outs, packed = refs[:8], refs[8:-1], refs[-1]
    prediction_ref, latent_ref, pos_ref, one_ref, mid_ref, two_ref, out_ref, bias_out_ref, loss_ref = outs
    my_block = place_ref[0]
    device = place_ref[2] * plan.tiles + place_ref[1]
    starts = list(range(0, plan.coded_rows, SUB))
    for number, ref in enumerate(sources):
        read = decoder(plan, ref)
        block = jnp.bitwise_xor(number, my_block)
        for start in starts:
            packed[block, start : start + SUB, :] = read(start, SUB)
        packed[block, plan.coded_rows :, :] = read(plan.coded_rows, 8)

    hidden = mid_ref.shape[0]
    latents = latent_ref.shape[0]
    split = plan.main_rows
    for part in range(hidden // LANES):
        lanes = slice(part * LANES, (part + 1) * LANES)
        mid_ref[0:split, lanes] = packed[2 * part, 0:split, :]
        mid_ref[split:, lanes] = packed[2 * part + 1, 0 : hidden - split, :]
        latent_ref[:, lanes] = packed[2 * part + 1, hidden - split : split, :]
        misc = packed[2 * part, plan.coded_rows :, :]
        pos_ref[:, lanes] = misc[0:3]
        one_ref[:, lanes] = misc[3:4]
        two_ref[:, lanes] = misc[4:5]
        out_ref[:, lanes] = packed[2 * part + 1, plan.coded_rows : plan.coded_rows + 5, :]
        if part == 0:
            bias_out_ref[...] = misc[5:6, 0:5]
            loss_ref[...] = misc[5:6, 5:6]
    row = pl.multiple_of(plan.main_rows + (device >> 3) * 8, 8)
    fields = packed[device & 7, pl.ds(row, 8), :]
    for f in range(5):
        prediction_ref[f] = fields[f : f + 1]


def unpack(place, blocks, plan, hidden, latents):
    shapes = [
        (5, 1, LANES),
        (latents, hidden),
        (3, hidden),
        (1, hidden),
        (hidden, hidden),
        (1, hidden),
        (5, hidden),
        (1, 5),
        (1, 1),
    ]
    return pl.pallas_call(
        functools.partial(unpack_kernel, plan),
        out_shape=tuple(jax.ShapeDtypeStruct(shape, F32) for shape in shapes),
        in_specs=[SMEM] + [VMEM] * 8,
        out_specs=tuple([VMEM] * len(shapes)),
        scratch_shapes=[pltpu.VMEM((8, plan.rows, LANES), F32)],
        compiler_params=pltpu.CompilerParams(vmem_limit_bytes=16 << 20),
        name="unpack",
    )(place, *blocks)


def body(
    fields,
    convolution_weight,
    convolution_bias,
    query_owner,
    query_cell,
    query_frac,
    target,
    w_latent,
    w_pos,
    bias_one,
    w_mid,
    bias_two,
    w_out,
    bias_out,
):
    tiles = lax.axis_size("tile")
    replicas = lax.axis_size("replica")
    my_tile = lax.axis_index("tile")
    my_replica = lax.axis_index("replica")
    channels = fields.shape[1]
    queries = query_cell.shape[1]
    hidden = w_mid.shape[0]
    plan = Plan(tiles, replicas, queries, fields.shape[2], hidden, channels)
    device = my_replica * tiles + my_tile
    place = jnp.stack([plan.my_block(device), my_tile, my_replica]).astype(jnp.int32)

    here = fields[0].transpose(1, 2, 0, 3)
    up = [(i, (i + 1) % tiles) for i in range(tiles)]
    down = [((i + 1) % tiles, i) for i in range(tiles)]
    to_left, to_right, query_owner = lax.optimization_barrier(
        (here[: DILATION_RATE + 1], here[-DILATION_RATE:], query_owner)
    )
    taps = convolution_weight.reshape(channels, 3, 3, 3, channels)
    taps = taps.transpose(1, 3, 0, 2, 4).reshape(3, 3 * channels, 3 * channels)
    right = lax.ppermute(to_left, "tile", down)
    left = lax.ppermute(to_right, "tile", up)
    words = route(
        query_owner[:, :, 0],
        query_cell,
        query_frac.transpose(1, 0, 2),
        target.transpose(1, 0, 2),
        tiles,
        plan.slots,
    )
    words = lax.all_to_all(
        words.reshape(tiles, 8, WORDS), "tile", split_axis=0, concat_axis=0, tiled=True
    ).reshape(tiles * 8, WORDS)

    lat = convolve(left, here, right, taps, convolution_bias[:, None])
    weights = (w_latent, w_pos, bias_one[None], w_mid, bias_two[None], w_out, bias_out[None])
    send, keep = main(place, lat, words, weights, plan)

    mine, *others = first_sum(keep, swapped(send, plan, plan.core, 1), plan)
    arrived = [swapped(block, plan, plan.plane, step + 1) for step, block in enumerate(others)]
    block = coded_sum(plane_kernel, [mine] + arrived, plan, "sum_plane")
    for bit in plan.rest:
        block = coded_sum(pair_kernel, [block, swapped(block, plan, [bit], 1)], plan, "sum_line")
    blocks = [block] + [swapped(block, plan, plan.plane, step) for step in range(1, 4)]
    blocks = blocks + [swapped(block, plan, plan.core, 1) for block in blocks]
    prediction, g_latent, g_pos, g_one, g_mid, g_two, g_out, g_bias, loss = unpack(
        place, blocks, plan, hidden, channels
    )
    return (
        prediction.transpose(1, 0, 2),
        g_latent,
        g_pos,
        g_one.reshape(hidden),
        g_mid,
        g_two.reshape(hidden),
        g_out,
        g_bias.reshape(5),
        loss.reshape(()),
    )


def solution(mesh):
    return jax.shard_map(
        body,
        mesh=mesh,
        in_specs=(
            P("replica", None, "tile", None, None),
            P(),
            P(),
            P("replica", "tile", None),
            P("replica", "tile"),
            P("replica", None, "tile"),
            P("replica", None, "tile"),
            P(),
            P(),
            P(),
            P(),
            P(),
            P(),
            P(),
        ),
        out_specs=(P("replica", None, "tile"), P(), P(), P(), P(), P(), P(), P(), P()),
        check_vma=False,
    )
```

```python
import functools

import jax
import jax.numpy as jnp
from jax import lax
from jax.experimental import pallas as pl
from jax.experimental.pallas import tpu as pltpu
from jax.sharding import PartitionSpec as P

DILATION_RATE = 2
VISCOSITY = 0.05
DIFFUSIVITY = 0.05
RESIDUAL_WEIGHT = 0.5

F32 = jnp.float32
BF16 = jnp.bfloat16
LANES = 128
BLOCK = 32
WORDS = 128
SUB = 32
NN = (((1,), (0,)), ((), ()))
NT = (((1,), (1,)), ((), ()))
TN = (((0,), (0,)), ((), ()))
VMEM = pl.BlockSpec(memory_space=pltpu.VMEM)
SMEM = pl.BlockSpec(memory_space=pltpu.SMEM)
HBM = pl.BlockSpec(memory_space=pltpu.HBM)


def mul(left, right, dims=NN):
    return lax.dot_general(left, right, dims, preferred_element_type=F32)


def halves(value):
    high = value.astype(BF16)
    return high, (value - high.astype(F32)).astype(BF16)


def thirds(value):
    high = value.astype(BF16)
    rest = value - high.astype(F32)
    middle = rest.astype(BF16)
    return high, middle, (rest - middle.astype(F32)).astype(BF16)


def mul3(left, right, dims=NN):
    return mul(left[0], right[0], dims) + mul(left[0], right[1], dims) + mul(left[1], right[0], dims)


def fetches(sources, targets, sems):
    copies = [
        pltpu.make_async_copy(source, target, sems.at[number])
        for number, (source, target) in enumerate(zip(sources, targets))
    ]
    for copy in copies:
        copy.start()
    return copies


def route_kernel(tiles, slots, *refs):
    out_ref, owner_ref, cell_ref, frac_ref, target_ref, words, sems = refs[4:]
    queries = owner_ref.shape[1]
    for copy in fetches(refs[:4], (owner_ref, cell_ref, frac_ref, target_ref), sems):
        copy.wait()
    owner = owner_ref[...]
    hits = (lax.broadcasted_iota(jnp.int32, (tiles, queries), 0) == owner).astype(F32)
    before = lax.broadcasted_iota(jnp.int32, (queries, queries), 0) < lax.broadcasted_iota(
        jnp.int32, (queries, queries), 1
    )
    earlier = mul(hits.astype(BF16), before.astype(F32).astype(BF16))
    slot = jnp.sum(hits * earlier, axis=0, keepdims=True)
    place = owner * slots + slot.astype(jnp.int32)
    spot = lax.broadcasted_iota(jnp.int32, (tiles * 8, queries), 0)
    spot = (spot >> 3) * slots + (spot & 7)
    groups = slots // 8
    chosen = [jnp.where(spot + 8 * group == place, 1.0, 0.0) for group in range(groups)]
    chosen = jnp.concatenate(chosen, axis=1).astype(BF16)
    words[...] = jnp.zeros_like(words)
    for group in range(groups):
        row, lanes = 16 * group, slice(group * queries, (group + 1) * queries)
        words[row : row + 1, lanes] = cell_ref[...].astype(F32)
        for d in range(3):
            words[row + 1 + d : row + 2 + d, lanes] = frac_ref[d]
        for f in range(5):
            words[row + 4 + f : row + 5 + f, lanes] = target_ref[f]
        words[row + 9 : row + 10, lanes] = jnp.ones((1, queries), F32)
        words[row + 10 : row + 11, lanes] = lax.broadcasted_iota(jnp.int32, (1, queries), 1).astype(F32)
    high, middle, low = thirds(words[...])
    out_ref[...] = mul(chosen, high, NT) + mul(chosen, middle, NT) + mul(chosen, low, NT)


def route(owner, cell, frac, target, tiles, slots):
    queries = owner.shape[1]
    return pl.pallas_call(
        functools.partial(route_kernel, tiles, slots),
        out_shape=jax.ShapeDtypeStruct((tiles * 8, WORDS), F32),
        in_specs=[HBM] * 4,
        out_specs=VMEM,
        scratch_shapes=[
            pltpu.VMEM(owner.shape, owner.dtype),
            pltpu.VMEM(cell.shape, cell.dtype),
            pltpu.VMEM(frac.shape, F32),
            pltpu.VMEM(target.shape, F32),
            pltpu.VMEM((WORDS, queries * (slots // 8)), F32),
            pltpu.SemaphoreType.DMA((4,)),
        ],
        compiler_params=pltpu.CompilerParams(vmem_limit_bytes=4 << 20),
        name="route",
    )(owner, cell, frac, target)


def tap_sum(weight_ref, planes, pair):
    total = None
    for step_x, ref, index in planes:
        rows_y = ref.shape[1]
        blocks = [
            jnp.concatenate([ref[index, (2 * pair + half + step_y) % rows_y] for half in (0, 1)], axis=1)
            for step_y in (-1, 0, 1)
        ]
        term = mul(weight_ref[step_x], jnp.concatenate(blocks, axis=0))
        total = term if total is None else total + term
    channels = total.shape[0] // 3
    sides = []
    for half in (0, 1):
        part = total[:, half * LANES : (half + 1) * LANES]
        sides.append(
            part[channels : 2 * channels]
            + pltpu.roll(part[:channels], 1, 1)
            + pltpu.roll(part[2 * channels :], LANES - 1, 1)
        )
    return jnp.concatenate(sides, axis=1)


def conv_kernel(left_ref, here_ref, right_ref, weight_ref, bias_ref, lat_ref):
    planes, rows_y = here_ref.shape[0], here_ref.shape[1]
    bias = bias_ref[...]
    for x in range(planes + 1):
        taps = []
        for step in range(3):
            plane = x + DILATION_RATE * (step - 1)
            if plane < 0:
                taps.append((step, left_ref, plane + left_ref.shape[0]))
            elif plane >= planes:
                taps.append((step, right_ref, plane - planes))
            else:
                taps.append((step, here_ref, plane))
        for pair in range(rows_y // 2):
            summed = tap_sum(weight_ref, taps, pair) + bias
            lat_ref[x * (rows_y // 2) + pair] = jax.nn.gelu(summed).astype(BF16)


def convolve(left, here, right, taps, conv_bias):
    planes, rows_y, channels, rows_z = here.shape
    pairs = (planes + 1) * rows_y // 2
    return pl.pallas_call(
        conv_kernel,
        out_shape=jax.ShapeDtypeStruct((pairs, channels, 2 * rows_z), BF16),
        in_specs=[VMEM] * 5,
        out_specs=VMEM,
        compiler_params=pltpu.CompilerParams(vmem_limit_bytes=8 << 20),
        cost_estimate=pl.CostEstimate(flops=3 << 30, bytes_accessed=4 << 20, transcendentals=0),
        name="convolve",
    )(left, here, right, taps, conv_bias)


def interpolate(words, lat, planes, rows_y, rows_z):
    rows = words.shape[0]
    cell = jnp.broadcast_to(words[:, 0:1], (rows, LANES)).astype(jnp.int32)
    frac = [jnp.broadcast_to(words[:, 1 + d : 2 + d], (rows, LANES)) for d in range(3)]
    shift_z = rows_z.bit_length() - 1
    shift_y = rows_y.bit_length() - 1
    base_x = cell >> (shift_z + shift_y)
    base_y = (cell >> shift_z) & (rows_y - 1)
    base_z = cell & (rows_z - 1)
    spot = lax.broadcasted_iota(jnp.int32, (rows, rows_z), 1)
    part_z = jnp.where(spot == base_z, 1.0 - frac[2], 0.0) + jnp.where(
        spot == ((base_z + 1) & (rows_z - 1)), frac[2], 0.0
    )
    part_yz = []
    for y in range(rows_y):
        part_y = jnp.where(
            base_y == y, 1.0 - frac[1], jnp.where(base_y == (y - 1) % rows_y, frac[1], 0.0)
        )
        part_yz.append(part_y * part_z)
    total = None
    for x in range(planes + 1):
        part_x = jnp.where(base_x == x, 1.0 - frac[0], jnp.where(base_x == x - 1, frac[0], 0.0))
        for pair in range(rows_y // 2):
            sides = [(part_x * part_yz[2 * pair + half]).astype(BF16) for half in (0, 1)]
            term = mul(jnp.concatenate(sides, axis=1), lat[x * (rows_y // 2) + pair], NT)
            total = term if total is None else total + term
    return total.astype(BF16), base_x, base_y, base_z, frac


def folded(value):
    return jnp.sum(value.reshape(value.shape[0] // 8, 8, value.shape[1]), axis=0)


def main_kernel(
    plan,
    place_ref,
    lat,
    words_ref,
    w_latent_hbm,
    w_pos_hbm,
    bias_one_hbm,
    w_mid_hbm,
    bias_two_hbm,
    w_out_hbm,
    bias_out_hbm,
    send_ref,
    keep_ref,
    code,
    pos,
    z_one,
    one_high,
    one_low,
    mixed,
    two_high,
    two_low,
    back,
    mixed_back,
    first_high,
    first_low,
    sums_ref,
    d_high,
    d_low,
    out_t,
    d_out_t,
    packed,
    mid_high,
    mid_low,
    w_latent_ref,
    w_pos_ref,
    bias_one_ref,
    w_mid_ref,
    bias_two_ref,
    w_out_ref,
    bias_out_ref,
    sems,
):
    rows = plan.tiles * plan.slots
    hidden = w_mid_ref.shape[0]
    latents = w_latent_ref.shape[0]
    weights = fetches(
        (w_latent_hbm, w_pos_hbm, bias_one_hbm, w_mid_hbm, bias_two_hbm, w_out_hbm, bias_out_hbm),
        (w_latent_ref, w_pos_ref, bias_one_ref, w_mid_ref, bias_two_ref, w_out_ref, bias_out_ref),
        sems,
    )
    planes, rows_z = plan.planes, lat.shape[2] // 2
    rows_y = lat.shape[0] // (planes + 1) * 2
    slots = rows // plan.tiles
    my_block = place_ref[0]
    my_tile = place_ref[1]
    my_replica = place_ref[2]
    always = my_tile >= 0

    words = words_ref[...]
    words = jnp.concatenate(
        [words] + [pltpu.roll(words, LANES - 16 * group, 1) for group in range(1, slots // 8)], axis=0
    )
    interp, base_x, base_y, base_z, frac = interpolate(words, lat, planes, rows_y, rows_z)
    code[...] = interp
    global_x = my_tile * planes + base_x
    lane = lax.broadcasted_iota(jnp.int32, (rows, LANES), 1)
    pos[...] = jnp.where(
        lane == 0,
        (global_x.astype(F32) + frac[0]) / (planes * plan.tiles),
        jnp.where(
            lane == 1,
            (base_y.astype(F32) + frac[1]) / rows_y,
            (base_z.astype(F32) + frac[2]) / rows_z,
        ),
    )

    for copy in weights:
        copy.wait()
    high, low = halves(w_latent_ref[...])
    z_one[...] = mul(interp, high) + mul(interp, low)
    high, low = halves(w_mid_ref[...])
    mid_high[...] = high
    mid_low[...] = low
    w_pos = [w_pos_ref[d : d + 1, :] for d in range(3)]
    square = w_pos[0] * w_pos[0] + w_pos[1] * w_pos[1] + w_pos[2] * w_pos[2]
    bias_one = bias_one_ref[...]
    bias_two = bias_two_ref[...]

    part_rows = rows // 2

    def at(part, index, block=None):
        first = (part * 5 + index) * part_rows
        if block is None:
            return slice(first, first + part_rows)
        return slice(first + block * BLOCK, first + (block + 1) * BLOCK)

    def rows_at(part, block):
        first = part * part_rows + block * BLOCK
        return slice(first, first + BLOCK)

    def store(refs, span, value):
        high, low = halves(value)
        refs[0][span, :] = high
        refs[1][span, :] = low

    def layer_one(part):
        refs = (one_high, one_low)
        for block in range(part_rows // BLOCK):
            here = rows_at(part, block)
            where = pos[here, :]
            pre = (
                z_one[here, :]
                + (where[:, 0:1] * w_pos[0] + where[:, 1:2] * w_pos[1] + where[:, 2:3] * w_pos[2])
                + bias_one
            )
            act = jnp.tanh(pre)
            slope = 1.0 - act * act
            curve = -2.0 * act * slope
            z_one[here, :] = act
            store(refs, at(part, 0, block), act)
            for d in range(3):
                store(refs, at(part, 1 + d, block), slope * w_pos[d])
            store(refs, at(part, 4, block), curve * square)

    def times_mid(dims, source, result, part):
        for index in range(5):
            span = at(part, index)
            left = (source[0][span, :], source[1][span, :])
            result[span, :] = mul3(left, (mid_high[...], mid_low[...]), dims)

    def layer_two(part):
        refs = (two_high, two_low)
        for block in range(part_rows // BLOCK):
            act = jnp.tanh(mixed[at(part, 0, block), :] + bias_two)
            slope = 1.0 - act * act
            curve = -2.0 * act * slope
            store(refs, at(part, 0, block), act)
            mixed[at(part, 0, block), :] = act
            norm = None
            for d in range(3):
                tangent = mixed[at(part, 1 + d, block), :]
                store(refs, at(part, 1 + d, block), slope * tangent)
                norm = tangent * tangent if norm is None else norm + tangent * tangent
            store(refs, at(part, 4, block), slope * mixed[at(part, 4, block), :] + curve * norm)

    out_fields = jnp.concatenate([w_out_ref[...], jnp.zeros((3, hidden), F32)], axis=0)
    wo_high, wo_low = halves(out_fields)
    wo_three = jnp.concatenate([out_fields, wo_low.astype(F32), out_fields], axis=0).astype(BF16)
    wo_both = jnp.concatenate([out_fields, wo_low.astype(F32)], axis=0).astype(BF16)

    def outputs(part):
        for s in range(5):
            span = at(part, s)
            both = mul(wo_both, two_high[span, :], NT)
            both = both[:8] + both[8:] + mul(wo_high, two_low[span, :], NT)
            out_t[8 * s : 8 * s + 8, part * part_rows : (part + 1) * part_rows] = both

    @pl.when(always)
    def _():
        layer_one(0)
        times_mid(NN, (one_high, one_low), mixed, 0)
        layer_one(1)
        times_mid(NN, (one_high, one_low), mixed, 1)
        layer_two(0)
        layer_two(1)

    @pl.when(always)
    def _():
        outputs(0)
        outputs(1)

    words_t = words.T
    target = [words_t[4 + f : 5 + f, :] for f in range(5)]
    valid = words_t[9:10, :]
    value = [out_t[f : f + 1, :] + bias_out_ref[0:1, f : f + 1] for f in range(5)]
    grad = [[out_t[8 * (d + 1) + f : 8 * (d + 1) + f + 1, :] for f in range(5)] for d in range(3)]
    laplace = [out_t[32 + f : 33 + f, :] for f in range(5)]
    velocity = value[2:5]
    advection = [
        velocity[0] * grad[0][f] + velocity[1] * grad[1][f] + velocity[2] * grad[2][f] for f in range(5)
    ]
    continuity = grad[0][2] + grad[1][3] + grad[2][4]
    momentum = [advection[2 + j] + grad[j][1] - VISCOSITY * laplace[2 + j] for j in range(3)]
    momentum[2] = momentum[2] - value[0]
    energy = advection[0] - DIFFUSIVITY * laplace[0]
    misfit = [value[f] - target[f] for f in range(5)]
    physics = (
        continuity * continuity
        + (momentum[0] * momentum[0] + momentum[1] * momentum[1] + momentum[2] * momentum[2])
        + energy * energy
    )
    squares = (
        misfit[0] * misfit[0]
        + misfit[1] * misfit[1]
        + misfit[2] * misfit[2]
        + misfit[3] * misfit[3]
        + misfit[4] * misfit[4]
    )
    point_loss = valid * (squares + RESIDUAL_WEIGHT * physics) * (1.0 / plan.query_total)

    rate = valid * (1.0 / plan.query_total)
    twice = RESIDUAL_WEIGHT * 2.0
    d_cont = rate * twice * continuity
    d_mom = [rate * twice * m for m in momentum]
    d_energy = rate * twice * energy
    d_value = [2.0 * rate * m for m in misfit]
    for d in range(3):
        d_value[2 + d] = d_value[2 + d] + (
            d_mom[0] * grad[d][2] + d_mom[1] * grad[d][3] + d_mom[2] * grad[d][4] + d_energy * grad[d][0]
        )
    d_value[0] = d_value[0] - d_mom[2]
    d_out_t[...] = jnp.zeros_like(d_out_t)
    for f in range(5):
        d_out_t[f : f + 1, :] = d_value[f]
    for d in range(3):
        first = 8 * (d + 1)
        d_out_t[first : first + 1, :] = d_energy * velocity[d]
        d_out_t[first + 1 : first + 2, :] = d_mom[d]
        for j in range(3):
            term = d_mom[j] * velocity[d]
            if j == d:
                term = term + d_cont
            d_out_t[first + 2 + j : first + 3 + j, :] = term
    d_out_t[32:33, :] = -DIFFUSIVITY * d_energy
    for j in range(3):
        d_out_t[34 + j : 35 + j, :] = -VISCOSITY * d_mom[j]

    def out_back(part):
        for s in range(5):
            wanted = d_out_t[8 * s : 8 * s + 8, part * part_rows : (part + 1) * part_rows]
            do_low = halves(wanted)[1].astype(F32)
            wanted = jnp.concatenate([wanted, wanted, do_low], axis=0).astype(BF16)
            back[at(part, s), :] = mul(wanted, wo_three, TN)

    def second_back(part, total):
        refs = (d_high, d_low)
        for block in range(part_rows // BLOCK):
            act = mixed[at(part, 0, block), :]
            slope = 1.0 - act * act
            curve = -2.0 * act * slope
            cot_l = back[at(part, 4, block), :]
            d_slope = cot_l * mixed[at(part, 4, block), :]
            norm = None
            bent = 2.0 * curve * cot_l
            for d in range(3):
                tangent = mixed[at(part, 1 + d, block), :]
                cot_t = back[at(part, 1 + d, block), :]
                store(refs, at(part, 1 + d, block), slope * cot_t + bent * tangent)
                d_slope = d_slope + cot_t * tangent
                norm = tangent * tangent if norm is None else norm + tangent * tangent
            store(refs, at(part, 4, block), slope * cot_l)
            d_curve = cot_l * norm
            d_slope = d_slope - 2.0 * act * d_curve
            d_act = back[at(part, 0, block), :] - 2.0 * slope * d_curve - 2.0 * act * d_slope
            d_pre = slope * d_act
            store(refs, at(part, 0, block), d_pre)
            total = total + folded(d_pre)
        return total

    def first_back(part, sums):
        for block in range(part_rows // BLOCK):
            here = rows_at(part, block)
            act = z_one[here, :]
            slope = 1.0 - act * act
            curve = -2.0 * act * slope
            where = pos[here, :]
            cot_t = [mixed_back[at(part, 1 + d, block), :] for d in range(3)]
            cot_l = mixed_back[at(part, 4, block), :]
            d_curve = cot_l * square
            d_slope = cot_t[0] * w_pos[0] + cot_t[1] * w_pos[1] + cot_t[2] * w_pos[2] - 2.0 * act * d_curve
            d_act = mixed_back[at(part, 0, block), :] - 2.0 * slope * d_curve - 2.0 * act * d_slope
            d_pre = slope * d_act
            high, low = halves(d_pre)
            first_high[here, :] = high
            first_low[here, :] = low
            sums = (
                [sums[0] + folded(d_pre)]
                + [sums[1 + d] + folded(where[:, d : d + 1] * d_pre + slope * cot_t[d]) for d in range(3)]
                + [sums[4] + folded(curve * cot_l)]
            )
        return sums

    @pl.when(always)
    def _():
        out_back(0)
        total = second_back(0, jnp.zeros((8, hidden), F32))
        out_back(1)
        sums_ref[5] = second_back(1, total)

    @pl.when(always)
    def _():
        times_mid(NT, (d_high, d_low), mixed_back, 0)
        total = first_back(0, [jnp.zeros((8, hidden), F32)] * 5)
        times_mid(NT, (d_high, d_low), mixed_back, 1)
        for number, value in enumerate(first_back(1, total)):
            sums_ref[number] = value

    def put(part, first, value):
        while value.shape[0]:
            block, row = first // plan.main_rows, first % plan.main_rows
            count = min(value.shape[0], plan.main_rows - row)
            packed[2 * part + block, row : row + count, :] = value[:count]
            first, value = first + count, value[count:]

    wide = 2 * LANES
    for left in range(hidden // wide):
        for right in range(hidden // wide):
            lefts = slice(left * wide, (left + 1) * wide)
            rights = slice(right * wide, (right + 1) * wide)
            part = mul3(
                (one_high[:, lefts], one_low[:, lefts]), (d_high[:, rights], d_low[:, rights]), TN
            )
            for side in range(2):
                put(2 * right + side, left * wide, part[:, side * LANES : (side + 1) * LANES])

    sums = [sums_ref[number] for number in range(6)]
    d_square = jnp.sum(sums[4], axis=0, keepdims=True)
    grad_latent = mul(code[...], first_high[...], TN) + mul(code[...], first_low[...], TN)

    parts = [d_out_t[8 * s : 8 * s + 8, p * part_rows : (p + 1) * part_rows] for p in range(2) for s in range(5)]
    flat = jnp.concatenate(parts, axis=1)
    fl_high, fl_low = halves(flat)
    fl_both = jnp.concatenate([flat, fl_low.astype(F32)], axis=0).astype(BF16)
    grad_out = mul(fl_both, two_high[...])
    grad_out = grad_out[:8] + grad_out[8:] + mul(fl_high, two_low[...])

    lane_row = lax.broadcasted_iota(jnp.int32, (1, hidden), 1)
    last = jnp.where(lane_row == 5, jnp.sum(point_loss), 0.0)
    for f in range(5):
        last = last + jnp.where(lane_row == f, jnp.sum(d_value[f]), 0.0)
    grad_pos = [jnp.sum(sums[1 + d], axis=0, keepdims=True) + 2.0 * w_pos[d] * d_square for d in range(3)]
    misc = grad_pos + [
        jnp.sum(sums[0], axis=0, keepdims=True),
        jnp.sum(sums[5], axis=0, keepdims=True),
        last,
    ]
    misc = jnp.concatenate(misc + [jnp.zeros((2, hidden), F32)], axis=0)
    for part in range(hidden // LANES):
        lanes = slice(part * LANES, (part + 1) * LANES)
        put(part, hidden, grad_latent[:, lanes])
        packed[2 * part, plan.coded_rows :, :] = misc[:, lanes]
        packed[2 * part + 1, plan.coded_rows :, :] = grad_out[:, lanes]

    chosen = jnp.where(
        lane == jnp.broadcast_to(words[:, 10:11], (rows, LANES)).astype(jnp.int32), words[:, 9:10], 0.0
    ).astype(BF16)
    fields = jnp.concatenate(value + [jnp.zeros((3, rows), F32)], axis=0)
    source = (lax.broadcasted_iota(jnp.int32, (8, rows), 1) & (plan.tiles * 8 - 1)) >> 3
    spread = jnp.concatenate([jnp.where(source == t, fields, 0.0) for t in range(plan.tiles)], axis=0)
    high, middle, low = thirds(spread)
    spread = mul(high, chosen) + mul(middle, chosen) + mul(low, chosen)
    packed[:, plan.main_rows : plan.coded_rows, :] = jnp.zeros((8, plan.devices, LANES), F32)
    for t in range(plan.tiles):
        row = plan.main_rows + (my_replica * (plan.tiles // 8) + t // 8) * 8
        packed[t % 8, pl.ds(pl.multiple_of(row, 8), 8), :] = spread[8 * t : 8 * t + 8]

    for block in range(8):
        spot = jnp.bitwise_xor(block, my_block) & 3

        @pl.when((my_block >> 2) == block // 4)
        def _():
            keep_ref[spot] = packed[block]

        @pl.when((my_block >> 2) != block // 4)
        def _():
            send_ref[spot] = packed[block]


class Plan:
    def __init__(self, tiles, replicas, queries, planes, hidden, latents):
        self.tiles, self.replicas, self.planes = tiles, replicas, planes
        self.slots = 2 * queries // tiles
        self.devices = tiles * replicas
        self.query_total = float(queries * self.devices)
        self.main_rows = (hidden + latents) // 2
        self.coded_rows = self.main_rows + self.devices
        self.rows = self.coded_rows + 8
        self.scales = -(-(self.coded_rows // SUB + 1) // 16) * 16
        self.sent_rows = self.coded_rows + 16 + self.scales
        top = self.devices.bit_length() - 1
        self.core, self.plane, self.rest = [0], [1, top - 1], list(range(2, top - 1))

    def mask(self, bits, steps):
        return sum(1 << bit for number, bit in enumerate(bits) if steps >> number & 1)

    def my_block(self, device):
        return (device & 1) * 4 + (device >> 1 & 1) + 2 * (device >> self.plane[1] & 1)


def swapped(value, plan, bits, steps):
    mask = plan.mask(bits, steps)
    return lax.ppermute(value, ("replica", "tile"), [(i, i ^ mask) for i in range(plan.devices)])


def encode(plan, read, out_ref):
    starts = list(range(0, plan.coded_rows, SUB))
    parts = [read(start, SUB) for start in starts] + [read(plan.coded_rows, 8)]
    tops = [jnp.max(jnp.abs(part), axis=0, keepdims=True) for part in parts]
    tops = tops + [jnp.zeros_like(tops[0])] * (plan.scales - len(tops))
    power = jnp.floor(jnp.log2(jnp.maximum(jnp.concatenate(tops, axis=0), 1e-30)))
    scale = jnp.exp2(14.0 - power)

    def whole(value):
        return jnp.clip(jnp.round(value), -32767.0, 32767.0)

    def narrow(value):
        return value.astype(jnp.int32).astype(jnp.int16)

    for number, start in enumerate(starts):
        out_ref[start : start + SUB, :] = narrow(whole(parts[number] * scale[number : number + 1]))
    last = len(starts)
    exact = parts[last] * scale[last : last + 1]
    high = whole(exact)
    low = whole((exact - high) * 32768.0)
    out_ref[plan.coded_rows : plan.coded_rows + 16, :] = narrow(jnp.concatenate([high, low], axis=0))
    out_ref[plan.coded_rows + 16 :, :] = narrow(power)


def decoder(plan, ref):
    def widen(value):
        return value.astype(jnp.int32).astype(F32)

    scale = jnp.exp2(widen(ref[plan.coded_rows + 16 :, :]) - 14.0)

    def read(start, count):
        if start < plan.coded_rows:
            number = start // SUB
            return widen(ref[start : start + count, :]) * scale[number : number + 1]
        both = widen(ref[plan.coded_rows : plan.coded_rows + 16, :])
        number = plan.coded_rows // SUB
        return (both[:8] + both[8:] * (1.0 / 32768.0)) * scale[number : number + 1]

    return read


def added(readers):
    def read(start, count):
        total = readers[0](start, count)
        for reader in readers[1:]:
            total = total + reader(start, count)
        return total

    return read


def first_kernel(plan, keep_ref, got_ref, mine_ref, *out_refs):
    def reader(block):
        return lambda start, count: (
            keep_ref[block, start : start + count, :] + got_ref[block, start : start + count, :]
        )

    for number, out_ref in enumerate(out_refs):
        encode(plan, reader(number + 1), out_ref)
    mine_ref[...] = keep_ref[0] + got_ref[0]


def first_sum(keep, got, plan):
    sent = jax.ShapeDtypeStruct((plan.sent_rows, LANES), jnp.int16)
    return pl.pallas_call(
        functools.partial(first_kernel, plan),
        out_shape=(jax.ShapeDtypeStruct(keep.shape[1:], F32), sent, sent, sent),
        in_specs=[VMEM] * 2,
        out_specs=tuple([VMEM] * 4),
        compiler_params=pltpu.CompilerParams(vmem_limit_bytes=6 << 20),
        name="sum_core",
    )(keep, got)


def plane_kernel(plan, mine_ref, *refs):
    readers = [lambda start, count: mine_ref[start : start + count, :]]
    encode(plan, added(readers + [decoder(plan, ref) for ref in refs[:-1]]), refs[-1])


def pair_kernel(plan, mine_ref, other_ref, out_ref):
    encode(plan, added([decoder(plan, mine_ref), decoder(plan, other_ref)]), out_ref)


def coded_sum(kernel, blocks, plan, name):
    return pl.pallas_call(
        functools.partial(kernel, plan),
        out_shape=jax.ShapeDtypeStruct((plan.sent_rows, LANES), jnp.int16),
        in_specs=[VMEM] * len(blocks),
        out_specs=VMEM,
        compiler_params=pltpu.CompilerParams(vmem_limit_bytes=4 << 20),
        name=name,
    )(*blocks)


def main(place, lat, words, weights, plan):
    rows = plan.tiles * plan.slots
    hidden = weights[3].shape[0]
    channels = lat.shape[1]
    outs = jax.ShapeDtypeStruct((4, plan.rows, LANES), F32)
    wide = lambda kind: pltpu.VMEM((5 * rows, hidden), kind)
    return pl.pallas_call(
        functools.partial(main_kernel, plan),
        out_shape=(outs, outs),
        in_specs=[SMEM] + [VMEM] * 2 + [HBM] * 7,
        out_specs=(VMEM, VMEM),
        scratch_shapes=[
            pltpu.VMEM((rows, channels), BF16),
            pltpu.VMEM((rows, LANES), F32),
            pltpu.VMEM((rows, hidden), F32),
            wide(BF16),
            wide(BF16),
            wide(F32),
            wide(BF16),
            wide(BF16),
            wide(F32),
            wide(F32),
            pltpu.VMEM((rows, hidden), BF16),
            pltpu.VMEM((rows, hidden), BF16),
            pltpu.VMEM((6, 8, hidden), F32),
            wide(BF16),
            wide(BF16),
            pltpu.VMEM((40, rows), F32),
            pltpu.VMEM((40, rows), F32),
            pltpu.VMEM((8, plan.rows, LANES), F32),
            pltpu.VMEM((hidden, hidden), BF16),
            pltpu.VMEM((hidden, hidden), BF16),
        ]
        + [pltpu.VMEM(weight.shape, F32) for weight in weights]
        + [pltpu.SemaphoreType.DMA((7,))],
        compiler_params=pltpu.CompilerParams(vmem_limit_bytes=32 << 20),
        name="encode_decode",
    )(place, lat, words, *weights)


def unpack_kernel(plan, place_ref, *refs):
    sources, outs, packed = refs[:8], refs[8:-1], refs[-1]
    prediction_ref, latent_ref, pos_ref, one_ref, mid_ref, two_ref, out_ref, bias_out_ref, loss_ref = outs
    my_block = place_ref[0]
    device = place_ref[2] * plan.tiles + place_ref[1]
    starts = list(range(0, plan.coded_rows, SUB))
    for number, ref in enumerate(sources):
        read = decoder(plan, ref)
        block = jnp.bitwise_xor(number, my_block)
        for start in starts:
            packed[block, start : start + SUB, :] = read(start, SUB)
        packed[block, plan.coded_rows :, :] = read(plan.coded_rows, 8)

    hidden = mid_ref.shape[0]
    latents = latent_ref.shape[0]
    split = plan.main_rows
    for part in range(hidden // LANES):
        lanes = slice(part * LANES, (part + 1) * LANES)
        mid_ref[0:split, lanes] = packed[2 * part, 0:split, :]
        mid_ref[split:, lanes] = packed[2 * part + 1, 0 : hidden - split, :]
        latent_ref[:, lanes] = packed[2 * part + 1, hidden - split : split, :]
        misc = packed[2 * part, plan.coded_rows :, :]
        pos_ref[:, lanes] = misc[0:3]
        one_ref[:, lanes] = misc[3:4]
        two_ref[:, lanes] = misc[4:5]
        out_ref[:, lanes] = packed[2 * part + 1, plan.coded_rows : plan.coded_rows + 5, :]
        if part == 0:
            bias_out_ref[...] = misc[5:6, 0:5]
            loss_ref[...] = misc[5:6, 5:6]
    row = pl.multiple_of(plan.main_rows + (device >> 3) * 8, 8)
    fields = packed[device & 7, pl.ds(row, 8), :]
    for f in range(5):
        prediction_ref[f] = fields[f : f + 1]


def unpack(place, blocks, plan, hidden, latents):
    shapes = [
        (5, 1, LANES),
        (latents, hidden),
        (3, hidden),
        (1, hidden),
        (hidden, hidden),
        (1, hidden),
        (5, hidden),
        (1, 5),
        (1, 1),
    ]
    return pl.pallas_call(
        functools.partial(unpack_kernel, plan),
        out_shape=tuple(jax.ShapeDtypeStruct(shape, F32) for shape in shapes),
        in_specs=[SMEM] + [VMEM] * 8,
        out_specs=tuple([VMEM] * len(shapes)),
        scratch_shapes=[pltpu.VMEM((8, plan.rows, LANES), F32)],
        compiler_params=pltpu.CompilerParams(vmem_limit_bytes=16 << 20),
        name="unpack",
    )(place, *blocks)


def body(
    fields,
    convolution_weight,
    convolution_bias,
    query_owner,
    query_cell,
    query_frac,
    target,
    w_latent,
    w_pos,
    bias_one,
    w_mid,
    bias_two,
    w_out,
    bias_out,
):
    tiles = lax.axis_size("tile")
    replicas = lax.axis_size("replica")
    my_tile = lax.axis_index("tile")
    my_replica = lax.axis_index("replica")
    channels = fields.shape[1]
    queries = query_cell.shape[1]
    hidden = w_mid.shape[0]
    plan = Plan(tiles, replicas, queries, fields.shape[2], hidden, channels)
    device = my_replica * tiles + my_tile
    place = jnp.stack([plan.my_block(device), my_tile, my_replica]).astype(jnp.int32)

    here = fields[0].transpose(1, 2, 0, 3)
    up = [(i, (i + 1) % tiles) for i in range(tiles)]
    down = [((i + 1) % tiles, i) for i in range(tiles)]
    to_left, to_right, query_owner = lax.optimization_barrier(
        (here[: DILATION_RATE + 1], here[-DILATION_RATE:], query_owner)
    )
    taps = convolution_weight.reshape(channels, 3, 3, 3, channels)
    taps = taps.transpose(1, 3, 0, 2, 4).reshape(3, 3 * channels, 3 * channels)
    right = lax.ppermute(to_left, "tile", down)
    left = lax.ppermute(to_right, "tile", up)
    words = route(
        query_owner[:, :, 0],
        query_cell,
        query_frac.transpose(1, 0, 2),
        target.transpose(1, 0, 2),
        tiles,
        plan.slots,
    )
    words = lax.all_to_all(
        words.reshape(tiles, 8, WORDS), "tile", split_axis=0, concat_axis=0, tiled=True
    ).reshape(tiles * 8, WORDS)

    lat = convolve(left, here, right, taps, convolution_bias[:, None])
    weights = (w_latent, w_pos, bias_one[None], w_mid, bias_two[None], w_out, bias_out[None])
    send, keep = main(place, lat, words, weights, plan)

    mine, *others = first_sum(keep, swapped(send, plan, plan.core, 1), plan)
    arrived = [swapped(block, plan, plan.plane, step + 1) for step, block in enumerate(others)]
    block = coded_sum(plane_kernel, [mine] + arrived, plan, "sum_plane")
    for bit in plan.rest:
        block = coded_sum(pair_kernel, [block, swapped(block, plan, [bit], 1)], plan, "sum_line")
    blocks = [block] + [swapped(block, plan, plan.plane, step) for step in range(1, 4)]
    blocks = blocks + [swapped(block, plan, plan.core, 1) for block in blocks]
    prediction, g_latent, g_pos, g_one, g_mid, g_two, g_out, g_bias, loss = unpack(
        place, blocks, plan, hidden, channels
    )
    return (
        prediction.transpose(1, 0, 2),
        g_latent,
        g_pos,
        g_one.reshape(hidden),
        g_mid,
        g_two.reshape(hidden),
        g_out,
        g_bias.reshape(5),
        loss.reshape(()),
    )


def solution(mesh):
    return jax.shard_map(
        body,
        mesh=mesh,
        in_specs=(
            P("replica", None, "tile", None, None),
            P(),
            P(),
            P("replica", "tile", None),
            P("replica", "tile"),
            P("replica", None, "tile"),
            P("replica", None, "tile"),
            P(),
            P(),
            P(),
            P(),
            P(),
            P(),
            P(),
        ),
        out_specs=(P("replica", None, "tile"), P(), P(), P(), P(), P(), P(), P(), P()),
        check_vma=False,
    )
```

```python
import functools

import jax
import jax.numpy as jnp
from jax import lax
from jax.experimental import pallas as pl
from jax.experimental.pallas import tpu as pltpu
from jax.sharding import PartitionSpec as P

DILATION_RATE = 2
VISCOSITY = 0.05
DIFFUSIVITY = 0.05
RESIDUAL_WEIGHT = 0.5

F32 = jnp.float32
BF16 = jnp.bfloat16
LANES = 128
BLOCK = 32
WORDS = 128
SUB = 32
NN = (((1,), (0,)), ((), ()))
NT = (((1,), (1,)), ((), ()))
TN = (((0,), (0,)), ((), ()))
VMEM = pl.BlockSpec(memory_space=pltpu.VMEM)
SMEM = pl.BlockSpec(memory_space=pltpu.SMEM)
HBM = pl.BlockSpec(memory_space=pltpu.HBM)


def mul(left, right, dims=NN):
    return lax.dot_general(left, right, dims, preferred_element_type=F32)


def halves(value):
    high = value.astype(BF16)
    return high, (value - high.astype(F32)).astype(BF16)


def thirds(value):
    high = value.astype(BF16)
    rest = value - high.astype(F32)
    middle = rest.astype(BF16)
    return high, middle, (rest - middle.astype(F32)).astype(BF16)


def mul3(left, right, dims=NN):
    return mul(left[0], right[0], dims) + mul(left[0], right[1], dims) + mul(left[1], right[0], dims)


def fetches(sources, targets, sems):
    copies = [
        pltpu.make_async_copy(source, target, sems.at[number])
        for number, (source, target) in enumerate(zip(sources, targets))
    ]
    for copy in copies:
        copy.start()
    return copies


def route_kernel(tiles, slots, *refs):
    out_ref, owner_ref, cell_ref, frac_ref, target_ref, words, sems = refs[4:]
    queries = owner_ref.shape[1]
    for copy in fetches(refs[:4], (owner_ref, cell_ref, frac_ref, target_ref), sems):
        copy.wait()
    owner = owner_ref[...]
    hits = (lax.broadcasted_iota(jnp.int32, (tiles, queries), 0) == owner).astype(F32)
    before = lax.broadcasted_iota(jnp.int32, (queries, queries), 0) < lax.broadcasted_iota(
        jnp.int32, (queries, queries), 1
    )
    earlier = mul(hits.astype(BF16), before.astype(F32).astype(BF16))
    slot = jnp.sum(hits * earlier, axis=0, keepdims=True)
    place = owner * slots + slot.astype(jnp.int32)
    spot = lax.broadcasted_iota(jnp.int32, (tiles * 8, queries), 0)
    spot = (spot >> 3) * slots + (spot & 7)
    groups = slots // 8
    chosen = [jnp.where(spot + 8 * group == place, 1.0, 0.0) for group in range(groups)]
    chosen = jnp.concatenate(chosen, axis=1).astype(BF16)
    words[...] = jnp.zeros_like(words)
    for group in range(groups):
        row, lanes = 16 * group, slice(group * queries, (group + 1) * queries)
        words[row : row + 1, lanes] = cell_ref[...].astype(F32)
        for d in range(3):
            words[row + 1 + d : row + 2 + d, lanes] = frac_ref[d]
        for f in range(5):
            words[row + 4 + f : row + 5 + f, lanes] = target_ref[f]
        words[row + 9 : row + 10, lanes] = jnp.ones((1, queries), F32)
        words[row + 10 : row + 11, lanes] = lax.broadcasted_iota(jnp.int32, (1, queries), 1).astype(F32)
    high, middle, low = thirds(words[...])
    out_ref[...] = mul(chosen, high, NT) + mul(chosen, middle, NT) + mul(chosen, low, NT)


def route(owner, cell, frac, target, tiles, slots):
    queries = owner.shape[1]
    return pl.pallas_call(
        functools.partial(route_kernel, tiles, slots),
        out_shape=jax.ShapeDtypeStruct((tiles * 8, WORDS), F32),
        in_specs=[HBM] * 4,
        out_specs=VMEM,
        scratch_shapes=[
            pltpu.VMEM(owner.shape, owner.dtype),
            pltpu.VMEM(cell.shape, cell.dtype),
            pltpu.VMEM(frac.shape, F32),
            pltpu.VMEM(target.shape, F32),
            pltpu.VMEM((WORDS, queries * (slots // 8)), F32),
            pltpu.SemaphoreType.DMA((4,)),
        ],
        compiler_params=pltpu.CompilerParams(vmem_limit_bytes=4 << 20),
        name="route",
    )(owner, cell, frac, target)


def tap_sum(weight_ref, planes, pair):
    total = None
    for step_x, ref, index in planes:
        rows_y = ref.shape[1]
        blocks = [
            jnp.concatenate([ref[index, (2 * pair + half + step_y) % rows_y] for half in (0, 1)], axis=1)
            for step_y in (-1, 0, 1)
        ]
        term = mul(weight_ref[step_x], jnp.concatenate(blocks, axis=0))
        total = term if total is None else total + term
    channels = total.shape[0] // 3
    sides = []
    for half in (0, 1):
        part = total[:, half * LANES : (half + 1) * LANES]
        sides.append(
            part[channels : 2 * channels]
            + pltpu.roll(part[:channels], 1, 1)
            + pltpu.roll(part[2 * channels :], LANES - 1, 1)
        )
    return jnp.concatenate(sides, axis=1)


def conv_kernel(
    left_ref,
    here_ref,
    right_ref,
    taps_ref,
    bias_ref,
    bias_one_ref,
    bias_two_ref,
    bias_out_ref,
    lat_ref,
    small_ref,
    weight_ref,
):
    planes, rows_y, channels = here_ref.shape[:3]
    taps = taps_ref[...].astype(F32)
    for step in range(3):
        rows = []
        for step_z in range(3):
            numbers = [9 * step + 3 * step_y + step_z for step_y in range(3)]
            rows.append(
                jnp.concatenate([taps[:, n * channels : (n + 1) * channels] for n in numbers], axis=1)
            )
        weight_ref[step] = jnp.concatenate(rows, axis=0).astype(BF16)
    diagonal = lax.broadcasted_iota(jnp.int32, (channels, channels), 0) == lax.broadcasted_iota(
        jnp.int32, (channels, channels), 1
    )
    bias = jnp.sum(jnp.where(diagonal, bias_ref[...], 0.0), axis=1, keepdims=True)
    small_ref[...] = jnp.zeros_like(small_ref)
    small_ref[0:1, :] = bias_one_ref[...]
    small_ref[1:2, :] = bias_two_ref[...]
    small_ref[2:3, 0:5] = bias_out_ref[...]
    for x in range(planes + 1):
        taps = []
        for step in range(3):
            plane = x + DILATION_RATE * (step - 1)
            if plane < 0:
                taps.append((step, left_ref, plane + left_ref.shape[0]))
            elif plane >= planes:
                taps.append((step, right_ref, plane - planes))
            else:
                taps.append((step, here_ref, plane))
        for pair in range(rows_y // 2):
            summed = tap_sum(weight_ref, taps, pair) + bias
            lat_ref[x * (rows_y // 2) + pair] = jax.nn.gelu(summed).astype(BF16)


def convolve(left, here, right, taps, conv_bias, biases):
    planes, rows_y, channels, rows_z = here.shape
    pairs = (planes + 1) * rows_y // 2
    return pl.pallas_call(
        conv_kernel,
        out_shape=(
            jax.ShapeDtypeStruct((pairs, channels, 2 * rows_z), BF16),
            jax.ShapeDtypeStruct((8, biases[0].shape[1]), F32),
        ),
        in_specs=[VMEM] * 8,
        out_specs=(VMEM, VMEM),
        scratch_shapes=[pltpu.VMEM((3, 3 * channels, 3 * channels), BF16)],
        compiler_params=pltpu.CompilerParams(vmem_limit_bytes=8 << 20),
        cost_estimate=pl.CostEstimate(flops=3 << 30, bytes_accessed=4 << 20, transcendentals=0),
        name="convolve",
    )(left, here, right, taps, conv_bias, *biases)


def interpolate(words, lat, planes, rows_y, rows_z):
    rows = words.shape[0]
    cell = jnp.broadcast_to(words[:, 0:1], (rows, LANES)).astype(jnp.int32)
    frac = [jnp.broadcast_to(words[:, 1 + d : 2 + d], (rows, LANES)) for d in range(3)]
    shift_z = rows_z.bit_length() - 1
    shift_y = rows_y.bit_length() - 1
    base_x = cell >> (shift_z + shift_y)
    base_y = (cell >> shift_z) & (rows_y - 1)
    base_z = cell & (rows_z - 1)
    spot = lax.broadcasted_iota(jnp.int32, (rows, rows_z), 1)
    part_z = jnp.where(spot == base_z, 1.0 - frac[2], 0.0) + jnp.where(
        spot == ((base_z + 1) & (rows_z - 1)), frac[2], 0.0
    )
    part_yz = []
    for y in range(rows_y):
        part_y = jnp.where(
            base_y == y, 1.0 - frac[1], jnp.where(base_y == (y - 1) % rows_y, frac[1], 0.0)
        )
        part_yz.append(part_y * part_z)
    total = None
    for x in range(planes + 1):
        part_x = jnp.where(base_x == x, 1.0 - frac[0], jnp.where(base_x == x - 1, frac[0], 0.0))
        for pair in range(rows_y // 2):
            sides = [(part_x * part_yz[2 * pair + half]).astype(BF16) for half in (0, 1)]
            term = mul(jnp.concatenate(sides, axis=1), lat[x * (rows_y // 2) + pair], NT)
            total = term if total is None else total + term
    return total.astype(BF16), base_x, base_y, base_z, frac


def folded(value):
    return jnp.sum(value.reshape(value.shape[0] // 8, 8, value.shape[1]), axis=0)


def main_kernel(
    plan,
    place_ref,
    lat,
    words_ref,
    small_ref,
    w_latent_hbm,
    w_pos_hbm,
    w_mid_hbm,
    w_out_hbm,
    send_ref,
    keep_ref,
    code,
    pos,
    z_one,
    one_high,
    one_low,
    mixed,
    two_high,
    two_low,
    back,
    mixed_back,
    first_high,
    first_low,
    sums_ref,
    d_high,
    d_low,
    out_t,
    d_out_t,
    packed,
    mid_high,
    mid_low,
    w_latent_ref,
    w_pos_ref,
    w_mid_ref,
    w_out_ref,
    sems,
):
    rows = plan.tiles * plan.slots
    hidden = w_mid_ref.shape[0]
    latents = w_latent_ref.shape[0]
    weights = fetches(
        (w_latent_hbm, w_pos_hbm, w_mid_hbm, w_out_hbm),
        (w_latent_ref, w_pos_ref, w_mid_ref, w_out_ref),
        sems,
    )
    planes, rows_z = plan.planes, lat.shape[2] // 2
    rows_y = lat.shape[0] // (planes + 1) * 2
    slots = rows // plan.tiles
    my_block = place_ref[0]
    my_tile = place_ref[1]
    my_replica = place_ref[2]
    always = my_tile >= 0

    words = words_ref[...]
    words = jnp.concatenate(
        [words] + [pltpu.roll(words, LANES - 16 * group, 1) for group in range(1, slots // 8)], axis=0
    )
    interp, base_x, base_y, base_z, frac = interpolate(words, lat, planes, rows_y, rows_z)
    code[...] = interp
    global_x = my_tile * planes + base_x
    lane = lax.broadcasted_iota(jnp.int32, (rows, LANES), 1)
    pos[...] = jnp.where(
        lane == 0,
        (global_x.astype(F32) + frac[0]) / (planes * plan.tiles),
        jnp.where(
            lane == 1,
            (base_y.astype(F32) + frac[1]) / rows_y,
            (base_z.astype(F32) + frac[2]) / rows_z,
        ),
    )

    for copy in weights:
        copy.wait()
    high, low = halves(w_latent_ref[...])
    z_one[...] = mul(interp, high) + mul(interp, low)
    high, low = halves(w_mid_ref[...])
    mid_high[...] = high
    mid_low[...] = low
    w_pos = [w_pos_ref[d : d + 1, :] for d in range(3)]
    square = w_pos[0] * w_pos[0] + w_pos[1] * w_pos[1] + w_pos[2] * w_pos[2]
    bias_one = small_ref[0:1, :]
    bias_two = small_ref[1:2, :]

    part_rows = rows // 2

    def at(part, index, block=None):
        first = (part * 5 + index) * part_rows
        if block is None:
            return slice(first, first + part_rows)
        return slice(first + block * BLOCK, first + (block + 1) * BLOCK)

    def rows_at(part, block):
        first = part * part_rows + block * BLOCK
        return slice(first, first + BLOCK)

    def store(refs, span, value):
        high, low = halves(value)
        refs[0][span, :] = high
        refs[1][span, :] = low

    def layer_one(part):
        refs = (one_high, one_low)
        for block in range(part_rows // BLOCK):
            here = rows_at(part, block)
            where = pos[here, :]
            pre = (
                z_one[here, :]
                + (where[:, 0:1] * w_pos[0] + where[:, 1:2] * w_pos[1] + where[:, 2:3] * w_pos[2])
                + bias_one
            )
            act = jnp.tanh(pre)
            slope = 1.0 - act * act
            curve = -2.0 * act * slope
            z_one[here, :] = act
            store(refs, at(part, 0, block), act)
            for d in range(3):
                store(refs, at(part, 1 + d, block), slope * w_pos[d])
            store(refs, at(part, 4, block), curve * square)

    def times_mid(dims, source, result, part):
        for index in range(5):
            span = at(part, index)
            left = (source[0][span, :], source[1][span, :])
            result[span, :] = mul3(left, (mid_high[...], mid_low[...]), dims)

    def layer_two(part):
        refs = (two_high, two_low)
        for block in range(part_rows // BLOCK):
            act = jnp.tanh(mixed[at(part, 0, block), :] + bias_two)
            slope = 1.0 - act * act
            curve = -2.0 * act * slope
            store(refs, at(part, 0, block), act)
            mixed[at(part, 0, block), :] = act
            norm = None
            for d in range(3):
                tangent = mixed[at(part, 1 + d, block), :]
                store(refs, at(part, 1 + d, block), slope * tangent)
                norm = tangent * tangent if norm is None else norm + tangent * tangent
            store(refs, at(part, 4, block), slope * mixed[at(part, 4, block), :] + curve * norm)

    out_fields = jnp.concatenate([w_out_ref[...], jnp.zeros((3, hidden), F32)], axis=0)
    wo_high, wo_low = halves(out_fields)
    wo_three = jnp.concatenate([out_fields, wo_low.astype(F32), out_fields], axis=0).astype(BF16)
    wo_both = jnp.concatenate([out_fields, wo_low.astype(F32)], axis=0).astype(BF16)

    def outputs(part):
        for s in range(5):
            span = at(part, s)
            both = mul(wo_both, two_high[span, :], NT)
            both = both[:8] + both[8:] + mul(wo_high, two_low[span, :], NT)
            out_t[8 * s : 8 * s + 8, part * part_rows : (part + 1) * part_rows] = both

    @pl.when(always)
    def _():
        layer_one(0)
        times_mid(NN, (one_high, one_low), mixed, 0)
        layer_one(1)
        times_mid(NN, (one_high, one_low), mixed, 1)
        layer_two(0)
        outputs(0)
        layer_two(1)
        outputs(1)

    words_t = words.T
    target = [words_t[4 + f : 5 + f, :] for f in range(5)]
    valid = words_t[9:10, :]
    value = [out_t[f : f + 1, :] + small_ref[2:3, f : f + 1] for f in range(5)]
    grad = [[out_t[8 * (d + 1) + f : 8 * (d + 1) + f + 1, :] for f in range(5)] for d in range(3)]
    laplace = [out_t[32 + f : 33 + f, :] for f in range(5)]
    velocity = value[2:5]
    advection = [
        velocity[0] * grad[0][f] + velocity[1] * grad[1][f] + velocity[2] * grad[2][f] for f in range(5)
    ]
    continuity = grad[0][2] + grad[1][3] + grad[2][4]
    momentum = [advection[2 + j] + grad[j][1] - VISCOSITY * laplace[2 + j] for j in range(3)]
    momentum[2] = momentum[2] - value[0]
    energy = advection[0] - DIFFUSIVITY * laplace[0]
    misfit = [value[f] - target[f] for f in range(5)]
    physics = (
        continuity * continuity
        + (momentum[0] * momentum[0] + momentum[1] * momentum[1] + momentum[2] * momentum[2])
        + energy * energy
    )
    squares = (
        misfit[0] * misfit[0]
        + misfit[1] * misfit[1]
        + misfit[2] * misfit[2]
        + misfit[3] * misfit[3]
        + misfit[4] * misfit[4]
    )
    point_loss = valid * (squares + RESIDUAL_WEIGHT * physics) * (1.0 / plan.query_total)

    rate = valid * (1.0 / plan.query_total)
    twice = RESIDUAL_WEIGHT * 2.0
    d_cont = rate * twice * continuity
    d_mom = [rate * twice * m for m in momentum]
    d_energy = rate * twice * energy
    d_value = [2.0 * rate * m for m in misfit]
    for d in range(3):
        d_value[2 + d] = d_value[2 + d] + (
            d_mom[0] * grad[d][2] + d_mom[1] * grad[d][3] + d_mom[2] * grad[d][4] + d_energy * grad[d][0]
        )
    d_value[0] = d_value[0] - d_mom[2]
    d_out_t[...] = jnp.zeros_like(d_out_t)
    for f in range(5):
        d_out_t[f : f + 1, :] = d_value[f]
    for d in range(3):
        first = 8 * (d + 1)
        d_out_t[first : first + 1, :] = d_energy * velocity[d]
        d_out_t[first + 1 : first + 2, :] = d_mom[d]
        for j in range(3):
            term = d_mom[j] * velocity[d]
            if j == d:
                term = term + d_cont
            d_out_t[first + 2 + j : first + 3 + j, :] = term
    d_out_t[32:33, :] = -DIFFUSIVITY * d_energy
    for j in range(3):
        d_out_t[34 + j : 35 + j, :] = -VISCOSITY * d_mom[j]

    def out_back(part):
        for s in range(5):
            wanted = d_out_t[8 * s : 8 * s + 8, part * part_rows : (part + 1) * part_rows]
            do_low = halves(wanted)[1].astype(F32)
            wanted = jnp.concatenate([wanted, wanted, do_low], axis=0).astype(BF16)
            back[at(part, s), :] = mul(wanted, wo_three, TN)

    def second_back(part, total):
        refs = (d_high, d_low)
        for block in range(part_rows // BLOCK):
            act = mixed[at(part, 0, block), :]
            slope = 1.0 - act * act
            curve = -2.0 * act * slope
            cot_l = back[at(part, 4, block), :]
            d_slope = cot_l * mixed[at(part, 4, block), :]
            norm = None
            bent = 2.0 * curve * cot_l
            for d in range(3):
                tangent = mixed[at(part, 1 + d, block), :]
                cot_t = back[at(part, 1 + d, block), :]
                store(refs, at(part, 1 + d, block), slope * cot_t + bent * tangent)
                d_slope = d_slope + cot_t * tangent
                norm = tangent * tangent if norm is None else norm + tangent * tangent
            store(refs, at(part, 4, block), slope * cot_l)
            d_curve = cot_l * norm
            d_slope = d_slope - 2.0 * act * d_curve
            d_act = back[at(part, 0, block), :] - 2.0 * slope * d_curve - 2.0 * act * d_slope
            d_pre = slope * d_act
            store(refs, at(part, 0, block), d_pre)
            total = total + folded(d_pre)
        return total

    def first_back(part, sums):
        for block in range(part_rows // BLOCK):
            here = rows_at(part, block)
            act = z_one[here, :]
            slope = 1.0 - act * act
            curve = -2.0 * act * slope
            where = pos[here, :]
            cot_t = [mixed_back[at(part, 1 + d, block), :] for d in range(3)]
            cot_l = mixed_back[at(part, 4, block), :]
            d_curve = cot_l * square
            d_slope = cot_t[0] * w_pos[0] + cot_t[1] * w_pos[1] + cot_t[2] * w_pos[2] - 2.0 * act * d_curve
            d_act = mixed_back[at(part, 0, block), :] - 2.0 * slope * d_curve - 2.0 * act * d_slope
            d_pre = slope * d_act
            high, low = halves(d_pre)
            first_high[here, :] = high
            first_low[here, :] = low
            sums = (
                [sums[0] + folded(d_pre)]
                + [sums[1 + d] + folded(where[:, d : d + 1] * d_pre + slope * cot_t[d]) for d in range(3)]
                + [sums[4] + folded(curve * cot_l)]
            )
        return sums


    def put(part, first, value):
        while value.shape[0]:
            block, row = first // plan.main_rows, first % plan.main_rows
            count = min(value.shape[0], plan.main_rows - row)
            packed[2 * part + block, row : row + count, :] = value[:count]
            first, value = first + count, value[count:]

    wide = 2 * LANES
    def mid_gradient():
        for left in range(hidden // wide):
            for right in range(hidden // wide):
                lefts = slice(left * wide, (left + 1) * wide)
                rights = slice(right * wide, (right + 1) * wide)
                part = mul3(
                    (one_high[:, lefts], one_low[:, lefts]), (d_high[:, rights], d_low[:, rights]), TN
                )
                for side in range(2):
                    put(2 * right + side, left * wide, part[:, side * LANES : (side + 1) * LANES])

    @pl.when(always)
    def _():
        out_back(0)
        total = second_back(0, jnp.zeros((8, hidden), F32))
        out_back(1)
        times_mid(NT, (d_high, d_low), mixed_back, 0)
        sums_ref[5] = second_back(1, total)
        times_mid(NT, (d_high, d_low), mixed_back, 1)
        total = first_back(0, [jnp.zeros((8, hidden), F32)] * 5)
        mid_gradient()
        for number, value in enumerate(first_back(1, total)):
            sums_ref[number] = value

    sums = [sums_ref[number] for number in range(6)]
    d_square = jnp.sum(sums[4], axis=0, keepdims=True)
    grad_latent = mul(code[...], first_high[...], TN) + mul(code[...], first_low[...], TN)

    parts = [d_out_t[8 * s : 8 * s + 8, p * part_rows : (p + 1) * part_rows] for p in range(2) for s in range(5)]
    flat = jnp.concatenate(parts, axis=1)
    fl_high, fl_low = halves(flat)
    fl_both = jnp.concatenate([flat, fl_low.astype(F32)], axis=0).astype(BF16)
    grad_out = mul(fl_both, two_high[...])
    grad_out = grad_out[:8] + grad_out[8:] + mul(fl_high, two_low[...])

    lane_row = lax.broadcasted_iota(jnp.int32, (1, hidden), 1)
    last = jnp.where(lane_row == 5, jnp.sum(point_loss), 0.0)
    for f in range(5):
        last = last + jnp.where(lane_row == f, jnp.sum(d_value[f]), 0.0)
    grad_pos = [jnp.sum(sums[1 + d], axis=0, keepdims=True) + 2.0 * w_pos[d] * d_square for d in range(3)]
    misc = grad_pos + [
        jnp.sum(sums[0], axis=0, keepdims=True),
        jnp.sum(sums[5], axis=0, keepdims=True),
        last,
    ]
    misc = jnp.concatenate(misc + [jnp.zeros((2, hidden), F32)], axis=0)
    for part in range(hidden // LANES):
        lanes = slice(part * LANES, (part + 1) * LANES)
        put(part, hidden, grad_latent[:, lanes])
        packed[2 * part, plan.coded_rows :, :] = misc[:, lanes]
        packed[2 * part + 1, plan.coded_rows :, :] = grad_out[:, lanes]

    chosen = jnp.where(
        lane == jnp.broadcast_to(words[:, 10:11], (rows, LANES)).astype(jnp.int32), words[:, 9:10], 0.0
    ).astype(BF16)
    fields = jnp.concatenate(value + [jnp.zeros((3, rows), F32)], axis=0)
    source = (lax.broadcasted_iota(jnp.int32, (8, rows), 1) & (plan.tiles * 8 - 1)) >> 3
    spread = jnp.concatenate([jnp.where(source == t, fields, 0.0) for t in range(plan.tiles)], axis=0)
    high, middle, low = thirds(spread)
    spread = mul(high, chosen) + mul(middle, chosen) + mul(low, chosen)
    packed[:, plan.main_rows : plan.coded_rows, :] = jnp.zeros((8, plan.devices, LANES), F32)
    for t in range(plan.tiles):
        row = plan.main_rows + (my_replica * (plan.tiles // 8) + t // 8) * 8
        packed[t % 8, pl.ds(pl.multiple_of(row, 8), 8), :] = spread[8 * t : 8 * t + 8]

    for block in range(8):
        spot = jnp.bitwise_xor(block, my_block) & 3

        @pl.when((my_block >> 2) == block // 4)
        def _():
            keep_ref[spot] = packed[block]

        @pl.when((my_block >> 2) != block // 4)
        def _():
            send_ref[spot] = packed[block]


class Plan:
    def __init__(self, tiles, replicas, queries, planes, hidden, latents):
        self.tiles, self.replicas, self.planes = tiles, replicas, planes
        self.slots = 2 * queries // tiles
        self.devices = tiles * replicas
        self.query_total = float(queries * self.devices)
        self.main_rows = (hidden + latents) // 2
        self.coded_rows = self.main_rows + self.devices
        self.rows = self.coded_rows + 8
        self.scales = -(-(self.coded_rows // SUB + 1) // 16) * 16
        self.sent_rows = self.coded_rows + 16 + self.scales
        top = self.devices.bit_length() - 1
        self.core, self.plane, self.rest = [0], [1, top - 1], list(range(2, top - 1))

    def mask(self, bits, steps):
        return sum(1 << bit for number, bit in enumerate(bits) if steps >> number & 1)

    def my_block(self, device):
        return (device & 1) * 4 + (device >> 1 & 1) + 2 * (device >> self.plane[1] & 1)


def swapped(value, plan, bits, steps):
    mask = plan.mask(bits, steps)
    return lax.ppermute(value, ("replica", "tile"), [(i, i ^ mask) for i in range(plan.devices)])


def encode(plan, read, out_ref):
    starts = list(range(0, plan.coded_rows, SUB))
    parts = [read(start, SUB) for start in starts] + [read(plan.coded_rows, 8)]
    tops = [jnp.max(jnp.abs(part), axis=0, keepdims=True) for part in parts]
    tops = tops + [jnp.zeros_like(tops[0])] * (plan.scales - len(tops))
    power = jnp.floor(jnp.log2(jnp.maximum(jnp.concatenate(tops, axis=0), 1e-30)))
    scale = jnp.exp2(14.0 - power)

    def whole(value):
        return jnp.clip(jnp.round(value), -32767.0, 32767.0)

    def narrow(value):
        return value.astype(jnp.int32).astype(jnp.int16)

    for number, start in enumerate(starts):
        out_ref[start : start + SUB, :] = narrow(whole(parts[number] * scale[number : number + 1]))
    last = len(starts)
    exact = parts[last] * scale[last : last + 1]
    high = whole(exact)
    low = whole((exact - high) * 32768.0)
    out_ref[plan.coded_rows : plan.coded_rows + 16, :] = narrow(jnp.concatenate([high, low], axis=0))
    out_ref[plan.coded_rows + 16 :, :] = narrow(power)


def decoder(plan, ref):
    def widen(value):
        return value.astype(jnp.int32).astype(F32)

    scale = jnp.exp2(widen(ref[plan.coded_rows + 16 :, :]) - 14.0)

    def read(start, count):
        if start < plan.coded_rows:
            number = start // SUB
            return widen(ref[start : start + count, :]) * scale[number : number + 1]
        both = widen(ref[plan.coded_rows : plan.coded_rows + 16, :])
        number = plan.coded_rows // SUB
        return (both[:8] + both[8:] * (1.0 / 32768.0)) * scale[number : number + 1]

    return read


def added(readers):
    def read(start, count):
        total = readers[0](start, count)
        for reader in readers[1:]:
            total = total + reader(start, count)
        return total

    return read


def first_kernel(plan, numbers, keep_ref, got_ref, *refs):
    def reader(block):
        return lambda start, count: (
            keep_ref[block, start : start + count, :] + got_ref[block, start : start + count, :]
        )

    for number, out_ref in zip(numbers, refs):
        if number:
            encode(plan, reader(number), out_ref)
        else:
            out_ref[...] = keep_ref[0] + got_ref[0]


def first_sum(keep, got, numbers, plan):
    sent = jax.ShapeDtypeStruct((plan.sent_rows, LANES), jnp.int16)
    own = jax.ShapeDtypeStruct(keep.shape[1:], F32)
    return pl.pallas_call(
        functools.partial(first_kernel, plan, numbers),
        out_shape=tuple(sent if number else own for number in numbers),
        in_specs=[VMEM] * 2,
        out_specs=tuple([VMEM] * len(numbers)),
        compiler_params=pltpu.CompilerParams(vmem_limit_bytes=6 << 20),
        name="sum_core",
    )(keep, got)


def plane_kernel(plan, mine_ref, *refs):
    readers = [lambda start, count: mine_ref[start : start + count, :]]
    encode(plan, added(readers + [decoder(plan, ref) for ref in refs[:-1]]), refs[-1])


def pair_kernel(plan, mine_ref, other_ref, out_ref):
    encode(plan, added([decoder(plan, mine_ref), decoder(plan, other_ref)]), out_ref)


def coded_sum(kernel, blocks, plan, name):
    return pl.pallas_call(
        functools.partial(kernel, plan),
        out_shape=jax.ShapeDtypeStruct((plan.sent_rows, LANES), jnp.int16),
        in_specs=[VMEM] * len(blocks),
        out_specs=VMEM,
        compiler_params=pltpu.CompilerParams(vmem_limit_bytes=4 << 20),
        name=name,
    )(*blocks)


def main(place, lat, words, small, weights, plan):
    rows = plan.tiles * plan.slots
    hidden = weights[2].shape[0]
    channels = lat.shape[1]
    outs = jax.ShapeDtypeStruct((4, plan.rows, LANES), F32)
    wide = lambda kind: pltpu.VMEM((5 * rows, hidden), kind)
    return pl.pallas_call(
        functools.partial(main_kernel, plan),
        out_shape=(outs, outs),
        in_specs=[SMEM] + [VMEM] * 3 + [HBM] * 4,
        out_specs=(VMEM, VMEM),
        scratch_shapes=[
            pltpu.VMEM((rows, channels), BF16),
            pltpu.VMEM((rows, LANES), F32),
            pltpu.VMEM((rows, hidden), F32),
            wide(BF16),
            wide(BF16),
            wide(F32),
            wide(BF16),
            wide(BF16),
            wide(F32),
            wide(F32),
            pltpu.VMEM((rows, hidden), BF16),
            pltpu.VMEM((rows, hidden), BF16),
            pltpu.VMEM((6, 8, hidden), F32),
            wide(BF16),
            wide(BF16),
            pltpu.VMEM((40, rows), F32),
            pltpu.VMEM((40, rows), F32),
            pltpu.VMEM((8, plan.rows, LANES), F32),
            pltpu.VMEM((hidden, hidden), BF16),
            pltpu.VMEM((hidden, hidden), BF16),
        ]
        + [pltpu.VMEM(weight.shape, F32) for weight in weights]
        + [pltpu.SemaphoreType.DMA((4,))],
        compiler_params=pltpu.CompilerParams(vmem_limit_bytes=32 << 20),
        name="encode_decode",
    )(place, lat, words, small, *weights)


def unpack_kernel(plan, place_ref, *refs):
    sources, outs, packed = refs[:8], refs[8:-1], refs[-1]
    prediction_ref, latent_ref, pos_ref, one_ref, mid_ref, two_ref, out_ref, bias_out_ref, loss_ref = outs
    my_block = place_ref[0]
    device = place_ref[2] * plan.tiles + place_ref[1]
    starts = list(range(0, plan.coded_rows, SUB))
    for number, ref in enumerate(sources):
        read = decoder(plan, ref)
        block = jnp.bitwise_xor(number, my_block)
        for start in starts:
            packed[block, start : start + SUB, :] = read(start, SUB)
        packed[block, plan.coded_rows :, :] = read(plan.coded_rows, 8)

    hidden = mid_ref.shape[0]
    latents = latent_ref.shape[0]
    split = plan.main_rows
    for part in range(hidden // LANES):
        lanes = slice(part * LANES, (part + 1) * LANES)
        mid_ref[0:split, lanes] = packed[2 * part, 0:split, :]
        mid_ref[split:, lanes] = packed[2 * part + 1, 0 : hidden - split, :]
        latent_ref[:, lanes] = packed[2 * part + 1, hidden - split : split, :]
        misc = packed[2 * part, plan.coded_rows :, :]
        pos_ref[:, lanes] = misc[0:3]
        one_ref[:, lanes] = misc[3:4]
        two_ref[:, lanes] = misc[4:5]
        out_ref[:, lanes] = packed[2 * part + 1, plan.coded_rows : plan.coded_rows + 5, :]
        if part == 0:
            bias_out_ref[...] = misc[5:6, 0:5]
            loss_ref[...] = misc[5:6, 5:6]
    row = pl.multiple_of(plan.main_rows + (device >> 3) * 8, 8)
    fields = packed[device & 7, pl.ds(row, 8), :]
    for f in range(5):
        prediction_ref[f] = fields[f : f + 1]


def unpack(place, blocks, plan, hidden, latents):
    shapes = [
        (5, 1, LANES),
        (latents, hidden),
        (3, hidden),
        (1, hidden),
        (hidden, hidden),
        (1, hidden),
        (5, hidden),
        (1, 5),
        (1, 1),
    ]
    return pl.pallas_call(
        functools.partial(unpack_kernel, plan),
        out_shape=tuple(jax.ShapeDtypeStruct(shape, F32) for shape in shapes),
        in_specs=[SMEM] + [VMEM] * 8,
        out_specs=tuple([VMEM] * len(shapes)),
        scratch_shapes=[pltpu.VMEM((8, plan.rows, LANES), F32)],
        compiler_params=pltpu.CompilerParams(vmem_limit_bytes=16 << 20),
        name="unpack",
    )(place, *blocks)


def body(
    fields,
    convolution_weight,
    convolution_bias,
    query_owner,
    query_cell,
    query_frac,
    target,
    w_latent,
    w_pos,
    bias_one,
    w_mid,
    bias_two,
    w_out,
    bias_out,
):
    tiles = lax.axis_size("tile")
    replicas = lax.axis_size("replica")
    my_tile = lax.axis_index("tile")
    my_replica = lax.axis_index("replica")
    channels = fields.shape[1]
    queries = query_cell.shape[1]
    hidden = w_mid.shape[0]
    plan = Plan(tiles, replicas, queries, fields.shape[2], hidden, channels)
    device = my_replica * tiles + my_tile
    place = jnp.stack([plan.my_block(device), my_tile, my_replica]).astype(jnp.int32)

    here = fields[0].transpose(1, 2, 0, 3)
    up = [(i, (i + 1) % tiles) for i in range(tiles)]
    down = [((i + 1) % tiles, i) for i in range(tiles)]
    to_left, to_right, query_owner = lax.optimization_barrier(
        (here[: DILATION_RATE + 1], here[-DILATION_RATE:], query_owner)
    )
    right = lax.ppermute(to_left, "tile", down)
    left = lax.ppermute(to_right, "tile", up)
    words = route(
        query_owner[:, :, 0],
        query_cell,
        query_frac.transpose(1, 0, 2),
        target.transpose(1, 0, 2),
        tiles,
        plan.slots,
    )
    words = lax.all_to_all(
        words.reshape(tiles, 8, WORDS), "tile", split_axis=0, concat_axis=0, tiled=True
    ).reshape(tiles * 8, WORDS)

    biases = (bias_one[None], bias_two[None], bias_out[None])
    lat, small = convolve(left, here, right, convolution_weight, convolution_bias[None], biases)
    weights = (w_latent, w_pos, w_mid, w_out)
    send, keep = main(place, lat, words, small, weights, plan)

    got = swapped(send, plan, plan.core, 1)
    (far,) = first_sum(keep, got, (3,), plan)
    far, keep = lax.optimization_barrier((far, keep))
    mine, *near = first_sum(keep, got, (0, 1, 2), plan)
    arrived = [swapped(block, plan, plan.plane, step) for step, block in ((3, far), (1, near[0]), (2, near[1]))]
    block = coded_sum(plane_kernel, [mine] + arrived, plan, "sum_plane")
    for bit in plan.rest:
        block = coded_sum(pair_kernel, [block, swapped(block, plan, [bit], 1)], plan, "sum_line")
    blocks = [block] + [swapped(block, plan, plan.plane, step) for step in range(1, 4)]
    blocks = blocks + [swapped(block, plan, plan.core, 1) for block in blocks]
    prediction, g_latent, g_pos, g_one, g_mid, g_two, g_out, g_bias, loss = unpack(
        place, blocks, plan, hidden, channels
    )
    return (
        prediction.transpose(1, 0, 2),
        g_latent,
        g_pos,
        g_one.reshape(hidden),
        g_mid,
        g_two.reshape(hidden),
        g_out,
        g_bias.reshape(5),
        loss.reshape(()),
    )


def solution(mesh):
    return jax.shard_map(
        body,
        mesh=mesh,
        in_specs=(
            P("replica", None, "tile", None, None),
            P(),
            P(),
            P("replica", "tile", None),
            P("replica", "tile"),
            P("replica", None, "tile"),
            P("replica", None, "tile"),
            P(),
            P(),
            P(),
            P(),
            P(),
            P(),
            P(),
        ),
        out_specs=(P("replica", None, "tile"), P(), P(), P(), P(), P(), P(), P(), P()),
        check_vma=False,
    )
```

```python
import functools

import jax
import jax.numpy as jnp
from jax import lax
from jax.experimental import pallas as pl
from jax.experimental.pallas import tpu as pltpu
from jax.sharding import PartitionSpec as P

DILATION_RATE = 2
VISCOSITY = 0.05
DIFFUSIVITY = 0.05
RESIDUAL_WEIGHT = 0.5

F32 = jnp.float32
BF16 = jnp.bfloat16
LANES = 128
BLOCK = 32
WORDS = 128
SUB = 32
NN = (((1,), (0,)), ((), ()))
NT = (((1,), (1,)), ((), ()))
TN = (((0,), (0,)), ((), ()))
VMEM = pl.BlockSpec(memory_space=pltpu.VMEM)
SMEM = pl.BlockSpec(memory_space=pltpu.SMEM)
HBM = pl.BlockSpec(memory_space=pltpu.HBM)


def mul(left, right, dims=NN):
    return lax.dot_general(left, right, dims, preferred_element_type=F32)


def halves(value):
    high = value.astype(BF16)
    return high, (value - high.astype(F32)).astype(BF16)


def thirds(value):
    high = value.astype(BF16)
    rest = value - high.astype(F32)
    middle = rest.astype(BF16)
    return high, middle, (rest - middle.astype(F32)).astype(BF16)


def mul3(left, right, dims=NN):
    return mul(left[0], right[0], dims) + mul(left[0], right[1], dims) + mul(left[1], right[0], dims)


def fetches(sources, targets, sems):
    copies = [
        pltpu.make_async_copy(source, target, sems.at[number])
        for number, (source, target) in enumerate(zip(sources, targets))
    ]
    for copy in copies:
        copy.start()
    return copies


def route_kernel(tiles, slots, *refs):
    out_ref, owner_ref, cell_ref, frac_ref, target_ref, words, sems = refs[4:]
    queries = owner_ref.shape[1]
    for copy in fetches(refs[:4], (owner_ref, cell_ref, frac_ref, target_ref), sems):
        copy.wait()
    owner = owner_ref[...]
    hits = (lax.broadcasted_iota(jnp.int32, (tiles, queries), 0) == owner).astype(F32)
    before = lax.broadcasted_iota(jnp.int32, (queries, queries), 0) < lax.broadcasted_iota(
        jnp.int32, (queries, queries), 1
    )
    earlier = mul(hits.astype(BF16), before.astype(F32).astype(BF16))
    slot = jnp.sum(hits * earlier, axis=0, keepdims=True)
    place = owner * slots + slot.astype(jnp.int32)
    spot = lax.broadcasted_iota(jnp.int32, (tiles * 8, queries), 0)
    spot = (spot >> 3) * slots + (spot & 7)
    groups = slots // 8
    chosen = [jnp.where(spot + 8 * group == place, 1.0, 0.0) for group in range(groups)]
    chosen = jnp.concatenate(chosen, axis=1).astype(BF16)
    words[...] = jnp.zeros_like(words)
    for group in range(groups):
        row, lanes = 16 * group, slice(group * queries, (group + 1) * queries)
        words[row : row + 1, lanes] = cell_ref[...].astype(F32)
        for d in range(3):
            words[row + 1 + d : row + 2 + d, lanes] = frac_ref[d]
        for f in range(5):
            words[row + 4 + f : row + 5 + f, lanes] = target_ref[f]
        words[row + 9 : row + 10, lanes] = jnp.ones((1, queries), F32)
        words[row + 10 : row + 11, lanes] = lax.broadcasted_iota(jnp.int32, (1, queries), 1).astype(F32)
    high, middle, low = thirds(words[...])
    out_ref[...] = mul(chosen, high, NT) + mul(chosen, middle, NT) + mul(chosen, low, NT)


def route(owner, cell, frac, target, tiles, slots):
    queries = owner.shape[1]
    return pl.pallas_call(
        functools.partial(route_kernel, tiles, slots),
        out_shape=jax.ShapeDtypeStruct((tiles * 8, WORDS), F32),
        in_specs=[HBM] * 4,
        out_specs=VMEM,
        scratch_shapes=[
            pltpu.VMEM(owner.shape, owner.dtype),
            pltpu.VMEM(cell.shape, cell.dtype),
            pltpu.VMEM(frac.shape, F32),
            pltpu.VMEM(target.shape, F32),
            pltpu.VMEM((WORDS, queries * (slots // 8)), F32),
            pltpu.SemaphoreType.DMA((4,)),
        ],
        compiler_params=pltpu.CompilerParams(vmem_limit_bytes=4 << 20),
        name="route",
    )(owner, cell, frac, target)


def tap_sum(weight_ref, planes, pair):
    total = None
    for step_x, ref, index in planes:
        rows_y = ref.shape[1]
        blocks = [
            jnp.concatenate([ref[index, (2 * pair + half + step_y) % rows_y] for half in (0, 1)], axis=1)
            for step_y in (-1, 0, 1)
        ]
        term = mul(weight_ref[step_x], jnp.concatenate(blocks, axis=0))
        total = term if total is None else total + term
    channels = total.shape[0] // 3
    sides = []
    for half in (0, 1):
        part = total[:, half * LANES : (half + 1) * LANES]
        sides.append(
            part[channels : 2 * channels]
            + pltpu.roll(part[:channels], 1, 1)
            + pltpu.roll(part[2 * channels :], LANES - 1, 1)
        )
    return jnp.concatenate(sides, axis=1)


def conv_kernel(
    left_ref,
    here_ref,
    right_ref,
    taps_ref,
    bias_ref,
    bias_one_ref,
    bias_two_ref,
    bias_out_ref,
    lat_ref,
    small_ref,
    weight_ref,
):
    planes, rows_y, channels = here_ref.shape[:3]
    taps = taps_ref[...].astype(F32)
    for step in range(3):
        rows = []
        for step_z in range(3):
            numbers = [9 * step + 3 * step_y + step_z for step_y in range(3)]
            rows.append(
                jnp.concatenate([taps[:, n * channels : (n + 1) * channels] for n in numbers], axis=1)
            )
        weight_ref[step] = jnp.concatenate(rows, axis=0).astype(BF16)
    diagonal = lax.broadcasted_iota(jnp.int32, (channels, channels), 0) == lax.broadcasted_iota(
        jnp.int32, (channels, channels), 1
    )
    bias = jnp.sum(jnp.where(diagonal, bias_ref[...], 0.0), axis=1, keepdims=True)
    small_ref[...] = jnp.zeros_like(small_ref)
    small_ref[0:1, :] = bias_one_ref[...]
    small_ref[1:2, :] = bias_two_ref[...]
    small_ref[2:3, 0:5] = bias_out_ref[...]
    for x in range(planes + 1):
        taps = []
        for step in range(3):
            plane = x + DILATION_RATE * (step - 1)
            if plane < 0:
                taps.append((step, left_ref, plane + left_ref.shape[0]))
            elif plane >= planes:
                taps.append((step, right_ref, plane - planes))
            else:
                taps.append((step, here_ref, plane))
        for pair in range(rows_y // 2):
            summed = tap_sum(weight_ref, taps, pair) + bias
            lat_ref[x * (rows_y // 2) + pair] = jax.nn.gelu(summed).astype(BF16)


def convolve(left, here, right, taps, conv_bias, biases):
    planes, rows_y, channels, rows_z = here.shape
    pairs = (planes + 1) * rows_y // 2
    return pl.pallas_call(
        conv_kernel,
        out_shape=(
            jax.ShapeDtypeStruct((pairs, channels, 2 * rows_z), BF16),
            jax.ShapeDtypeStruct((8, biases[0].shape[1]), F32),
        ),
        in_specs=[VMEM] * 8,
        out_specs=(VMEM, VMEM),
        scratch_shapes=[pltpu.VMEM((3, 3 * channels, 3 * channels), BF16)],
        compiler_params=pltpu.CompilerParams(vmem_limit_bytes=8 << 20),
        cost_estimate=pl.CostEstimate(flops=3 << 30, bytes_accessed=4 << 20, transcendentals=0),
        name="convolve",
    )(left, here, right, taps, conv_bias, *biases)


def interpolate(words, lat, planes, rows_y, rows_z):
    rows = words.shape[0]
    cell = jnp.broadcast_to(words[:, 0:1], (rows, LANES)).astype(jnp.int32)
    frac = [jnp.broadcast_to(words[:, 1 + d : 2 + d], (rows, LANES)) for d in range(3)]
    shift_z = rows_z.bit_length() - 1
    shift_y = rows_y.bit_length() - 1
    base_x = cell >> (shift_z + shift_y)
    base_y = (cell >> shift_z) & (rows_y - 1)
    base_z = cell & (rows_z - 1)
    spot = lax.broadcasted_iota(jnp.int32, (rows, rows_z), 1)
    part_z = jnp.where(spot == base_z, 1.0 - frac[2], 0.0) + jnp.where(
        spot == ((base_z + 1) & (rows_z - 1)), frac[2], 0.0
    )
    part_yz = []
    for y in range(rows_y):
        part_y = jnp.where(
            base_y == y, 1.0 - frac[1], jnp.where(base_y == (y - 1) % rows_y, frac[1], 0.0)
        )
        part_yz.append(part_y * part_z)
    total = None
    for x in range(planes + 1):
        part_x = jnp.where(base_x == x, 1.0 - frac[0], jnp.where(base_x == x - 1, frac[0], 0.0))
        for pair in range(rows_y // 2):
            sides = [(part_x * part_yz[2 * pair + half]).astype(BF16) for half in (0, 1)]
            term = mul(jnp.concatenate(sides, axis=1), lat[x * (rows_y // 2) + pair], NT)
            total = term if total is None else total + term
    return total.astype(BF16), base_x, base_y, base_z, frac


def folded(value):
    return jnp.sum(value.reshape(value.shape[0] // 8, 8, value.shape[1]), axis=0)


def main_kernel(
    plan,
    place_ref,
    lat,
    words_ref,
    small_ref,
    w_latent_hbm,
    w_pos_hbm,
    w_mid_hbm,
    w_out_hbm,
    send_ref,
    keep_ref,
    code,
    pos,
    z_one,
    one_high,
    one_low,
    mixed,
    two_high,
    two_low,
    back,
    mixed_back,
    first_high,
    first_low,
    sums_ref,
    d_both,
    out_t,
    d_out_t,
    packed,
    mid_high,
    mid_low,
    w_latent_ref,
    w_pos_ref,
    w_mid_ref,
    w_out_ref,
    sems,
):
    rows = plan.tiles * plan.slots
    hidden = w_mid_ref.shape[0]
    latents = w_latent_ref.shape[0]
    weights = fetches(
        (w_latent_hbm, w_pos_hbm, w_mid_hbm, w_out_hbm),
        (w_latent_ref, w_pos_ref, w_mid_ref, w_out_ref),
        sems,
    )
    planes, rows_z = plan.planes, lat.shape[2] // 2
    rows_y = lat.shape[0] // (planes + 1) * 2
    slots = rows // plan.tiles
    my_block = place_ref[0]
    my_tile = place_ref[1]
    my_replica = place_ref[2]
    always = my_tile >= 0

    words = words_ref[...]
    words = jnp.concatenate(
        [words] + [pltpu.roll(words, LANES - 16 * group, 1) for group in range(1, slots // 8)], axis=0
    )
    interp, base_x, base_y, base_z, frac = interpolate(words, lat, planes, rows_y, rows_z)
    code[...] = interp
    global_x = my_tile * planes + base_x
    lane = lax.broadcasted_iota(jnp.int32, (rows, LANES), 1)
    pos[...] = jnp.where(
        lane == 0,
        (global_x.astype(F32) + frac[0]) / (planes * plan.tiles),
        jnp.where(
            lane == 1,
            (base_y.astype(F32) + frac[1]) / rows_y,
            (base_z.astype(F32) + frac[2]) / rows_z,
        ),
    )

    for copy in weights:
        copy.wait()
    high, low = halves(w_latent_ref[...])
    z_one[...] = mul(interp, high) + mul(interp, low)
    high, low = halves(w_mid_ref[...])
    mid_high[...] = high
    mid_low[...] = low
    w_pos = [w_pos_ref[d : d + 1, :] for d in range(3)]
    square = w_pos[0] * w_pos[0] + w_pos[1] * w_pos[1] + w_pos[2] * w_pos[2]
    bias_one = small_ref[0:1, :]
    bias_two = small_ref[1:2, :]

    part_rows = rows // 2

    def at(part, index, block=None):
        first = (part * 5 + index) * part_rows
        if block is None:
            return slice(first, first + part_rows)
        return slice(first + block * BLOCK, first + (block + 1) * BLOCK)

    def rows_at(part, block):
        first = part * part_rows + block * BLOCK
        return slice(first, first + BLOCK)

    def store(refs, span, value):
        high, low = halves(value)
        refs[0][span, :] = high
        refs[1][span, :] = low

    def layer_one(part):
        refs = (one_high, one_low)
        for block in range(part_rows // BLOCK):
            here = rows_at(part, block)
            where = pos[here, :]
            pre = (
                z_one[here, :]
                + (where[:, 0:1] * w_pos[0] + where[:, 1:2] * w_pos[1] + where[:, 2:3] * w_pos[2])
                + bias_one
            )
            act = jnp.tanh(pre)
            slope = 1.0 - act * act
            curve = -2.0 * act * slope
            z_one[here, :] = act
            store(refs, at(part, 0, block), act)
            for d in range(3):
                store(refs, at(part, 1 + d, block), slope * w_pos[d])
            store(refs, at(part, 4, block), curve * square)

    def times_mid(dims, source, result, part):
        span = slice(part * 5 * part_rows, (part + 1) * 5 * part_rows)
        left = (source[0][span, :], source[1][span, :])
        result[span, :] = mul3(left, (mid_high[...], mid_low[...]), dims)

    def layer_two(part):
        refs = (two_high, two_low)
        for block in range(part_rows // BLOCK):
            act = jnp.tanh(mixed[at(part, 0, block), :] + bias_two)
            slope = 1.0 - act * act
            curve = -2.0 * act * slope
            store(refs, at(part, 0, block), act)
            mixed[at(part, 0, block), :] = act
            norm = None
            for d in range(3):
                tangent = mixed[at(part, 1 + d, block), :]
                store(refs, at(part, 1 + d, block), slope * tangent)
                norm = tangent * tangent if norm is None else norm + tangent * tangent
            store(refs, at(part, 4, block), slope * mixed[at(part, 4, block), :] + curve * norm)

    out_fields = jnp.concatenate([w_out_ref[...], jnp.zeros((3, hidden), F32)], axis=0)
    wo_high, wo_low = halves(out_fields)
    wo_three = jnp.concatenate([out_fields, wo_low.astype(F32), out_fields], axis=0).astype(BF16)
    wo_both = jnp.concatenate([out_fields, wo_low.astype(F32)], axis=0).astype(BF16)

    def outputs(part):
        for s in range(5):
            span = at(part, s)
            both = mul(wo_both, two_high[span, :], NT)
            both = both[:8] + both[8:] + mul(wo_high, two_low[span, :], NT)
            out_t[8 * s : 8 * s + 8, part * part_rows : (part + 1) * part_rows] = both

    @pl.when(always)
    def _():
        layer_one(0)
        times_mid(NN, (one_high, one_low), mixed, 0)
        layer_one(1)
        times_mid(NN, (one_high, one_low), mixed, 1)
        layer_two(0)
        outputs(0)
        layer_two(1)
        outputs(1)

    words_t = words.T
    target = [words_t[4 + f : 5 + f, :] for f in range(5)]
    valid = words_t[9:10, :]
    value = [out_t[f : f + 1, :] + small_ref[2:3, f : f + 1] for f in range(5)]
    grad = [[out_t[8 * (d + 1) + f : 8 * (d + 1) + f + 1, :] for f in range(5)] for d in range(3)]
    laplace = [out_t[32 + f : 33 + f, :] for f in range(5)]
    velocity = value[2:5]
    advection = [
        velocity[0] * grad[0][f] + velocity[1] * grad[1][f] + velocity[2] * grad[2][f] for f in range(5)
    ]
    continuity = grad[0][2] + grad[1][3] + grad[2][4]
    momentum = [advection[2 + j] + grad[j][1] - VISCOSITY * laplace[2 + j] for j in range(3)]
    momentum[2] = momentum[2] - value[0]
    energy = advection[0] - DIFFUSIVITY * laplace[0]
    misfit = [value[f] - target[f] for f in range(5)]
    physics = (
        continuity * continuity
        + (momentum[0] * momentum[0] + momentum[1] * momentum[1] + momentum[2] * momentum[2])
        + energy * energy
    )
    squares = (
        misfit[0] * misfit[0]
        + misfit[1] * misfit[1]
        + misfit[2] * misfit[2]
        + misfit[3] * misfit[3]
        + misfit[4] * misfit[4]
    )
    point_loss = valid * (squares + RESIDUAL_WEIGHT * physics) * (1.0 / plan.query_total)

    rate = valid * (1.0 / plan.query_total)
    twice = RESIDUAL_WEIGHT * 2.0
    d_cont = rate * twice * continuity
    d_mom = [rate * twice * m for m in momentum]
    d_energy = rate * twice * energy
    d_value = [2.0 * rate * m for m in misfit]
    for d in range(3):
        d_value[2 + d] = d_value[2 + d] + (
            d_mom[0] * grad[d][2] + d_mom[1] * grad[d][3] + d_mom[2] * grad[d][4] + d_energy * grad[d][0]
        )
    d_value[0] = d_value[0] - d_mom[2]
    d_out_t[...] = jnp.zeros_like(d_out_t)
    for f in range(5):
        d_out_t[f : f + 1, :] = d_value[f]
    for d in range(3):
        first = 8 * (d + 1)
        d_out_t[first : first + 1, :] = d_energy * velocity[d]
        d_out_t[first + 1 : first + 2, :] = d_mom[d]
        for j in range(3):
            term = d_mom[j] * velocity[d]
            if j == d:
                term = term + d_cont
            d_out_t[first + 2 + j : first + 3 + j, :] = term
    d_out_t[32:33, :] = -DIFFUSIVITY * d_energy
    for j in range(3):
        d_out_t[34 + j : 35 + j, :] = -VISCOSITY * d_mom[j]

    def out_back(part):
        for s in range(5):
            wanted = d_out_t[8 * s : 8 * s + 8, part * part_rows : (part + 1) * part_rows]
            do_low = halves(wanted)[1].astype(F32)
            wanted = jnp.concatenate([wanted, wanted, do_low], axis=0).astype(BF16)
            back[at(part, s), :] = mul(wanted, wo_three, TN)

    def second_back(part, total):
        refs = (d_both.at[:, :hidden], d_both.at[:, hidden:])
        for block in range(part_rows // BLOCK):
            act = mixed[at(part, 0, block), :]
            slope = 1.0 - act * act
            curve = -2.0 * act * slope
            cot_l = back[at(part, 4, block), :]
            d_slope = cot_l * mixed[at(part, 4, block), :]
            norm = None
            bent = 2.0 * curve * cot_l
            for d in range(3):
                tangent = mixed[at(part, 1 + d, block), :]
                cot_t = back[at(part, 1 + d, block), :]
                store(refs, at(part, 1 + d, block), slope * cot_t + bent * tangent)
                d_slope = d_slope + cot_t * tangent
                norm = tangent * tangent if norm is None else norm + tangent * tangent
            store(refs, at(part, 4, block), slope * cot_l)
            d_curve = cot_l * norm
            d_slope = d_slope - 2.0 * act * d_curve
            d_act = back[at(part, 0, block), :] - 2.0 * slope * d_curve - 2.0 * act * d_slope
            d_pre = slope * d_act
            store(refs, at(part, 0, block), d_pre)
            total = total + folded(d_pre)
        return total

    def first_back(part, sums):
        for block in range(part_rows // BLOCK):
            here = rows_at(part, block)
            act = z_one[here, :]
            slope = 1.0 - act * act
            curve = -2.0 * act * slope
            where = pos[here, :]
            cot_t = [mixed_back[at(part, 1 + d, block), :] for d in range(3)]
            cot_l = mixed_back[at(part, 4, block), :]
            d_curve = cot_l * square
            d_slope = cot_t[0] * w_pos[0] + cot_t[1] * w_pos[1] + cot_t[2] * w_pos[2] - 2.0 * act * d_curve
            d_act = mixed_back[at(part, 0, block), :] - 2.0 * slope * d_curve - 2.0 * act * d_slope
            d_pre = slope * d_act
            high, low = halves(d_pre)
            first_high[here, :] = high
            first_low[here, :] = low
            sums = (
                [sums[0] + folded(d_pre)]
                + [sums[1 + d] + folded(where[:, d : d + 1] * d_pre + slope * cot_t[d]) for d in range(3)]
                + [sums[4] + folded(curve * cot_l)]
            )
        return sums


    def put(part, first, value):
        while value.shape[0]:
            block, row = first // plan.main_rows, first % plan.main_rows
            count = min(value.shape[0], plan.main_rows - row)
            packed[2 * part + block, row : row + count, :] = value[:count]
            first, value = first + count, value[count:]

    wide = 2 * LANES
    def mid_gradient():
        for left in range(hidden // wide):
            lefts = slice(left * wide, (left + 1) * wide)
            both = mul(one_high[:, lefts], d_both[...], TN)
            both = both[:, :hidden] + both[:, hidden:] + mul(one_low[:, lefts], d_both[:, :hidden], TN)
            for part in range(hidden // LANES):
                put(part, left * wide, both[:, part * LANES : (part + 1) * LANES])

    @pl.when(always)
    def _():
        out_back(0)
        total = second_back(0, jnp.zeros((8, hidden), F32))
        out_back(1)
        times_mid(NT, (d_both.at[:, :hidden], d_both.at[:, hidden:]), mixed_back, 0)
        sums_ref[5] = second_back(1, total)
        times_mid(NT, (d_both.at[:, :hidden], d_both.at[:, hidden:]), mixed_back, 1)
        total = first_back(0, [jnp.zeros((8, hidden), F32)] * 5)
        mid_gradient()
        for number, value in enumerate(first_back(1, total)):
            sums_ref[number] = value

    sums = [sums_ref[number] for number in range(6)]
    d_square = jnp.sum(sums[4], axis=0, keepdims=True)
    grad_latent = mul(code[...], first_high[...], TN) + mul(code[...], first_low[...], TN)

    parts = [d_out_t[8 * s : 8 * s + 8, p * part_rows : (p + 1) * part_rows] for p in range(2) for s in range(5)]
    flat = jnp.concatenate(parts, axis=1)
    fl_high, fl_low = halves(flat)
    fl_both = jnp.concatenate([flat, fl_low.astype(F32)], axis=0).astype(BF16)
    grad_out = mul(fl_both, two_high[...])
    grad_out = grad_out[:8] + grad_out[8:] + mul(fl_high, two_low[...])

    lane_row = lax.broadcasted_iota(jnp.int32, (1, hidden), 1)
    last = jnp.where(lane_row == 5, jnp.sum(point_loss), 0.0)
    for f in range(5):
        last = last + jnp.where(lane_row == f, jnp.sum(d_value[f]), 0.0)
    grad_pos = [jnp.sum(sums[1 + d], axis=0, keepdims=True) + 2.0 * w_pos[d] * d_square for d in range(3)]
    misc = grad_pos + [
        jnp.sum(sums[0], axis=0, keepdims=True),
        jnp.sum(sums[5], axis=0, keepdims=True),
        last,
    ]
    misc = jnp.concatenate(misc + [jnp.zeros((2, hidden), F32)], axis=0)
    for part in range(hidden // LANES):
        lanes = slice(part * LANES, (part + 1) * LANES)
        put(part, hidden, grad_latent[:, lanes])
        packed[2 * part, plan.coded_rows :, :] = misc[:, lanes]
        packed[2 * part + 1, plan.coded_rows :, :] = grad_out[:, lanes]

    chosen = jnp.where(
        lane == jnp.broadcast_to(words[:, 10:11], (rows, LANES)).astype(jnp.int32), words[:, 9:10], 0.0
    ).astype(BF16)
    fields = jnp.concatenate(value + [jnp.zeros((3, rows), F32)], axis=0)
    source = (lax.broadcasted_iota(jnp.int32, (8, rows), 1) & (plan.tiles * 8 - 1)) >> 3
    spread = jnp.concatenate([jnp.where(source == t, fields, 0.0) for t in range(plan.tiles)], axis=0)
    high, middle, low = thirds(spread)
    spread = mul(high, chosen) + mul(middle, chosen) + mul(low, chosen)
    packed[:, plan.main_rows : plan.coded_rows, :] = jnp.zeros((8, plan.devices, LANES), F32)
    for t in range(plan.tiles):
        row = plan.main_rows + (my_replica * (plan.tiles // 8) + t // 8) * 8
        packed[t % 8, pl.ds(pl.multiple_of(row, 8), 8), :] = spread[8 * t : 8 * t + 8]

    for block in range(8):
        spot = jnp.bitwise_xor(block, my_block) & 3

        @pl.when((my_block >> 2) == block // 4)
        def _():
            keep_ref[spot] = packed[block]

        @pl.when((my_block >> 2) != block // 4)
        def _():
            send_ref[spot] = packed[block]


class Plan:
    def __init__(self, tiles, replicas, queries, planes, hidden, latents):
        self.tiles, self.replicas, self.planes = tiles, replicas, planes
        self.slots = 2 * queries // tiles
        self.devices = tiles * replicas
        self.query_total = float(queries * self.devices)
        self.main_rows = (hidden + latents) // 2
        self.coded_rows = self.main_rows + self.devices
        self.rows = self.coded_rows + 8
        self.scales = -(-(self.coded_rows // SUB + 1) // 16) * 16
        self.sent_rows = self.coded_rows + 16 + self.scales
        top = self.devices.bit_length() - 1
        self.core, self.plane, self.rest = [0], [1, top - 1], list(range(2, top - 1))

    def mask(self, bits, steps):
        return sum(1 << bit for number, bit in enumerate(bits) if steps >> number & 1)

    def my_block(self, device):
        return (device & 1) * 4 + (device >> 1 & 1) + 2 * (device >> self.plane[1] & 1)


def swapped(value, plan, bits, steps):
    mask = plan.mask(bits, steps)
    return lax.ppermute(value, ("replica", "tile"), [(i, i ^ mask) for i in range(plan.devices)])


def encode(plan, read, out_ref):
    starts = list(range(0, plan.coded_rows, SUB))
    parts = [read(start, SUB) for start in starts] + [read(plan.coded_rows, 8)]
    tops = [jnp.max(jnp.abs(part), axis=0, keepdims=True) for part in parts]
    tops = tops + [jnp.zeros_like(tops[0])] * (plan.scales - len(tops))
    power = jnp.floor(jnp.log2(jnp.maximum(jnp.concatenate(tops, axis=0), 1e-30)))
    scale = jnp.exp2(14.0 - power)

    def whole(value):
        return jnp.clip(jnp.round(value), -32767.0, 32767.0)

    def narrow(value):
        return value.astype(jnp.int32).astype(jnp.int16)

    for number, start in enumerate(starts):
        out_ref[start : start + SUB, :] = narrow(whole(parts[number] * scale[number : number + 1]))
    last = len(starts)
    exact = parts[last] * scale[last : last + 1]
    high = whole(exact)
    low = whole((exact - high) * 32768.0)
    out_ref[plan.coded_rows : plan.coded_rows + 16, :] = narrow(jnp.concatenate([high, low], axis=0))
    out_ref[plan.coded_rows + 16 :, :] = narrow(power)


def decoder(plan, ref):
    def widen(value):
        return value.astype(jnp.int32).astype(F32)

    scale = jnp.exp2(widen(ref[plan.coded_rows + 16 :, :]) - 14.0)

    def read(start, count):
        if start < plan.coded_rows:
            number = start // SUB
            return widen(ref[start : start + count, :]) * scale[number : number + 1]
        both = widen(ref[plan.coded_rows : plan.coded_rows + 16, :])
        number = plan.coded_rows // SUB
        return (both[:8] + both[8:] * (1.0 / 32768.0)) * scale[number : number + 1]

    return read


def added(readers):
    def read(start, count):
        total = readers[0](start, count)
        for reader in readers[1:]:
            total = total + reader(start, count)
        return total

    return read


def first_kernel(plan, numbers, keep_ref, got_ref, *refs):
    def reader(block):
        return lambda start, count: (
            keep_ref[block, start : start + count, :] + got_ref[block, start : start + count, :]
        )

    for number, out_ref in zip(numbers, refs):
        if number:
            encode(plan, reader(number), out_ref)
        else:
            out_ref[...] = keep_ref[0] + got_ref[0]


def first_sum(keep, got, numbers, plan):
    sent = jax.ShapeDtypeStruct((plan.sent_rows, LANES), jnp.int16)
    own = jax.ShapeDtypeStruct(keep.shape[1:], F32)
    return pl.pallas_call(
        functools.partial(first_kernel, plan, numbers),
        out_shape=tuple(sent if number else own for number in numbers),
        in_specs=[VMEM] * 2,
        out_specs=tuple([VMEM] * len(numbers)),
        compiler_params=pltpu.CompilerParams(vmem_limit_bytes=6 << 20),
        name="sum_core",
    )(keep, got)


def plane_kernel(plan, mine_ref, *refs):
    readers = [lambda start, count: mine_ref[start : start + count, :]]
    encode(plan, added(readers + [decoder(plan, ref) for ref in refs[:-1]]), refs[-1])


def pair_kernel(plan, mine_ref, other_ref, out_ref):
    encode(plan, added([decoder(plan, mine_ref), decoder(plan, other_ref)]), out_ref)


def coded_sum(kernel, blocks, plan, name):
    return pl.pallas_call(
        functools.partial(kernel, plan),
        out_shape=jax.ShapeDtypeStruct((plan.sent_rows, LANES), jnp.int16),
        in_specs=[VMEM] * len(blocks),
        out_specs=VMEM,
        compiler_params=pltpu.CompilerParams(vmem_limit_bytes=4 << 20),
        name=name,
    )(*blocks)


def main(place, lat, words, small, weights, plan):
    rows = plan.tiles * plan.slots
    hidden = weights[2].shape[0]
    channels = lat.shape[1]
    outs = jax.ShapeDtypeStruct((4, plan.rows, LANES), F32)
    wide = lambda kind: pltpu.VMEM((5 * rows, hidden), kind)
    return pl.pallas_call(
        functools.partial(main_kernel, plan),
        out_shape=(outs, outs),
        in_specs=[SMEM] + [VMEM] * 3 + [HBM] * 4,
        out_specs=(VMEM, VMEM),
        scratch_shapes=[
            pltpu.VMEM((rows, channels), BF16),
            pltpu.VMEM((rows, LANES), F32),
            pltpu.VMEM((rows, hidden), F32),
            wide(BF16),
            wide(BF16),
            wide(F32),
            wide(BF16),
            wide(BF16),
            wide(F32),
            wide(F32),
            pltpu.VMEM((rows, hidden), BF16),
            pltpu.VMEM((rows, hidden), BF16),
            pltpu.VMEM((6, 8, hidden), F32),
            pltpu.VMEM((5 * rows, 2 * hidden), BF16),
            pltpu.VMEM((40, rows), F32),
            pltpu.VMEM((40, rows), F32),
            pltpu.VMEM((8, plan.rows, LANES), F32),
            pltpu.VMEM((hidden, hidden), BF16),
            pltpu.VMEM((hidden, hidden), BF16),
        ]
        + [pltpu.VMEM(weight.shape, F32) for weight in weights]
        + [pltpu.SemaphoreType.DMA((4,))],
        compiler_params=pltpu.CompilerParams(vmem_limit_bytes=32 << 20),
        name="encode_decode",
    )(place, lat, words, small, *weights)


def unpack_kernel(plan, place_ref, *refs):
    sources, outs, packed = refs[:8], refs[8:-1], refs[-1]
    prediction_ref, latent_ref, pos_ref, one_ref, mid_ref, two_ref, out_ref, bias_out_ref, loss_ref = outs
    my_block = place_ref[0]
    device = place_ref[2] * plan.tiles + place_ref[1]
    starts = list(range(0, plan.coded_rows, SUB))
    for number, ref in enumerate(sources):
        read = decoder(plan, ref)
        block = jnp.bitwise_xor(number, my_block)
        for start in starts:
            packed[block, start : start + SUB, :] = read(start, SUB)
        packed[block, plan.coded_rows :, :] = read(plan.coded_rows, 8)

    hidden = mid_ref.shape[0]
    latents = latent_ref.shape[0]
    split = plan.main_rows
    for part in range(hidden // LANES):
        lanes = slice(part * LANES, (part + 1) * LANES)
        mid_ref[0:split, lanes] = packed[2 * part, 0:split, :]
        mid_ref[split:, lanes] = packed[2 * part + 1, 0 : hidden - split, :]
        latent_ref[:, lanes] = packed[2 * part + 1, hidden - split : split, :]
        misc = packed[2 * part, plan.coded_rows :, :]
        pos_ref[:, lanes] = misc[0:3]
        one_ref[:, lanes] = misc[3:4]
        two_ref[:, lanes] = misc[4:5]
        out_ref[:, lanes] = packed[2 * part + 1, plan.coded_rows : plan.coded_rows + 5, :]
        if part == 0:
            bias_out_ref[...] = misc[5:6, 0:5]
            loss_ref[...] = misc[5:6, 5:6]
    row = pl.multiple_of(plan.main_rows + (device >> 3) * 8, 8)
    fields = packed[device & 7, pl.ds(row, 8), :]
    for f in range(5):
        prediction_ref[f] = fields[f : f + 1]


def unpack(place, blocks, plan, hidden, latents):
    shapes = [
        (5, 1, LANES),
        (latents, hidden),
        (3, hidden),
        (1, hidden),
        (hidden, hidden),
        (1, hidden),
        (5, hidden),
        (1, 5),
        (1, 1),
    ]
    return pl.pallas_call(
        functools.partial(unpack_kernel, plan),
        out_shape=tuple(jax.ShapeDtypeStruct(shape, F32) for shape in shapes),
        in_specs=[SMEM] + [VMEM] * 8,
        out_specs=tuple([VMEM] * len(shapes)),
        scratch_shapes=[pltpu.VMEM((8, plan.rows, LANES), F32)],
        compiler_params=pltpu.CompilerParams(vmem_limit_bytes=16 << 20),
        name="unpack",
    )(place, *blocks)


def body(
    fields,
    convolution_weight,
    convolution_bias,
    query_owner,
    query_cell,
    query_frac,
    target,
    w_latent,
    w_pos,
    bias_one,
    w_mid,
    bias_two,
    w_out,
    bias_out,
):
    tiles = lax.axis_size("tile")
    replicas = lax.axis_size("replica")
    my_tile = lax.axis_index("tile")
    my_replica = lax.axis_index("replica")
    channels = fields.shape[1]
    queries = query_cell.shape[1]
    hidden = w_mid.shape[0]
    plan = Plan(tiles, replicas, queries, fields.shape[2], hidden, channels)
    device = my_replica * tiles + my_tile
    place = jnp.stack([plan.my_block(device), my_tile, my_replica]).astype(jnp.int32)

    here = fields[0].transpose(1, 2, 0, 3)
    up = [(i, (i + 1) % tiles) for i in range(tiles)]
    down = [((i + 1) % tiles, i) for i in range(tiles)]
    to_left, to_right, query_owner = lax.optimization_barrier(
        (here[: DILATION_RATE + 1], here[-DILATION_RATE:], query_owner)
    )
    right = lax.ppermute(to_left, "tile", down)
    left = lax.ppermute(to_right, "tile", up)
    words = route(
        query_owner[:, :, 0],
        query_cell,
        query_frac.transpose(1, 0, 2),
        target.transpose(1, 0, 2),
        tiles,
        plan.slots,
    )
    words = lax.all_to_all(
        words.reshape(tiles, 8, WORDS), "tile", split_axis=0, concat_axis=0, tiled=True
    ).reshape(tiles * 8, WORDS)

    biases = (bias_one[None], bias_two[None], bias_out[None])
    lat, small = convolve(left, here, right, convolution_weight, convolution_bias[None], biases)
    weights = (w_latent, w_pos, w_mid, w_out)
    send, keep = main(place, lat, words, small, weights, plan)

    got = swapped(send, plan, plan.core, 1)
    (far,) = first_sum(keep, got, (3,), plan)
    far, keep = lax.optimization_barrier((far, keep))
    mine, *near = first_sum(keep, got, (0, 1, 2), plan)
    arrived = [swapped(block, plan, plan.plane, step) for step, block in ((3, far), (1, near[0]), (2, near[1]))]
    block = coded_sum(plane_kernel, [mine] + arrived, plan, "sum_plane")
    for bit in plan.rest:
        block = coded_sum(pair_kernel, [block, swapped(block, plan, [bit], 1)], plan, "sum_line")
    blocks = [block] + [swapped(block, plan, plan.plane, step) for step in range(1, 4)]
    blocks = blocks + [swapped(block, plan, plan.core, 1) for block in blocks]
    prediction, g_latent, g_pos, g_one, g_mid, g_two, g_out, g_bias, loss = unpack(
        place, blocks, plan, hidden, channels
    )
    return (
        prediction.transpose(1, 0, 2),
        g_latent,
        g_pos,
        g_one.reshape(hidden),
        g_mid,
        g_two.reshape(hidden),
        g_out,
        g_bias.reshape(5),
        loss.reshape(()),
    )


def solution(mesh):
    return jax.shard_map(
        body,
        mesh=mesh,
        in_specs=(
            P("replica", None, "tile", None, None),
            P(),
            P(),
            P("replica", "tile", None),
            P("replica", "tile"),
            P("replica", None, "tile"),
            P("replica", None, "tile"),
            P(),
            P(),
            P(),
            P(),
            P(),
            P(),
            P(),
        ),
        out_specs=(P("replica", None, "tile"), P(), P(), P(), P(), P(), P(), P(), P()),
        check_vma=False,
    )
```

```python
import functools

import jax
import jax.numpy as jnp
from jax import lax
from jax.experimental import pallas as pl
from jax.experimental.pallas import tpu as pltpu
from jax.sharding import PartitionSpec as P

DILATION_RATE = 2
VISCOSITY = 0.05
DIFFUSIVITY = 0.05
RESIDUAL_WEIGHT = 0.5

F32 = jnp.float32
BF16 = jnp.bfloat16
LANES = 128
BLOCK = 32
WORDS = 128
SUB = 32
NN = (((1,), (0,)), ((), ()))
NT = (((1,), (1,)), ((), ()))
TN = (((0,), (0,)), ((), ()))
VMEM = pl.BlockSpec(memory_space=pltpu.VMEM)
SMEM = pl.BlockSpec(memory_space=pltpu.SMEM)
HBM = pl.BlockSpec(memory_space=pltpu.HBM)


def mul(left, right, dims=NN):
    return lax.dot_general(left, right, dims, preferred_element_type=F32)


def halves(value):
    high = value.astype(BF16)
    return high, (value - high.astype(F32)).astype(BF16)


def thirds(value):
    high = value.astype(BF16)
    rest = value - high.astype(F32)
    middle = rest.astype(BF16)
    return high, middle, (rest - middle.astype(F32)).astype(BF16)


def mul3(left, right, dims=NN):
    return mul(left[0], right[0], dims) + mul(left[0], right[1], dims) + mul(left[1], right[0], dims)


def fetches(sources, targets, sems):
    copies = [
        pltpu.make_async_copy(source, target, sems.at[number])
        for number, (source, target) in enumerate(zip(sources, targets))
    ]
    for copy in copies:
        copy.start()
    return copies


def route_kernel(tiles, slots, *refs):
    out_ref, small_ref, *scratch, words, sems = refs[8:]
    for copy in fetches(refs[:8], scratch, sems):
        copy.wait()
    owner_ref, cell_ref, frac_ref, target_ref, *bias_refs = scratch
    queries = owner_ref.shape[1]
    small_ref[...] = jnp.zeros_like(small_ref)
    for number, ref in enumerate(bias_refs):
        small_ref[number : number + 1, 0 : ref.shape[1]] = ref[...]
    owner = owner_ref[...]
    hits = (lax.broadcasted_iota(jnp.int32, (tiles, queries), 0) == owner).astype(F32)
    before = lax.broadcasted_iota(jnp.int32, (queries, queries), 0) < lax.broadcasted_iota(
        jnp.int32, (queries, queries), 1
    )
    earlier = mul(hits.astype(BF16), before.astype(F32).astype(BF16))
    slot = jnp.sum(hits * earlier, axis=0, keepdims=True)
    place = owner * slots + slot.astype(jnp.int32)
    spot = lax.broadcasted_iota(jnp.int32, (tiles * 8, queries), 0)
    spot = (spot >> 3) * slots + (spot & 7)
    groups = slots // 8
    chosen = [jnp.where(spot + 8 * group == place, 1.0, 0.0) for group in range(groups)]
    chosen = jnp.concatenate(chosen, axis=1).astype(BF16)
    words[...] = jnp.zeros_like(words)
    for group in range(groups):
        row, lanes = 16 * group, slice(group * queries, (group + 1) * queries)
        words[row : row + 1, lanes] = cell_ref[...].astype(F32)
        for d in range(3):
            words[row + 1 + d : row + 2 + d, lanes] = frac_ref[d]
        for f in range(5):
            words[row + 4 + f : row + 5 + f, lanes] = target_ref[f]
        words[row + 9 : row + 10, lanes] = jnp.ones((1, queries), F32)
        words[row + 10 : row + 11, lanes] = lax.broadcasted_iota(jnp.int32, (1, queries), 1).astype(F32)
    high, middle, low = thirds(words[...])
    out_ref[...] = mul(chosen, high, NT) + mul(chosen, middle, NT) + mul(chosen, low, NT)


def route(inputs, biases, tiles, slots):
    queries = inputs[0].shape[1]
    arrays = inputs + biases
    return pl.pallas_call(
        functools.partial(route_kernel, tiles, slots),
        out_shape=(
            jax.ShapeDtypeStruct((tiles * 8, WORDS), F32),
            jax.ShapeDtypeStruct((8, biases[0].shape[1]), F32),
        ),
        in_specs=[HBM] * 8,
        out_specs=(VMEM, VMEM),
        scratch_shapes=[pltpu.VMEM(array.shape, array.dtype) for array in arrays]
        + [pltpu.VMEM((WORDS, queries * (slots // 8)), F32), pltpu.SemaphoreType.DMA((8,))],
        compiler_params=pltpu.CompilerParams(vmem_limit_bytes=4 << 20),
        name="route",
    )(*arrays)


def tap_sum(weight_ref, planes, pair):
    total = None
    for step_x, ref, index in planes:
        rows_y = ref.shape[1]
        blocks = [
            jnp.concatenate([ref[index, (2 * pair + half + step_y) % rows_y] for half in (0, 1)], axis=1)
            for step_y in (-1, 0, 1)
        ]
        term = mul(weight_ref[step_x], jnp.concatenate(blocks, axis=0))
        total = term if total is None else total + term
    channels = total.shape[0] // 3
    sides = []
    for half in (0, 1):
        part = total[:, half * LANES : (half + 1) * LANES]
        sides.append(
            part[channels : 2 * channels]
            + pltpu.roll(part[:channels], 1, 1)
            + pltpu.roll(part[2 * channels :], LANES - 1, 1)
        )
    return jnp.concatenate(sides, axis=1)


def conv_kernel(
    left_ref,
    here_ref,
    right_ref,
    taps_ref,
    small_ref,
    lat_ref,
    weight_ref,
):
    planes, rows_y, channels = here_ref.shape[:3]
    taps = taps_ref[...].astype(F32)
    for step in range(3):
        rows = []
        for step_z in range(3):
            numbers = [9 * step + 3 * step_y + step_z for step_y in range(3)]
            rows.append(
                jnp.concatenate([taps[:, n * channels : (n + 1) * channels] for n in numbers], axis=1)
            )
        weight_ref[step] = jnp.concatenate(rows, axis=0).astype(BF16)
    diagonal = lax.broadcasted_iota(jnp.int32, (channels, channels), 0) == lax.broadcasted_iota(
        jnp.int32, (channels, channels), 1
    )
    bias = jnp.sum(jnp.where(diagonal, small_ref[3:4, 0:channels], 0.0), axis=1, keepdims=True)
    for x in range(planes + 1):
        taps = []
        for step in range(3):
            plane = x + DILATION_RATE * (step - 1)
            if plane < 0:
                taps.append((step, left_ref, plane + left_ref.shape[0]))
            elif plane >= planes:
                taps.append((step, right_ref, plane - planes))
            else:
                taps.append((step, here_ref, plane))
        for pair in range(rows_y // 2):
            summed = tap_sum(weight_ref, taps, pair) + bias
            lat_ref[x * (rows_y // 2) + pair] = jax.nn.gelu(summed).astype(BF16)


def convolve(left, here, right, taps, small):
    planes, rows_y, channels, rows_z = here.shape
    pairs = (planes + 1) * rows_y // 2
    return pl.pallas_call(
        conv_kernel,
        out_shape=jax.ShapeDtypeStruct((pairs, channels, 2 * rows_z), BF16),
        in_specs=[VMEM] * 5,
        out_specs=VMEM,
        scratch_shapes=[pltpu.VMEM((3, 3 * channels, 3 * channels), BF16)],
        compiler_params=pltpu.CompilerParams(vmem_limit_bytes=8 << 20),
        cost_estimate=pl.CostEstimate(flops=3 << 30, bytes_accessed=4 << 20, transcendentals=0),
        name="convolve",
    )(left, here, right, taps, small)


def interpolate(words, lat, planes, rows_y, rows_z):
    rows = words.shape[0]
    cell = jnp.broadcast_to(words[:, 0:1], (rows, LANES)).astype(jnp.int32)
    frac = [jnp.broadcast_to(words[:, 1 + d : 2 + d], (rows, LANES)) for d in range(3)]
    shift_z = rows_z.bit_length() - 1
    shift_y = rows_y.bit_length() - 1
    base_x = cell >> (shift_z + shift_y)
    base_y = (cell >> shift_z) & (rows_y - 1)
    base_z = cell & (rows_z - 1)
    spot = lax.broadcasted_iota(jnp.int32, (rows, rows_z), 1)
    part_z = jnp.where(spot == base_z, 1.0 - frac[2], 0.0) + jnp.where(
        spot == ((base_z + 1) & (rows_z - 1)), frac[2], 0.0
    )
    part_yz = []
    for y in range(rows_y):
        part_y = jnp.where(
            base_y == y, 1.0 - frac[1], jnp.where(base_y == (y - 1) % rows_y, frac[1], 0.0)
        )
        part_yz.append(part_y * part_z)
    total = None
    for x in range(planes + 1):
        part_x = jnp.where(base_x == x, 1.0 - frac[0], jnp.where(base_x == x - 1, frac[0], 0.0))
        for pair in range(rows_y // 2):
            sides = [(part_x * part_yz[2 * pair + half]).astype(BF16) for half in (0, 1)]
            term = mul(jnp.concatenate(sides, axis=1), lat[x * (rows_y // 2) + pair], NT)
            total = term if total is None else total + term
    return total.astype(BF16), base_x, base_y, base_z, frac


def folded(value):
    return jnp.sum(value.reshape(value.shape[0] // 8, 8, value.shape[1]), axis=0)


def main_kernel(
    plan,
    place_ref,
    lat,
    words_ref,
    small_ref,
    w_latent_hbm,
    w_pos_hbm,
    w_mid_hbm,
    w_out_hbm,
    send_ref,
    keep_ref,
    code,
    pos,
    z_one,
    one_high,
    one_low,
    mixed,
    two_high,
    two_low,
    back,
    mixed_back,
    first_high,
    first_low,
    sums_ref,
    d_both,
    out_t,
    d_out_t,
    packed,
    mid_high,
    mid_low,
    w_latent_ref,
    w_pos_ref,
    w_mid_ref,
    w_out_ref,
    sems,
):
    rows = plan.tiles * plan.slots
    hidden = w_mid_ref.shape[0]
    latents = w_latent_ref.shape[0]
    weights = fetches(
        (w_latent_hbm, w_pos_hbm, w_mid_hbm, w_out_hbm),
        (w_latent_ref, w_pos_ref, w_mid_ref, w_out_ref),
        sems,
    )
    planes, rows_z = plan.planes, lat.shape[2] // 2
    rows_y = lat.shape[0] // (planes + 1) * 2
    slots = rows // plan.tiles
    my_block = place_ref[0]
    my_tile = place_ref[1]
    my_replica = place_ref[2]
    always = my_tile >= 0

    words = words_ref[...]
    words = jnp.concatenate(
        [words] + [pltpu.roll(words, LANES - 16 * group, 1) for group in range(1, slots // 8)], axis=0
    )
    interp, base_x, base_y, base_z, frac = interpolate(words, lat, planes, rows_y, rows_z)
    code[...] = interp
    global_x = my_tile * planes + base_x
    lane = lax.broadcasted_iota(jnp.int32, (rows, LANES), 1)
    pos[...] = jnp.where(
        lane == 0,
        (global_x.astype(F32) + frac[0]) / (planes * plan.tiles),
        jnp.where(
            lane == 1,
            (base_y.astype(F32) + frac[1]) / rows_y,
            (base_z.astype(F32) + frac[2]) / rows_z,
        ),
    )

    for copy in weights:
        copy.wait()
    high, low = halves(w_latent_ref[...])
    z_one[...] = mul(interp, high) + mul(interp, low)
    high, low = halves(w_mid_ref[...])
    mid_high[...] = high
    mid_low[...] = low
    w_pos = [w_pos_ref[d : d + 1, :] for d in range(3)]
    square = w_pos[0] * w_pos[0] + w_pos[1] * w_pos[1] + w_pos[2] * w_pos[2]
    bias_one = small_ref[0:1, :]
    bias_two = small_ref[1:2, :]

    part_rows = rows // 2

    def at(part, index, block=None):
        first = (part * 5 + index) * part_rows
        if block is None:
            return slice(first, first + part_rows)
        return slice(first + block * BLOCK, first + (block + 1) * BLOCK)

    def rows_at(part, block):
        first = part * part_rows + block * BLOCK
        return slice(first, first + BLOCK)

    def store(refs, span, value):
        high, low = halves(value)
        refs[0][span, :] = high
        refs[1][span, :] = low

    def layer_one(part):
        refs = (one_high, one_low)
        for block in range(part_rows // BLOCK):
            here = rows_at(part, block)
            where = pos[here, :]
            pre = (
                z_one[here, :]
                + (where[:, 0:1] * w_pos[0] + where[:, 1:2] * w_pos[1] + where[:, 2:3] * w_pos[2])
                + bias_one
            )
            act = jnp.tanh(pre)
            slope = 1.0 - act * act
            curve = -2.0 * act * slope
            z_one[here, :] = act
            store(refs, at(part, 0, block), act)
            for d in range(3):
                store(refs, at(part, 1 + d, block), slope * w_pos[d])
            store(refs, at(part, 4, block), curve * square)

    def times_mid(dims, source, result, part):
        span = slice(part * 5 * part_rows, (part + 1) * 5 * part_rows)
        left = (source[0][span, :], source[1][span, :])
        result[span, :] = mul3(left, (mid_high[...], mid_low[...]), dims)

    def layer_two(part):
        refs = (two_high, two_low)
        for block in range(part_rows // BLOCK):
            act = jnp.tanh(mixed[at(part, 0, block), :] + bias_two)
            slope = 1.0 - act * act
            curve = -2.0 * act * slope
            store(refs, at(part, 0, block), act)
            mixed[at(part, 0, block), :] = act
            norm = None
            for d in range(3):
                tangent = mixed[at(part, 1 + d, block), :]
                store(refs, at(part, 1 + d, block), slope * tangent)
                norm = tangent * tangent if norm is None else norm + tangent * tangent
            store(refs, at(part, 4, block), slope * mixed[at(part, 4, block), :] + curve * norm)

    out_fields = jnp.concatenate([w_out_ref[...], jnp.zeros((3, hidden), F32)], axis=0)
    wo_high, wo_low = halves(out_fields)
    wo_three = jnp.concatenate([out_fields, wo_low.astype(F32), out_fields], axis=0).astype(BF16)
    wo_both = jnp.concatenate(
        [out_fields, wo_low.astype(F32), jnp.zeros((LANES - 16, hidden), F32)], axis=0
    ).astype(BF16)

    def outputs(part):
        span = slice(part * 5 * part_rows, (part + 1) * 5 * part_rows)
        both = mul(two_high[span, :], wo_both, NT)
        low = mul(two_low[span, :], wo_both, NT)
        for s in range(5):
            rows_s = slice(s * part_rows, (s + 1) * part_rows)
            both_t, low_t = both[rows_s].T, low[rows_s].T
            out_t[8 * s : 8 * s + 8, part * part_rows : (part + 1) * part_rows] = (
                both_t[0:8] + both_t[8:16] + low_t[0:8]
            )

    @pl.when(always)
    def _():
        layer_one(0)
        times_mid(NN, (one_high, one_low), mixed, 0)
        layer_one(1)
        times_mid(NN, (one_high, one_low), mixed, 1)
        layer_two(0)
        outputs(0)
        layer_two(1)
        outputs(1)

    words_t = words.T
    target = [words_t[4 + f : 5 + f, :] for f in range(5)]
    valid = words_t[9:10, :]
    value = [out_t[f : f + 1, :] + small_ref[2:3, f : f + 1] for f in range(5)]
    grad = [[out_t[8 * (d + 1) + f : 8 * (d + 1) + f + 1, :] for f in range(5)] for d in range(3)]
    laplace = [out_t[32 + f : 33 + f, :] for f in range(5)]
    velocity = value[2:5]
    advection = [
        velocity[0] * grad[0][f] + velocity[1] * grad[1][f] + velocity[2] * grad[2][f] for f in range(5)
    ]
    continuity = grad[0][2] + grad[1][3] + grad[2][4]
    momentum = [advection[2 + j] + grad[j][1] - VISCOSITY * laplace[2 + j] for j in range(3)]
    momentum[2] = momentum[2] - value[0]
    energy = advection[0] - DIFFUSIVITY * laplace[0]
    misfit = [value[f] - target[f] for f in range(5)]
    physics = (
        continuity * continuity
        + (momentum[0] * momentum[0] + momentum[1] * momentum[1] + momentum[2] * momentum[2])
        + energy * energy
    )
    squares = (
        misfit[0] * misfit[0]
        + misfit[1] * misfit[1]
        + misfit[2] * misfit[2]
        + misfit[3] * misfit[3]
        + misfit[4] * misfit[4]
    )
    point_loss = valid * (squares + RESIDUAL_WEIGHT * physics) * (1.0 / plan.query_total)

    rate = valid * (1.0 / plan.query_total)
    twice = RESIDUAL_WEIGHT * 2.0
    d_cont = rate * twice * continuity
    d_mom = [rate * twice * m for m in momentum]
    d_energy = rate * twice * energy
    d_value = [2.0 * rate * m for m in misfit]
    for d in range(3):
        d_value[2 + d] = d_value[2 + d] + (
            d_mom[0] * grad[d][2] + d_mom[1] * grad[d][3] + d_mom[2] * grad[d][4] + d_energy * grad[d][0]
        )
    d_value[0] = d_value[0] - d_mom[2]
    d_out_t[...] = jnp.zeros_like(d_out_t)
    for f in range(5):
        d_out_t[f : f + 1, :] = d_value[f]
    for d in range(3):
        first = 8 * (d + 1)
        d_out_t[first : first + 1, :] = d_energy * velocity[d]
        d_out_t[first + 1 : first + 2, :] = d_mom[d]
        for j in range(3):
            term = d_mom[j] * velocity[d]
            if j == d:
                term = term + d_cont
            d_out_t[first + 2 + j : first + 3 + j, :] = term
    d_out_t[32:33, :] = -DIFFUSIVITY * d_energy
    for j in range(3):
        d_out_t[34 + j : 35 + j, :] = -VISCOSITY * d_mom[j]

    def out_back(part):
        columns = slice(part * part_rows, (part + 1) * part_rows)
        wanted = jnp.concatenate([d_out_t[8 * s : 8 * s + 8, columns] for s in range(5)], axis=1)
        do_low = halves(wanted)[1].astype(F32)
        wanted = jnp.concatenate([wanted, wanted, do_low], axis=0).astype(BF16)
        back[part * 5 * part_rows : (part + 1) * 5 * part_rows, :] = mul(wanted, wo_three, TN)

    def second_back(part, total):
        refs = (d_both.at[:, :hidden], d_both.at[:, hidden:])
        for block in range(part_rows // BLOCK):
            act = mixed[at(part, 0, block), :]
            slope = 1.0 - act * act
            curve = -2.0 * act * slope
            cot_l = back[at(part, 4, block), :]
            d_slope = cot_l * mixed[at(part, 4, block), :]
            norm = None
            bent = 2.0 * curve * cot_l
            for d in range(3):
                tangent = mixed[at(part, 1 + d, block), :]
                cot_t = back[at(part, 1 + d, block), :]
                store(refs, at(part, 1 + d, block), slope * cot_t + bent * tangent)
                d_slope = d_slope + cot_t * tangent
                norm = tangent * tangent if norm is None else norm + tangent * tangent
            store(refs, at(part, 4, block), slope * cot_l)
            d_curve = cot_l * norm
            d_slope = d_slope - 2.0 * act * d_curve
            d_act = back[at(part, 0, block), :] - 2.0 * slope * d_curve - 2.0 * act * d_slope
            d_pre = slope * d_act
            store(refs, at(part, 0, block), d_pre)
            total = total + folded(d_pre)
        return total

    def first_back(part, sums):
        for block in range(part_rows // BLOCK):
            here = rows_at(part, block)
            act = z_one[here, :]
            slope = 1.0 - act * act
            curve = -2.0 * act * slope
            where = pos[here, :]
            cot_t = [mixed_back[at(part, 1 + d, block), :] for d in range(3)]
            cot_l = mixed_back[at(part, 4, block), :]
            d_curve = cot_l * square
            d_slope = cot_t[0] * w_pos[0] + cot_t[1] * w_pos[1] + cot_t[2] * w_pos[2] - 2.0 * act * d_curve
            d_act = mixed_back[at(part, 0, block), :] - 2.0 * slope * d_curve - 2.0 * act * d_slope
            d_pre = slope * d_act
            high, low = halves(d_pre)
            first_high[here, :] = high
            first_low[here, :] = low
            sums = (
                [sums[0] + folded(d_pre)]
                + [sums[1 + d] + folded(where[:, d : d + 1] * d_pre + slope * cot_t[d]) for d in range(3)]
                + [sums[4] + folded(curve * cot_l)]
            )
        return sums


    def put(part, first, value):
        while value.shape[0]:
            block, row = first // plan.main_rows, first % plan.main_rows
            count = min(value.shape[0], plan.main_rows - row)
            packed[2 * part + block, row : row + count, :] = value[:count]
            first, value = first + count, value[count:]

    def mid_gradient():
        both = mul(one_high[...], d_both[...], TN)
        both = both[:, :hidden] + both[:, hidden:] + mul(one_low[...], d_both[:, :hidden], TN)
        for part in range(hidden // LANES):
            put(part, 0, both[:, part * LANES : (part + 1) * LANES])

    @pl.when(always)
    def _():
        out_back(0)
        total = second_back(0, jnp.zeros((8, hidden), F32))
        out_back(1)
        times_mid(NT, (d_both.at[:, :hidden], d_both.at[:, hidden:]), mixed_back, 0)
        sums_ref[5] = second_back(1, total)
        times_mid(NT, (d_both.at[:, :hidden], d_both.at[:, hidden:]), mixed_back, 1)
        total = first_back(0, [jnp.zeros((8, hidden), F32)] * 5)
        mid_gradient()
        for number, value in enumerate(first_back(1, total)):
            sums_ref[number] = value

    sums = [sums_ref[number] for number in range(6)]
    d_square = jnp.sum(sums[4], axis=0, keepdims=True)
    grad_latent = mul(code[...], first_high[...], TN) + mul(code[...], first_low[...], TN)

    parts = [d_out_t[8 * s : 8 * s + 8, p * part_rows : (p + 1) * part_rows] for p in range(2) for s in range(5)]
    flat = jnp.concatenate(parts, axis=1)
    fl_high, fl_low = halves(flat)
    fl_both = jnp.concatenate([flat, fl_low.astype(F32)], axis=0).astype(BF16)
    grad_out = mul(fl_both, two_high[...])
    grad_out = grad_out[:8] + grad_out[8:] + mul(fl_high, two_low[...])

    lane_row = lax.broadcasted_iota(jnp.int32, (1, hidden), 1)
    last = jnp.where(lane_row == 5, jnp.sum(point_loss), 0.0)
    for f in range(5):
        last = last + jnp.where(lane_row == f, jnp.sum(d_value[f]), 0.0)
    grad_pos = [jnp.sum(sums[1 + d], axis=0, keepdims=True) + 2.0 * w_pos[d] * d_square for d in range(3)]
    misc = grad_pos + [
        jnp.sum(sums[0], axis=0, keepdims=True),
        jnp.sum(sums[5], axis=0, keepdims=True),
        last,
    ]
    misc = jnp.concatenate(misc + [jnp.zeros((2, hidden), F32)], axis=0)
    for part in range(hidden // LANES):
        lanes = slice(part * LANES, (part + 1) * LANES)
        put(part, hidden, grad_latent[:, lanes])
        packed[2 * part, plan.coded_rows :, :] = misc[:, lanes]
        packed[2 * part + 1, plan.coded_rows :, :] = grad_out[:, lanes]

    chosen = jnp.where(
        lane == jnp.broadcast_to(words[:, 10:11], (rows, LANES)).astype(jnp.int32), words[:, 9:10], 0.0
    ).astype(BF16)
    fields = jnp.concatenate(value + [jnp.zeros((3, rows), F32)], axis=0)
    source = (lax.broadcasted_iota(jnp.int32, (8, rows), 1) & (plan.tiles * 8 - 1)) >> 3
    spread = jnp.concatenate([jnp.where(source == t, fields, 0.0) for t in range(plan.tiles)], axis=0)
    high, middle, low = thirds(spread)
    spread = mul(high, chosen) + mul(middle, chosen) + mul(low, chosen)
    packed[:, plan.main_rows : plan.coded_rows, :] = jnp.zeros((8, plan.devices, LANES), F32)
    for t in range(plan.tiles):
        row = plan.main_rows + (my_replica * (plan.tiles // 8) + t // 8) * 8
        packed[t % 8, pl.ds(pl.multiple_of(row, 8), 8), :] = spread[8 * t : 8 * t + 8]

    for block in range(8):
        spot = jnp.bitwise_xor(block, my_block) & 3

        @pl.when((my_block >> 2) == block // 4)
        def _():
            keep_ref[spot] = packed[block]

        @pl.when((my_block >> 2) != block // 4)
        def _():
            encode(plan, lambda start, count: packed[block, start : start + count, :], send_ref.at[spot])


class Plan:
    def __init__(self, tiles, replicas, queries, planes, hidden, latents):
        self.tiles, self.replicas, self.planes = tiles, replicas, planes
        self.slots = 2 * queries // tiles
        self.devices = tiles * replicas
        self.query_total = float(queries * self.devices)
        self.main_rows = (hidden + latents) // 2
        self.coded_rows = self.main_rows + self.devices
        self.rows = self.coded_rows + 8
        self.scales = -(-(self.coded_rows // SUB + 1) // 16) * 16
        self.sent_rows = self.coded_rows + 16 + self.scales
        top = self.devices.bit_length() - 1
        self.core, self.plane, self.rest = [0], [1, top - 1], list(range(2, top - 1))

    def mask(self, bits, steps):
        return sum(1 << bit for number, bit in enumerate(bits) if steps >> number & 1)

    def my_block(self, device):
        return (device & 1) * 4 + (device >> 1 & 1) + 2 * (device >> self.plane[1] & 1)


def swapped(value, plan, bits, steps):
    mask = plan.mask(bits, steps)
    return lax.ppermute(value, ("replica", "tile"), [(i, i ^ mask) for i in range(plan.devices)])


def encode(plan, read, out_ref):
    starts = list(range(0, plan.coded_rows, SUB))
    parts = [read(start, SUB) for start in starts] + [read(plan.coded_rows, 8)]
    tops = [jnp.max(jnp.abs(part), axis=0, keepdims=True) for part in parts]
    tops = tops + [jnp.zeros_like(tops[0])] * (plan.scales - len(tops))
    power = jnp.floor(jnp.log2(jnp.maximum(jnp.concatenate(tops, axis=0), 1e-30)))
    scale = jnp.exp2(14.0 - power)

    def whole(value):
        return jnp.clip(jnp.round(value), -32767.0, 32767.0)

    def narrow(value):
        return value.astype(jnp.int32).astype(jnp.int16)

    for number, start in enumerate(starts):
        out_ref[start : start + SUB, :] = narrow(whole(parts[number] * scale[number : number + 1]))
    last = len(starts)
    exact = parts[last] * scale[last : last + 1]
    high = whole(exact)
    low = whole((exact - high) * 32768.0)
    out_ref[plan.coded_rows : plan.coded_rows + 16, :] = narrow(jnp.concatenate([high, low], axis=0))
    out_ref[plan.coded_rows + 16 :, :] = narrow(power)


def decoder(plan, ref):
    def widen(value):
        return value.astype(jnp.int32).astype(F32)

    scale = jnp.exp2(widen(ref[plan.coded_rows + 16 :, :]) - 14.0)

    def read(start, count):
        if start < plan.coded_rows:
            number = start // SUB
            return widen(ref[start : start + count, :]) * scale[number : number + 1]
        both = widen(ref[plan.coded_rows : plan.coded_rows + 16, :])
        number = plan.coded_rows // SUB
        return (both[:8] + both[8:] * (1.0 / 32768.0)) * scale[number : number + 1]

    return read


def added(readers):
    def read(start, count):
        total = readers[0](start, count)
        for reader in readers[1:]:
            total = total + reader(start, count)
        return total

    return read


def first_kernel(plan, numbers, keep_ref, got_ref, *refs):
    def reader(block):
        got = decoder(plan, got_ref.at[block])
        return lambda start, count: keep_ref[block, start : start + count, :] + got(start, count)

    for number, out_ref in zip(numbers, refs):
        if number:
            encode(plan, reader(number), out_ref)
        else:
            read = reader(0)
            for start in range(0, plan.coded_rows, SUB):
                out_ref[start : start + SUB, :] = read(start, SUB)
            out_ref[plan.coded_rows :, :] = read(plan.coded_rows, 8)


def first_sum(keep, got, numbers, plan):
    sent = jax.ShapeDtypeStruct((plan.sent_rows, LANES), jnp.int16)
    own = jax.ShapeDtypeStruct(keep.shape[1:], F32)
    return pl.pallas_call(
        functools.partial(first_kernel, plan, numbers),
        out_shape=tuple(sent if number else own for number in numbers),
        in_specs=[VMEM] * 2,
        out_specs=tuple([VMEM] * len(numbers)),
        compiler_params=pltpu.CompilerParams(vmem_limit_bytes=6 << 20),
        name="sum_core",
    )(keep, got)


def plane_kernel(plan, mine_ref, *refs):
    readers = [lambda start, count: mine_ref[start : start + count, :]]
    encode(plan, added(readers + [decoder(plan, ref) for ref in refs[:-1]]), refs[-1])


def pair_kernel(plan, mine_ref, other_ref, out_ref):
    encode(plan, added([decoder(plan, mine_ref), decoder(plan, other_ref)]), out_ref)


def coded_sum(kernel, blocks, plan, name):
    return pl.pallas_call(
        functools.partial(kernel, plan),
        out_shape=jax.ShapeDtypeStruct((plan.sent_rows, LANES), jnp.int16),
        in_specs=[VMEM] * len(blocks),
        out_specs=VMEM,
        compiler_params=pltpu.CompilerParams(vmem_limit_bytes=4 << 20),
        name=name,
    )(*blocks)


def main(place, lat, words, small, weights, plan):
    rows = plan.tiles * plan.slots
    hidden = weights[2].shape[0]
    channels = lat.shape[1]
    outs = jax.ShapeDtypeStruct((4, plan.rows, LANES), F32)
    wide = lambda kind: pltpu.VMEM((5 * rows, hidden), kind)
    return pl.pallas_call(
        functools.partial(main_kernel, plan),
        out_shape=(jax.ShapeDtypeStruct((4, plan.sent_rows, LANES), jnp.int16), outs),
        in_specs=[SMEM] + [VMEM] * 3 + [HBM] * 4,
        out_specs=(VMEM, VMEM),
        scratch_shapes=[
            pltpu.VMEM((rows, channels), BF16),
            pltpu.VMEM((rows, LANES), F32),
            pltpu.VMEM((rows, hidden), F32),
            wide(BF16),
            wide(BF16),
            wide(F32),
            wide(BF16),
            wide(BF16),
            wide(F32),
            wide(F32),
            pltpu.VMEM((rows, hidden), BF16),
            pltpu.VMEM((rows, hidden), BF16),
            pltpu.VMEM((6, 8, hidden), F32),
            pltpu.VMEM((5 * rows, 2 * hidden), BF16),
            pltpu.VMEM((40, rows), F32),
            pltpu.VMEM((40, rows), F32),
            pltpu.VMEM((8, plan.rows, LANES), F32),
            pltpu.VMEM((hidden, hidden), BF16),
            pltpu.VMEM((hidden, hidden), BF16),
        ]
        + [pltpu.VMEM(weight.shape, F32) for weight in weights]
        + [pltpu.SemaphoreType.DMA((4,))],
        compiler_params=pltpu.CompilerParams(vmem_limit_bytes=32 << 20),
        name="encode_decode",
    )(place, lat, words, small, *weights)


def unpack_kernel(plan, place_ref, *refs):
    sources, outs, packed = refs[:8], refs[8:-1], refs[-1]
    prediction_ref, latent_ref, pos_ref, one_ref, mid_ref, two_ref, out_ref, bias_out_ref, loss_ref = outs
    my_block = place_ref[0]
    device = place_ref[2] * plan.tiles + place_ref[1]
    starts = list(range(0, plan.coded_rows, SUB))
    for number, ref in enumerate(sources):
        read = decoder(plan, ref)
        block = jnp.bitwise_xor(number, my_block)
        for start in starts:
            packed[block, start : start + SUB, :] = read(start, SUB)
        packed[block, plan.coded_rows :, :] = read(plan.coded_rows, 8)

    hidden = mid_ref.shape[0]
    latents = latent_ref.shape[0]
    split = plan.main_rows
    for part in range(hidden // LANES):
        lanes = slice(part * LANES, (part + 1) * LANES)
        mid_ref[0:split, lanes] = packed[2 * part, 0:split, :]
        mid_ref[split:, lanes] = packed[2 * part + 1, 0 : hidden - split, :]
        latent_ref[:, lanes] = packed[2 * part + 1, hidden - split : split, :]
        misc = packed[2 * part, plan.coded_rows :, :]
        pos_ref[:, lanes] = misc[0:3]
        one_ref[:, lanes] = misc[3:4]
        two_ref[:, lanes] = misc[4:5]
        out_ref[:, lanes] = packed[2 * part + 1, plan.coded_rows : plan.coded_rows + 5, :]
        if part == 0:
            bias_out_ref[...] = misc[5:6, 0:5]
            loss_ref[...] = misc[5:6, 5:6]
    row = pl.multiple_of(plan.main_rows + (device >> 3) * 8, 8)
    fields = packed[device & 7, pl.ds(row, 8), :]
    for f in range(5):
        prediction_ref[f] = fields[f : f + 1]


def unpack(place, blocks, plan, hidden, latents):
    shapes = [
        (5, 1, LANES),
        (latents, hidden),
        (3, hidden),
        (1, hidden),
        (hidden, hidden),
        (1, hidden),
        (5, hidden),
        (1, 5),
        (1, 1),
    ]
    return pl.pallas_call(
        functools.partial(unpack_kernel, plan),
        out_shape=tuple(jax.ShapeDtypeStruct(shape, F32) for shape in shapes),
        in_specs=[SMEM] + [VMEM] * 8,
        out_specs=tuple([VMEM] * len(shapes)),
        scratch_shapes=[pltpu.VMEM((8, plan.rows, LANES), F32)],
        compiler_params=pltpu.CompilerParams(vmem_limit_bytes=16 << 20),
        name="unpack",
    )(place, *blocks)


def body(
    fields,
    convolution_weight,
    convolution_bias,
    query_owner,
    query_cell,
    query_frac,
    target,
    w_latent,
    w_pos,
    bias_one,
    w_mid,
    bias_two,
    w_out,
    bias_out,
):
    tiles = lax.axis_size("tile")
    replicas = lax.axis_size("replica")
    my_tile = lax.axis_index("tile")
    my_replica = lax.axis_index("replica")
    channels = fields.shape[1]
    queries = query_cell.shape[1]
    hidden = w_mid.shape[0]
    plan = Plan(tiles, replicas, queries, fields.shape[2], hidden, channels)
    device = my_replica * tiles + my_tile
    place = jnp.stack([plan.my_block(device), my_tile, my_replica]).astype(jnp.int32)

    here = fields[0].transpose(1, 2, 0, 3)
    up = [(i, (i + 1) % tiles) for i in range(tiles)]
    down = [((i + 1) % tiles, i) for i in range(tiles)]
    to_left, to_right, query_owner = lax.optimization_barrier(
        (here[: DILATION_RATE + 1], here[-DILATION_RATE:], query_owner)
    )
    right = lax.ppermute(to_left, "tile", down)
    left = lax.ppermute(to_right, "tile", up)
    words, small = route(
        (query_owner[:, :, 0], query_cell, query_frac.transpose(1, 0, 2), target.transpose(1, 0, 2)),
        (bias_one[None], bias_two[None], bias_out[None], convolution_bias[None]),
        tiles,
        plan.slots,
    )
    words = lax.all_to_all(
        words.reshape(tiles, 8, WORDS), "tile", split_axis=0, concat_axis=0, tiled=True
    ).reshape(tiles * 8, WORDS)

    lat = convolve(left, here, right, convolution_weight, small)
    weights = (w_latent, w_pos, w_mid, w_out)
    send, keep = main(place, lat, words, small, weights, plan)

    got = swapped(send, plan, plan.core, 1)
    (far,) = first_sum(keep, got, (3,), plan)
    far, keep = lax.optimization_barrier((far, keep))
    mine, *near = first_sum(keep, got, (0, 1, 2), plan)
    arrived = [swapped(block, plan, plan.plane, step) for step, block in ((3, far), (1, near[0]), (2, near[1]))]
    block = coded_sum(plane_kernel, [mine] + arrived, plan, "sum_plane")
    for bit in plan.rest:
        block = coded_sum(pair_kernel, [block, swapped(block, plan, [bit], 1)], plan, "sum_line")
    blocks = [block] + [swapped(block, plan, plan.plane, step) for step in range(1, 4)]
    blocks = blocks + [swapped(block, plan, plan.core, 1) for block in blocks]
    prediction, g_latent, g_pos, g_one, g_mid, g_two, g_out, g_bias, loss = unpack(
        place, blocks, plan, hidden, channels
    )
    return (
        prediction.transpose(1, 0, 2),
        g_latent,
        g_pos,
        g_one.reshape(hidden),
        g_mid,
        g_two.reshape(hidden),
        g_out,
        g_bias.reshape(5),
        loss.reshape(()),
    )


def solution(mesh):
    return jax.shard_map(
        body,
        mesh=mesh,
        in_specs=(
            P("replica", None, "tile", None, None),
            P(),
            P(),
            P("replica", "tile", None),
            P("replica", "tile"),
            P("replica", None, "tile"),
            P("replica", None, "tile"),
            P(),
            P(),
            P(),
            P(),
            P(),
            P(),
            P(),
        ),
        out_specs=(P("replica", None, "tile"), P(), P(), P(), P(), P(), P(), P(), P()),
        check_vma=False,
    )
```

```python
import functools

import jax
import jax.numpy as jnp
from jax import lax
from jax.experimental import pallas as pl
from jax.experimental.pallas import tpu as pltpu
from jax.sharding import PartitionSpec as P

DILATION_RATE = 2
VISCOSITY = 0.05
DIFFUSIVITY = 0.05
RESIDUAL_WEIGHT = 0.5

F32 = jnp.float32
BF16 = jnp.bfloat16
LANES = 128
BLOCK = 32
WORDS = 128
SUB = 32
NN = (((1,), (0,)), ((), ()))
NT = (((1,), (1,)), ((), ()))
TN = (((0,), (0,)), ((), ()))
VMEM = pl.BlockSpec(memory_space=pltpu.VMEM)
SMEM = pl.BlockSpec(memory_space=pltpu.SMEM)
HBM = pl.BlockSpec(memory_space=pltpu.HBM)


def mul(left, right, dims=NN):
    return lax.dot_general(left, right, dims, preferred_element_type=F32)


def halves(value):
    high = value.astype(BF16)
    return high, (value - high.astype(F32)).astype(BF16)


def thirds(value):
    high = value.astype(BF16)
    rest = value - high.astype(F32)
    middle = rest.astype(BF16)
    return high, middle, (rest - middle.astype(F32)).astype(BF16)


def mul3(left, right, dims=NN):
    return mul(left[0], right[0], dims) + mul(left[0], right[1], dims) + mul(left[1], right[0], dims)


def fetches(sources, targets, sems):
    copies = [
        pltpu.make_async_copy(source, target, sems.at[number])
        for number, (source, target) in enumerate(zip(sources, targets))
    ]
    for copy in copies:
        copy.start()
    return copies


def route_kernel(tiles, slots, *refs):
    out_ref, small_ref, *scratch, words, sems = refs[8:]
    for copy in fetches(refs[:8], scratch, sems):
        copy.wait()
    owner_ref, cell_ref, frac_ref, target_ref, *bias_refs = scratch
    queries = owner_ref.shape[1]
    small_ref[...] = jnp.zeros_like(small_ref)
    for number, ref in enumerate(bias_refs):
        small_ref[number : number + 1, 0 : ref.shape[1]] = ref[...]
    owner = owner_ref[...]
    hits = (lax.broadcasted_iota(jnp.int32, (tiles, queries), 0) == owner).astype(F32)
    before = lax.broadcasted_iota(jnp.int32, (queries, queries), 0) < lax.broadcasted_iota(
        jnp.int32, (queries, queries), 1
    )
    earlier = mul(hits.astype(BF16), before.astype(F32).astype(BF16))
    slot = jnp.sum(hits * earlier, axis=0, keepdims=True)
    place = owner * slots + slot.astype(jnp.int32)
    spot = lax.broadcasted_iota(jnp.int32, (tiles * 8, queries), 0)
    spot = (spot >> 3) * slots + (spot & 7)
    groups = slots // 8
    chosen = [jnp.where(spot + 8 * group == place, 1.0, 0.0) for group in range(groups)]
    chosen = jnp.concatenate(chosen, axis=1).astype(BF16)
    words[...] = jnp.zeros_like(words)
    for group in range(groups):
        row, lanes = 16 * group, slice(group * queries, (group + 1) * queries)
        words[row : row + 1, lanes] = cell_ref[...].astype(F32)
        for d in range(3):
            words[row + 1 + d : row + 2 + d, lanes] = frac_ref[d]
        for f in range(5):
            words[row + 4 + f : row + 5 + f, lanes] = target_ref[f]
        words[row + 9 : row + 10, lanes] = jnp.ones((1, queries), F32)
        words[row + 10 : row + 11, lanes] = lax.broadcasted_iota(jnp.int32, (1, queries), 1).astype(F32)
    high, middle, low = thirds(words[...])
    out_ref[...] = mul(chosen, high, NT) + mul(chosen, middle, NT) + mul(chosen, low, NT)


def route(inputs, biases, tiles, slots):
    queries = inputs[0].shape[1]
    arrays = inputs + biases
    return pl.pallas_call(
        functools.partial(route_kernel, tiles, slots),
        out_shape=(
            jax.ShapeDtypeStruct((tiles * 8, WORDS), F32),
            jax.ShapeDtypeStruct((8, biases[0].shape[1]), F32),
        ),
        in_specs=[HBM] * 8,
        out_specs=(VMEM, VMEM),
        scratch_shapes=[pltpu.VMEM(array.shape, array.dtype) for array in arrays]
        + [pltpu.VMEM((WORDS, queries * (slots // 8)), F32), pltpu.SemaphoreType.DMA((8,))],
        compiler_params=pltpu.CompilerParams(vmem_limit_bytes=4 << 20),
        name="route",
    )(*arrays)


def tap_sum(weight_ref, planes, pair):
    total = None
    for step_x, ref, index in planes:
        rows_y = ref.shape[1]
        blocks = [
            jnp.concatenate([ref[index, (2 * pair + half + step_y) % rows_y] for half in (0, 1)], axis=1)
            for step_y in (-1, 0, 1)
        ]
        term = mul(weight_ref[step_x], jnp.concatenate(blocks, axis=0))
        total = term if total is None else total + term
    channels = total.shape[0] // 3
    sides = []
    for half in (0, 1):
        part = total[:, half * LANES : (half + 1) * LANES]
        sides.append(
            part[channels : 2 * channels]
            + pltpu.roll(part[:channels], 1, 1)
            + pltpu.roll(part[2 * channels :], LANES - 1, 1)
        )
    return jnp.concatenate(sides, axis=1)


def conv_kernel(
    place_ref,
    near_ref,
    here_ref,
    far_ref,
    taps_ref,
    small_ref,
    lat_ref,
    weight_ref,
):
    planes, rows_y, channels = here_ref.shape[:3]
    taps = taps_ref[...].astype(F32)
    for step in range(3):
        rows = []
        for step_z in range(3):
            numbers = [9 * step + 3 * step_y + step_z for step_y in range(3)]
            rows.append(
                jnp.concatenate([taps[:, n * channels : (n + 1) * channels] for n in numbers], axis=1)
            )
        weight_ref[step] = jnp.concatenate(rows, axis=0).astype(BF16)
    diagonal = lax.broadcasted_iota(jnp.int32, (channels, channels), 0) == lax.broadcasted_iota(
        jnp.int32, (channels, channels), 1
    )
    bias = jnp.sum(jnp.where(diagonal, small_ref[3:4, 0:channels], 0.0), axis=1, keepdims=True)
    def all_planes(left_ref, right_ref):
        for x in range(planes + 1):
            taps = []
            for step in range(3):
                plane = x + DILATION_RATE * (step - 1)
                if plane < 0:
                    taps.append((step, left_ref, plane + left_ref.shape[0]))
                elif plane >= planes:
                    taps.append((step, right_ref, plane - planes))
                else:
                    taps.append((step, here_ref, plane))
            for pair in range(rows_y // 2):
                summed = tap_sum(weight_ref, taps, pair) + bias
                lat_ref[x * (rows_y // 2) + pair] = jax.nn.gelu(summed).astype(BF16)

    even = (place_ref[1] & 1) == 0

    @pl.when(even)
    def _():
        all_planes(far_ref, near_ref)

    @pl.when(jnp.logical_not(even))
    def _():
        all_planes(near_ref, far_ref)


def convolve(place, near, here, far, taps, small):
    planes, rows_y, channels, rows_z = here.shape
    pairs = (planes + 1) * rows_y // 2
    return pl.pallas_call(
        conv_kernel,
        out_shape=jax.ShapeDtypeStruct((pairs, channels, 2 * rows_z), BF16),
        in_specs=[SMEM] + [VMEM] * 5,
        out_specs=VMEM,
        scratch_shapes=[pltpu.VMEM((3, 3 * channels, 3 * channels), BF16)],
        compiler_params=pltpu.CompilerParams(vmem_limit_bytes=8 << 20),
        cost_estimate=pl.CostEstimate(flops=3 << 30, bytes_accessed=4 << 20, transcendentals=0),
        name="convolve",
    )(place, near, here, far, taps, small)


def interpolate(words, lat, planes, rows_y, rows_z):
    rows = words.shape[0]
    cell = jnp.broadcast_to(words[:, 0:1], (rows, LANES)).astype(jnp.int32)
    frac = [jnp.broadcast_to(words[:, 1 + d : 2 + d], (rows, LANES)) for d in range(3)]
    shift_z = rows_z.bit_length() - 1
    shift_y = rows_y.bit_length() - 1
    base_x = cell >> (shift_z + shift_y)
    base_y = (cell >> shift_z) & (rows_y - 1)
    base_z = cell & (rows_z - 1)
    spot = lax.broadcasted_iota(jnp.int32, (rows, rows_z), 1)
    part_z = jnp.where(spot == base_z, 1.0 - frac[2], 0.0) + jnp.where(
        spot == ((base_z + 1) & (rows_z - 1)), frac[2], 0.0
    )
    part_yz = []
    for y in range(rows_y):
        part_y = jnp.where(
            base_y == y, 1.0 - frac[1], jnp.where(base_y == (y - 1) % rows_y, frac[1], 0.0)
        )
        part_yz.append(part_y * part_z)
    total = None
    for x in range(planes + 1):
        part_x = jnp.where(base_x == x, 1.0 - frac[0], jnp.where(base_x == x - 1, frac[0], 0.0))
        for pair in range(rows_y // 2):
            sides = [(part_x * part_yz[2 * pair + half]).astype(BF16) for half in (0, 1)]
            term = mul(jnp.concatenate(sides, axis=1), lat[x * (rows_y // 2) + pair], NT)
            total = term if total is None else total + term
    return total.astype(BF16), base_x, base_y, base_z, frac


def folded(value):
    return jnp.sum(value.reshape(value.shape[0] // 8, 8, value.shape[1]), axis=0)


def main_kernel(
    plan,
    place_ref,
    lat,
    words_ref,
    small_ref,
    w_latent_hbm,
    w_pos_hbm,
    w_mid_hbm,
    w_out_hbm,
    send_ref,
    keep_ref,
    code,
    pos,
    z_one,
    one_high,
    one_low,
    mixed,
    two_high,
    two_low,
    back,
    mixed_back,
    first_high,
    first_low,
    sums_ref,
    d_both,
    out_t,
    d_out_t,
    packed,
    mid_high,
    mid_low,
    w_latent_ref,
    w_pos_ref,
    w_mid_ref,
    w_out_ref,
    sems,
):
    rows = plan.tiles * plan.slots
    hidden = w_mid_ref.shape[0]
    latents = w_latent_ref.shape[0]
    weights = fetches(
        (w_latent_hbm, w_pos_hbm, w_mid_hbm, w_out_hbm),
        (w_latent_ref, w_pos_ref, w_mid_ref, w_out_ref),
        sems,
    )
    planes, rows_z = plan.planes, lat.shape[2] // 2
    rows_y = lat.shape[0] // (planes + 1) * 2
    slots = rows // plan.tiles
    my_block = place_ref[0]
    my_tile = place_ref[1]
    my_replica = place_ref[2]
    always = my_tile >= 0

    words = words_ref[...]
    words = jnp.concatenate(
        [words] + [pltpu.roll(words, LANES - 16 * group, 1) for group in range(1, slots // 8)], axis=0
    )
    interp, base_x, base_y, base_z, frac = interpolate(words, lat, planes, rows_y, rows_z)
    code[...] = interp
    global_x = my_tile * planes + base_x
    lane = lax.broadcasted_iota(jnp.int32, (rows, LANES), 1)
    pos[...] = jnp.where(
        lane == 0,
        (global_x.astype(F32) + frac[0]) / (planes * plan.tiles),
        jnp.where(
            lane == 1,
            (base_y.astype(F32) + frac[1]) / rows_y,
            (base_z.astype(F32) + frac[2]) / rows_z,
        ),
    )

    for copy in weights:
        copy.wait()
    high, low = halves(w_latent_ref[...])
    z_one[...] = mul(interp, high) + mul(interp, low)
    high, low = halves(w_mid_ref[...])
    mid_high[...] = high
    mid_low[...] = low
    w_pos = [w_pos_ref[d : d + 1, :] for d in range(3)]
    square = w_pos[0] * w_pos[0] + w_pos[1] * w_pos[1] + w_pos[2] * w_pos[2]
    bias_one = small_ref[0:1, :]
    bias_two = small_ref[1:2, :]

    part_rows = rows // 2

    def at(part, index, block=None):
        first = (part * 5 + index) * part_rows
        if block is None:
            return slice(first, first + part_rows)
        return slice(first + block * BLOCK, first + (block + 1) * BLOCK)

    def rows_at(part, block):
        first = part * part_rows + block * BLOCK
        return slice(first, first + BLOCK)

    def store(refs, span, value):
        high, low = halves(value)
        refs[0][span, :] = high
        refs[1][span, :] = low

    def layer_one(part):
        refs = (one_high, one_low)
        for block in range(part_rows // BLOCK):
            here = rows_at(part, block)
            where = pos[here, :]
            pre = (
                z_one[here, :]
                + (where[:, 0:1] * w_pos[0] + where[:, 1:2] * w_pos[1] + where[:, 2:3] * w_pos[2])
                + bias_one
            )
            act = jnp.tanh(pre)
            slope = 1.0 - act * act
            curve = -2.0 * act * slope
            z_one[here, :] = act
            store(refs, at(part, 0, block), act)
            for d in range(3):
                store(refs, at(part, 1 + d, block), slope * w_pos[d])
            store(refs, at(part, 4, block), curve * square)

    def times_mid(dims, source, result, part):
        span = slice(part * 5 * part_rows, (part + 1) * 5 * part_rows)
        left = (source[0][span, :], source[1][span, :])
        result[span, :] = mul3(left, (mid_high[...], mid_low[...]), dims)

    def layer_two(part):
        refs = (two_high, two_low)
        for block in range(part_rows // BLOCK):
            act = jnp.tanh(mixed[at(part, 0, block), :] + bias_two)
            slope = 1.0 - act * act
            curve = -2.0 * act * slope
            store(refs, at(part, 0, block), act)
            mixed[at(part, 0, block), :] = act
            norm = None
            for d in range(3):
                tangent = mixed[at(part, 1 + d, block), :]
                store(refs, at(part, 1 + d, block), slope * tangent)
                norm = tangent * tangent if norm is None else norm + tangent * tangent
            store(refs, at(part, 4, block), slope * mixed[at(part, 4, block), :] + curve * norm)

    out_fields = jnp.concatenate([w_out_ref[...], jnp.zeros((3, hidden), F32)], axis=0)
    wo_high, wo_low = halves(out_fields)
    wo_three = jnp.concatenate([out_fields, wo_low.astype(F32), out_fields], axis=0).astype(BF16)
    wo_both = jnp.concatenate(
        [out_fields, wo_low.astype(F32), jnp.zeros((LANES - 16, hidden), F32)], axis=0
    ).astype(BF16)

    def outputs(part):
        span = slice(part * 5 * part_rows, (part + 1) * 5 * part_rows)
        both = mul(two_high[span, :], wo_both, NT)
        low = mul(two_low[span, :], wo_both, NT)
        for s in range(5):
            rows_s = slice(s * part_rows, (s + 1) * part_rows)
            both_t, low_t = both[rows_s].T, low[rows_s].T
            out_t[8 * s : 8 * s + 8, part * part_rows : (part + 1) * part_rows] = (
                both_t[0:8] + both_t[8:16] + low_t[0:8]
            )

    @pl.when(always)
    def _():
        layer_one(0)
        times_mid(NN, (one_high, one_low), mixed, 0)
        layer_one(1)
        times_mid(NN, (one_high, one_low), mixed, 1)
        layer_two(0)
        outputs(0)
        layer_two(1)
        outputs(1)

    words_t = words.T
    target = [words_t[4 + f : 5 + f, :] for f in range(5)]
    valid = words_t[9:10, :]
    value = [out_t[f : f + 1, :] + small_ref[2:3, f : f + 1] for f in range(5)]
    grad = [[out_t[8 * (d + 1) + f : 8 * (d + 1) + f + 1, :] for f in range(5)] for d in range(3)]
    laplace = [out_t[32 + f : 33 + f, :] for f in range(5)]
    velocity = value[2:5]
    advection = [
        velocity[0] * grad[0][f] + velocity[1] * grad[1][f] + velocity[2] * grad[2][f] for f in range(5)
    ]
    continuity = grad[0][2] + grad[1][3] + grad[2][4]
    momentum = [advection[2 + j] + grad[j][1] - VISCOSITY * laplace[2 + j] for j in range(3)]
    momentum[2] = momentum[2] - value[0]
    energy = advection[0] - DIFFUSIVITY * laplace[0]
    misfit = [value[f] - target[f] for f in range(5)]
    physics = (
        continuity * continuity
        + (momentum[0] * momentum[0] + momentum[1] * momentum[1] + momentum[2] * momentum[2])
        + energy * energy
    )
    squares = (
        misfit[0] * misfit[0]
        + misfit[1] * misfit[1]
        + misfit[2] * misfit[2]
        + misfit[3] * misfit[3]
        + misfit[4] * misfit[4]
    )
    point_loss = valid * (squares + RESIDUAL_WEIGHT * physics) * (1.0 / plan.query_total)

    rate = valid * (1.0 / plan.query_total)
    twice = RESIDUAL_WEIGHT * 2.0
    d_cont = rate * twice * continuity
    d_mom = [rate * twice * m for m in momentum]
    d_energy = rate * twice * energy
    d_value = [2.0 * rate * m for m in misfit]
    for d in range(3):
        d_value[2 + d] = d_value[2 + d] + (
            d_mom[0] * grad[d][2] + d_mom[1] * grad[d][3] + d_mom[2] * grad[d][4] + d_energy * grad[d][0]
        )
    d_value[0] = d_value[0] - d_mom[2]
    d_out_t[...] = jnp.zeros_like(d_out_t)
    for f in range(5):
        d_out_t[f : f + 1, :] = d_value[f]
    for d in range(3):
        first = 8 * (d + 1)
        d_out_t[first : first + 1, :] = d_energy * velocity[d]
        d_out_t[first + 1 : first + 2, :] = d_mom[d]
        for j in range(3):
            term = d_mom[j] * velocity[d]
            if j == d:
                term = term + d_cont
            d_out_t[first + 2 + j : first + 3 + j, :] = term
    d_out_t[32:33, :] = -DIFFUSIVITY * d_energy
    for j in range(3):
        d_out_t[34 + j : 35 + j, :] = -VISCOSITY * d_mom[j]

    def out_back(part):
        columns = slice(part * part_rows, (part + 1) * part_rows)
        wanted = jnp.concatenate([d_out_t[8 * s : 8 * s + 8, columns] for s in range(5)], axis=1)
        do_low = halves(wanted)[1].astype(F32)
        wanted = jnp.concatenate([wanted, wanted, do_low], axis=0).astype(BF16)
        back[part * 5 * part_rows : (part + 1) * 5 * part_rows, :] = mul(wanted, wo_three, TN)

    def second_back(part, total):
        refs = (d_both.at[:, :hidden], d_both.at[:, hidden:])
        for block in range(part_rows // BLOCK):
            act = mixed[at(part, 0, block), :]
            slope = 1.0 - act * act
            curve = -2.0 * act * slope
            cot_l = back[at(part, 4, block), :]
            d_slope = cot_l * mixed[at(part, 4, block), :]
            norm = None
            bent = 2.0 * curve * cot_l
            for d in range(3):
                tangent = mixed[at(part, 1 + d, block), :]
                cot_t = back[at(part, 1 + d, block), :]
                store(refs, at(part, 1 + d, block), slope * cot_t + bent * tangent)
                d_slope = d_slope + cot_t * tangent
                norm = tangent * tangent if norm is None else norm + tangent * tangent
            store(refs, at(part, 4, block), slope * cot_l)
            d_curve = cot_l * norm
            d_slope = d_slope - 2.0 * act * d_curve
            d_act = back[at(part, 0, block), :] - 2.0 * slope * d_curve - 2.0 * act * d_slope
            d_pre = slope * d_act
            store(refs, at(part, 0, block), d_pre)
            total = total + folded(d_pre)
        return total

    def first_back(part, sums):
        for block in range(part_rows // BLOCK):
            here = rows_at(part, block)
            act = z_one[here, :]
            slope = 1.0 - act * act
            curve = -2.0 * act * slope
            where = pos[here, :]
            cot_t = [mixed_back[at(part, 1 + d, block), :] for d in range(3)]
            cot_l = mixed_back[at(part, 4, block), :]
            d_curve = cot_l * square
            d_slope = cot_t[0] * w_pos[0] + cot_t[1] * w_pos[1] + cot_t[2] * w_pos[2] - 2.0 * act * d_curve
            d_act = mixed_back[at(part, 0, block), :] - 2.0 * slope * d_curve - 2.0 * act * d_slope
            d_pre = slope * d_act
            high, low = halves(d_pre)
            first_high[here, :] = high
            first_low[here, :] = low
            sums = (
                [sums[0] + folded(d_pre)]
                + [sums[1 + d] + folded(where[:, d : d + 1] * d_pre + slope * cot_t[d]) for d in range(3)]
                + [sums[4] + folded(curve * cot_l)]
            )
        return sums


    def put(part, first, value):
        while value.shape[0]:
            block, row = first // plan.main_rows, first % plan.main_rows
            count = min(value.shape[0], plan.main_rows - row)
            packed[2 * part + block, row : row + count, :] = value[:count]
            first, value = first + count, value[count:]

    def mid_gradient():
        both = mul(one_high[...], d_both[...], TN)
        both = both[:, :hidden] + both[:, hidden:] + mul(one_low[...], d_both[:, :hidden], TN)
        for part in range(hidden // LANES):
            put(part, 0, both[:, part * LANES : (part + 1) * LANES])

    @pl.when(always)
    def _():
        out_back(0)
        total = second_back(0, jnp.zeros((8, hidden), F32))
        out_back(1)
        times_mid(NT, (d_both.at[:, :hidden], d_both.at[:, hidden:]), mixed_back, 0)
        sums_ref[5] = second_back(1, total)
        times_mid(NT, (d_both.at[:, :hidden], d_both.at[:, hidden:]), mixed_back, 1)
        total = first_back(0, [jnp.zeros((8, hidden), F32)] * 5)
        mid_gradient()
        for number, value in enumerate(first_back(1, total)):
            sums_ref[number] = value

    sums = [sums_ref[number] for number in range(6)]
    d_square = jnp.sum(sums[4], axis=0, keepdims=True)
    grad_latent = mul(code[...], first_high[...], TN) + mul(code[...], first_low[...], TN)

    parts = [d_out_t[8 * s : 8 * s + 8, p * part_rows : (p + 1) * part_rows] for p in range(2) for s in range(5)]
    flat = jnp.concatenate(parts, axis=1)
    fl_high, fl_low = halves(flat)
    fl_both = jnp.concatenate([flat, fl_low.astype(F32)], axis=0).astype(BF16)
    grad_out = mul(fl_both, two_high[...])
    grad_out = grad_out[:8] + grad_out[8:] + mul(fl_high, two_low[...])

    lane_row = lax.broadcasted_iota(jnp.int32, (1, hidden), 1)
    last = jnp.where(lane_row == 5, jnp.sum(point_loss), 0.0)
    for f in range(5):
        last = last + jnp.where(lane_row == f, jnp.sum(d_value[f]), 0.0)
    grad_pos = [jnp.sum(sums[1 + d], axis=0, keepdims=True) + 2.0 * w_pos[d] * d_square for d in range(3)]
    misc = grad_pos + [
        jnp.sum(sums[0], axis=0, keepdims=True),
        jnp.sum(sums[5], axis=0, keepdims=True),
        last,
    ]
    misc = jnp.concatenate(misc + [jnp.zeros((2, hidden), F32)], axis=0)
    for part in range(hidden // LANES):
        lanes = slice(part * LANES, (part + 1) * LANES)
        put(part, hidden, grad_latent[:, lanes])
        packed[2 * part, plan.coded_rows :, :] = misc[:, lanes]
        packed[2 * part + 1, plan.coded_rows :, :] = grad_out[:, lanes]

    chosen = jnp.where(
        lane == jnp.broadcast_to(words[:, 10:11], (rows, LANES)).astype(jnp.int32), words[:, 9:10], 0.0
    ).astype(BF16)
    fields = jnp.concatenate(value + [jnp.zeros((3, rows), F32)], axis=0)
    source = (lax.broadcasted_iota(jnp.int32, (8, rows), 1) & (plan.tiles * 8 - 1)) >> 3
    spread = jnp.concatenate([jnp.where(source == t, fields, 0.0) for t in range(plan.tiles)], axis=0)
    high, middle, low = thirds(spread)
    spread = mul(high, chosen) + mul(middle, chosen) + mul(low, chosen)
    packed[:, plan.main_rows : plan.coded_rows, :] = jnp.zeros((8, plan.devices, LANES), F32)
    for t in range(plan.tiles):
        row = plan.main_rows + (my_replica * (plan.tiles // 8) + t // 8) * 8
        packed[t % 8, pl.ds(pl.multiple_of(row, 8), 8), :] = spread[8 * t : 8 * t + 8]

    for block in range(8):
        spot = jnp.bitwise_xor(block, my_block) & 3

        @pl.when((my_block >> 2) == block // 4)
        def _():
            keep_ref[spot] = packed[block]

        @pl.when((my_block >> 2) != block // 4)
        def _():
            encode(plan, lambda start, count: packed[block, start : start + count, :], send_ref.at[spot])


class Plan:
    def __init__(self, tiles, replicas, queries, planes, hidden, latents):
        self.tiles, self.replicas, self.planes = tiles, replicas, planes
        self.slots = 2 * queries // tiles
        self.devices = tiles * replicas
        self.query_total = float(queries * self.devices)
        self.main_rows = (hidden + latents) // 2
        self.coded_rows = self.main_rows + self.devices
        self.rows = self.coded_rows + 8
        self.scales = -(-(self.coded_rows // SUB + 1) // 16) * 16
        self.sent_rows = self.coded_rows + 16 + self.scales
        top = self.devices.bit_length() - 1
        self.core, self.plane, self.rest = [0], [1, top - 1], list(range(2, top - 1))

    def mask(self, bits, steps):
        return sum(1 << bit for number, bit in enumerate(bits) if steps >> number & 1)

    def my_block(self, device):
        return (device & 1) * 4 + (device >> 1 & 1) + 2 * (device >> self.plane[1] & 1)


def swapped(value, plan, bits, steps):
    mask = plan.mask(bits, steps)
    return lax.ppermute(value, ("replica", "tile"), [(i, i ^ mask) for i in range(plan.devices)])


def encode(plan, read, out_ref):
    starts = list(range(0, plan.coded_rows, SUB))
    parts = [read(start, SUB) for start in starts] + [read(plan.coded_rows, 8)]
    tops = [jnp.max(jnp.abs(part), axis=0, keepdims=True) for part in parts]
    tops = tops + [jnp.zeros_like(tops[0])] * (plan.scales - len(tops))
    power = jnp.floor(jnp.log2(jnp.maximum(jnp.concatenate(tops, axis=0), 1e-30)))
    scale = jnp.exp2(14.0 - power)

    def whole(value):
        return jnp.clip(jnp.round(value), -32767.0, 32767.0)

    def narrow(value):
        return value.astype(jnp.int32).astype(jnp.int16)

    for number, start in enumerate(starts):
        out_ref[start : start + SUB, :] = narrow(whole(parts[number] * scale[number : number + 1]))
    last = len(starts)
    exact = parts[last] * scale[last : last + 1]
    high = whole(exact)
    low = whole((exact - high) * 32768.0)
    out_ref[plan.coded_rows : plan.coded_rows + 16, :] = narrow(jnp.concatenate([high, low], axis=0))
    out_ref[plan.coded_rows + 16 :, :] = narrow(power)


def decoder(plan, ref):
    def widen(value):
        return value.astype(jnp.int32).astype(F32)

    scale = jnp.exp2(widen(ref[plan.coded_rows + 16 :, :]) - 14.0)

    def read(start, count):
        if start < plan.coded_rows:
            number = start // SUB
            return widen(ref[start : start + count, :]) * scale[number : number + 1]
        both = widen(ref[plan.coded_rows : plan.coded_rows + 16, :])
        number = plan.coded_rows // SUB
        return (both[:8] + both[8:] * (1.0 / 32768.0)) * scale[number : number + 1]

    return read


def added(readers):
    def read(start, count):
        total = readers[0](start, count)
        for reader in readers[1:]:
            total = total + reader(start, count)
        return total

    return read


def first_kernel(plan, numbers, keep_ref, got_ref, *refs):
    def reader(block):
        got = decoder(plan, got_ref.at[block])
        return lambda start, count: keep_ref[block, start : start + count, :] + got(start, count)

    for number, out_ref in zip(numbers, refs):
        if number:
            encode(plan, reader(number), out_ref)
        else:
            read = reader(0)
            for start in range(0, plan.coded_rows, SUB):
                out_ref[start : start + SUB, :] = read(start, SUB)
            out_ref[plan.coded_rows :, :] = read(plan.coded_rows, 8)


def first_sum(keep, got, numbers, plan):
    sent = jax.ShapeDtypeStruct((plan.sent_rows, LANES), jnp.int16)
    own = jax.ShapeDtypeStruct(keep.shape[1:], F32)
    return pl.pallas_call(
        functools.partial(first_kernel, plan, numbers),
        out_shape=tuple(sent if number else own for number in numbers),
        in_specs=[VMEM] * 2,
        out_specs=tuple([VMEM] * len(numbers)),
        compiler_params=pltpu.CompilerParams(vmem_limit_bytes=6 << 20),
        name="sum_core",
    )(keep, got)


def plane_kernel(plan, mine_ref, *refs):
    readers = [lambda start, count: mine_ref[start : start + count, :]]
    encode(plan, added(readers + [decoder(plan, ref) for ref in refs[:-1]]), refs[-1])


def pair_kernel(plan, mine_ref, other_ref, out_ref):
    encode(plan, added([decoder(plan, mine_ref), decoder(plan, other_ref)]), out_ref)


def coded_sum(kernel, blocks, plan, name):
    return pl.pallas_call(
        functools.partial(kernel, plan),
        out_shape=jax.ShapeDtypeStruct((plan.sent_rows, LANES), jnp.int16),
        in_specs=[VMEM] * len(blocks),
        out_specs=VMEM,
        compiler_params=pltpu.CompilerParams(vmem_limit_bytes=4 << 20),
        name=name,
    )(*blocks)


def main(place, lat, words, small, weights, plan):
    rows = plan.tiles * plan.slots
    hidden = weights[2].shape[0]
    channels = lat.shape[1]
    outs = jax.ShapeDtypeStruct((4, plan.rows, LANES), F32)
    wide = lambda kind: pltpu.VMEM((5 * rows, hidden), kind)
    return pl.pallas_call(
        functools.partial(main_kernel, plan),
        out_shape=(jax.ShapeDtypeStruct((4, plan.sent_rows, LANES), jnp.int16), outs),
        in_specs=[SMEM] + [VMEM] * 3 + [HBM] * 4,
        out_specs=(VMEM, VMEM),
        scratch_shapes=[
            pltpu.VMEM((rows, channels), BF16),
            pltpu.VMEM((rows, LANES), F32),
            pltpu.VMEM((rows, hidden), F32),
            wide(BF16),
            wide(BF16),
            wide(F32),
            wide(BF16),
            wide(BF16),
            wide(F32),
            wide(F32),
            pltpu.VMEM((rows, hidden), BF16),
            pltpu.VMEM((rows, hidden), BF16),
            pltpu.VMEM((6, 8, hidden), F32),
            pltpu.VMEM((5 * rows, 2 * hidden), BF16),
            pltpu.VMEM((40, rows), F32),
            pltpu.VMEM((40, rows), F32),
            pltpu.VMEM((8, plan.rows, LANES), F32),
            pltpu.VMEM((hidden, hidden), BF16),
            pltpu.VMEM((hidden, hidden), BF16),
        ]
        + [pltpu.VMEM(weight.shape, F32) for weight in weights]
        + [pltpu.SemaphoreType.DMA((4,))],
        compiler_params=pltpu.CompilerParams(vmem_limit_bytes=32 << 20),
        name="encode_decode",
    )(place, lat, words, small, *weights)


def unpack_kernel(plan, place_ref, *refs):
    sources, outs, packed = refs[:8], refs[8:-1], refs[-1]
    prediction_ref, latent_ref, pos_ref, one_ref, mid_ref, two_ref, out_ref, bias_out_ref, loss_ref = outs
    my_block = place_ref[0]
    device = place_ref[2] * plan.tiles + place_ref[1]
    starts = list(range(0, plan.coded_rows, SUB))
    for number, ref in enumerate(sources):
        read = decoder(plan, ref)
        block = jnp.bitwise_xor(number, my_block)
        for start in starts:
            packed[block, start : start + SUB, :] = read(start, SUB)
        packed[block, plan.coded_rows :, :] = read(plan.coded_rows, 8)

    hidden = mid_ref.shape[0]
    latents = latent_ref.shape[0]
    split = plan.main_rows
    for part in range(hidden // LANES):
        lanes = slice(part * LANES, (part + 1) * LANES)
        mid_ref[0:split, lanes] = packed[2 * part, 0:split, :]
        mid_ref[split:, lanes] = packed[2 * part + 1, 0 : hidden - split, :]
        latent_ref[:, lanes] = packed[2 * part + 1, hidden - split : split, :]
        misc = packed[2 * part, plan.coded_rows :, :]
        pos_ref[:, lanes] = misc[0:3]
        one_ref[:, lanes] = misc[3:4]
        two_ref[:, lanes] = misc[4:5]
        out_ref[:, lanes] = packed[2 * part + 1, plan.coded_rows : plan.coded_rows + 5, :]
        if part == 0:
            bias_out_ref[...] = misc[5:6, 0:5]
            loss_ref[...] = misc[5:6, 5:6]
    row = pl.multiple_of(plan.main_rows + (device >> 3) * 8, 8)
    fields = packed[device & 7, pl.ds(row, 8), :]
    for f in range(5):
        prediction_ref[f] = fields[f : f + 1]


def unpack(place, blocks, plan, hidden, latents):
    shapes = [
        (5, 1, LANES),
        (latents, hidden),
        (3, hidden),
        (1, hidden),
        (hidden, hidden),
        (1, hidden),
        (5, hidden),
        (1, 5),
        (1, 1),
    ]
    return pl.pallas_call(
        functools.partial(unpack_kernel, plan),
        out_shape=tuple(jax.ShapeDtypeStruct(shape, F32) for shape in shapes),
        in_specs=[SMEM] + [VMEM] * 8,
        out_specs=tuple([VMEM] * len(shapes)),
        scratch_shapes=[pltpu.VMEM((8, plan.rows, LANES), F32)],
        compiler_params=pltpu.CompilerParams(vmem_limit_bytes=16 << 20),
        name="unpack",
    )(place, *blocks)


def body(
    fields,
    convolution_weight,
    convolution_bias,
    query_owner,
    query_cell,
    query_frac,
    target,
    w_latent,
    w_pos,
    bias_one,
    w_mid,
    bias_two,
    w_out,
    bias_out,
):
    tiles = lax.axis_size("tile")
    replicas = lax.axis_size("replica")
    my_tile = lax.axis_index("tile")
    my_replica = lax.axis_index("replica")
    channels = fields.shape[1]
    queries = query_cell.shape[1]
    hidden = w_mid.shape[0]
    plan = Plan(tiles, replicas, queries, fields.shape[2], hidden, channels)
    device = my_replica * tiles + my_tile
    place = jnp.stack([plan.my_block(device), my_tile, my_replica]).astype(jnp.int32)

    here = fields[0].transpose(1, 2, 0, 3)
    odd = my_tile & 1
    count = DILATION_RATE + 1
    first = lax.dynamic_slice_in_dim(here, (1 - odd) * (here.shape[0] - count), count, axis=0)
    second = lax.dynamic_slice_in_dim(here, odd * (here.shape[0] - count), count, axis=0)
    first, second, query_owner = lax.optimization_barrier((first, second, query_owner))
    near = lax.ppermute(first, "tile", [(i, i ^ 1) for i in range(tiles)])
    far = lax.ppermute(second, "tile", [(i, (i - 1 + 2 * (i & 1)) % tiles) for i in range(tiles)])
    words, small = route(
        (query_owner[:, :, 0], query_cell, query_frac.transpose(1, 0, 2), target.transpose(1, 0, 2)),
        (bias_one[None], bias_two[None], bias_out[None], convolution_bias[None]),
        tiles,
        plan.slots,
    )
    words = lax.all_to_all(
        words.reshape(tiles, 8, WORDS), "tile", split_axis=0, concat_axis=0, tiled=True
    ).reshape(tiles * 8, WORDS)

    lat = convolve(place, near, here, far, convolution_weight, small)
    weights = (w_latent, w_pos, w_mid, w_out)
    send, keep = main(place, lat, words, small, weights, plan)

    got = swapped(send, plan, plan.core, 1)
    (far,) = first_sum(keep, got, (3,), plan)
    far, keep = lax.optimization_barrier((far, keep))
    mine, *near = first_sum(keep, got, (0, 1, 2), plan)
    arrived = [swapped(block, plan, plan.plane, step) for step, block in ((3, far), (1, near[0]), (2, near[1]))]
    block = coded_sum(plane_kernel, [mine] + arrived, plan, "sum_plane")
    for bit in plan.rest:
        block = coded_sum(pair_kernel, [block, swapped(block, plan, [bit], 1)], plan, "sum_line")
    blocks = [block] + [swapped(block, plan, plan.plane, step) for step in range(1, 4)]
    blocks = blocks + [swapped(block, plan, plan.core, 1) for block in blocks]
    prediction, g_latent, g_pos, g_one, g_mid, g_two, g_out, g_bias, loss = unpack(
        place, blocks, plan, hidden, channels
    )
    return (
        prediction.transpose(1, 0, 2),
        g_latent,
        g_pos,
        g_one.reshape(hidden),
        g_mid,
        g_two.reshape(hidden),
        g_out,
        g_bias.reshape(5),
        loss.reshape(()),
    )


def solution(mesh):
    return jax.shard_map(
        body,
        mesh=mesh,
        in_specs=(
            P("replica", None, "tile", None, None),
            P(),
            P(),
            P("replica", "tile", None),
            P("replica", "tile"),
            P("replica", None, "tile"),
            P("replica", None, "tile"),
            P(),
            P(),
            P(),
            P(),
            P(),
            P(),
            P(),
        ),
        out_specs=(P("replica", None, "tile"), P(), P(), P(), P(), P(), P(), P(), P()),
        check_vma=False,
    )
```

```python
import functools

import jax
import jax.numpy as jnp
from jax import lax
from jax.experimental import pallas as pl
from jax.experimental.pallas import tpu as pltpu
from jax.sharding import PartitionSpec as P

DILATION_RATE = 2
VISCOSITY = 0.05
DIFFUSIVITY = 0.05
RESIDUAL_WEIGHT = 0.5

F32 = jnp.float32
BF16 = jnp.bfloat16
LANES = 128
BLOCK = 32
WORDS = 128
SUB = 32
NN = (((1,), (0,)), ((), ()))
NT = (((1,), (1,)), ((), ()))
TN = (((0,), (0,)), ((), ()))
VMEM = pl.BlockSpec(memory_space=pltpu.VMEM)
SMEM = pl.BlockSpec(memory_space=pltpu.SMEM)
HBM = pl.BlockSpec(memory_space=pltpu.HBM)


def mul(left, right, dims=NN):
    return lax.dot_general(left, right, dims, preferred_element_type=F32)


def halves(value):
    high = value.astype(BF16)
    return high, (value - high.astype(F32)).astype(BF16)


def thirds(value):
    high = value.astype(BF16)
    rest = value - high.astype(F32)
    middle = rest.astype(BF16)
    return high, middle, (rest - middle.astype(F32)).astype(BF16)


def mul3(left, right, dims=NN):
    return mul(left[0], right[0], dims) + mul(left[0], right[1], dims) + mul(left[1], right[0], dims)


def fetches(sources, targets, sems):
    copies = [
        pltpu.make_async_copy(source, target, sems.at[number])
        for number, (source, target) in enumerate(zip(sources, targets))
    ]
    for copy in copies:
        copy.start()
    return copies


def route_kernel(tiles, slots, *refs):
    out_ref, small_ref, *scratch, words, sems = refs[8:]
    for copy in fetches(refs[:8], scratch, sems):
        copy.wait()
    owner_ref, cell_ref, frac_ref, target_ref, *bias_refs = scratch
    queries = owner_ref.shape[1]
    small_ref[...] = jnp.zeros_like(small_ref)
    for number, ref in enumerate(bias_refs):
        small_ref[number : number + 1, 0 : ref.shape[1]] = ref[...]
    owner = owner_ref[...]
    hits = (lax.broadcasted_iota(jnp.int32, (tiles, queries), 0) == owner).astype(F32)
    before = lax.broadcasted_iota(jnp.int32, (queries, queries), 0) < lax.broadcasted_iota(
        jnp.int32, (queries, queries), 1
    )
    earlier = mul(hits.astype(BF16), before.astype(F32).astype(BF16))
    slot = jnp.sum(hits * earlier, axis=0, keepdims=True)
    place = owner * slots + slot.astype(jnp.int32)
    spot = lax.broadcasted_iota(jnp.int32, (tiles * 8, queries), 0)
    spot = (spot >> 3) * slots + (spot & 7)
    groups = slots // 8
    chosen = [jnp.where(spot + 8 * group == place, 1.0, 0.0) for group in range(groups)]
    chosen = jnp.concatenate(chosen, axis=1).astype(BF16)
    words[...] = jnp.zeros_like(words)
    for group in range(groups):
        row, lanes = 16 * group, slice(group * queries, (group + 1) * queries)
        words[row : row + 1, lanes] = cell_ref[...].astype(F32)
        for d in range(3):
            words[row + 1 + d : row + 2 + d, lanes] = frac_ref[d]
        for f in range(5):
            words[row + 4 + f : row + 5 + f, lanes] = target_ref[f]
        words[row + 9 : row + 10, lanes] = jnp.ones((1, queries), F32)
        words[row + 10 : row + 11, lanes] = lax.broadcasted_iota(jnp.int32, (1, queries), 1).astype(F32)
    high, middle, low = thirds(words[...])
    out_ref[...] = mul(chosen, high, NT) + mul(chosen, middle, NT) + mul(chosen, low, NT)


def route(inputs, biases, tiles, slots):
    queries = inputs[0].shape[1]
    arrays = inputs + biases
    return pl.pallas_call(
        functools.partial(route_kernel, tiles, slots),
        out_shape=(
            jax.ShapeDtypeStruct((tiles * 8, WORDS), F32),
            jax.ShapeDtypeStruct((8, biases[0].shape[1]), F32),
        ),
        in_specs=[HBM] * 8,
        out_specs=(VMEM, VMEM),
        scratch_shapes=[pltpu.VMEM(array.shape, array.dtype) for array in arrays]
        + [pltpu.VMEM((WORDS, queries * (slots // 8)), F32), pltpu.SemaphoreType.DMA((8,))],
        compiler_params=pltpu.CompilerParams(vmem_limit_bytes=4 << 20),
        name="route",
    )(*arrays)


def tap_sum(weight_ref, planes, pair):
    total = None
    for step_x, ref, index in planes:
        rows_y = ref.shape[1]
        blocks = [
            jnp.concatenate([ref[index, (2 * pair + half + step_y) % rows_y] for half in (0, 1)], axis=1)
            for step_y in (-1, 0, 1)
        ]
        term = mul(weight_ref[step_x], jnp.concatenate(blocks, axis=0))
        total = term if total is None else total + term
    channels = total.shape[0] // 3
    sides = []
    for half in (0, 1):
        part = total[:, half * LANES : (half + 1) * LANES]
        sides.append(
            part[channels : 2 * channels]
            + pltpu.roll(part[:channels], 1, 1)
            + pltpu.roll(part[2 * channels :], LANES - 1, 1)
        )
    return jnp.concatenate(sides, axis=1)


def conv_kernel(
    place_ref,
    near_ref,
    here_ref,
    far_ref,
    taps_ref,
    small_ref,
    lat_ref,
    weight_ref,
):
    planes, rows_y, channels = here_ref.shape[:3]
    taps = taps_ref[...].astype(F32)
    for step in range(3):
        rows = []
        for step_z in range(3):
            numbers = [9 * step + 3 * step_y + step_z for step_y in range(3)]
            rows.append(
                jnp.concatenate([taps[:, n * channels : (n + 1) * channels] for n in numbers], axis=1)
            )
        weight_ref[step] = jnp.concatenate(rows, axis=0).astype(BF16)
    diagonal = lax.broadcasted_iota(jnp.int32, (channels, channels), 0) == lax.broadcasted_iota(
        jnp.int32, (channels, channels), 1
    )
    bias = jnp.sum(jnp.where(diagonal, small_ref[3:4, 0:channels], 0.0), axis=1, keepdims=True)
    def all_planes(left_ref, right_ref):
        for x in range(planes + 1):
            taps = []
            for step in range(3):
                plane = x + DILATION_RATE * (step - 1)
                if plane < 0:
                    taps.append((step, left_ref, plane + left_ref.shape[0]))
                elif plane >= planes:
                    taps.append((step, right_ref, plane - planes))
                else:
                    taps.append((step, here_ref, plane))
            for pair in range(rows_y // 2):
                summed = tap_sum(weight_ref, taps, pair) + bias
                lat_ref[x * (rows_y // 2) + pair] = jax.nn.gelu(summed).astype(BF16)

    even = (place_ref[1] & 1) == 0

    @pl.when(even)
    def _():
        all_planes(far_ref, near_ref)

    @pl.when(jnp.logical_not(even))
    def _():
        all_planes(near_ref, far_ref)


def convolve(place, near, here, far, taps, small):
    planes, rows_y, channels, rows_z = here.shape
    pairs = (planes + 1) * rows_y // 2
    return pl.pallas_call(
        conv_kernel,
        out_shape=jax.ShapeDtypeStruct((pairs, channels, 2 * rows_z), BF16),
        in_specs=[SMEM] + [VMEM] * 5,
        out_specs=VMEM,
        scratch_shapes=[pltpu.VMEM((3, 3 * channels, 3 * channels), BF16)],
        compiler_params=pltpu.CompilerParams(vmem_limit_bytes=8 << 20),
        cost_estimate=pl.CostEstimate(flops=3 << 30, bytes_accessed=4 << 20, transcendentals=0),
        name="convolve",
    )(place, near, here, far, taps, small)


def interpolate(words, lat, planes, rows_y, rows_z):
    rows = words.shape[0]
    cell = jnp.broadcast_to(words[:, 0:1], (rows, LANES)).astype(jnp.int32)
    frac = [jnp.broadcast_to(words[:, 1 + d : 2 + d], (rows, LANES)) for d in range(3)]
    shift_z = rows_z.bit_length() - 1
    shift_y = rows_y.bit_length() - 1
    base_x = cell >> (shift_z + shift_y)
    base_y = (cell >> shift_z) & (rows_y - 1)
    base_z = cell & (rows_z - 1)
    spot = lax.broadcasted_iota(jnp.int32, (rows, rows_z), 1)
    part_z = jnp.where(spot == base_z, 1.0 - frac[2], 0.0) + jnp.where(
        spot == ((base_z + 1) & (rows_z - 1)), frac[2], 0.0
    )
    part_yz = []
    for y in range(rows_y):
        part_y = jnp.where(
            base_y == y, 1.0 - frac[1], jnp.where(base_y == (y - 1) % rows_y, frac[1], 0.0)
        )
        part_yz.append(part_y * part_z)
    total = None
    for x in range(planes + 1):
        part_x = jnp.where(base_x == x, 1.0 - frac[0], jnp.where(base_x == x - 1, frac[0], 0.0))
        for pair in range(rows_y // 2):
            sides = [(part_x * part_yz[2 * pair + half]).astype(BF16) for half in (0, 1)]
            term = mul(jnp.concatenate(sides, axis=1), lat[x * (rows_y // 2) + pair], NT)
            total = term if total is None else total + term
    return total.astype(BF16), base_x, base_y, base_z, frac


def folded(value):
    return jnp.sum(value.reshape(value.shape[0] // 8, 8, value.shape[1]), axis=0)


def main_kernel(
    plan,
    place_ref,
    lat,
    words_ref,
    small_ref,
    w_latent_hbm,
    w_pos_hbm,
    w_mid_hbm,
    w_out_hbm,
    send_ref,
    keep_ref,
    code,
    pos,
    z_one,
    one_high,
    one_low,
    mixed,
    two_high,
    two_low,
    back,
    mixed_back,
    first_high,
    first_low,
    sums_ref,
    d_both,
    out_t,
    d_out_t,
    packed,
    mid_high,
    mid_low,
    w_latent_ref,
    w_pos_ref,
    w_mid_ref,
    w_out_ref,
    sems,
):
    rows = plan.tiles * plan.slots
    hidden = w_mid_ref.shape[0]
    latents = w_latent_ref.shape[0]
    weights = fetches(
        (w_latent_hbm, w_pos_hbm, w_mid_hbm, w_out_hbm),
        (w_latent_ref, w_pos_ref, w_mid_ref, w_out_ref),
        sems,
    )
    planes, rows_z = plan.planes, lat.shape[2] // 2
    rows_y = lat.shape[0] // (planes + 1) * 2
    slots = rows // plan.tiles
    my_block = place_ref[0]
    my_tile = place_ref[1]
    my_replica = place_ref[2]
    always = my_tile >= 0

    words = words_ref[...]
    words = jnp.concatenate(
        [words] + [pltpu.roll(words, LANES - 16 * group, 1) for group in range(1, slots // 8)], axis=0
    )
    interp, base_x, base_y, base_z, frac = interpolate(words, lat, planes, rows_y, rows_z)
    code[...] = interp
    global_x = my_tile * planes + base_x
    lane = lax.broadcasted_iota(jnp.int32, (rows, LANES), 1)
    pos[...] = jnp.where(
        lane == 0,
        (global_x.astype(F32) + frac[0]) / (planes * plan.tiles),
        jnp.where(
            lane == 1,
            (base_y.astype(F32) + frac[1]) / rows_y,
            (base_z.astype(F32) + frac[2]) / rows_z,
        ),
    )

    for copy in weights:
        copy.wait()
    high, low = halves(w_latent_ref[...])
    z_one[...] = mul(interp, high) + mul(interp, low)
    high, low = halves(w_mid_ref[...])
    mid_high[...] = high
    mid_low[...] = low
    w_pos = [w_pos_ref[d : d + 1, :] for d in range(3)]
    square = w_pos[0] * w_pos[0] + w_pos[1] * w_pos[1] + w_pos[2] * w_pos[2]
    bias_one = small_ref[0:1, :]
    bias_two = small_ref[1:2, :]

    part_rows = rows // 2

    def at(part, index, block=None):
        first = (part * 5 + index) * part_rows
        if block is None:
            return slice(first, first + part_rows)
        return slice(first + block * BLOCK, first + (block + 1) * BLOCK)

    def rows_at(part, block):
        first = part * part_rows + block * BLOCK
        return slice(first, first + BLOCK)

    def store(refs, span, value):
        high, low = halves(value)
        refs[0][span, :] = high
        refs[1][span, :] = low

    def layer_one(part):
        refs = (one_high, one_low)
        for block in range(part_rows // BLOCK):
            here = rows_at(part, block)
            where = pos[here, :]
            pre = (
                z_one[here, :]
                + (where[:, 0:1] * w_pos[0] + where[:, 1:2] * w_pos[1] + where[:, 2:3] * w_pos[2])
                + bias_one
            )
            act = jnp.tanh(pre)
            slope = 1.0 - act * act
            curve = -2.0 * act * slope
            z_one[here, :] = act
            store(refs, at(part, 0, block), act)
            for d in range(3):
                store(refs, at(part, 1 + d, block), slope * w_pos[d])
            store(refs, at(part, 4, block), curve * square)

    def times_mid(dims, source, result):
        left = (source[0][...], source[1][...])
        result[...] = mul3(left, (mid_high[...], mid_low[...]), dims)

    def layer_two(part):
        refs = (two_high, two_low)
        for block in range(part_rows // BLOCK):
            act = jnp.tanh(mixed[at(part, 0, block), :] + bias_two)
            slope = 1.0 - act * act
            curve = -2.0 * act * slope
            store(refs, at(part, 0, block), act)
            mixed[at(part, 0, block), :] = act
            norm = None
            for d in range(3):
                tangent = mixed[at(part, 1 + d, block), :]
                store(refs, at(part, 1 + d, block), slope * tangent)
                norm = tangent * tangent if norm is None else norm + tangent * tangent
            store(refs, at(part, 4, block), slope * mixed[at(part, 4, block), :] + curve * norm)

    out_fields = jnp.concatenate([w_out_ref[...], jnp.zeros((3, hidden), F32)], axis=0)
    wo_high, wo_low = halves(out_fields)
    wo_three = jnp.concatenate([out_fields, wo_low.astype(F32), out_fields], axis=0).astype(BF16)
    wo_both = jnp.concatenate(
        [out_fields, wo_low.astype(F32), jnp.zeros((LANES - 16, hidden), F32)], axis=0
    ).astype(BF16)

    def outputs(part):
        span = slice(part * 5 * part_rows, (part + 1) * 5 * part_rows)
        both = mul(two_high[span, :], wo_both, NT)
        low = mul(two_low[span, :], wo_both, NT)
        for s in range(5):
            rows_s = slice(s * part_rows, (s + 1) * part_rows)
            both_t, low_t = both[rows_s].T, low[rows_s].T
            out_t[8 * s : 8 * s + 8, part * part_rows : (part + 1) * part_rows] = (
                both_t[0:8] + both_t[8:16] + low_t[0:8]
            )

    @pl.when(always)
    def _():
        layer_one(0)
        layer_one(1)
        times_mid(NN, (one_high, one_low), mixed)
        layer_two(0)
        outputs(0)
        layer_two(1)
        outputs(1)

    words_t = words.T
    target = [words_t[4 + f : 5 + f, :] for f in range(5)]
    valid = words_t[9:10, :]
    value = [out_t[f : f + 1, :] + small_ref[2:3, f : f + 1] for f in range(5)]
    grad = [[out_t[8 * (d + 1) + f : 8 * (d + 1) + f + 1, :] for f in range(5)] for d in range(3)]
    laplace = [out_t[32 + f : 33 + f, :] for f in range(5)]
    velocity = value[2:5]
    advection = [
        velocity[0] * grad[0][f] + velocity[1] * grad[1][f] + velocity[2] * grad[2][f] for f in range(5)
    ]
    continuity = grad[0][2] + grad[1][3] + grad[2][4]
    momentum = [advection[2 + j] + grad[j][1] - VISCOSITY * laplace[2 + j] for j in range(3)]
    momentum[2] = momentum[2] - value[0]
    energy = advection[0] - DIFFUSIVITY * laplace[0]
    misfit = [value[f] - target[f] for f in range(5)]
    physics = (
        continuity * continuity
        + (momentum[0] * momentum[0] + momentum[1] * momentum[1] + momentum[2] * momentum[2])
        + energy * energy
    )
    squares = (
        misfit[0] * misfit[0]
        + misfit[1] * misfit[1]
        + misfit[2] * misfit[2]
        + misfit[3] * misfit[3]
        + misfit[4] * misfit[4]
    )
    point_loss = valid * (squares + RESIDUAL_WEIGHT * physics) * (1.0 / plan.query_total)

    rate = valid * (1.0 / plan.query_total)
    twice = RESIDUAL_WEIGHT * 2.0
    d_cont = rate * twice * continuity
    d_mom = [rate * twice * m for m in momentum]
    d_energy = rate * twice * energy
    d_value = [2.0 * rate * m for m in misfit]
    for d in range(3):
        d_value[2 + d] = d_value[2 + d] + (
            d_mom[0] * grad[d][2] + d_mom[1] * grad[d][3] + d_mom[2] * grad[d][4] + d_energy * grad[d][0]
        )
    d_value[0] = d_value[0] - d_mom[2]
    d_out_t[...] = jnp.zeros_like(d_out_t)
    for f in range(5):
        d_out_t[f : f + 1, :] = d_value[f]
    for d in range(3):
        first = 8 * (d + 1)
        d_out_t[first : first + 1, :] = d_energy * velocity[d]
        d_out_t[first + 1 : first + 2, :] = d_mom[d]
        for j in range(3):
            term = d_mom[j] * velocity[d]
            if j == d:
                term = term + d_cont
            d_out_t[first + 2 + j : first + 3 + j, :] = term
    d_out_t[32:33, :] = -DIFFUSIVITY * d_energy
    for j in range(3):
        d_out_t[34 + j : 35 + j, :] = -VISCOSITY * d_mom[j]

    def out_back(part):
        columns = slice(part * part_rows, (part + 1) * part_rows)
        wanted = jnp.concatenate([d_out_t[8 * s : 8 * s + 8, columns] for s in range(5)], axis=1)
        do_low = halves(wanted)[1].astype(F32)
        wanted = jnp.concatenate([wanted, wanted, do_low], axis=0).astype(BF16)
        back[part * 5 * part_rows : (part + 1) * 5 * part_rows, :] = mul(wanted, wo_three, TN)

    def second_back(part, total):
        refs = (d_both.at[:, :hidden], d_both.at[:, hidden:])
        for block in range(part_rows // BLOCK):
            act = mixed[at(part, 0, block), :]
            slope = 1.0 - act * act
            curve = -2.0 * act * slope
            cot_l = back[at(part, 4, block), :]
            d_slope = cot_l * mixed[at(part, 4, block), :]
            norm = None
            bent = 2.0 * curve * cot_l
            for d in range(3):
                tangent = mixed[at(part, 1 + d, block), :]
                cot_t = back[at(part, 1 + d, block), :]
                store(refs, at(part, 1 + d, block), slope * cot_t + bent * tangent)
                d_slope = d_slope + cot_t * tangent
                norm = tangent * tangent if norm is None else norm + tangent * tangent
            store(refs, at(part, 4, block), slope * cot_l)
            d_curve = cot_l * norm
            d_slope = d_slope - 2.0 * act * d_curve
            d_act = back[at(part, 0, block), :] - 2.0 * slope * d_curve - 2.0 * act * d_slope
            d_pre = slope * d_act
            store(refs, at(part, 0, block), d_pre)
            total = total + folded(d_pre)
        return total

    def first_back(part, sums):
        for block in range(part_rows // BLOCK):
            here = rows_at(part, block)
            act = z_one[here, :]
            slope = 1.0 - act * act
            curve = -2.0 * act * slope
            where = pos[here, :]
            cot_t = [mixed_back[at(part, 1 + d, block), :] for d in range(3)]
            cot_l = mixed_back[at(part, 4, block), :]
            d_curve = cot_l * square
            d_slope = cot_t[0] * w_pos[0] + cot_t[1] * w_pos[1] + cot_t[2] * w_pos[2] - 2.0 * act * d_curve
            d_act = mixed_back[at(part, 0, block), :] - 2.0 * slope * d_curve - 2.0 * act * d_slope
            d_pre = slope * d_act
            high, low = halves(d_pre)
            first_high[here, :] = high
            first_low[here, :] = low
            sums = (
                [sums[0] + folded(d_pre)]
                + [sums[1 + d] + folded(where[:, d : d + 1] * d_pre + slope * cot_t[d]) for d in range(3)]
                + [sums[4] + folded(curve * cot_l)]
            )
        return sums


    def put(part, first, value):
        while value.shape[0]:
            block, row = first // plan.main_rows, first % plan.main_rows
            count = min(value.shape[0], plan.main_rows - row)
            packed[2 * part + block, row : row + count, :] = value[:count]
            first, value = first + count, value[count:]

    def mid_gradient():
        both = mul(one_high[...], d_both[...], TN)
        both = both[:, :hidden] + both[:, hidden:] + mul(one_low[...], d_both[:, :hidden], TN)
        for part in range(hidden // LANES):
            put(part, 0, both[:, part * LANES : (part + 1) * LANES])

    @pl.when(always)
    def _():
        out_back(0)
        out_back(1)
        total = second_back(0, jnp.zeros((8, hidden), F32))
        sums_ref[5] = second_back(1, total)
        times_mid(NT, (d_both.at[:, :hidden], d_both.at[:, hidden:]), mixed_back)
        total = first_back(0, [jnp.zeros((8, hidden), F32)] * 5)
        mid_gradient()
        for number, value in enumerate(first_back(1, total)):
            sums_ref[number] = value

    sums = [sums_ref[number] for number in range(6)]
    d_square = jnp.sum(sums[4], axis=0, keepdims=True)
    grad_latent = mul(code[...], first_high[...], TN) + mul(code[...], first_low[...], TN)

    parts = [d_out_t[8 * s : 8 * s + 8, p * part_rows : (p + 1) * part_rows] for p in range(2) for s in range(5)]
    flat = jnp.concatenate(parts, axis=1)
    fl_high, fl_low = halves(flat)
    fl_both = jnp.concatenate([flat, fl_low.astype(F32)], axis=0).astype(BF16)
    grad_out = mul(fl_both, two_high[...])
    grad_out = grad_out[:8] + grad_out[8:] + mul(fl_high, two_low[...])

    lane_row = lax.broadcasted_iota(jnp.int32, (1, hidden), 1)
    last = jnp.where(lane_row == 5, jnp.sum(point_loss), 0.0)
    for f in range(5):
        last = last + jnp.where(lane_row == f, jnp.sum(d_value[f]), 0.0)
    grad_pos = [jnp.sum(sums[1 + d], axis=0, keepdims=True) + 2.0 * w_pos[d] * d_square for d in range(3)]
    misc = grad_pos + [
        jnp.sum(sums[0], axis=0, keepdims=True),
        jnp.sum(sums[5], axis=0, keepdims=True),
        last,
    ]
    misc = jnp.concatenate(misc + [jnp.zeros((2, hidden), F32)], axis=0)
    for part in range(hidden // LANES):
        lanes = slice(part * LANES, (part + 1) * LANES)
        put(part, hidden, grad_latent[:, lanes])
        packed[2 * part, plan.coded_rows :, :] = misc[:, lanes]
        packed[2 * part + 1, plan.coded_rows :, :] = grad_out[:, lanes]

    chosen = jnp.where(
        lane == jnp.broadcast_to(words[:, 10:11], (rows, LANES)).astype(jnp.int32), words[:, 9:10], 0.0
    ).astype(BF16)
    fields = jnp.concatenate(value + [jnp.zeros((3, rows), F32)], axis=0)
    source = (lax.broadcasted_iota(jnp.int32, (8, rows), 1) & (plan.tiles * 8 - 1)) >> 3
    spread = jnp.concatenate([jnp.where(source == t, fields, 0.0) for t in range(plan.tiles)], axis=0)
    high, middle, low = thirds(spread)
    spread = mul(high, chosen) + mul(middle, chosen) + mul(low, chosen)
    packed[:, plan.main_rows : plan.coded_rows, :] = jnp.zeros((8, plan.devices, LANES), F32)
    for t in range(plan.tiles):
        row = plan.main_rows + (my_replica * (plan.tiles // 8) + t // 8) * 8
        packed[t % 8, pl.ds(pl.multiple_of(row, 8), 8), :] = spread[8 * t : 8 * t + 8]

    for block in range(8):
        spot = jnp.bitwise_xor(block, my_block) & 3

        @pl.when((my_block >> 2) == block // 4)
        def _():
            keep_ref[spot] = packed[block]

        @pl.when((my_block >> 2) != block // 4)
        def _():
            encode(plan, lambda start, count: packed[block, start : start + count, :], send_ref.at[spot])


class Plan:
    def __init__(self, tiles, replicas, queries, planes, hidden, latents):
        self.tiles, self.replicas, self.planes = tiles, replicas, planes
        self.slots = 2 * queries // tiles
        self.devices = tiles * replicas
        self.query_total = float(queries * self.devices)
        self.main_rows = (hidden + latents) // 2
        self.coded_rows = self.main_rows + self.devices
        self.rows = self.coded_rows + 8
        self.scales = -(-(self.coded_rows // SUB + 1) // 16) * 16
        self.sent_rows = self.coded_rows + 16 + self.scales
        top = self.devices.bit_length() - 1
        self.core, self.plane, self.rest = [0], [1, top - 1], list(range(2, top - 1))

    def mask(self, bits, steps):
        return sum(1 << bit for number, bit in enumerate(bits) if steps >> number & 1)

    def my_block(self, device):
        return (device & 1) * 4 + (device >> 1 & 1) + 2 * (device >> self.plane[1] & 1)


def swapped(value, plan, bits, steps):
    mask = plan.mask(bits, steps)
    return lax.ppermute(value, ("replica", "tile"), [(i, i ^ mask) for i in range(plan.devices)])


def encode(plan, read, out_ref):
    starts = list(range(0, plan.coded_rows, SUB))
    parts = [read(start, SUB) for start in starts] + [read(plan.coded_rows, 8)]
    tops = [jnp.max(jnp.abs(part), axis=0, keepdims=True) for part in parts]
    tops = tops + [jnp.zeros_like(tops[0])] * (plan.scales - len(tops))
    power = jnp.floor(jnp.log2(jnp.maximum(jnp.concatenate(tops, axis=0), 1e-30)))
    scale = jnp.exp2(14.0 - power)

    def whole(value):
        return jnp.clip(jnp.round(value), -32767.0, 32767.0)

    def narrow(value):
        return value.astype(jnp.int32).astype(jnp.int16)

    for number, start in enumerate(starts):
        out_ref[start : start + SUB, :] = narrow(whole(parts[number] * scale[number : number + 1]))
    last = len(starts)
    exact = parts[last] * scale[last : last + 1]
    high = whole(exact)
    low = whole((exact - high) * 32768.0)
    out_ref[plan.coded_rows : plan.coded_rows + 16, :] = narrow(jnp.concatenate([high, low], axis=0))
    out_ref[plan.coded_rows + 16 :, :] = narrow(power)


def decoder(plan, ref):
    def widen(value):
        return value.astype(jnp.int32).astype(F32)

    scale = jnp.exp2(widen(ref[plan.coded_rows + 16 :, :]) - 14.0)

    def read(start, count):
        if start < plan.coded_rows:
            number = start // SUB
            return widen(ref[start : start + count, :]) * scale[number : number + 1]
        both = widen(ref[plan.coded_rows : plan.coded_rows + 16, :])
        number = plan.coded_rows // SUB
        return (both[:8] + both[8:] * (1.0 / 32768.0)) * scale[number : number + 1]

    return read


def added(readers):
    def read(start, count):
        total = readers[0](start, count)
        for reader in readers[1:]:
            total = total + reader(start, count)
        return total

    return read


def first_kernel(plan, numbers, keep_ref, got_ref, *refs):
    def reader(block):
        got = decoder(plan, got_ref.at[block])
        return lambda start, count: keep_ref[block, start : start + count, :] + got(start, count)

    for number, out_ref in zip(numbers, refs):
        if number:
            encode(plan, reader(number), out_ref)
        else:
            read = reader(0)
            for start in range(0, plan.coded_rows, SUB):
                out_ref[start : start + SUB, :] = read(start, SUB)
            out_ref[plan.coded_rows :, :] = read(plan.coded_rows, 8)


def first_sum(keep, got, numbers, plan):
    sent = jax.ShapeDtypeStruct((plan.sent_rows, LANES), jnp.int16)
    own = jax.ShapeDtypeStruct(keep.shape[1:], F32)
    return pl.pallas_call(
        functools.partial(first_kernel, plan, numbers),
        out_shape=tuple(sent if number else own for number in numbers),
        in_specs=[VMEM] * 2,
        out_specs=tuple([VMEM] * len(numbers)),
        compiler_params=pltpu.CompilerParams(vmem_limit_bytes=6 << 20),
        name="sum_core",
    )(keep, got)


def plane_kernel(plan, mine_ref, *refs):
    readers = [lambda start, count: mine_ref[start : start + count, :]]
    encode(plan, added(readers + [decoder(plan, ref) for ref in refs[:-1]]), refs[-1])


def pair_kernel(plan, mine_ref, other_ref, out_ref):
    encode(plan, added([decoder(plan, mine_ref), decoder(plan, other_ref)]), out_ref)


def coded_sum(kernel, blocks, plan, name):
    return pl.pallas_call(
        functools.partial(kernel, plan),
        out_shape=jax.ShapeDtypeStruct((plan.sent_rows, LANES), jnp.int16),
        in_specs=[VMEM] * len(blocks),
        out_specs=VMEM,
        compiler_params=pltpu.CompilerParams(vmem_limit_bytes=4 << 20),
        name=name,
    )(*blocks)


def main(place, lat, words, small, weights, plan):
    rows = plan.tiles * plan.slots
    hidden = weights[2].shape[0]
    channels = lat.shape[1]
    outs = jax.ShapeDtypeStruct((4, plan.rows, LANES), F32)
    wide = lambda kind: pltpu.VMEM((5 * rows, hidden), kind)
    return pl.pallas_call(
        functools.partial(main_kernel, plan),
        out_shape=(jax.ShapeDtypeStruct((4, plan.sent_rows, LANES), jnp.int16), outs),
        in_specs=[SMEM] + [VMEM] * 3 + [HBM] * 4,
        out_specs=(VMEM, VMEM),
        scratch_shapes=[
            pltpu.VMEM((rows, channels), BF16),
            pltpu.VMEM((rows, LANES), F32),
            pltpu.VMEM((rows, hidden), F32),
            wide(BF16),
            wide(BF16),
            wide(F32),
            wide(BF16),
            wide(BF16),
            wide(F32),
            wide(F32),
            pltpu.VMEM((rows, hidden), BF16),
            pltpu.VMEM((rows, hidden), BF16),
            pltpu.VMEM((6, 8, hidden), F32),
            pltpu.VMEM((5 * rows, 2 * hidden), BF16),
            pltpu.VMEM((40, rows), F32),
            pltpu.VMEM((40, rows), F32),
            pltpu.VMEM((8, plan.rows, LANES), F32),
            pltpu.VMEM((hidden, hidden), BF16),
            pltpu.VMEM((hidden, hidden), BF16),
        ]
        + [pltpu.VMEM(weight.shape, F32) for weight in weights]
        + [pltpu.SemaphoreType.DMA((4,))],
        compiler_params=pltpu.CompilerParams(vmem_limit_bytes=32 << 20),
        name="encode_decode",
    )(place, lat, words, small, *weights)


def unpack_kernel(plan, place_ref, *refs):
    sources, outs, (packed, mid_part, latent_part, sems) = refs[:8], refs[8:-4], refs[-4:]
    prediction_ref, latent_hbm, pos_ref, one_ref, mid_hbm, two_ref, out_ref, bias_out_ref, loss_ref = outs
    my_block = place_ref[0]
    device = place_ref[2] * plan.tiles + place_ref[1]
    starts = list(range(0, plan.coded_rows, SUB))
    hidden = mid_hbm.shape[0]
    split = plan.main_rows
    copies = []
    for half in range(2):
        for number in range(4):
            read = decoder(plan, sources[4 * half + number])
            block = jnp.bitwise_xor(4 * half + number, my_block)
            for start in starts:
                packed[block, start : start + SUB, :] = read(start, SUB)
            packed[block, plan.coded_rows :, :] = read(plan.coded_rows, 8)
        core = (my_block >> 2) ^ half
        for part in range(2):
            lanes = slice(part * LANES, (part + 1) * LANES)
            upper, lower = packed.at[core * 4 + 2 * part], packed.at[core * 4 + 2 * part + 1]
            mid_part[half, 0:split, lanes] = upper[0:split, :]
            mid_part[half, split:, lanes] = lower[0 : hidden - split, :]
            latent_part[half, :, lanes] = lower[hidden - split : split, :]
        columns = pl.ds(pl.multiple_of(core * 2 * LANES, 2 * LANES), 2 * LANES)
        for number, (source, target) in enumerate(((mid_part, mid_hbm), (latent_part, latent_hbm))):
            copy = pltpu.make_async_copy(source.at[half], target.at[:, columns], sems.at[half, number])
            copy.start()
            copies.append(copy)

    for part in range(hidden // LANES):
        lanes = slice(part * LANES, (part + 1) * LANES)
        misc = packed[2 * part, plan.coded_rows :, :]
        pos_ref[:, lanes] = misc[0:3]
        one_ref[:, lanes] = misc[3:4]
        two_ref[:, lanes] = misc[4:5]
        out_ref[:, lanes] = packed[2 * part + 1, plan.coded_rows : plan.coded_rows + 5, :]
        if part == 0:
            bias_out_ref[...] = misc[5:6, 0:5]
            loss_ref[...] = misc[5:6, 5:6]
    row = pl.multiple_of(plan.main_rows + (device >> 3) * 8, 8)
    fields = packed[device & 7, pl.ds(row, 8), :]
    for f in range(5):
        prediction_ref[f] = fields[f : f + 1]
    for copy in copies:
        copy.wait()


def unpack(place, blocks, plan, hidden, latents):
    shapes = [
        (5, 1, LANES),
        (latents, hidden),
        (3, hidden),
        (1, hidden),
        (hidden, hidden),
        (1, hidden),
        (5, hidden),
        (1, 5),
        (1, 1),
    ]
    return pl.pallas_call(
        functools.partial(unpack_kernel, plan),
        out_shape=tuple(jax.ShapeDtypeStruct(shape, F32) for shape in shapes),
        in_specs=[SMEM] + [VMEM] * 8,
        out_specs=(VMEM, HBM, VMEM, VMEM, HBM, VMEM, VMEM, VMEM, VMEM),
        scratch_shapes=[
            pltpu.VMEM((8, plan.rows, LANES), F32),
            pltpu.VMEM((2, hidden, 2 * LANES), F32),
            pltpu.VMEM((2, latents, 2 * LANES), F32),
            pltpu.SemaphoreType.DMA((2, 2)),
        ],
        compiler_params=pltpu.CompilerParams(vmem_limit_bytes=16 << 20),
        name="unpack",
    )(place, *blocks)


def body(
    fields,
    convolution_weight,
    convolution_bias,
    query_owner,
    query_cell,
    query_frac,
    target,
    w_latent,
    w_pos,
    bias_one,
    w_mid,
    bias_two,
    w_out,
    bias_out,
):
    tiles = lax.axis_size("tile")
    replicas = lax.axis_size("replica")
    my_tile = lax.axis_index("tile")
    my_replica = lax.axis_index("replica")
    channels = fields.shape[1]
    queries = query_cell.shape[1]
    hidden = w_mid.shape[0]
    plan = Plan(tiles, replicas, queries, fields.shape[2], hidden, channels)
    device = my_replica * tiles + my_tile
    place = jnp.stack([plan.my_block(device), my_tile, my_replica]).astype(jnp.int32)

    here = fields[0].transpose(1, 2, 0, 3)
    odd = my_tile & 1
    count = DILATION_RATE + 1
    first = lax.dynamic_slice_in_dim(here, (1 - odd) * (here.shape[0] - count), count, axis=0)
    second = lax.dynamic_slice_in_dim(here, odd * (here.shape[0] - count), count, axis=0)
    first, second, query_owner = lax.optimization_barrier((first, second, query_owner))
    near = lax.ppermute(first, "tile", [(i, i ^ 1) for i in range(tiles)])
    far = lax.ppermute(second, "tile", [(i, (i - 1 + 2 * (i & 1)) % tiles) for i in range(tiles)])
    words, small = route(
        (query_owner[:, :, 0], query_cell, query_frac.transpose(1, 0, 2), target.transpose(1, 0, 2)),
        (bias_one[None], bias_two[None], bias_out[None], convolution_bias[None]),
        tiles,
        plan.slots,
    )
    words = lax.all_to_all(
        words.reshape(tiles, 8, WORDS), "tile", split_axis=0, concat_axis=0, tiled=True
    ).reshape(tiles * 8, WORDS)

    lat = convolve(place, near, here, far, convolution_weight, small)
    weights = (w_latent, w_pos, w_mid, w_out)
    send, keep = main(place, lat, words, small, weights, plan)

    got = swapped(send, plan, plan.core, 1)
    (far,) = first_sum(keep, got, (3,), plan)
    far, keep = lax.optimization_barrier((far, keep))
    mine, *near = first_sum(keep, got, (0, 1, 2), plan)
    arrived = [swapped(block, plan, plan.plane, step) for step, block in ((3, far), (1, near[0]), (2, near[1]))]
    block = coded_sum(plane_kernel, [mine] + arrived, plan, "sum_plane")
    for bit in plan.rest:
        block = coded_sum(pair_kernel, [block, swapped(block, plan, [bit], 1)], plan, "sum_line")
    blocks = [block] + [swapped(block, plan, plan.plane, step) for step in range(1, 4)]
    blocks = blocks + [swapped(block, plan, plan.core, 1) for block in blocks]
    prediction, g_latent, g_pos, g_one, g_mid, g_two, g_out, g_bias, loss = unpack(
        place, blocks, plan, hidden, channels
    )
    return (
        prediction.transpose(1, 0, 2),
        g_latent,
        g_pos,
        g_one.reshape(hidden),
        g_mid,
        g_two.reshape(hidden),
        g_out,
        g_bias.reshape(5),
        loss.reshape(()),
    )


def solution(mesh):
    return jax.shard_map(
        body,
        mesh=mesh,
        in_specs=(
            P("replica", None, "tile", None, None),
            P(),
            P(),
            P("replica", "tile", None),
            P("replica", "tile"),
            P("replica", None, "tile"),
            P("replica", None, "tile"),
            P(),
            P(),
            P(),
            P(),
            P(),
            P(),
            P(),
        ),
        out_specs=(P("replica", None, "tile"), P(), P(), P(), P(), P(), P(), P(), P()),
        check_vma=False,
    )
```

```python
import functools

import jax
import jax.numpy as jnp
from jax import lax
from jax.experimental import pallas as pl
from jax.experimental.pallas import tpu as pltpu
from jax.sharding import PartitionSpec as P

DILATION_RATE = 2
VISCOSITY = 0.05
DIFFUSIVITY = 0.05
RESIDUAL_WEIGHT = 0.5

F32 = jnp.float32
BF16 = jnp.bfloat16
LANES = 128
BLOCK = 32
WORDS = 128
SUB = 32
NN = (((1,), (0,)), ((), ()))
NT = (((1,), (1,)), ((), ()))
TN = (((0,), (0,)), ((), ()))
VMEM = pl.BlockSpec(memory_space=pltpu.VMEM)
SMEM = pl.BlockSpec(memory_space=pltpu.SMEM)
HBM = pl.BlockSpec(memory_space=pltpu.HBM)


def mul(left, right, dims=NN):
    return lax.dot_general(left, right, dims, preferred_element_type=F32)


def halves(value):
    high = value.astype(BF16)
    return high, (value - high.astype(F32)).astype(BF16)


def thirds(value):
    high = value.astype(BF16)
    rest = value - high.astype(F32)
    middle = rest.astype(BF16)
    return high, middle, (rest - middle.astype(F32)).astype(BF16)


def mul3(left, right, dims=NN):
    return mul(left[0], right[0], dims) + mul(left[0], right[1], dims) + mul(left[1], right[0], dims)


def fetches(sources, targets, sems):
    copies = [
        pltpu.make_async_copy(source, target, sems.at[number])
        for number, (source, target) in enumerate(zip(sources, targets))
    ]
    for copy in copies:
        copy.start()
    return copies


def route_kernel(tiles, slots, *refs):
    out_ref, small_ref, *scratch, words, sems = refs[8:]
    for copy in fetches(refs[:8], scratch, sems):
        copy.wait()
    owner_ref, cell_ref, frac_ref, target_ref, *bias_refs = scratch
    queries = owner_ref.shape[1]
    small_ref[...] = jnp.zeros_like(small_ref)
    for number, ref in enumerate(bias_refs):
        small_ref[number : number + 1, 0 : ref.shape[1]] = ref[...]
    owner = owner_ref[...]
    hits = (lax.broadcasted_iota(jnp.int32, (tiles, queries), 0) == owner).astype(F32)
    before = lax.broadcasted_iota(jnp.int32, (queries, queries), 0) < lax.broadcasted_iota(
        jnp.int32, (queries, queries), 1
    )
    earlier = mul(hits.astype(BF16), before.astype(F32).astype(BF16))
    slot = jnp.sum(hits * earlier, axis=0, keepdims=True)
    place = owner * slots + slot.astype(jnp.int32)
    spot = lax.broadcasted_iota(jnp.int32, (tiles * 8, queries), 0)
    spot = (spot >> 3) * slots + (spot & 7)
    groups = slots // 8
    chosen = [jnp.where(spot + 8 * group == place, 1.0, 0.0) for group in range(groups)]
    chosen = jnp.concatenate(chosen, axis=1).astype(BF16)
    words[...] = jnp.zeros_like(words)
    for group in range(groups):
        row, lanes = 16 * group, slice(group * queries, (group + 1) * queries)
        words[row : row + 1, lanes] = cell_ref[...].astype(F32)
        for d in range(3):
            words[row + 1 + d : row + 2 + d, lanes] = frac_ref[d]
        for f in range(5):
            words[row + 4 + f : row + 5 + f, lanes] = target_ref[f]
        words[row + 9 : row + 10, lanes] = jnp.ones((1, queries), F32)
        words[row + 10 : row + 11, lanes] = lax.broadcasted_iota(jnp.int32, (1, queries), 1).astype(F32)
    high, middle, low = thirds(words[...])
    out_ref[...] = mul(chosen, high, NT) + mul(chosen, middle, NT) + mul(chosen, low, NT)


def route(inputs, biases, tiles, slots):
    queries = inputs[0].shape[1]
    arrays = inputs + biases
    return pl.pallas_call(
        functools.partial(route_kernel, tiles, slots),
        out_shape=(
            jax.ShapeDtypeStruct((tiles * 8, WORDS), F32),
            jax.ShapeDtypeStruct((8, biases[0].shape[1]), F32),
        ),
        in_specs=[HBM] * 8,
        out_specs=(VMEM, VMEM),
        scratch_shapes=[pltpu.VMEM(array.shape, array.dtype) for array in arrays]
        + [pltpu.VMEM((WORDS, queries * (slots // 8)), F32), pltpu.SemaphoreType.DMA((8,))],
        compiler_params=pltpu.CompilerParams(vmem_limit_bytes=4 << 20),
        name="route",
    )(*arrays)


def tap_sum(weight_ref, planes, pair):
    total = None
    for step_x, ref, index in planes:
        rows_y = ref.shape[1]
        blocks = [
            jnp.concatenate([ref[index, (2 * pair + half + step_y) % rows_y] for half in (0, 1)], axis=1)
            for step_y in (-1, 0, 1)
        ]
        term = mul(weight_ref[step_x], jnp.concatenate(blocks, axis=0))
        total = term if total is None else total + term
    channels = total.shape[0] // 3
    sides = []
    for half in (0, 1):
        part = total[:, half * LANES : (half + 1) * LANES]
        sides.append(
            part[channels : 2 * channels]
            + pltpu.roll(part[:channels], 1, 1)
            + pltpu.roll(part[2 * channels :], LANES - 1, 1)
        )
    return jnp.concatenate(sides, axis=1)


def conv_kernel(
    place_ref,
    near_ref,
    here_ref,
    far_ref,
    taps_ref,
    small_ref,
    lat_ref,
    weight_ref,
):
    planes, rows_y, channels = here_ref.shape[:3]
    taps = taps_ref[...].astype(F32)
    for step in range(3):
        rows = []
        for step_z in range(3):
            numbers = [9 * step + 3 * step_y + step_z for step_y in range(3)]
            rows.append(
                jnp.concatenate([taps[:, n * channels : (n + 1) * channels] for n in numbers], axis=1)
            )
        weight_ref[step] = jnp.concatenate(rows, axis=0).astype(BF16)
    diagonal = lax.broadcasted_iota(jnp.int32, (channels, channels), 0) == lax.broadcasted_iota(
        jnp.int32, (channels, channels), 1
    )
    bias = jnp.sum(jnp.where(diagonal, small_ref[3:4, 0:channels], 0.0), axis=1, keepdims=True)
    def all_planes(left_ref, right_ref):
        for x in range(planes + 1):
            taps = []
            for step in range(3):
                plane = x + DILATION_RATE * (step - 1)
                if plane < 0:
                    taps.append((step, left_ref, plane + left_ref.shape[0]))
                elif plane >= planes:
                    taps.append((step, right_ref, plane - planes))
                else:
                    taps.append((step, here_ref, plane))
            for pair in range(rows_y // 2):
                summed = tap_sum(weight_ref, taps, pair) + bias
                lat_ref[x * (rows_y // 2) + pair] = jax.nn.gelu(summed).astype(BF16)

    even = (place_ref[1] & 1) == 0

    @pl.when(even)
    def _():
        all_planes(far_ref, near_ref)

    @pl.when(jnp.logical_not(even))
    def _():
        all_planes(near_ref, far_ref)


def convolve(place, near, here, far, taps, small):
    planes, rows_y, channels, rows_z = here.shape
    pairs = (planes + 1) * rows_y // 2
    return pl.pallas_call(
        conv_kernel,
        out_shape=jax.ShapeDtypeStruct((pairs, channels, 2 * rows_z), BF16),
        in_specs=[SMEM] + [VMEM] * 5,
        out_specs=VMEM,
        scratch_shapes=[pltpu.VMEM((3, 3 * channels, 3 * channels), BF16)],
        compiler_params=pltpu.CompilerParams(vmem_limit_bytes=8 << 20),
        cost_estimate=pl.CostEstimate(flops=3 << 30, bytes_accessed=4 << 20, transcendentals=0),
        name="convolve",
    )(place, near, here, far, taps, small)


def interpolate(words, lat, planes, rows_y, rows_z):
    rows = words.shape[0]
    cell = jnp.broadcast_to(words[:, 0:1], (rows, LANES)).astype(jnp.int32)
    frac = [jnp.broadcast_to(words[:, 1 + d : 2 + d], (rows, LANES)) for d in range(3)]
    shift_z = rows_z.bit_length() - 1
    shift_y = rows_y.bit_length() - 1
    base_x = cell >> (shift_z + shift_y)
    base_y = (cell >> shift_z) & (rows_y - 1)
    base_z = cell & (rows_z - 1)
    spot = lax.broadcasted_iota(jnp.int32, (rows, rows_z), 1)
    part_z = jnp.where(spot == base_z, 1.0 - frac[2], 0.0) + jnp.where(
        spot == ((base_z + 1) & (rows_z - 1)), frac[2], 0.0
    )
    part_yz = []
    for y in range(rows_y):
        part_y = jnp.where(
            base_y == y, 1.0 - frac[1], jnp.where(base_y == (y - 1) % rows_y, frac[1], 0.0)
        )
        part_yz.append(part_y * part_z)
    total = None
    for x in range(planes + 1):
        part_x = jnp.where(base_x == x, 1.0 - frac[0], jnp.where(base_x == x - 1, frac[0], 0.0))
        for pair in range(rows_y // 2):
            sides = [(part_x * part_yz[2 * pair + half]).astype(BF16) for half in (0, 1)]
            term = mul(jnp.concatenate(sides, axis=1), lat[x * (rows_y // 2) + pair], NT)
            total = term if total is None else total + term
    return total.astype(BF16), base_x, base_y, base_z, frac


def folded(value):
    return jnp.sum(value.reshape(value.shape[0] // 8, 8, value.shape[1]), axis=0)


def main_kernel(
    plan,
    place_ref,
    lat,
    words_ref,
    small_ref,
    w_latent_hbm,
    w_pos_hbm,
    w_mid_hbm,
    w_out_hbm,
    send_ref,
    keep_ref,
    code,
    pos,
    z_one,
    one_high,
    one_low,
    mixed,
    two_high,
    two_low,
    back,
    mixed_back,
    first_high,
    first_low,
    sums_ref,
    d_both,
    out_t,
    d_out_t,
    packed,
    mid_high,
    mid_low,
    w_latent_ref,
    w_pos_ref,
    w_mid_ref,
    w_out_ref,
    sems,
):
    rows = plan.tiles * plan.slots
    hidden = w_mid_ref.shape[0]
    latents = w_latent_ref.shape[0]
    weights = fetches(
        (w_latent_hbm, w_pos_hbm, w_mid_hbm, w_out_hbm),
        (w_latent_ref, w_pos_ref, w_mid_ref, w_out_ref),
        sems,
    )
    planes, rows_z = plan.planes, lat.shape[2] // 2
    rows_y = lat.shape[0] // (planes + 1) * 2
    slots = rows // plan.tiles
    my_block = place_ref[0]
    my_tile = place_ref[1]
    my_replica = place_ref[2]
    always = my_tile >= 0

    words = words_ref[...]
    words = jnp.concatenate(
        [words] + [pltpu.roll(words, LANES - 16 * group, 1) for group in range(1, slots // 8)], axis=0
    )
    interp, base_x, base_y, base_z, frac = interpolate(words, lat, planes, rows_y, rows_z)
    code[...] = interp
    global_x = my_tile * planes + base_x
    lane = lax.broadcasted_iota(jnp.int32, (rows, LANES), 1)
    pos[...] = jnp.where(
        lane == 0,
        (global_x.astype(F32) + frac[0]) / (planes * plan.tiles),
        jnp.where(
            lane == 1,
            (base_y.astype(F32) + frac[1]) / rows_y,
            (base_z.astype(F32) + frac[2]) / rows_z,
        ),
    )

    for copy in weights:
        copy.wait()
    high, low = halves(w_latent_ref[...])
    z_one[...] = mul(interp, high) + mul(interp, low)
    high, low = halves(w_mid_ref[...])
    mid_high[...] = high
    mid_low[...] = low
    w_pos = [w_pos_ref[d : d + 1, :] for d in range(3)]
    square = w_pos[0] * w_pos[0] + w_pos[1] * w_pos[1] + w_pos[2] * w_pos[2]
    bias_one = small_ref[0:1, :]
    bias_two = small_ref[1:2, :]

    part_rows = rows // 2

    def at(part, index, block=None):
        first = (part * 5 + index) * part_rows
        if block is None:
            return slice(first, first + part_rows)
        return slice(first + block * BLOCK, first + (block + 1) * BLOCK)

    def rows_at(part, block):
        first = part * part_rows + block * BLOCK
        return slice(first, first + BLOCK)

    def store(refs, span, value):
        high, low = halves(value)
        refs[0][span, :] = high
        refs[1][span, :] = low

    def layer_one(part):
        refs = (one_high, one_low)
        for block in range(part_rows // BLOCK):
            here = rows_at(part, block)
            where = pos[here, :]
            pre = (
                z_one[here, :]
                + (where[:, 0:1] * w_pos[0] + where[:, 1:2] * w_pos[1] + where[:, 2:3] * w_pos[2])
                + bias_one
            )
            act = jnp.tanh(pre)
            slope = 1.0 - act * act
            curve = -2.0 * act * slope
            z_one[here, :] = act
            store(refs, at(part, 0, block), act)
            for d in range(3):
                store(refs, at(part, 1 + d, block), slope * w_pos[d])
            store(refs, at(part, 4, block), curve * square)

    def times_mid(dims, source, result, part):
        span = slice(part * 5 * part_rows, (part + 1) * 5 * part_rows)
        left = (source[0][span, :], source[1][span, :])
        result[span, :] = mul3(left, (mid_high[...], mid_low[...]), dims)

    def layer_two(part):
        refs = (two_high, two_low)
        for block in range(part_rows // BLOCK):
            act = jnp.tanh(mixed[at(part, 0, block), :] + bias_two)
            slope = 1.0 - act * act
            curve = -2.0 * act * slope
            store(refs, at(part, 0, block), act)
            mixed[at(part, 0, block), :] = act
            norm = None
            for d in range(3):
                tangent = mixed[at(part, 1 + d, block), :]
                store(refs, at(part, 1 + d, block), slope * tangent)
                norm = tangent * tangent if norm is None else norm + tangent * tangent
            store(refs, at(part, 4, block), slope * mixed[at(part, 4, block), :] + curve * norm)

    out_fields = jnp.concatenate([w_out_ref[...], jnp.zeros((3, hidden), F32)], axis=0)
    wo_high, wo_low = halves(out_fields)
    wo_three = jnp.concatenate([out_fields, wo_low.astype(F32), out_fields], axis=0).astype(BF16)
    wo_both = jnp.concatenate(
        [out_fields, wo_low.astype(F32), jnp.zeros((LANES - 16, hidden), F32)], axis=0
    ).astype(BF16)

    def outputs(part):
        span = slice(part * 5 * part_rows, (part + 1) * 5 * part_rows)
        both = mul(two_high[span, :], wo_both, NT)
        low = mul(two_low[span, :], wo_both, NT)
        for s in range(5):
            rows_s = slice(s * part_rows, (s + 1) * part_rows)
            both_t, low_t = both[rows_s].T, low[rows_s].T
            out_t[8 * s : 8 * s + 8, part * part_rows : (part + 1) * part_rows] = (
                both_t[0:8] + both_t[8:16] + low_t[0:8]
            )

    @pl.when(always)
    def _():
        layer_one(0)
        times_mid(NN, (one_high, one_low), mixed, 0)
        layer_one(1)
        times_mid(NN, (one_high, one_low), mixed, 1)
        layer_two(0)
        outputs(0)
        layer_two(1)
        outputs(1)

    words_t = words.T
    target = [words_t[4 + f : 5 + f, :] for f in range(5)]
    valid = words_t[9:10, :]
    value = [out_t[f : f + 1, :] + small_ref[2:3, f : f + 1] for f in range(5)]
    grad = [[out_t[8 * (d + 1) + f : 8 * (d + 1) + f + 1, :] for f in range(5)] for d in range(3)]
    laplace = [out_t[32 + f : 33 + f, :] for f in range(5)]
    velocity = value[2:5]
    advection = [
        velocity[0] * grad[0][f] + velocity[1] * grad[1][f] + velocity[2] * grad[2][f] for f in range(5)
    ]
    continuity = grad[0][2] + grad[1][3] + grad[2][4]
    momentum = [advection[2 + j] + grad[j][1] - VISCOSITY * laplace[2 + j] for j in range(3)]
    momentum[2] = momentum[2] - value[0]
    energy = advection[0] - DIFFUSIVITY * laplace[0]
    misfit = [value[f] - target[f] for f in range(5)]
    physics = (
        continuity * continuity
        + (momentum[0] * momentum[0] + momentum[1] * momentum[1] + momentum[2] * momentum[2])
        + energy * energy
    )
    squares = (
        misfit[0] * misfit[0]
        + misfit[1] * misfit[1]
        + misfit[2] * misfit[2]
        + misfit[3] * misfit[3]
        + misfit[4] * misfit[4]
    )
    point_loss = valid * (squares + RESIDUAL_WEIGHT * physics) * (1.0 / plan.query_total)

    rate = valid * (1.0 / plan.query_total)
    twice = RESIDUAL_WEIGHT * 2.0
    d_cont = rate * twice * continuity
    d_mom = [rate * twice * m for m in momentum]
    d_energy = rate * twice * energy
    d_value = [2.0 * rate * m for m in misfit]
    for d in range(3):
        d_value[2 + d] = d_value[2 + d] + (
            d_mom[0] * grad[d][2] + d_mom[1] * grad[d][3] + d_mom[2] * grad[d][4] + d_energy * grad[d][0]
        )
    d_value[0] = d_value[0] - d_mom[2]
    d_out_t[...] = jnp.zeros_like(d_out_t)
    for f in range(5):
        d_out_t[f : f + 1, :] = d_value[f]
    for d in range(3):
        first = 8 * (d + 1)
        d_out_t[first : first + 1, :] = d_energy * velocity[d]
        d_out_t[first + 1 : first + 2, :] = d_mom[d]
        for j in range(3):
            term = d_mom[j] * velocity[d]
            if j == d:
                term = term + d_cont
            d_out_t[first + 2 + j : first + 3 + j, :] = term
    d_out_t[32:33, :] = -DIFFUSIVITY * d_energy
    for j in range(3):
        d_out_t[34 + j : 35 + j, :] = -VISCOSITY * d_mom[j]

    def out_back(part):
        columns = slice(part * part_rows, (part + 1) * part_rows)
        wanted = jnp.concatenate([d_out_t[8 * s : 8 * s + 8, columns] for s in range(5)], axis=1)
        do_low = halves(wanted)[1].astype(F32)
        wanted = jnp.concatenate([wanted, wanted, do_low], axis=0).astype(BF16)
        back[part * 5 * part_rows : (part + 1) * 5 * part_rows, :] = mul(wanted, wo_three, TN)

    def second_back(part, total):
        refs = (d_both.at[:, :hidden], d_both.at[:, hidden:])
        for block in range(part_rows // BLOCK):
            act = mixed[at(part, 0, block), :]
            slope = 1.0 - act * act
            curve = -2.0 * act * slope
            cot_l = back[at(part, 4, block), :]
            d_slope = cot_l * mixed[at(part, 4, block), :]
            norm = None
            bent = 2.0 * curve * cot_l
            for d in range(3):
                tangent = mixed[at(part, 1 + d, block), :]
                cot_t = back[at(part, 1 + d, block), :]
                store(refs, at(part, 1 + d, block), slope * cot_t + bent * tangent)
                d_slope = d_slope + cot_t * tangent
                norm = tangent * tangent if norm is None else norm + tangent * tangent
            store(refs, at(part, 4, block), slope * cot_l)
            d_curve = cot_l * norm
            d_slope = d_slope - 2.0 * act * d_curve
            d_act = back[at(part, 0, block), :] - 2.0 * slope * d_curve - 2.0 * act * d_slope
            d_pre = slope * d_act
            store(refs, at(part, 0, block), d_pre)
            total = total + folded(d_pre)
        return total

    def first_back(part, sums):
        for block in range(part_rows // BLOCK):
            here = rows_at(part, block)
            act = z_one[here, :]
            slope = 1.0 - act * act
            curve = -2.0 * act * slope
            where = pos[here, :]
            cot_t = [mixed_back[at(part, 1 + d, block), :] for d in range(3)]
            cot_l = mixed_back[at(part, 4, block), :]
            d_curve = cot_l * square
            d_slope = cot_t[0] * w_pos[0] + cot_t[1] * w_pos[1] + cot_t[2] * w_pos[2] - 2.0 * act * d_curve
            d_act = mixed_back[at(part, 0, block), :] - 2.0 * slope * d_curve - 2.0 * act * d_slope
            d_pre = slope * d_act
            high, low = halves(d_pre)
            first_high[here, :] = high
            first_low[here, :] = low
            sums = (
                [sums[0] + folded(d_pre)]
                + [sums[1 + d] + folded(where[:, d : d + 1] * d_pre + slope * cot_t[d]) for d in range(3)]
                + [sums[4] + folded(curve * cot_l)]
            )
        return sums


    def put(part, first, value):
        while value.shape[0]:
            block, row = first // plan.main_rows, first % plan.main_rows
            count = min(value.shape[0], plan.main_rows - row)
            packed[2 * part + block, row : row + count, :] = value[:count]
            first, value = first + count, value[count:]

    def mid_gradient():
        both = mul(one_high[...], d_both[...], TN)
        both = both[:, :hidden] + both[:, hidden:] + mul(one_low[...], d_both[:, :hidden], TN)
        for part in range(hidden // LANES):
            put(part, 0, both[:, part * LANES : (part + 1) * LANES])

    @pl.when(always)
    def _():
        out_back(0)
        total = second_back(0, jnp.zeros((8, hidden), F32))
        out_back(1)
        times_mid(NT, (d_both.at[:, :hidden], d_both.at[:, hidden:]), mixed_back, 0)
        sums_ref[5] = second_back(1, total)
        times_mid(NT, (d_both.at[:, :hidden], d_both.at[:, hidden:]), mixed_back, 1)
        total = first_back(0, [jnp.zeros((8, hidden), F32)] * 5)
        mid_gradient()
        for number, value in enumerate(first_back(1, total)):
            sums_ref[number] = value

    sums = [sums_ref[number] for number in range(6)]
    d_square = jnp.sum(sums[4], axis=0, keepdims=True)
    grad_latent = mul(code[...], first_high[...], TN) + mul(code[...], first_low[...], TN)

    parts = [d_out_t[8 * s : 8 * s + 8, p * part_rows : (p + 1) * part_rows] for p in range(2) for s in range(5)]
    flat = jnp.concatenate(parts, axis=1)
    fl_high, fl_low = halves(flat)
    fl_both = jnp.concatenate([flat, fl_low.astype(F32)], axis=0).astype(BF16)
    grad_out = mul(fl_both, two_high[...])
    grad_out = grad_out[:8] + grad_out[8:] + mul(fl_high, two_low[...])

    lane_row = lax.broadcasted_iota(jnp.int32, (1, hidden), 1)
    last = jnp.where(lane_row == 5, jnp.sum(point_loss), 0.0)
    for f in range(5):
        last = last + jnp.where(lane_row == f, jnp.sum(d_value[f]), 0.0)
    grad_pos = [jnp.sum(sums[1 + d], axis=0, keepdims=True) + 2.0 * w_pos[d] * d_square for d in range(3)]
    misc = grad_pos + [
        jnp.sum(sums[0], axis=0, keepdims=True),
        jnp.sum(sums[5], axis=0, keepdims=True),
        last,
    ]
    misc = jnp.concatenate(misc + [jnp.zeros((2, hidden), F32)], axis=0)
    for part in range(hidden // LANES):
        lanes = slice(part * LANES, (part + 1) * LANES)
        put(part, hidden, grad_latent[:, lanes])
        packed[2 * part, plan.coded_rows :, :] = misc[:, lanes]
        packed[2 * part + 1, plan.coded_rows :, :] = grad_out[:, lanes]

    chosen = jnp.where(
        lane == jnp.broadcast_to(words[:, 10:11], (rows, LANES)).astype(jnp.int32), words[:, 9:10], 0.0
    ).astype(BF16)
    fields = jnp.concatenate(value + [jnp.zeros((3, rows), F32)], axis=0)
    source = (lax.broadcasted_iota(jnp.int32, (8, rows), 1) & (plan.tiles * 8 - 1)) >> 3
    spread = jnp.concatenate([jnp.where(source == t, fields, 0.0) for t in range(plan.tiles)], axis=0)
    high, middle, low = thirds(spread)
    spread = mul(high, chosen) + mul(middle, chosen) + mul(low, chosen)
    packed[:, plan.main_rows : plan.coded_rows, :] = jnp.zeros((8, plan.devices, LANES), F32)
    for t in range(plan.tiles):
        row = plan.main_rows + (my_replica * (plan.tiles // 8) + t // 8) * 8
        packed[t % 8, pl.ds(pl.multiple_of(row, 8), 8), :] = spread[8 * t : 8 * t + 8]

    for block in range(8):
        spot = jnp.bitwise_xor(block, my_block) & 3

        @pl.when((my_block >> 2) == block // 4)
        def _():
            keep_ref[spot] = packed[block]

        @pl.when((my_block >> 2) != block // 4)
        def _():
            encode(plan, lambda start, count: packed[block, start : start + count, :], send_ref.at[spot])


class Plan:
    def __init__(self, tiles, replicas, queries, planes, hidden, latents):
        self.tiles, self.replicas, self.planes = tiles, replicas, planes
        self.slots = 2 * queries // tiles
        self.devices = tiles * replicas
        self.query_total = float(queries * self.devices)
        self.main_rows = (hidden + latents) // 2
        self.coded_rows = self.main_rows + self.devices
        self.rows = self.coded_rows + 8
        self.scales = -(-(self.coded_rows // SUB + 1) // 16) * 16
        self.sent_rows = self.coded_rows + 16 + self.scales
        top = self.devices.bit_length() - 1
        self.core, self.plane, self.rest = [0], [1, top - 1], list(range(2, top - 1))

    def mask(self, bits, steps):
        return sum(1 << bit for number, bit in enumerate(bits) if steps >> number & 1)

    def my_block(self, device):
        return (device & 1) * 4 + (device >> 1 & 1) + 2 * (device >> self.plane[1] & 1)


def swapped(value, plan, bits, steps):
    mask = plan.mask(bits, steps)
    return lax.ppermute(value, ("replica", "tile"), [(i, i ^ mask) for i in range(plan.devices)])


def encode(plan, read, out_ref):
    starts = list(range(0, plan.coded_rows, SUB))
    parts = [read(start, SUB) for start in starts] + [read(plan.coded_rows, 8)]
    tops = [jnp.max(jnp.abs(part), axis=0, keepdims=True) for part in parts]
    tops = tops + [jnp.zeros_like(tops[0])] * (plan.scales - len(tops))
    power = jnp.floor(jnp.log2(jnp.maximum(jnp.concatenate(tops, axis=0), 1e-30)))
    scale = jnp.exp2(14.0 - power)

    def whole(value):
        return jnp.clip(jnp.round(value), -32767.0, 32767.0)

    def narrow(value):
        return value.astype(jnp.int32).astype(jnp.int16)

    for number, start in enumerate(starts):
        out_ref[start : start + SUB, :] = narrow(whole(parts[number] * scale[number : number + 1]))
    last = len(starts)
    exact = parts[last] * scale[last : last + 1]
    high = whole(exact)
    low = whole((exact - high) * 32768.0)
    out_ref[plan.coded_rows : plan.coded_rows + 16, :] = narrow(jnp.concatenate([high, low], axis=0))
    out_ref[plan.coded_rows + 16 :, :] = narrow(power)


def decoder(plan, ref):
    def widen(value):
        return value.astype(jnp.int32).astype(F32)

    scale = jnp.exp2(widen(ref[plan.coded_rows + 16 :, :]) - 14.0)

    def read(start, count):
        if start < plan.coded_rows:
            number = start // SUB
            return widen(ref[start : start + count, :]) * scale[number : number + 1]
        both = widen(ref[plan.coded_rows : plan.coded_rows + 16, :])
        number = plan.coded_rows // SUB
        return (both[:8] + both[8:] * (1.0 / 32768.0)) * scale[number : number + 1]

    return read


def added(readers):
    def read(start, count):
        total = readers[0](start, count)
        for reader in readers[1:]:
            total = total + reader(start, count)
        return total

    return read


def first_kernel(plan, numbers, keep_ref, got_ref, *refs):
    def reader(block):
        got = decoder(plan, got_ref.at[block])
        return lambda start, count: keep_ref[block, start : start + count, :] + got(start, count)

    for number, out_ref in zip(numbers, refs):
        if number:
            encode(plan, reader(number), out_ref)
        else:
            read = reader(0)
            for start in range(0, plan.coded_rows, SUB):
                out_ref[start : start + SUB, :] = read(start, SUB)
            out_ref[plan.coded_rows :, :] = read(plan.coded_rows, 8)


def first_sum(keep, got, numbers, plan):
    sent = jax.ShapeDtypeStruct((plan.sent_rows, LANES), jnp.int16)
    own = jax.ShapeDtypeStruct(keep.shape[1:], F32)
    return pl.pallas_call(
        functools.partial(first_kernel, plan, numbers),
        out_shape=tuple(sent if number else own for number in numbers),
        in_specs=[VMEM] * 2,
        out_specs=tuple([VMEM] * len(numbers)),
        compiler_params=pltpu.CompilerParams(vmem_limit_bytes=6 << 20),
        name="sum_core",
    )(keep, got)


def plane_kernel(plan, mine_ref, *refs):
    readers = [lambda start, count: mine_ref[start : start + count, :]]
    encode(plan, added(readers + [decoder(plan, ref) for ref in refs[:-1]]), refs[-1])


def pair_kernel(plan, mine_ref, other_ref, out_ref):
    encode(plan, added([decoder(plan, mine_ref), decoder(plan, other_ref)]), out_ref)


def coded_sum(kernel, blocks, plan, name):
    return pl.pallas_call(
        functools.partial(kernel, plan),
        out_shape=jax.ShapeDtypeStruct((plan.sent_rows, LANES), jnp.int16),
        in_specs=[VMEM] * len(blocks),
        out_specs=VMEM,
        compiler_params=pltpu.CompilerParams(vmem_limit_bytes=4 << 20),
        name=name,
    )(*blocks)


def main(place, lat, words, small, weights, plan):
    rows = plan.tiles * plan.slots
    hidden = weights[2].shape[0]
    channels = lat.shape[1]
    outs = jax.ShapeDtypeStruct((4, plan.rows, LANES), F32)
    wide = lambda kind: pltpu.VMEM((5 * rows, hidden), kind)
    return pl.pallas_call(
        functools.partial(main_kernel, plan),
        out_shape=(jax.ShapeDtypeStruct((4, plan.sent_rows, LANES), jnp.int16), outs),
        in_specs=[SMEM] + [VMEM] * 3 + [HBM] * 4,
        out_specs=(VMEM, VMEM),
        scratch_shapes=[
            pltpu.VMEM((rows, channels), BF16),
            pltpu.VMEM((rows, LANES), F32),
            pltpu.VMEM((rows, hidden), F32),
            wide(BF16),
            wide(BF16),
            wide(F32),
            wide(BF16),
            wide(BF16),
            wide(F32),
            wide(F32),
            pltpu.VMEM((rows, hidden), BF16),
            pltpu.VMEM((rows, hidden), BF16),
            pltpu.VMEM((6, 8, hidden), F32),
            pltpu.VMEM((5 * rows, 2 * hidden), BF16),
            pltpu.VMEM((40, rows), F32),
            pltpu.VMEM((40, rows), F32),
            pltpu.VMEM((8, plan.rows, LANES), F32),
            pltpu.VMEM((hidden, hidden), BF16),
            pltpu.VMEM((hidden, hidden), BF16),
        ]
        + [pltpu.VMEM(weight.shape, F32) for weight in weights]
        + [pltpu.SemaphoreType.DMA((4,))],
        compiler_params=pltpu.CompilerParams(vmem_limit_bytes=32 << 20),
        name="encode_decode",
    )(place, lat, words, small, *weights)


def unpack_kernel(plan, place_ref, *refs):
    sources, outs, packed = refs[:8], refs[8:-1], refs[-1]
    prediction_ref, latent_ref, pos_ref, one_ref, mid_ref, two_ref, out_ref, bias_out_ref, loss_ref = outs
    my_block = place_ref[0]
    device = place_ref[2] * plan.tiles + place_ref[1]
    starts = list(range(0, plan.coded_rows, SUB))
    for number, ref in enumerate(sources):
        read = decoder(plan, ref)
        block = jnp.bitwise_xor(number, my_block)
        for start in starts:
            packed[block, start : start + SUB, :] = read(start, SUB)
        packed[block, plan.coded_rows :, :] = read(plan.coded_rows, 8)

    hidden = mid_ref.shape[0]
    latents = latent_ref.shape[0]
    split = plan.main_rows
    for part in range(hidden // LANES):
        lanes = slice(part * LANES, (part + 1) * LANES)
        mid_ref[0:split, lanes] = packed[2 * part, 0:split, :]
        mid_ref[split:, lanes] = packed[2 * part + 1, 0 : hidden - split, :]
        latent_ref[:, lanes] = packed[2 * part + 1, hidden - split : split, :]
        misc = packed[2 * part, plan.coded_rows :, :]
        pos_ref[:, lanes] = misc[0:3]
        one_ref[:, lanes] = misc[3:4]
        two_ref[:, lanes] = misc[4:5]
        out_ref[:, lanes] = packed[2 * part + 1, plan.coded_rows : plan.coded_rows + 5, :]
        if part == 0:
            bias_out_ref[...] = misc[5:6, 0:5]
            loss_ref[...] = misc[5:6, 5:6]
    row = pl.multiple_of(plan.main_rows + (device >> 3) * 8, 8)
    fields = packed[device & 7, pl.ds(row, 8), :]
    for f in range(5):
        prediction_ref[f] = fields[f : f + 1]


def unpack(place, blocks, plan, hidden, latents):
    shapes = [
        (5, 1, LANES),
        (latents, hidden),
        (3, hidden),
        (1, hidden),
        (hidden, hidden),
        (1, hidden),
        (5, hidden),
        (1, 5),
        (1, 1),
    ]
    return pl.pallas_call(
        functools.partial(unpack_kernel, plan),
        out_shape=tuple(jax.ShapeDtypeStruct(shape, F32) for shape in shapes),
        in_specs=[SMEM] + [VMEM] * 8,
        out_specs=tuple([VMEM] * len(shapes)),
        scratch_shapes=[pltpu.VMEM((8, plan.rows, LANES), F32)],
        compiler_params=pltpu.CompilerParams(vmem_limit_bytes=16 << 20),
        name="unpack",
    )(place, *blocks)


def body(
    fields,
    convolution_weight,
    convolution_bias,
    query_owner,
    query_cell,
    query_frac,
    target,
    w_latent,
    w_pos,
    bias_one,
    w_mid,
    bias_two,
    w_out,
    bias_out,
):
    tiles = lax.axis_size("tile")
    replicas = lax.axis_size("replica")
    my_tile = lax.axis_index("tile")
    my_replica = lax.axis_index("replica")
    channels = fields.shape[1]
    queries = query_cell.shape[1]
    hidden = w_mid.shape[0]
    plan = Plan(tiles, replicas, queries, fields.shape[2], hidden, channels)
    device = my_replica * tiles + my_tile
    place = jnp.stack([plan.my_block(device), my_tile, my_replica]).astype(jnp.int32)

    here = fields[0].transpose(1, 2, 0, 3)
    odd = my_tile & 1
    count = DILATION_RATE + 1
    first = lax.dynamic_slice_in_dim(here, (1 - odd) * (here.shape[0] - count), count, axis=0)
    second = lax.dynamic_slice_in_dim(here, odd * (here.shape[0] - count), count, axis=0)
    first, second, query_owner = lax.optimization_barrier((first, second, query_owner))
    near = lax.ppermute(first, "tile", [(i, i ^ 1) for i in range(tiles)])
    far = lax.ppermute(second, "tile", [(i, (i - 1 + 2 * (i & 1)) % tiles) for i in range(tiles)])
    words, small = route(
        (query_owner[:, :, 0], query_cell, query_frac.transpose(1, 0, 2), target.transpose(1, 0, 2)),
        (bias_one[None], bias_two[None], bias_out[None], convolution_bias[None]),
        tiles,
        plan.slots,
    )
    words = lax.all_to_all(
        words.reshape(tiles, 8, WORDS), "tile", split_axis=0, concat_axis=0, tiled=True
    ).reshape(tiles * 8, WORDS)

    lat = convolve(place, near, here, far, convolution_weight, small)
    weights = (w_latent, w_pos, w_mid, w_out)
    send, keep = main(place, lat, words, small, weights, plan)

    got = swapped(send, plan, plan.core, 1)
    (far,) = first_sum(keep, got, (3,), plan)
    far, keep = lax.optimization_barrier((far, keep))
    mine, *near = first_sum(keep, got, (0, 1, 2), plan)
    arrived = [swapped(block, plan, plan.plane, step) for step, block in ((3, far), (1, near[0]), (2, near[1]))]
    block = coded_sum(plane_kernel, [mine] + arrived, plan, "sum_plane")
    for bits in zip(plan.rest, reversed(plan.rest)):
        pairs = [(i, i ^ (1 << bits[i & 1])) for i in range(plan.devices)]
        other = lax.ppermute(block, ("replica", "tile"), pairs)
        block = coded_sum(pair_kernel, [block, other], plan, "sum_line")
    blocks = [block] + [swapped(block, plan, plan.plane, step) for step in range(1, 4)]
    blocks = blocks + [swapped(block, plan, plan.core, 1) for block in blocks]
    prediction, g_latent, g_pos, g_one, g_mid, g_two, g_out, g_bias, loss = unpack(
        place, blocks, plan, hidden, channels
    )
    return (
        prediction.transpose(1, 0, 2),
        g_latent,
        g_pos,
        g_one.reshape(hidden),
        g_mid,
        g_two.reshape(hidden),
        g_out,
        g_bias.reshape(5),
        loss.reshape(()),
    )


def solution(mesh):
    return jax.shard_map(
        body,
        mesh=mesh,
        in_specs=(
            P("replica", None, "tile", None, None),
            P(),
            P(),
            P("replica", "tile", None),
            P("replica", "tile"),
            P("replica", None, "tile"),
            P("replica", None, "tile"),
            P(),
            P(),
            P(),
            P(),
            P(),
            P(),
            P(),
        ),
        out_specs=(P("replica", None, "tile"), P(), P(), P(), P(), P(), P(), P(), P()),
        check_vma=False,
    )
```

```python
import functools

import jax
import jax.numpy as jnp
from jax import lax
from jax.experimental import pallas as pl
from jax.experimental.pallas import tpu as pltpu
from jax.sharding import PartitionSpec as P

DILATION_RATE = 2
VISCOSITY = 0.05
DIFFUSIVITY = 0.05
RESIDUAL_WEIGHT = 0.5

F32 = jnp.float32
BF16 = jnp.bfloat16
LANES = 128
BLOCK = 16
WORDS = 128
SUB = 32
NN = (((1,), (0,)), ((), ()))
NT = (((1,), (1,)), ((), ()))
TN = (((0,), (0,)), ((), ()))
VMEM = pl.BlockSpec(memory_space=pltpu.VMEM)
SMEM = pl.BlockSpec(memory_space=pltpu.SMEM)
HBM = pl.BlockSpec(memory_space=pltpu.HBM)


def mul(left, right, dims=NN):
    return lax.dot_general(left, right, dims, preferred_element_type=F32)


def halves(value):
    high = value.astype(BF16)
    return high, (value - high.astype(F32)).astype(BF16)


def thirds(value):
    high = value.astype(BF16)
    rest = value - high.astype(F32)
    middle = rest.astype(BF16)
    return high, middle, (rest - middle.astype(F32)).astype(BF16)


def mul3(left, right, dims=NN):
    return mul(left[0], right[0], dims) + mul(left[0], right[1], dims) + mul(left[1], right[0], dims)


def fetches(sources, targets, sems):
    copies = [
        pltpu.make_async_copy(source, target, sems.at[number])
        for number, (source, target) in enumerate(zip(sources, targets))
    ]
    for copy in copies:
        copy.start()
    return copies


def route_kernel(tiles, slots, *refs):
    out_ref, small_ref, *scratch, words, sems = refs[8:]
    for copy in fetches(refs[:8], scratch, sems):
        copy.wait()
    owner_ref, cell_ref, frac_ref, target_ref, *bias_refs = scratch
    queries = owner_ref.shape[1]
    small_ref[...] = jnp.zeros_like(small_ref)
    for number, ref in enumerate(bias_refs):
        small_ref[number : number + 1, 0 : ref.shape[1]] = ref[...]
    owner = owner_ref[...]
    hits = (lax.broadcasted_iota(jnp.int32, (tiles, queries), 0) == owner).astype(F32)
    before = lax.broadcasted_iota(jnp.int32, (queries, queries), 0) < lax.broadcasted_iota(
        jnp.int32, (queries, queries), 1
    )
    earlier = mul(hits.astype(BF16), before.astype(F32).astype(BF16))
    slot = jnp.sum(hits * earlier, axis=0, keepdims=True)
    place = owner * slots + slot.astype(jnp.int32)
    spot = lax.broadcasted_iota(jnp.int32, (tiles * 8, queries), 0)
    spot = (spot >> 3) * slots + (spot & 7)
    groups = slots // 8
    chosen = [jnp.where(spot + 8 * group == place, 1.0, 0.0) for group in range(groups)]
    chosen = jnp.concatenate(chosen, axis=1).astype(BF16)
    words[...] = jnp.zeros_like(words)
    for group in range(groups):
        row, lanes = 16 * group, slice(group * queries, (group + 1) * queries)
        words[row : row + 1, lanes] = cell_ref[...].astype(F32)
        for d in range(3):
            words[row + 1 + d : row + 2 + d, lanes] = frac_ref[d]
        for f in range(5):
            words[row + 4 + f : row + 5 + f, lanes] = target_ref[f]
        words[row + 9 : row + 10, lanes] = jnp.ones((1, queries), F32)
        words[row + 10 : row + 11, lanes] = lax.broadcasted_iota(jnp.int32, (1, queries), 1).astype(F32)
    high, middle, low = thirds(words[...])
    out_ref[...] = mul(chosen, high, NT) + mul(chosen, middle, NT) + mul(chosen, low, NT)


def route(inputs, biases, tiles, slots):
    queries = inputs[0].shape[1]
    arrays = inputs + biases
    return pl.pallas_call(
        functools.partial(route_kernel, tiles, slots),
        out_shape=(
            jax.ShapeDtypeStruct((tiles * 8, WORDS), F32),
            jax.ShapeDtypeStruct((8, biases[0].shape[1]), F32),
        ),
        in_specs=[HBM] * 8,
        out_specs=(VMEM, VMEM),
        scratch_shapes=[pltpu.VMEM(array.shape, array.dtype) for array in arrays]
        + [pltpu.VMEM((WORDS, queries * (slots // 8)), F32), pltpu.SemaphoreType.DMA((8,))],
        compiler_params=pltpu.CompilerParams(vmem_limit_bytes=4 << 20),
        name="route",
    )(*arrays)


def tap_sum(weight_ref, planes, pair):
    total = None
    for step_x, ref, index in planes:
        rows_y = ref.shape[1]
        blocks = [
            jnp.concatenate([ref[index, (2 * pair + half + step_y) % rows_y] for half in (0, 1)], axis=1)
            for step_y in (-1, 0, 1)
        ]
        term = mul(weight_ref[step_x], jnp.concatenate(blocks, axis=0))
        total = term if total is None else total + term
    channels = total.shape[0] // 3
    sides = []
    for half in (0, 1):
        part = total[:, half * LANES : (half + 1) * LANES]
        sides.append(
            part[channels : 2 * channels]
            + pltpu.roll(part[:channels], 1, 1)
            + pltpu.roll(part[2 * channels :], LANES - 1, 1)
        )
    return jnp.concatenate(sides, axis=1)


def conv_kernel(
    place_ref,
    near_ref,
    here_ref,
    far_ref,
    taps_ref,
    small_ref,
    lat_ref,
    weight_ref,
):
    planes, rows_y, channels = here_ref.shape[:3]
    taps = taps_ref[...].astype(F32)
    for step in range(3):
        rows = []
        for step_z in range(3):
            numbers = [9 * step + 3 * step_y + step_z for step_y in range(3)]
            rows.append(
                jnp.concatenate([taps[:, n * channels : (n + 1) * channels] for n in numbers], axis=1)
            )
        weight_ref[step] = jnp.concatenate(rows, axis=0).astype(BF16)
    diagonal = lax.broadcasted_iota(jnp.int32, (channels, channels), 0) == lax.broadcasted_iota(
        jnp.int32, (channels, channels), 1
    )
    bias = jnp.sum(jnp.where(diagonal, small_ref[3:4, 0:channels], 0.0), axis=1, keepdims=True)
    def all_planes(left_ref, right_ref):
        for x in range(planes + 1):
            taps = []
            for step in range(3):
                plane = x + DILATION_RATE * (step - 1)
                if plane < 0:
                    taps.append((step, left_ref, plane + left_ref.shape[0]))
                elif plane >= planes:
                    taps.append((step, right_ref, plane - planes))
                else:
                    taps.append((step, here_ref, plane))
            for pair in range(rows_y // 2):
                summed = tap_sum(weight_ref, taps, pair) + bias
                lat_ref[x * (rows_y // 2) + pair] = jax.nn.gelu(summed).astype(BF16)

    even = (place_ref[1] & 1) == 0

    @pl.when(even)
    def _():
        all_planes(far_ref, near_ref)

    @pl.when(jnp.logical_not(even))
    def _():
        all_planes(near_ref, far_ref)


def convolve(place, near, here, far, taps, small):
    planes, rows_y, channels, rows_z = here.shape
    pairs = (planes + 1) * rows_y // 2
    return pl.pallas_call(
        conv_kernel,
        out_shape=jax.ShapeDtypeStruct((pairs, channels, 2 * rows_z), BF16),
        in_specs=[SMEM] + [VMEM] * 5,
        out_specs=VMEM,
        scratch_shapes=[pltpu.VMEM((3, 3 * channels, 3 * channels), BF16)],
        compiler_params=pltpu.CompilerParams(vmem_limit_bytes=8 << 20),
        cost_estimate=pl.CostEstimate(flops=3 << 30, bytes_accessed=4 << 20, transcendentals=0),
        name="convolve",
    )(place, near, here, far, taps, small)


def interpolate(words, lat, planes, rows_y, rows_z):
    rows = words.shape[0]
    cell = jnp.broadcast_to(words[:, 0:1], (rows, LANES)).astype(jnp.int32)
    frac = [jnp.broadcast_to(words[:, 1 + d : 2 + d], (rows, LANES)) for d in range(3)]
    shift_z = rows_z.bit_length() - 1
    shift_y = rows_y.bit_length() - 1
    base_x = cell >> (shift_z + shift_y)
    base_y = (cell >> shift_z) & (rows_y - 1)
    base_z = cell & (rows_z - 1)
    spot = lax.broadcasted_iota(jnp.int32, (rows, rows_z), 1)
    part_z = jnp.where(spot == base_z, 1.0 - frac[2], 0.0) + jnp.where(
        spot == ((base_z + 1) & (rows_z - 1)), frac[2], 0.0
    )
    part_yz = []
    for y in range(rows_y):
        part_y = jnp.where(
            base_y == y, 1.0 - frac[1], jnp.where(base_y == (y - 1) % rows_y, frac[1], 0.0)
        )
        part_yz.append(part_y * part_z)
    total = None
    for x in range(planes + 1):
        part_x = jnp.where(base_x == x, 1.0 - frac[0], jnp.where(base_x == x - 1, frac[0], 0.0))
        for pair in range(rows_y // 2):
            sides = [(part_x * part_yz[2 * pair + half]).astype(BF16) for half in (0, 1)]
            term = mul(jnp.concatenate(sides, axis=1), lat[x * (rows_y // 2) + pair], NT)
            total = term if total is None else total + term
    return total.astype(BF16), base_x, base_y, base_z, frac


def folded(value):
    return jnp.sum(value.reshape(value.shape[0] // 8, 8, value.shape[1]), axis=0)


def main_kernel(
    plan,
    place_ref,
    lat,
    words_ref,
    small_ref,
    w_latent_hbm,
    w_pos_hbm,
    w_mid_hbm,
    w_out_hbm,
    send_ref,
    keep_ref,
    code,
    pos,
    z_one,
    one_high,
    one_low,
    mixed,
    two_high,
    two_low,
    back,
    mixed_back,
    first_high,
    first_low,
    sums_ref,
    d_both,
    out_t,
    d_out_t,
    packed,
    mid_high,
    mid_low,
    w_latent_ref,
    w_pos_ref,
    w_mid_ref,
    w_out_ref,
    sems,
):
    rows = plan.tiles * plan.slots
    hidden = w_mid_ref.shape[0]
    latents = w_latent_ref.shape[0]
    weights = fetches(
        (w_latent_hbm, w_pos_hbm, w_mid_hbm, w_out_hbm),
        (w_latent_ref, w_pos_ref, w_mid_ref, w_out_ref),
        sems,
    )
    planes, rows_z = plan.planes, lat.shape[2] // 2
    rows_y = lat.shape[0] // (planes + 1) * 2
    slots = rows // plan.tiles
    my_block = place_ref[0]
    my_tile = place_ref[1]
    my_replica = place_ref[2]
    always = my_tile >= 0

    words = words_ref[...]
    words = jnp.concatenate(
        [words] + [pltpu.roll(words, LANES - 16 * group, 1) for group in range(1, slots // 8)], axis=0
    )
    interp, base_x, base_y, base_z, frac = interpolate(words, lat, planes, rows_y, rows_z)
    code[...] = interp
    global_x = my_tile * planes + base_x
    lane = lax.broadcasted_iota(jnp.int32, (rows, LANES), 1)
    pos[...] = jnp.where(
        lane == 0,
        (global_x.astype(F32) + frac[0]) / (planes * plan.tiles),
        jnp.where(
            lane == 1,
            (base_y.astype(F32) + frac[1]) / rows_y,
            (base_z.astype(F32) + frac[2]) / rows_z,
        ),
    )

    for copy in weights:
        copy.wait()
    high, low = halves(w_latent_ref[...])
    z_one[...] = mul(interp, high) + mul(interp, low)
    high, low = halves(w_mid_ref[...])
    mid_high[...] = high
    mid_low[...] = low
    w_pos = [w_pos_ref[d : d + 1, :] for d in range(3)]
    square = w_pos[0] * w_pos[0] + w_pos[1] * w_pos[1] + w_pos[2] * w_pos[2]
    bias_one = small_ref[0:1, :]
    bias_two = small_ref[1:2, :]

    part_rows = rows // 2

    def at(part, index, block=None):
        first = (part * 5 + index) * part_rows
        if block is None:
            return slice(first, first + part_rows)
        return slice(first + block * BLOCK, first + (block + 1) * BLOCK)

    def rows_at(part, block):
        first = part * part_rows + block * BLOCK
        return slice(first, first + BLOCK)

    def store(refs, span, value):
        high, low = halves(value)
        refs[0][span, :] = high
        refs[1][span, :] = low

    def layer_one(part):
        refs = (one_high, one_low)
        for block in range(part_rows // BLOCK):
            here = rows_at(part, block)
            where = pos[here, :]
            pre = (
                z_one[here, :]
                + (where[:, 0:1] * w_pos[0] + where[:, 1:2] * w_pos[1] + where[:, 2:3] * w_pos[2])
                + bias_one
            )
            act = jnp.tanh(pre)
            slope = 1.0 - act * act
            curve = -2.0 * act * slope
            z_one[here, :] = act
            store(refs, at(part, 0, block), act)
            for d in range(3):
                store(refs, at(part, 1 + d, block), slope * w_pos[d])
            store(refs, at(part, 4, block), curve * square)

    def times_mid(dims, source, result, part):
        span = slice(part * 5 * part_rows, (part + 1) * 5 * part_rows)
        left = (source[0][span, :], source[1][span, :])
        result[span, :] = mul3(left, (mid_high[...], mid_low[...]), dims)

    def layer_two(part):
        refs = (two_high, two_low)
        for block in range(part_rows // BLOCK):
            act = jnp.tanh(mixed[at(part, 0, block), :] + bias_two)
            slope = 1.0 - act * act
            curve = -2.0 * act * slope
            store(refs, at(part, 0, block), act)
            mixed[at(part, 0, block), :] = act
            norm = None
            for d in range(3):
                tangent = mixed[at(part, 1 + d, block), :]
                store(refs, at(part, 1 + d, block), slope * tangent)
                norm = tangent * tangent if norm is None else norm + tangent * tangent
            store(refs, at(part, 4, block), slope * mixed[at(part, 4, block), :] + curve * norm)

    out_fields = jnp.concatenate([w_out_ref[...], jnp.zeros((3, hidden), F32)], axis=0)
    wo_high, wo_low = halves(out_fields)
    wo_three = jnp.concatenate([out_fields, wo_low.astype(F32), out_fields], axis=0).astype(BF16)
    wo_both = jnp.concatenate(
        [out_fields, wo_low.astype(F32), jnp.zeros((LANES - 16, hidden), F32)], axis=0
    ).astype(BF16)

    def outputs(part):
        span = slice(part * 5 * part_rows, (part + 1) * 5 * part_rows)
        both = mul(two_high[span, :], wo_both, NT)
        low = mul(two_low[span, :], wo_both, NT)
        for s in range(5):
            rows_s = slice(s * part_rows, (s + 1) * part_rows)
            both_t, low_t = both[rows_s].T, low[rows_s].T
            out_t[8 * s : 8 * s + 8, part * part_rows : (part + 1) * part_rows] = (
                both_t[0:8] + both_t[8:16] + low_t[0:8]
            )

    @pl.when(always)
    def _():
        layer_one(0)
        times_mid(NN, (one_high, one_low), mixed, 0)
        layer_one(1)
        times_mid(NN, (one_high, one_low), mixed, 1)
        layer_two(0)
        outputs(0)
        layer_two(1)
        outputs(1)

    words_t = words.T
    target = [words_t[4 + f : 5 + f, :] for f in range(5)]
    valid = words_t[9:10, :]
    value = [out_t[f : f + 1, :] + small_ref[2:3, f : f + 1] for f in range(5)]
    grad = [[out_t[8 * (d + 1) + f : 8 * (d + 1) + f + 1, :] for f in range(5)] for d in range(3)]
    laplace = [out_t[32 + f : 33 + f, :] for f in range(5)]
    velocity = value[2:5]
    advection = [
        velocity[0] * grad[0][f] + velocity[1] * grad[1][f] + velocity[2] * grad[2][f] for f in range(5)
    ]
    continuity = grad[0][2] + grad[1][3] + grad[2][4]
    momentum = [advection[2 + j] + grad[j][1] - VISCOSITY * laplace[2 + j] for j in range(3)]
    momentum[2] = momentum[2] - value[0]
    energy = advection[0] - DIFFUSIVITY * laplace[0]
    misfit = [value[f] - target[f] for f in range(5)]
    physics = (
        continuity * continuity
        + (momentum[0] * momentum[0] + momentum[1] * momentum[1] + momentum[2] * momentum[2])
        + energy * energy
    )
    squares = (
        misfit[0] * misfit[0]
        + misfit[1] * misfit[1]
        + misfit[2] * misfit[2]
        + misfit[3] * misfit[3]
        + misfit[4] * misfit[4]
    )
    point_loss = valid * (squares + RESIDUAL_WEIGHT * physics) * (1.0 / plan.query_total)

    rate = valid * (1.0 / plan.query_total)
    twice = RESIDUAL_WEIGHT * 2.0
    d_cont = rate * twice * continuity
    d_mom = [rate * twice * m for m in momentum]
    d_energy = rate * twice * energy
    d_value = [2.0 * rate * m for m in misfit]
    for d in range(3):
        d_value[2 + d] = d_value[2 + d] + (
            d_mom[0] * grad[d][2] + d_mom[1] * grad[d][3] + d_mom[2] * grad[d][4] + d_energy * grad[d][0]
        )
    d_value[0] = d_value[0] - d_mom[2]
    d_out_t[...] = jnp.zeros_like(d_out_t)
    for f in range(5):
        d_out_t[f : f + 1, :] = d_value[f]
    for d in range(3):
        first = 8 * (d + 1)
        d_out_t[first : first + 1, :] = d_energy * velocity[d]
        d_out_t[first + 1 : first + 2, :] = d_mom[d]
        for j in range(3):
            term = d_mom[j] * velocity[d]
            if j == d:
                term = term + d_cont
            d_out_t[first + 2 + j : first + 3 + j, :] = term
    d_out_t[32:33, :] = -DIFFUSIVITY * d_energy
    for j in range(3):
        d_out_t[34 + j : 35 + j, :] = -VISCOSITY * d_mom[j]

    def out_back(part):
        columns = slice(part * part_rows, (part + 1) * part_rows)
        wanted = jnp.concatenate([d_out_t[8 * s : 8 * s + 8, columns] for s in range(5)], axis=1)
        do_low = halves(wanted)[1].astype(F32)
        wanted = jnp.concatenate([wanted, wanted, do_low], axis=0).astype(BF16)
        back[part * 5 * part_rows : (part + 1) * 5 * part_rows, :] = mul(wanted, wo_three, TN)

    def second_back(part, total):
        refs = (d_both.at[:, :hidden], d_both.at[:, hidden:])
        for block in range(part_rows // BLOCK):
            act = mixed[at(part, 0, block), :]
            slope = 1.0 - act * act
            curve = -2.0 * act * slope
            cot_l = back[at(part, 4, block), :]
            d_slope = cot_l * mixed[at(part, 4, block), :]
            norm = None
            bent = 2.0 * curve * cot_l
            for d in range(3):
                tangent = mixed[at(part, 1 + d, block), :]
                cot_t = back[at(part, 1 + d, block), :]
                store(refs, at(part, 1 + d, block), slope * cot_t + bent * tangent)
                d_slope = d_slope + cot_t * tangent
                norm = tangent * tangent if norm is None else norm + tangent * tangent
            store(refs, at(part, 4, block), slope * cot_l)
            d_curve = cot_l * norm
            d_slope = d_slope - 2.0 * act * d_curve
            d_act = back[at(part, 0, block), :] - 2.0 * slope * d_curve - 2.0 * act * d_slope
            d_pre = slope * d_act
            store(refs, at(part, 0, block), d_pre)
            total = total + folded(d_pre)
        return total

    def first_back(part, sums):
        for block in range(part_rows // BLOCK):
            here = rows_at(part, block)
            act = z_one[here, :]
            slope = 1.0 - act * act
            curve = -2.0 * act * slope
            where = pos[here, :]
            cot_t = [mixed_back[at(part, 1 + d, block), :] for d in range(3)]
            cot_l = mixed_back[at(part, 4, block), :]
            d_curve = cot_l * square
            d_slope = cot_t[0] * w_pos[0] + cot_t[1] * w_pos[1] + cot_t[2] * w_pos[2] - 2.0 * act * d_curve
            d_act = mixed_back[at(part, 0, block), :] - 2.0 * slope * d_curve - 2.0 * act * d_slope
            d_pre = slope * d_act
            high, low = halves(d_pre)
            first_high[here, :] = high
            first_low[here, :] = low
            sums = (
                [sums[0] + folded(d_pre)]
                + [sums[1 + d] + folded(where[:, d : d + 1] * d_pre + slope * cot_t[d]) for d in range(3)]
                + [sums[4] + folded(curve * cot_l)]
            )
        return sums


    def put(part, first, value):
        while value.shape[0]:
            block, row = first // plan.main_rows, first % plan.main_rows
            count = min(value.shape[0], plan.main_rows - row)
            packed[2 * part + block, row : row + count, :] = value[:count]
            first, value = first + count, value[count:]

    def mid_gradient():
        both = mul(one_high[...], d_both[...], TN)
        both = both[:, :hidden] + both[:, hidden:] + mul(one_low[...], d_both[:, :hidden], TN)
        for part in range(hidden // LANES):
            put(part, 0, both[:, part * LANES : (part + 1) * LANES])

    @pl.when(always)
    def _():
        out_back(0)
        total = second_back(0, jnp.zeros((8, hidden), F32))
        out_back(1)
        times_mid(NT, (d_both.at[:, :hidden], d_both.at[:, hidden:]), mixed_back, 0)
        sums_ref[5] = second_back(1, total)
        times_mid(NT, (d_both.at[:, :hidden], d_both.at[:, hidden:]), mixed_back, 1)
        total = first_back(0, [jnp.zeros((8, hidden), F32)] * 5)
        mid_gradient()
        for number, value in enumerate(first_back(1, total)):
            sums_ref[number] = value

    sums = [sums_ref[number] for number in range(6)]
    d_square = jnp.sum(sums[4], axis=0, keepdims=True)
    grad_latent = mul(code[...], first_high[...], TN) + mul(code[...], first_low[...], TN)

    parts = [d_out_t[8 * s : 8 * s + 8, p * part_rows : (p + 1) * part_rows] for p in range(2) for s in range(5)]
    flat = jnp.concatenate(parts, axis=1)
    fl_high, fl_low = halves(flat)
    fl_both = jnp.concatenate([flat, fl_low.astype(F32)], axis=0).astype(BF16)
    grad_out = mul(fl_both, two_high[...])
    grad_out = grad_out[:8] + grad_out[8:] + mul(fl_high, two_low[...])

    lane_row = lax.broadcasted_iota(jnp.int32, (1, hidden), 1)
    last = jnp.where(lane_row == 5, jnp.sum(point_loss), 0.0)
    for f in range(5):
        last = last + jnp.where(lane_row == f, jnp.sum(d_value[f]), 0.0)
    grad_pos = [jnp.sum(sums[1 + d], axis=0, keepdims=True) + 2.0 * w_pos[d] * d_square for d in range(3)]
    misc = grad_pos + [
        jnp.sum(sums[0], axis=0, keepdims=True),
        jnp.sum(sums[5], axis=0, keepdims=True),
        last,
    ]
    misc = jnp.concatenate(misc + [jnp.zeros((2, hidden), F32)], axis=0)
    for part in range(hidden // LANES):
        lanes = slice(part * LANES, (part + 1) * LANES)
        put(part, hidden, grad_latent[:, lanes])
        packed[2 * part, plan.coded_rows :, :] = misc[:, lanes]
        packed[2 * part + 1, plan.coded_rows :, :] = grad_out[:, lanes]

    chosen = jnp.where(
        lane == jnp.broadcast_to(words[:, 10:11], (rows, LANES)).astype(jnp.int32), words[:, 9:10], 0.0
    ).astype(BF16)
    fields = jnp.concatenate(value + [jnp.zeros((3, rows), F32)], axis=0)
    source = (lax.broadcasted_iota(jnp.int32, (8, rows), 1) & (plan.tiles * 8 - 1)) >> 3
    spread = jnp.concatenate([jnp.where(source == t, fields, 0.0) for t in range(plan.tiles)], axis=0)
    high, middle, low = thirds(spread)
    spread = mul(high, chosen) + mul(middle, chosen) + mul(low, chosen)
    packed[:, plan.main_rows : plan.coded_rows, :] = jnp.zeros((8, plan.devices, LANES), F32)
    for t in range(plan.tiles):
        row = plan.main_rows + (my_replica * (plan.tiles // 8) + t // 8) * 8
        packed[t % 8, pl.ds(pl.multiple_of(row, 8), 8), :] = spread[8 * t : 8 * t + 8]

    for block in range(8):
        spot = jnp.bitwise_xor(block, my_block) & 3

        @pl.when((my_block >> 2) == block // 4)
        def _():
            keep_ref[spot] = packed[block]

        @pl.when((my_block >> 2) != block // 4)
        def _():
            encode(plan, lambda start, count: packed[block, start : start + count, :], send_ref.at[spot])


class Plan:
    def __init__(self, tiles, replicas, queries, planes, hidden, latents):
        self.tiles, self.replicas, self.planes = tiles, replicas, planes
        self.slots = 2 * queries // tiles
        self.devices = tiles * replicas
        self.query_total = float(queries * self.devices)
        self.main_rows = (hidden + latents) // 2
        self.coded_rows = self.main_rows + self.devices
        self.rows = self.coded_rows + 8
        self.scales = -(-(self.coded_rows // SUB + 1) // 16) * 16
        self.sent_rows = self.coded_rows + 16 + self.scales
        top = self.devices.bit_length() - 1
        self.core, self.plane, self.rest = [0], [1, top - 1], list(range(2, top - 1))

    def mask(self, bits, steps):
        return sum(1 << bit for number, bit in enumerate(bits) if steps >> number & 1)

    def my_block(self, device):
        return (device & 1) * 4 + (device >> 1 & 1) + 2 * (device >> self.plane[1] & 1)


def swapped(value, plan, bits, steps):
    mask = plan.mask(bits, steps)
    return lax.ppermute(value, ("replica", "tile"), [(i, i ^ mask) for i in range(plan.devices)])


def encode(plan, read, out_ref):
    starts = list(range(0, plan.coded_rows, SUB))
    parts = [read(start, SUB) for start in starts] + [read(plan.coded_rows, 8)]
    tops = [jnp.max(jnp.abs(part), axis=0, keepdims=True) for part in parts]
    tops = tops + [jnp.zeros_like(tops[0])] * (plan.scales - len(tops))
    power = jnp.floor(jnp.log2(jnp.maximum(jnp.concatenate(tops, axis=0), 1e-30)))
    scale = jnp.exp2(14.0 - power)

    def whole(value):
        return jnp.clip(jnp.round(value), -32767.0, 32767.0)

    def narrow(value):
        return value.astype(jnp.int32).astype(jnp.int16)

    for number, start in enumerate(starts):
        out_ref[start : start + SUB, :] = narrow(whole(parts[number] * scale[number : number + 1]))
    last = len(starts)
    exact = parts[last] * scale[last : last + 1]
    high = whole(exact)
    low = whole((exact - high) * 32768.0)
    out_ref[plan.coded_rows : plan.coded_rows + 16, :] = narrow(jnp.concatenate([high, low], axis=0))
    out_ref[plan.coded_rows + 16 :, :] = narrow(power)


def decoder(plan, ref):
    def widen(value):
        return value.astype(jnp.int32).astype(F32)

    scale = jnp.exp2(widen(ref[plan.coded_rows + 16 :, :]) - 14.0)

    def read(start, count):
        if start < plan.coded_rows:
            number = start // SUB
            return widen(ref[start : start + count, :]) * scale[number : number + 1]
        both = widen(ref[plan.coded_rows : plan.coded_rows + 16, :])
        number = plan.coded_rows // SUB
        return (both[:8] + both[8:] * (1.0 / 32768.0)) * scale[number : number + 1]

    return read


def added(readers):
    def read(start, count):
        total = readers[0](start, count)
        for reader in readers[1:]:
            total = total + reader(start, count)
        return total

    return read


def first_kernel(plan, numbers, keep_ref, got_ref, *refs):
    def reader(block):
        got = decoder(plan, got_ref.at[block])
        return lambda start, count: keep_ref[block, start : start + count, :] + got(start, count)

    for number, out_ref in zip(numbers, refs):
        if number:
            encode(plan, reader(number), out_ref)
        else:
            read = reader(0)
            for start in range(0, plan.coded_rows, SUB):
                out_ref[start : start + SUB, :] = read(start, SUB)
            out_ref[plan.coded_rows :, :] = read(plan.coded_rows, 8)


def first_sum(keep, got, numbers, plan):
    sent = jax.ShapeDtypeStruct((plan.sent_rows, LANES), jnp.int16)
    own = jax.ShapeDtypeStruct(keep.shape[1:], F32)
    return pl.pallas_call(
        functools.partial(first_kernel, plan, numbers),
        out_shape=tuple(sent if number else own for number in numbers),
        in_specs=[VMEM] * 2,
        out_specs=tuple([VMEM] * len(numbers)),
        compiler_params=pltpu.CompilerParams(vmem_limit_bytes=6 << 20),
        name="sum_core",
    )(keep, got)


def plane_kernel(plan, mine_ref, *refs):
    readers = [lambda start, count: mine_ref[start : start + count, :]]
    encode(plan, added(readers + [decoder(plan, ref) for ref in refs[:-1]]), refs[-1])


def pair_kernel(plan, mine_ref, other_ref, out_ref):
    encode(plan, added([decoder(plan, mine_ref), decoder(plan, other_ref)]), out_ref)


def coded_sum(kernel, blocks, plan, name):
    return pl.pallas_call(
        functools.partial(kernel, plan),
        out_shape=jax.ShapeDtypeStruct((plan.sent_rows, LANES), jnp.int16),
        in_specs=[VMEM] * len(blocks),
        out_specs=VMEM,
        compiler_params=pltpu.CompilerParams(vmem_limit_bytes=4 << 20),
        name=name,
    )(*blocks)


def main(place, lat, words, small, weights, plan):
    rows = plan.tiles * plan.slots
    hidden = weights[2].shape[0]
    channels = lat.shape[1]
    outs = jax.ShapeDtypeStruct((4, plan.rows, LANES), F32)
    wide = lambda kind: pltpu.VMEM((5 * rows, hidden), kind)
    return pl.pallas_call(
        functools.partial(main_kernel, plan),
        out_shape=(jax.ShapeDtypeStruct((4, plan.sent_rows, LANES), jnp.int16), outs),
        in_specs=[SMEM] + [VMEM] * 3 + [HBM] * 4,
        out_specs=(VMEM, VMEM),
        scratch_shapes=[
            pltpu.VMEM((rows, channels), BF16),
            pltpu.VMEM((rows, LANES), F32),
            pltpu.VMEM((rows, hidden), F32),
            wide(BF16),
            wide(BF16),
            wide(F32),
            wide(BF16),
            wide(BF16),
            wide(F32),
            wide(F32),
            pltpu.VMEM((rows, hidden), BF16),
            pltpu.VMEM((rows, hidden), BF16),
            pltpu.VMEM((6, 8, hidden), F32),
            pltpu.VMEM((5 * rows, 2 * hidden), BF16),
            pltpu.VMEM((40, rows), F32),
            pltpu.VMEM((40, rows), F32),
            pltpu.VMEM((8, plan.rows, LANES), F32),
            pltpu.VMEM((hidden, hidden), BF16),
            pltpu.VMEM((hidden, hidden), BF16),
        ]
        + [pltpu.VMEM(weight.shape, F32) for weight in weights]
        + [pltpu.SemaphoreType.DMA((4,))],
        compiler_params=pltpu.CompilerParams(vmem_limit_bytes=32 << 20),
        name="encode_decode",
    )(place, lat, words, small, *weights)


def unpack_kernel(plan, place_ref, *refs):
    sources, outs, packed = refs[:8], refs[8:-1], refs[-1]
    prediction_ref, latent_ref, pos_ref, one_ref, mid_ref, two_ref, out_ref, bias_out_ref, loss_ref = outs
    my_block = place_ref[0]
    device = place_ref[2] * plan.tiles + place_ref[1]
    starts = list(range(0, plan.coded_rows, SUB))
    for number, ref in enumerate(sources):
        read = decoder(plan, ref)
        block = jnp.bitwise_xor(number, my_block)
        for start in starts:
            packed[block, start : start + SUB, :] = read(start, SUB)
        packed[block, plan.coded_rows :, :] = read(plan.coded_rows, 8)

    hidden = mid_ref.shape[0]
    latents = latent_ref.shape[0]
    split = plan.main_rows
    for part in range(hidden // LANES):
        lanes = slice(part * LANES, (part + 1) * LANES)
        mid_ref[0:split, lanes] = packed[2 * part, 0:split, :]
        mid_ref[split:, lanes] = packed[2 * part + 1, 0 : hidden - split, :]
        latent_ref[:, lanes] = packed[2 * part + 1, hidden - split : split, :]
        misc = packed[2 * part, plan.coded_rows :, :]
        pos_ref[:, lanes] = misc[0:3]
        one_ref[:, lanes] = misc[3:4]
        two_ref[:, lanes] = misc[4:5]
        out_ref[:, lanes] = packed[2 * part + 1, plan.coded_rows : plan.coded_rows + 5, :]
        if part == 0:
            bias_out_ref[...] = misc[5:6, 0:5]
            loss_ref[...] = misc[5:6, 5:6]
    row = pl.multiple_of(plan.main_rows + (device >> 3) * 8, 8)
    fields = packed[device & 7, pl.ds(row, 8), :]
    for f in range(5):
        prediction_ref[f] = fields[f : f + 1]


def unpack(place, blocks, plan, hidden, latents):
    shapes = [
        (5, 1, LANES),
        (latents, hidden),
        (3, hidden),
        (1, hidden),
        (hidden, hidden),
        (1, hidden),
        (5, hidden),
        (1, 5),
        (1, 1),
    ]
    return pl.pallas_call(
        functools.partial(unpack_kernel, plan),
        out_shape=tuple(jax.ShapeDtypeStruct(shape, F32) for shape in shapes),
        in_specs=[SMEM] + [VMEM] * 8,
        out_specs=tuple([VMEM] * len(shapes)),
        scratch_shapes=[pltpu.VMEM((8, plan.rows, LANES), F32)],
        compiler_params=pltpu.CompilerParams(vmem_limit_bytes=16 << 20),
        name="unpack",
    )(place, *blocks)


def body(
    fields,
    convolution_weight,
    convolution_bias,
    query_owner,
    query_cell,
    query_frac,
    target,
    w_latent,
    w_pos,
    bias_one,
    w_mid,
    bias_two,
    w_out,
    bias_out,
):
    tiles = lax.axis_size("tile")
    replicas = lax.axis_size("replica")
    my_tile = lax.axis_index("tile")
    my_replica = lax.axis_index("replica")
    channels = fields.shape[1]
    queries = query_cell.shape[1]
    hidden = w_mid.shape[0]
    plan = Plan(tiles, replicas, queries, fields.shape[2], hidden, channels)
    device = my_replica * tiles + my_tile
    place = jnp.stack([plan.my_block(device), my_tile, my_replica]).astype(jnp.int32)

    here = fields[0].transpose(1, 2, 0, 3)
    odd = my_tile & 1
    count = DILATION_RATE + 1
    first = lax.dynamic_slice_in_dim(here, (1 - odd) * (here.shape[0] - count), count, axis=0)
    second = lax.dynamic_slice_in_dim(here, odd * (here.shape[0] - count), count, axis=0)
    first, second, query_owner = lax.optimization_barrier((first, second, query_owner))
    near = lax.ppermute(first, "tile", [(i, i ^ 1) for i in range(tiles)])
    far = lax.ppermute(second, "tile", [(i, (i - 1 + 2 * (i & 1)) % tiles) for i in range(tiles)])
    words, small = route(
        (query_owner[:, :, 0], query_cell, query_frac.transpose(1, 0, 2), target.transpose(1, 0, 2)),
        (bias_one[None], bias_two[None], bias_out[None], convolution_bias[None]),
        tiles,
        plan.slots,
    )
    words = lax.all_to_all(
        words.reshape(tiles, 8, WORDS), "tile", split_axis=0, concat_axis=0, tiled=True
    ).reshape(tiles * 8, WORDS)

    lat = convolve(place, near, here, far, convolution_weight, small)
    weights = (w_latent, w_pos, w_mid, w_out)
    send, keep = main(place, lat, words, small, weights, plan)

    got = swapped(send, plan, plan.core, 1)
    (far,) = first_sum(keep, got, (3,), plan)
    far, keep = lax.optimization_barrier((far, keep))
    mine, *near = first_sum(keep, got, (0, 1, 2), plan)
    arrived = [swapped(block, plan, plan.plane, step) for step, block in ((3, far), (1, near[0]), (2, near[1]))]
    block = coded_sum(plane_kernel, [mine] + arrived, plan, "sum_plane")
    for bits in zip(plan.rest, reversed(plan.rest)):
        pairs = [(i, i ^ (1 << bits[i & 1])) for i in range(plan.devices)]
        other = lax.ppermute(block, ("replica", "tile"), pairs)
        block = coded_sum(pair_kernel, [block, other], plan, "sum_line")
    blocks = [block] + [swapped(block, plan, plan.plane, step) for step in range(3, 0, -1)][::-1]
    blocks = blocks + [swapped(block, plan, plan.core, 1) for block in blocks]
    prediction, g_latent, g_pos, g_one, g_mid, g_two, g_out, g_bias, loss = unpack(
        place, blocks, plan, hidden, channels
    )
    return (
        prediction.transpose(1, 0, 2),
        g_latent,
        g_pos,
        g_one.reshape(hidden),
        g_mid,
        g_two.reshape(hidden),
        g_out,
        g_bias.reshape(5),
        loss.reshape(()),
    )


def solution(mesh):
    return jax.shard_map(
        body,
        mesh=mesh,
        in_specs=(
            P("replica", None, "tile", None, None),
            P(),
            P(),
            P("replica", "tile", None),
            P("replica", "tile"),
            P("replica", None, "tile"),
            P("replica", None, "tile"),
            P(),
            P(),
            P(),
            P(),
            P(),
            P(),
            P(),
        ),
        out_specs=(P("replica", None, "tile"), P(), P(), P(), P(), P(), P(), P(), P()),
        check_vma=False,
    )
```

```python
import functools

import jax
import jax.numpy as jnp
from jax import lax
from jax.experimental import pallas as pl
from jax.experimental.pallas import tpu as pltpu
from jax.sharding import PartitionSpec as P

DILATION_RATE = 2
VISCOSITY = 0.05
DIFFUSIVITY = 0.05
RESIDUAL_WEIGHT = 0.5

F32 = jnp.float32
BF16 = jnp.bfloat16
LANES = 128
BLOCK = 16
WORDS = 128
SUB = 32
NN = (((1,), (0,)), ((), ()))
NT = (((1,), (1,)), ((), ()))
TN = (((0,), (0,)), ((), ()))
VMEM = pl.BlockSpec(memory_space=pltpu.VMEM)
SMEM = pl.BlockSpec(memory_space=pltpu.SMEM)
HBM = pl.BlockSpec(memory_space=pltpu.HBM)


def mul(left, right, dims=NN):
    return lax.dot_general(left, right, dims, preferred_element_type=F32)


def halves(value):
    high = value.astype(BF16)
    return high, (value - high.astype(F32)).astype(BF16)


def thirds(value):
    high = value.astype(BF16)
    rest = value - high.astype(F32)
    middle = rest.astype(BF16)
    return high, middle, (rest - middle.astype(F32)).astype(BF16)


def mul3(left, right, dims=NN):
    return mul(left[0], right[0], dims) + mul(left[0], right[1], dims) + mul(left[1], right[0], dims)


def fetches(sources, targets, sems):
    copies = [
        pltpu.make_async_copy(source, target, sems.at[number])
        for number, (source, target) in enumerate(zip(sources, targets))
    ]
    for copy in copies:
        copy.start()
    return copies


def route_kernel(tiles, slots, *refs):
    out_ref, small_ref, *scratch, words, sems = refs[8:]
    for copy in fetches(refs[:8], scratch, sems):
        copy.wait()
    owner_ref, cell_ref, frac_ref, target_ref, *bias_refs = scratch
    queries = owner_ref.shape[1]
    small_ref[...] = jnp.zeros_like(small_ref)
    for number, ref in enumerate(bias_refs):
        small_ref[number : number + 1, 0 : ref.shape[1]] = ref[...]
    owner = owner_ref[...]
    hits = (lax.broadcasted_iota(jnp.int32, (tiles, queries), 0) == owner).astype(F32)
    before = lax.broadcasted_iota(jnp.int32, (queries, queries), 0) < lax.broadcasted_iota(
        jnp.int32, (queries, queries), 1
    )
    earlier = mul(hits.astype(BF16), before.astype(F32).astype(BF16))
    slot = jnp.sum(hits * earlier, axis=0, keepdims=True)
    place = owner * slots + slot.astype(jnp.int32)
    spot = lax.broadcasted_iota(jnp.int32, (tiles * 8, queries), 0)
    spot = (spot >> 3) * slots + (spot & 7)
    groups = slots // 8
    chosen = [jnp.where(spot + 8 * group == place, 1.0, 0.0) for group in range(groups)]
    chosen = jnp.concatenate(chosen, axis=1).astype(BF16)
    words[...] = jnp.zeros_like(words)
    for group in range(groups):
        row, lanes = 16 * group, slice(group * queries, (group + 1) * queries)
        words[row : row + 1, lanes] = cell_ref[...].astype(F32)
        for d in range(3):
            words[row + 1 + d : row + 2 + d, lanes] = frac_ref[d]
        for f in range(5):
            words[row + 4 + f : row + 5 + f, lanes] = target_ref[f]
        words[row + 9 : row + 10, lanes] = jnp.ones((1, queries), F32)
        words[row + 10 : row + 11, lanes] = lax.broadcasted_iota(jnp.int32, (1, queries), 1).astype(F32)
    high, middle, low = thirds(words[...])
    out_ref[...] = mul(chosen, high, NT) + mul(chosen, middle, NT) + mul(chosen, low, NT)


def route(inputs, biases, tiles, slots):
    queries = inputs[0].shape[1]
    arrays = inputs + biases
    return pl.pallas_call(
        functools.partial(route_kernel, tiles, slots),
        out_shape=(
            jax.ShapeDtypeStruct((tiles * 8, WORDS), F32),
            jax.ShapeDtypeStruct((8, biases[0].shape[1]), F32),
        ),
        in_specs=[HBM] * 8,
        out_specs=(VMEM, VMEM),
        scratch_shapes=[pltpu.VMEM(array.shape, array.dtype) for array in arrays]
        + [pltpu.VMEM((WORDS, queries * (slots // 8)), F32), pltpu.SemaphoreType.DMA((8,))],
        compiler_params=pltpu.CompilerParams(vmem_limit_bytes=4 << 20),
        name="route",
    )(*arrays)


def tap_sum(weight_ref, planes, pair):
    total = None
    for step_x, ref, index in planes:
        rows_y = ref.shape[1]
        blocks = [
            jnp.concatenate([ref[index, (2 * pair + half + step_y) % rows_y] for half in (0, 1)], axis=1)
            for step_y in (-1, 0, 1)
        ]
        term = mul(weight_ref[step_x], jnp.concatenate(blocks, axis=0))
        total = term if total is None else total + term
    channels = total.shape[0] // 3
    sides = []
    for half in (0, 1):
        part = total[:, half * LANES : (half + 1) * LANES]
        sides.append(
            part[channels : 2 * channels]
            + pltpu.roll(part[:channels], 1, 1)
            + pltpu.roll(part[2 * channels :], LANES - 1, 1)
        )
    return jnp.concatenate(sides, axis=1)


def conv_kernel(
    place_ref,
    near_ref,
    here_ref,
    far_ref,
    taps_ref,
    small_ref,
    lat_ref,
    weight_ref,
):
    planes, rows_y, channels = here_ref.shape[:3]
    taps = taps_ref[...].astype(F32)
    for step in range(3):
        rows = []
        for step_z in range(3):
            numbers = [9 * step + 3 * step_y + step_z for step_y in range(3)]
            rows.append(
                jnp.concatenate([taps[:, n * channels : (n + 1) * channels] for n in numbers], axis=1)
            )
        weight_ref[step] = jnp.concatenate(rows, axis=0).astype(BF16)
    diagonal = lax.broadcasted_iota(jnp.int32, (channels, channels), 0) == lax.broadcasted_iota(
        jnp.int32, (channels, channels), 1
    )
    bias = jnp.sum(jnp.where(diagonal, small_ref[3:4, 0:channels], 0.0), axis=1, keepdims=True)
    def all_planes(left_ref, right_ref):
        for x in range(planes + 1):
            taps = []
            for step in range(3):
                plane = x + DILATION_RATE * (step - 1)
                if plane < 0:
                    taps.append((step, left_ref, plane + left_ref.shape[0]))
                elif plane >= planes:
                    taps.append((step, right_ref, plane - planes))
                else:
                    taps.append((step, here_ref, plane))
            for pair in range(rows_y // 2):
                summed = tap_sum(weight_ref, taps, pair) + bias
                lat_ref[x * (rows_y // 2) + pair] = jax.nn.gelu(summed).astype(BF16)

    even = (place_ref[1] & 1) == 0

    @pl.when(even)
    def _():
        all_planes(far_ref, near_ref)

    @pl.when(jnp.logical_not(even))
    def _():
        all_planes(near_ref, far_ref)


def convolve(place, near, here, far, taps, small):
    planes, rows_y, channels, rows_z = here.shape
    pairs = (planes + 1) * rows_y // 2
    return pl.pallas_call(
        conv_kernel,
        out_shape=jax.ShapeDtypeStruct((pairs, channels, 2 * rows_z), BF16),
        in_specs=[SMEM] + [VMEM] * 5,
        out_specs=VMEM,
        scratch_shapes=[pltpu.VMEM((3, 3 * channels, 3 * channels), BF16)],
        compiler_params=pltpu.CompilerParams(vmem_limit_bytes=8 << 20),
        cost_estimate=pl.CostEstimate(flops=3 << 30, bytes_accessed=4 << 20, transcendentals=0),
        name="convolve",
    )(place, near, here, far, taps, small)


def interpolate(words, lat, planes, rows_y, rows_z):
    rows = words.shape[0]
    cell = jnp.broadcast_to(words[:, 0:1], (rows, LANES)).astype(jnp.int32)
    frac = [jnp.broadcast_to(words[:, 1 + d : 2 + d], (rows, LANES)) for d in range(3)]
    shift_z = rows_z.bit_length() - 1
    shift_y = rows_y.bit_length() - 1
    base_x = cell >> (shift_z + shift_y)
    base_y = (cell >> shift_z) & (rows_y - 1)
    base_z = cell & (rows_z - 1)
    spot = lax.broadcasted_iota(jnp.int32, (rows, rows_z), 1)
    part_z = jnp.where(spot == base_z, 1.0 - frac[2], 0.0) + jnp.where(
        spot == ((base_z + 1) & (rows_z - 1)), frac[2], 0.0
    )
    part_yz = []
    for y in range(rows_y):
        part_y = jnp.where(
            base_y == y, 1.0 - frac[1], jnp.where(base_y == (y - 1) % rows_y, frac[1], 0.0)
        )
        part_yz.append(part_y * part_z)
    total = None
    for x in range(planes + 1):
        part_x = jnp.where(base_x == x, 1.0 - frac[0], jnp.where(base_x == x - 1, frac[0], 0.0))
        for pair in range(rows_y // 2):
            sides = [(part_x * part_yz[2 * pair + half]).astype(BF16) for half in (0, 1)]
            term = mul(jnp.concatenate(sides, axis=1), lat[x * (rows_y // 2) + pair], NT)
            total = term if total is None else total + term
    return total.astype(BF16), base_x, base_y, base_z, frac


def folded(value):
    return jnp.sum(value.reshape(value.shape[0] // 8, 8, value.shape[1]), axis=0)


def main_kernel(
    plan,
    place_ref,
    lat,
    words_ref,
    small_ref,
    w_latent_hbm,
    w_pos_hbm,
    w_mid_hbm,
    w_out_hbm,
    send_ref,
    keep_ref,
    code,
    pos,
    z_one,
    one_high,
    one_low,
    mixed,
    two_high,
    two_low,
    back,
    mixed_back,
    first_high,
    first_low,
    sums_ref,
    d_both,
    out_t,
    d_out_t,
    packed,
    mid_high,
    mid_low,
    w_latent_ref,
    w_pos_ref,
    w_mid_ref,
    w_out_ref,
    sems,
):
    rows = plan.tiles * plan.slots
    hidden = w_mid_ref.shape[0]
    latents = w_latent_ref.shape[0]
    weights = fetches(
        (w_latent_hbm, w_pos_hbm, w_mid_hbm, w_out_hbm),
        (w_latent_ref, w_pos_ref, w_mid_ref, w_out_ref),
        sems,
    )
    planes, rows_z = plan.planes, lat.shape[2] // 2
    rows_y = lat.shape[0] // (planes + 1) * 2
    slots = rows // plan.tiles
    my_block = place_ref[0]
    my_tile = place_ref[1]
    my_replica = place_ref[2]
    always = my_tile >= 0

    words = words_ref[...]
    words = jnp.concatenate(
        [words] + [pltpu.roll(words, LANES - 16 * group, 1) for group in range(1, slots // 8)], axis=0
    )
    interp, base_x, base_y, base_z, frac = interpolate(words, lat, planes, rows_y, rows_z)
    code[...] = interp
    global_x = my_tile * planes + base_x
    lane = lax.broadcasted_iota(jnp.int32, (rows, LANES), 1)
    pos[...] = jnp.where(
        lane == 0,
        (global_x.astype(F32) + frac[0]) / (planes * plan.tiles),
        jnp.where(
            lane == 1,
            (base_y.astype(F32) + frac[1]) / rows_y,
            (base_z.astype(F32) + frac[2]) / rows_z,
        ),
    )

    for copy in weights:
        copy.wait()
    high, low = halves(w_latent_ref[...])
    z_one[...] = mul(interp, high) + mul(interp, low)
    high, low = halves(w_mid_ref[...])
    mid_high[...] = high
    mid_low[...] = low
    w_pos = [w_pos_ref[d : d + 1, :] for d in range(3)]
    square = w_pos[0] * w_pos[0] + w_pos[1] * w_pos[1] + w_pos[2] * w_pos[2]
    bias_one = small_ref[0:1, :]
    bias_two = small_ref[1:2, :]

    part_rows = rows // 2

    def at(part, index, block=None):
        first = (part * 5 + index) * part_rows
        if block is None:
            return slice(first, first + part_rows)
        return slice(first + block * BLOCK, first + (block + 1) * BLOCK)

    def rows_at(part, block):
        first = part * part_rows + block * BLOCK
        return slice(first, first + BLOCK)

    def store(refs, span, value):
        high, low = halves(value)
        refs[0][span, :] = high
        refs[1][span, :] = low

    def layer_one(part):
        refs = (one_high, one_low)
        for block in range(part_rows // BLOCK):
            here = rows_at(part, block)
            where = pos[here, :]
            pre = (
                z_one[here, :]
                + (where[:, 0:1] * w_pos[0] + where[:, 1:2] * w_pos[1] + where[:, 2:3] * w_pos[2])
                + bias_one
            )
            act = jnp.tanh(pre)
            slope = 1.0 - act * act
            curve = -2.0 * act * slope
            z_one[here, :] = act
            store(refs, at(part, 0, block), act)
            for d in range(3):
                store(refs, at(part, 1 + d, block), slope * w_pos[d])
            store(refs, at(part, 4, block), curve * square)

    def times_mid(dims, source, result, part):
        span = slice(part * 5 * part_rows, (part + 1) * 5 * part_rows)
        left = (source[0][span, :], source[1][span, :])
        result[span, :] = mul3(left, (mid_high[...], mid_low[...]), dims)

    def layer_two(part):
        refs = (two_high, two_low)
        for block in range(part_rows // BLOCK):
            act = jnp.tanh(mixed[at(part, 0, block), :] + bias_two)
            slope = 1.0 - act * act
            curve = -2.0 * act * slope
            store(refs, at(part, 0, block), act)
            mixed[at(part, 0, block), :] = act
            norm = None
            for d in range(3):
                tangent = mixed[at(part, 1 + d, block), :]
                store(refs, at(part, 1 + d, block), slope * tangent)
                norm = tangent * tangent if norm is None else norm + tangent * tangent
            store(refs, at(part, 4, block), slope * mixed[at(part, 4, block), :] + curve * norm)

    out_fields = jnp.concatenate([w_out_ref[...], jnp.zeros((3, hidden), F32)], axis=0)
    wo_high, wo_low = halves(out_fields)
    wo_three = jnp.concatenate([out_fields, wo_low.astype(F32), out_fields], axis=0).astype(BF16)
    wo_both = jnp.concatenate(
        [out_fields, wo_low.astype(F32), jnp.zeros((LANES - 16, hidden), F32)], axis=0
    ).astype(BF16)

    def outputs(part):
        span = slice(part * 5 * part_rows, (part + 1) * 5 * part_rows)
        both = mul(two_high[span, :], wo_both, NT)
        low = mul(two_low[span, :], wo_both, NT)
        for s in range(5):
            rows_s = slice(s * part_rows, (s + 1) * part_rows)
            both_t, low_t = both[rows_s].T, low[rows_s].T
            out_t[8 * s : 8 * s + 8, part * part_rows : (part + 1) * part_rows] = (
                both_t[0:8] + both_t[8:16] + low_t[0:8]
            )

    @pl.when(always)
    def _():
        layer_one(0)
        times_mid(NN, (one_high, one_low), mixed, 0)
        layer_one(1)
        times_mid(NN, (one_high, one_low), mixed, 1)
        layer_two(0)
        outputs(0)
        layer_two(1)
        outputs(1)

    words_t = words.T
    target = [words_t[4 + f : 5 + f, :] for f in range(5)]
    valid = words_t[9:10, :]
    value = [out_t[f : f + 1, :] + small_ref[2:3, f : f + 1] for f in range(5)]
    grad = [[out_t[8 * (d + 1) + f : 8 * (d + 1) + f + 1, :] for f in range(5)] for d in range(3)]
    laplace = [out_t[32 + f : 33 + f, :] for f in range(5)]
    velocity = value[2:5]
    advection = [
        velocity[0] * grad[0][f] + velocity[1] * grad[1][f] + velocity[2] * grad[2][f] for f in range(5)
    ]
    continuity = grad[0][2] + grad[1][3] + grad[2][4]
    momentum = [advection[2 + j] + grad[j][1] - VISCOSITY * laplace[2 + j] for j in range(3)]
    momentum[2] = momentum[2] - value[0]
    energy = advection[0] - DIFFUSIVITY * laplace[0]
    misfit = [value[f] - target[f] for f in range(5)]
    physics = (
        continuity * continuity
        + (momentum[0] * momentum[0] + momentum[1] * momentum[1] + momentum[2] * momentum[2])
        + energy * energy
    )
    squares = (
        misfit[0] * misfit[0]
        + misfit[1] * misfit[1]
        + misfit[2] * misfit[2]
        + misfit[3] * misfit[3]
        + misfit[4] * misfit[4]
    )
    point_loss = valid * (squares + RESIDUAL_WEIGHT * physics) * (1.0 / plan.query_total)

    rate = valid * (1.0 / plan.query_total)
    twice = RESIDUAL_WEIGHT * 2.0
    d_cont = rate * twice * continuity
    d_mom = [rate * twice * m for m in momentum]
    d_energy = rate * twice * energy
    d_value = [2.0 * rate * m for m in misfit]
    for d in range(3):
        d_value[2 + d] = d_value[2 + d] + (
            d_mom[0] * grad[d][2] + d_mom[1] * grad[d][3] + d_mom[2] * grad[d][4] + d_energy * grad[d][0]
        )
    d_value[0] = d_value[0] - d_mom[2]
    d_out_t[...] = jnp.zeros_like(d_out_t)
    for f in range(5):
        d_out_t[f : f + 1, :] = d_value[f]
    for d in range(3):
        first = 8 * (d + 1)
        d_out_t[first : first + 1, :] = d_energy * velocity[d]
        d_out_t[first + 1 : first + 2, :] = d_mom[d]
        for j in range(3):
            term = d_mom[j] * velocity[d]
            if j == d:
                term = term + d_cont
            d_out_t[first + 2 + j : first + 3 + j, :] = term
    d_out_t[32:33, :] = -DIFFUSIVITY * d_energy
    for j in range(3):
        d_out_t[34 + j : 35 + j, :] = -VISCOSITY * d_mom[j]

    def out_back(part):
        columns = slice(part * part_rows, (part + 1) * part_rows)
        wanted = jnp.concatenate([d_out_t[8 * s : 8 * s + 8, columns] for s in range(5)], axis=1)
        do_low = halves(wanted)[1].astype(F32)
        wanted = jnp.concatenate([wanted, wanted, do_low], axis=0).astype(BF16)
        back[part * 5 * part_rows : (part + 1) * 5 * part_rows, :] = mul(wanted, wo_three, TN)

    def second_back(part, total):
        refs = (d_both.at[:, :hidden], d_both.at[:, hidden:])
        for block in range(part_rows // BLOCK):
            act = mixed[at(part, 0, block), :]
            slope = 1.0 - act * act
            curve = -2.0 * act * slope
            cot_l = back[at(part, 4, block), :]
            d_slope = cot_l * mixed[at(part, 4, block), :]
            norm = None
            bent = 2.0 * curve * cot_l
            for d in range(3):
                tangent = mixed[at(part, 1 + d, block), :]
                cot_t = back[at(part, 1 + d, block), :]
                store(refs, at(part, 1 + d, block), slope * cot_t + bent * tangent)
                d_slope = d_slope + cot_t * tangent
                norm = tangent * tangent if norm is None else norm + tangent * tangent
            store(refs, at(part, 4, block), slope * cot_l)
            d_curve = cot_l * norm
            d_slope = d_slope - 2.0 * act * d_curve
            d_act = back[at(part, 0, block), :] - 2.0 * slope * d_curve - 2.0 * act * d_slope
            d_pre = slope * d_act
            store(refs, at(part, 0, block), d_pre)
            total = total + folded(d_pre)
        return total

    def first_back(part, sums):
        for block in range(part_rows // BLOCK):
            here = rows_at(part, block)
            act = z_one[here, :]
            slope = 1.0 - act * act
            curve = -2.0 * act * slope
            where = pos[here, :]
            cot_t = [mixed_back[at(part, 1 + d, block), :] for d in range(3)]
            cot_l = mixed_back[at(part, 4, block), :]
            d_curve = cot_l * square
            d_slope = cot_t[0] * w_pos[0] + cot_t[1] * w_pos[1] + cot_t[2] * w_pos[2] - 2.0 * act * d_curve
            d_act = mixed_back[at(part, 0, block), :] - 2.0 * slope * d_curve - 2.0 * act * d_slope
            d_pre = slope * d_act
            high, low = halves(d_pre)
            first_high[here, :] = high
            first_low[here, :] = low
            sums = (
                [sums[0] + folded(d_pre)]
                + [sums[1 + d] + folded(where[:, d : d + 1] * d_pre + slope * cot_t[d]) for d in range(3)]
                + [sums[4] + folded(curve * cot_l)]
            )
        return sums


    def put(part, first, value):
        while value.shape[0]:
            block, row = first // plan.main_rows, first % plan.main_rows
            count = min(value.shape[0], plan.main_rows - row)
            packed[2 * part + block, row : row + count, :] = value[:count]
            first, value = first + count, value[count:]

    def mid_gradient():
        both = mul(one_high[...], d_both[...], TN)
        both = both[:, :hidden] + both[:, hidden:] + mul(one_low[...], d_both[:, :hidden], TN)
        for part in range(hidden // LANES):
            put(part, 0, both[:, part * LANES : (part + 1) * LANES])

    @pl.when(always)
    def _():
        out_back(0)
        total = second_back(0, jnp.zeros((8, hidden), F32))
        out_back(1)
        times_mid(NT, (d_both.at[:, :hidden], d_both.at[:, hidden:]), mixed_back, 0)
        sums_ref[5] = second_back(1, total)
        times_mid(NT, (d_both.at[:, :hidden], d_both.at[:, hidden:]), mixed_back, 1)
        total = first_back(0, [jnp.zeros((8, hidden), F32)] * 5)
        mid_gradient()
        for number, value in enumerate(first_back(1, total)):
            sums_ref[number] = value

    sums = [sums_ref[number] for number in range(6)]
    d_square = jnp.sum(sums[4], axis=0, keepdims=True)
    grad_latent = mul(code[...], first_high[...], TN) + mul(code[...], first_low[...], TN)

    parts = [d_out_t[8 * s : 8 * s + 8, p * part_rows : (p + 1) * part_rows] for p in range(2) for s in range(5)]
    flat = jnp.concatenate(parts, axis=1)
    fl_high, fl_low = halves(flat)
    fl_both = jnp.concatenate([flat, fl_low.astype(F32)], axis=0).astype(BF16)
    grad_out = mul(fl_both, two_high[...])
    grad_out = grad_out[:8] + grad_out[8:] + mul(fl_high, two_low[...])

    lane_row = lax.broadcasted_iota(jnp.int32, (1, hidden), 1)
    last = jnp.where(lane_row == 5, jnp.sum(point_loss), 0.0)
    for f in range(5):
        last = last + jnp.where(lane_row == f, jnp.sum(d_value[f]), 0.0)
    grad_pos = [jnp.sum(sums[1 + d], axis=0, keepdims=True) + 2.0 * w_pos[d] * d_square for d in range(3)]
    misc = grad_pos + [
        jnp.sum(sums[0], axis=0, keepdims=True),
        jnp.sum(sums[5], axis=0, keepdims=True),
        last,
    ]
    misc = jnp.concatenate(misc + [jnp.zeros((2, hidden), F32)], axis=0)
    for part in range(hidden // LANES):
        lanes = slice(part * LANES, (part + 1) * LANES)
        put(part, hidden, grad_latent[:, lanes])
        packed[2 * part, plan.coded_rows :, :] = misc[:, lanes]
        packed[2 * part + 1, plan.coded_rows :, :] = grad_out[:, lanes]

    chosen = jnp.where(
        lane == jnp.broadcast_to(words[:, 10:11], (rows, LANES)).astype(jnp.int32), words[:, 9:10], 0.0
    ).astype(BF16)
    fields = jnp.concatenate(value + [jnp.zeros((3, rows), F32)], axis=0)
    source = (lax.broadcasted_iota(jnp.int32, (8, rows), 1) & (plan.tiles * 8 - 1)) >> 3
    spread = jnp.concatenate([jnp.where(source == t, fields, 0.0) for t in range(plan.tiles)], axis=0)
    high, middle, low = thirds(spread)
    spread = mul(high, chosen) + mul(middle, chosen) + mul(low, chosen)
    packed[:, plan.main_rows : plan.coded_rows, :] = jnp.zeros((8, plan.devices, LANES), F32)
    for t in range(plan.tiles):
        row = plan.main_rows + (my_replica * (plan.tiles // 8) + t // 8) * 8
        packed[t % 8, pl.ds(pl.multiple_of(row, 8), 8), :] = spread[8 * t : 8 * t + 8]

    for block in range(8):
        spot = jnp.bitwise_xor(block, my_block) & 3

        @pl.when((my_block >> 2) == block // 4)
        def _():
            keep_ref[spot] = packed[block]

        @pl.when((my_block >> 2) != block // 4)
        def _():
            encode(plan, lambda start, count: packed[block, start : start + count, :], send_ref.at[spot])


class Plan:
    def __init__(self, tiles, replicas, queries, planes, hidden, latents):
        self.tiles, self.replicas, self.planes = tiles, replicas, planes
        self.slots = 2 * queries // tiles
        self.devices = tiles * replicas
        self.query_total = float(queries * self.devices)
        self.main_rows = (hidden + latents) // 2
        self.coded_rows = self.main_rows + self.devices
        self.rows = self.coded_rows + 8
        self.scales = -(-(self.coded_rows // SUB + 1) // 16) * 16
        self.sent_rows = self.coded_rows + 16 + self.scales
        top = self.devices.bit_length() - 1
        self.core, self.plane, self.rest = [0], [1, top - 1], list(range(2, top - 1))

    def mask(self, bits, steps):
        return sum(1 << bit for number, bit in enumerate(bits) if steps >> number & 1)

    def my_block(self, device):
        return (device & 1) * 4 + (device >> 1 & 1) + 2 * (device >> self.plane[1] & 1)


def swapped(value, plan, bits, steps):
    mask = plan.mask(bits, steps)
    return lax.ppermute(value, ("replica", "tile"), [(i, i ^ mask) for i in range(plan.devices)])


def encode(plan, read, out_ref):
    starts = list(range(0, plan.coded_rows, SUB))
    parts = [read(start, SUB) for start in starts] + [read(plan.coded_rows, 8)]
    tops = [jnp.max(jnp.abs(part), axis=0, keepdims=True) for part in parts]
    tops = tops + [jnp.zeros_like(tops[0])] * (plan.scales - len(tops))
    power = jnp.floor(jnp.log2(jnp.maximum(jnp.concatenate(tops, axis=0), 1e-30)))
    scale = jnp.exp2(14.0 - power)

    def whole(value):
        return jnp.clip(jnp.round(value), -32767.0, 32767.0)

    def narrow(value):
        return value.astype(jnp.int32).astype(jnp.int16)

    for number, start in enumerate(starts):
        out_ref[start : start + SUB, :] = narrow(whole(parts[number] * scale[number : number + 1]))
    last = len(starts)
    exact = parts[last] * scale[last : last + 1]
    high = whole(exact)
    low = whole((exact - high) * 32768.0)
    out_ref[plan.coded_rows : plan.coded_rows + 16, :] = narrow(jnp.concatenate([high, low], axis=0))
    out_ref[plan.coded_rows + 16 :, :] = narrow(power)


def decoder(plan, ref):
    def widen(value):
        return value.astype(jnp.int32).astype(F32)

    scale = jnp.exp2(widen(ref[plan.coded_rows + 16 :, :]) - 14.0)

    def read(start, count):
        if start < plan.coded_rows:
            number = start // SUB
            return widen(ref[start : start + count, :]) * scale[number : number + 1]
        both = widen(ref[plan.coded_rows : plan.coded_rows + 16, :])
        number = plan.coded_rows // SUB
        return (both[:8] + both[8:] * (1.0 / 32768.0)) * scale[number : number + 1]

    return read


def added(readers):
    def read(start, count):
        total = readers[0](start, count)
        for reader in readers[1:]:
            total = total + reader(start, count)
        return total

    return read


def first_kernel(plan, numbers, keep_ref, got_ref, *refs):
    def reader(block):
        got = decoder(plan, got_ref.at[block])
        return lambda start, count: keep_ref[block, start : start + count, :] + got(start, count)

    for number, out_ref in zip(numbers, refs):
        if number:
            encode(plan, reader(number), out_ref)
        else:
            read = reader(0)
            for start in range(0, plan.coded_rows, SUB):
                out_ref[start : start + SUB, :] = read(start, SUB)
            out_ref[plan.coded_rows :, :] = read(plan.coded_rows, 8)


def first_sum(keep, got, numbers, plan):
    sent = jax.ShapeDtypeStruct((plan.sent_rows, LANES), jnp.int16)
    own = jax.ShapeDtypeStruct(keep.shape[1:], F32)
    return pl.pallas_call(
        functools.partial(first_kernel, plan, numbers),
        out_shape=tuple(sent if number else own for number in numbers),
        in_specs=[VMEM] * 2,
        out_specs=tuple([VMEM] * len(numbers)),
        compiler_params=pltpu.CompilerParams(vmem_limit_bytes=6 << 20),
        name="sum_core",
    )(keep, got)


def plane_kernel(plan, mine_ref, *refs):
    readers = [lambda start, count: mine_ref[start : start + count, :]]
    encode(plan, added(readers + [decoder(plan, ref) for ref in refs[:-1]]), refs[-1])


def pair_kernel(plan, mine_ref, other_ref, out_ref):
    encode(plan, added([decoder(plan, mine_ref), decoder(plan, other_ref)]), out_ref)


def coded_sum(kernel, blocks, plan, name):
    return pl.pallas_call(
        functools.partial(kernel, plan),
        out_shape=jax.ShapeDtypeStruct((plan.sent_rows, LANES), jnp.int16),
        in_specs=[VMEM] * len(blocks),
        out_specs=VMEM,
        compiler_params=pltpu.CompilerParams(vmem_limit_bytes=4 << 20),
        name=name,
    )(*blocks)


def main(place, lat, words, small, weights, plan):
    rows = plan.tiles * plan.slots
    hidden = weights[2].shape[0]
    channels = lat.shape[1]
    outs = jax.ShapeDtypeStruct((4, plan.rows, LANES), F32)
    wide = lambda kind: pltpu.VMEM((5 * rows, hidden), kind)
    return pl.pallas_call(
        functools.partial(main_kernel, plan),
        out_shape=(jax.ShapeDtypeStruct((4, plan.sent_rows, LANES), jnp.int16), outs),
        in_specs=[SMEM] + [VMEM] * 3 + [HBM] * 4,
        out_specs=(VMEM, VMEM),
        scratch_shapes=[
            pltpu.VMEM((rows, channels), BF16),
            pltpu.VMEM((rows, LANES), F32),
            pltpu.VMEM((rows, hidden), F32),
            wide(BF16),
            wide(BF16),
            wide(F32),
            wide(BF16),
            wide(BF16),
            wide(F32),
            wide(F32),
            pltpu.VMEM((rows, hidden), BF16),
            pltpu.VMEM((rows, hidden), BF16),
            pltpu.VMEM((6, 8, hidden), F32),
            pltpu.VMEM((5 * rows, 2 * hidden), BF16),
            pltpu.VMEM((40, rows), F32),
            pltpu.VMEM((40, rows), F32),
            pltpu.VMEM((8, plan.rows, LANES), F32),
            pltpu.VMEM((hidden, hidden), BF16),
            pltpu.VMEM((hidden, hidden), BF16),
        ]
        + [pltpu.VMEM(weight.shape, F32) for weight in weights]
        + [pltpu.SemaphoreType.DMA((4,))],
        compiler_params=pltpu.CompilerParams(vmem_limit_bytes=32 << 20),
        name="encode_decode",
    )(place, lat, words, small, *weights)


def unpack_kernel(plan, place_ref, *refs):
    sources, outs, packed = refs[:8], refs[8:-1], refs[-1]
    prediction_ref, latent_ref, pos_ref, one_ref, mid_ref, two_ref, out_ref, bias_out_ref, loss_ref = outs
    my_block = place_ref[0]
    device = place_ref[2] * plan.tiles + place_ref[1]
    starts = list(range(0, plan.coded_rows, SUB))
    for number, ref in enumerate(sources):
        read = decoder(plan, ref)
        block = jnp.bitwise_xor(number, my_block)
        for start in starts:
            packed[block, start : start + SUB, :] = read(start, SUB)
        packed[block, plan.coded_rows :, :] = read(plan.coded_rows, 8)

    hidden = mid_ref.shape[0]
    latents = latent_ref.shape[0]
    split = plan.main_rows
    for part in range(hidden // LANES):
        lanes = slice(part * LANES, (part + 1) * LANES)
        mid_ref[0:split, lanes] = packed[2 * part, 0:split, :]
        mid_ref[split:, lanes] = packed[2 * part + 1, 0 : hidden - split, :]
        latent_ref[:, lanes] = packed[2 * part + 1, hidden - split : split, :]
        misc = packed[2 * part, plan.coded_rows :, :]
        pos_ref[:, lanes] = misc[0:3]
        one_ref[:, lanes] = misc[3:4]
        two_ref[:, lanes] = misc[4:5]
        out_ref[:, lanes] = packed[2 * part + 1, plan.coded_rows : plan.coded_rows + 5, :]
        if part == 0:
            bias_out_ref[...] = misc[5:6, 0:5]
            loss_ref[...] = misc[5:6, 5:6]
    row = pl.multiple_of(plan.main_rows + (device >> 3) * 8, 8)
    fields = packed[device & 7, pl.ds(row, 8), :]
    for f in range(5):
        prediction_ref[f] = fields[f : f + 1]


def unpack(place, blocks, plan, hidden, latents):
    shapes = [
        (5, 1, LANES),
        (latents, hidden),
        (3, hidden),
        (1, hidden),
        (hidden, hidden),
        (1, hidden),
        (5, hidden),
        (1, 5),
        (1, 1),
    ]
    return pl.pallas_call(
        functools.partial(unpack_kernel, plan),
        out_shape=tuple(jax.ShapeDtypeStruct(shape, F32) for shape in shapes),
        in_specs=[SMEM] + [VMEM] * 8,
        out_specs=tuple([VMEM] * len(shapes)),
        scratch_shapes=[pltpu.VMEM((8, plan.rows, LANES), F32)],
        compiler_params=pltpu.CompilerParams(vmem_limit_bytes=16 << 20),
        name="unpack",
    )(place, *blocks)


def body(
    fields,
    convolution_weight,
    convolution_bias,
    query_owner,
    query_cell,
    query_frac,
    target,
    w_latent,
    w_pos,
    bias_one,
    w_mid,
    bias_two,
    w_out,
    bias_out,
):
    tiles = lax.axis_size("tile")
    replicas = lax.axis_size("replica")
    my_tile = lax.axis_index("tile")
    my_replica = lax.axis_index("replica")
    channels = fields.shape[1]
    queries = query_cell.shape[1]
    hidden = w_mid.shape[0]
    plan = Plan(tiles, replicas, queries, fields.shape[2], hidden, channels)
    device = my_replica * tiles + my_tile
    place = jnp.stack([plan.my_block(device), my_tile, my_replica]).astype(jnp.int32)

    here = fields[0].transpose(1, 2, 0, 3)
    odd = my_tile & 1
    count = DILATION_RATE + 1
    first = lax.dynamic_slice_in_dim(here, (1 - odd) * (here.shape[0] - count), count, axis=0)
    second = lax.dynamic_slice_in_dim(here, odd * (here.shape[0] - count), count, axis=0)
    first, second, query_owner = lax.optimization_barrier((first, second, query_owner))
    near = lax.ppermute(first, "tile", [(i, i ^ 1) for i in range(tiles)])
    far = lax.ppermute(second, "tile", [(i, (i - 1 + 2 * (i & 1)) % tiles) for i in range(tiles)])
    words, small = route(
        (query_owner[:, :, 0], query_cell, query_frac.transpose(1, 0, 2), target.transpose(1, 0, 2)),
        (bias_one[None], bias_two[None], bias_out[None], convolution_bias[None]),
        tiles,
        plan.slots,
    )
    words = lax.all_to_all(
        words.reshape(tiles, 8, WORDS), "tile", split_axis=0, concat_axis=0, tiled=True
    ).reshape(tiles * 8, WORDS)

    lat = convolve(place, near, here, far, convolution_weight, small)
    weights = (w_latent, w_pos, w_mid, w_out)
    send, keep = main(place, lat, words, small, weights, plan)

    got = swapped(send, plan, plan.core, 1)
    (far,) = first_sum(keep, got, (3,), plan)
    far, keep = lax.optimization_barrier((far, keep))
    mine, *near = first_sum(keep, got, (0, 1, 2), plan)
    arrived = [swapped(block, plan, plan.plane, step) for step, block in ((3, far), (1, near[0]), (2, near[1]))]
    block = coded_sum(plane_kernel, [mine] + arrived, plan, "sum_plane")
    for bit in plan.rest:
        block = coded_sum(pair_kernel, [block, swapped(block, plan, [bit], 1)], plan, "sum_line")
    blocks = [block] + [swapped(block, plan, plan.plane, step) for step in range(1, 4)]
    blocks = blocks + [swapped(block, plan, plan.core, 1) for block in blocks]
    prediction, g_latent, g_pos, g_one, g_mid, g_two, g_out, g_bias, loss = unpack(
        place, blocks, plan, hidden, channels
    )
    return (
        prediction.transpose(1, 0, 2),
        g_latent,
        g_pos,
        g_one.reshape(hidden),
        g_mid,
        g_two.reshape(hidden),
        g_out,
        g_bias.reshape(5),
        loss.reshape(()),
    )


def solution(mesh):
    return jax.shard_map(
        body,
        mesh=mesh,
        in_specs=(
            P("replica", None, "tile", None, None),
            P(),
            P(),
            P("replica", "tile", None),
            P("replica", "tile"),
            P("replica", None, "tile"),
            P("replica", None, "tile"),
            P(),
            P(),
            P(),
            P(),
            P(),
            P(),
            P(),
        ),
        out_specs=(P("replica", None, "tile"), P(), P(), P(), P(), P(), P(), P(), P()),
        check_vma=False,
    )
```
